32 devices in a mesh: dp: 8 (over z, x), mp: 4 (over y, core).
Axes of the slice: x: 2, y: 2, z: 4, core: 2. Of those that a mesh axis runs over, the one named last changes fastest.
Arguments:
- encoder_input: bfloat16 [12288, 512], P(('dp', 'mp')), may hold values from -6 to 6
- decoder_copy: bfloat16 [12288, 512], P(('dp', 'mp')), may hold values from -6 to 6
- decoder_target: bfloat16 [12288, 512], P(('dp', 'mp')), may hold values from -6 to 6
- decoder_cotangent: bfloat16 [12288, 512], P(('dp', 'mp')), may hold values from -6 to 6
- source_segments: int32 [8, 1536], P('dp'), may hold values from 0 to 23, never falling along the last dimension, each value on 1 to 128 neighbouring positions
- target_segments: int32 [8, 1536], P('dp'), may hold values from 0 to 23, never falling along the last dimension, each value on 1 to 128 neighbouring positions
- glance_mask: int32 [8, 1536], P('dp', 'mp'), may hold values 0 or 1
- attention_in: float32 [9, 512, 512], P(None, 'dp', 'mp')
- attention_out: float32 [3, 512, 512], P(None, 'mp', 'dp')
- feed_in: float32 [2, 512, 2048], P(None, 'dp', 'mp')
- feed_out: float32 [2, 2048, 512], P(None, 'mp', 'dp')
- norm_params: float32 [5, 2, 512], P(None, None, 'dp')
- attention_in_first: float32 [9, 512, 512], P(None, 'dp', 'mp')
- attention_out_first: float32 [3, 512, 512], P(None, 'mp', 'dp')
- feed_in_first: float32 [2, 512, 2048], P(None, 'dp', 'mp')
- feed_out_first: float32 [2, 2048, 512], P(None, 'mp', 'dp')
- norm_params_first: float32 [5, 2, 512], P(None, None, 'dp')
- attention_in_second: float32 [9, 512, 512], P(None, 'dp', 'mp'), as said below
- attention_out_second: float32 [3, 512, 512], P(None, 'mp', 'dp'), as said below
- feed_in_second: float32 [2, 512, 2048], P(None, 'dp', 'mp'), as said below
- feed_out_second: float32 [2, 2048, 512], P(None, 'mp', 'dp'), as said below
- norm_params_second: float32 [5, 2, 512], P(None, None, 'dp'), as said below
Outputs:
- encoder_output: bfloat16 [12288, 512], P(('dp', 'mp'))
- decoder_output: bfloat16 [12288, 512], P(('dp', 'mp'))
- encoder_input_grad: float32 [12288, 512], P(('dp', 'mp'))
- decoder_input_grad: float32 [12288, 512], P(('dp', 'mp'))
- grad_norm: float32 [], replicated
- attention_in_new: float32 [9, 512, 512], P(None, 'dp', 'mp')
- attention_out_new: float32 [3, 512, 512], P(None, 'mp', 'dp')
- feed_in_new: float32 [2, 512, 2048], P(None, 'dp', 'mp')
- feed_out_new: float32 [2, 2048, 512], P(None, 'mp', 'dp')
- norm_params_new: float32 [5, 2, 512], P(None, None, 'dp')
- attention_in_first_new: float32 [9, 512, 512], P(None, 'dp', 'mp')
- attention_out_first_new: float32 [3, 512, 512], P(None, 'mp', 'dp')
- feed_in_first_new: float32 [2, 512, 2048], P(None, 'dp', 'mp')
- feed_out_first_new: float32 [2, 2048, 512], P(None, 'mp', 'dp')
- norm_params_first_new: float32 [5, 2, 512], P(None, None, 'dp')
- attention_in_second_new: float32 [9, 512, 512], P(None, 'dp', 'mp')
- attention_out_second_new: float32 [3, 512, 512], P(None, 'mp', 'dp')
- feed_in_second_new: float32 [2, 512, 2048], P(None, 'dp', 'mp')
- feed_out_second_new: float32 [2, 2048, 512], P(None, 'mp', 'dp')
- norm_params_second_new: float32 [5, 2, 512], P(None, None, 'dp')
The draws below stay inside these ranges and needn't reach their ends.
Inputs may be any that keep to these rules, and one draw needn't show every extreme that they name: `source_segments`: in each row segment numbers start at 0, never fall and end at 23; every sentence has 1 to 128 positions. `target_segments`: in each row segment numbers start at 0, never fall and end at 23; every sentence has 1 to 128 positions. `attention_in_second`: positive. `attention_out_second`: positive. `feed_in_second`: positive. `feed_out_second`: positive. `norm_params_second`: positive.
All inputs are finite; a program needn't handle non-finite values. No bound on the sum of `glance_mask` on one device may be relied on, other than what follows from the above.
Results may differ from the reference program's by a relative error of at most 0.03.
The reference program's roundings to bfloat16 on the way count: a program that leaves them out, or rounds other values in their place, can miss the bound.
Values may be sent and summed in bfloat16 or wider, within the bound.
No kernel may reach another device: no remote copies, remote signals or barrier semaphores. Data moves between devices by JAX's collectives and lax.ppermute only.
A program may use at most 192 MiB of HBM per device.

```python
import math
import jax
import jax.numpy as jnp
import numpy as np
from jax import lax

D = 512
FF = 2048
HEADS = 8
HEAD_DIM = 64
TOK_DEV = 1536
SEG_MOST = 128
STEP = 10
SEGS = 24
ROWS = 8
TOKENS = 12288
PARAMS = 7345152


clip_level = 1.0


def rising(count, lower_end, upper_end):
    return lower_end + (upper_end - lower_end) * jnp.arange(count, dtype=jnp.float32) / max(count - 1, 1)


def moment_scale(kind_factor):
    return kind_factor * clip_level / math.sqrt(PARAMS)


def first_values(key, shape, kind_factor):
    return 0.111 * moment_scale(kind_factor) * jax.random.normal(key, shape, jnp.float32)


def second_values(key, shape, kind_factor):
    factor = jnp.exp(jax.random.uniform(key, shape, jnp.float32, 0.0, 1.3863))
    return 0.0204 * moment_scale(kind_factor) ** 2 * factor


def draw_attention_in(key, part):
    key = jax.random.fold_in(key, 101)
    values = jax.random.normal(key, (9, D, D), jnp.float32)
    slope = rising(D, 0.6, 1.8)
    chosen = (jnp.arange(9) % 3 == 2)[:, None, None]
    factor = jnp.where(chosen, slope[None, None, :], 1.0)
    return values * factor * D ** (-0.5)


def draw_attention_out(key, part):
    key = jax.random.fold_in(key, 102)
    values = jax.random.normal(key, (3, D, D), jnp.float32)
    slope = rising(D, 0.6, 1.8)
    return values * slope[None, :, None] * 4.0 * D ** (-0.5)


def draw_feed_in(key, part):
    key = jax.random.fold_in(key, 103)
    values = jax.random.normal(key, (2, D, FF), jnp.float32)
    slope = rising(FF, 0.6, 1.8)
    return values * slope[None, None, :] * D ** (-0.5)


def draw_feed_out(key, part):
    key = jax.random.fold_in(key, 104)
    values = jax.random.normal(key, (2, FF, D), jnp.float32)
    slope = rising(FF, 0.6, 1.8)
    return values * slope[None, :, None] * FF ** (-0.5)


def draw_norm_params(key, part):
    key = jax.random.fold_in(key, 105)
    gain_key, shift_key = jax.random.split(key)
    noise = jax.random.normal(gain_key, (5, D), jnp.float32)
    shifts = 0.3 * jax.random.normal(shift_key, (5, D), jnp.float32)
    slope = rising(D, 0.6, 1.8)
    gains = slope[None, :] * (1.0 + 0.1 * noise)
    return jnp.stack([gains, shifts], axis=1)


def draw_attention_in_first(key, part):
    key = jax.random.fold_in(key, 111)
    return first_values(key, (9, D, D), 1.0)


def draw_attention_out_first(key, part):
    key = jax.random.fold_in(key, 112)
    return first_values(key, (3, D, D), 1.0)


def draw_feed_in_first(key, part):
    key = jax.random.fold_in(key, 113)
    return first_values(key, (2, D, FF), 1.0)


def draw_feed_out_first(key, part):
    key = jax.random.fold_in(key, 114)
    return first_values(key, (2, FF, D), 1.0)


def draw_norm_params_first(key, part):
    key = jax.random.fold_in(key, 115)
    return first_values(key, (5, 2, D), 3.0)


def draw_attention_in_second(key, part):
    key = jax.random.fold_in(key, 121)
    return second_values(key, (9, D, D), 1.0)


def draw_attention_out_second(key, part):
    key = jax.random.fold_in(key, 122)
    return second_values(key, (3, D, D), 1.0)


def draw_feed_in_second(key, part):
    key = jax.random.fold_in(key, 123)
    return second_values(key, (2, D, FF), 1.0)


def draw_feed_out_second(key, part):
    key = jax.random.fold_in(key, 124)
    return second_values(key, (2, FF, D), 1.0)


def draw_norm_params_second(key, part):
    key = jax.random.fold_in(key, 125)
    return second_values(key, (5, 2, D), 3.0)


def set_ends(values, key, low, largest):
    longest = values.shape.index(max(values.shape))
    spots = []
    for shift in (0, 1):
        where = [jax.random.randint(jax.random.fold_in(key, axis), (), 0, length) for axis, length in enumerate(values.shape)]
        where[longest] = (where[longest] + shift) % values.shape[longest]
        spots.append(tuple(where))
    return values.at[spots[0]].set(low).at[spots[1]].set(largest)


def levels(key, dims, shards, low, largest):
    loudness = 1.0
    for dim, blocks in shards:
        steps = jax.random.uniform(jax.random.fold_in(jax.random.fold_in(key, 6), dim), (blocks,), jnp.float32, low / len(shards), largest / len(shards))
        loudness = loudness * jnp.repeat(jnp.exp(steps), dims[dim] // blocks).reshape((-1,) + (1,) * (len(dims) - 1 - dim))
    return loudness


def split_up(count, total, most, skew):
    loads = [(1 << 20) // math.isqrt(standing ** skew) + 1 for standing in range(2, count + 1)]
    spare, counts = total - most - (count - 1), [1] * (count - 1)
    while spare > 0:
        movable = [i for i in range(count - 1) if counts[i] < most]
        whole, budget = sum([loads[i] for i in movable]), spare
        for i in movable:
            addition = min(most - counts[i], max(1, budget * loads[i] // whole), spare)
            counts[i] = counts[i] + addition
            spare = spare - addition
    return np.array([most] + counts)


def ragged(own_key, amount, total, most, skew):
    if amount == 2:
        one = jax.random.randint(own_key, (), max(1, total - most), min(most, total - 1) + 1)
        return jnp.stack([one, total - one])
    lengths = jnp.asarray(split_up(amount, total, most, skew), jnp.int32)
    couples = (amount - 1) // 2
    giver, sink = lengths[1:1 + 2 * couples:2], lengths[2:2 + 2 * couples:2]
    room = jnp.minimum(giver - 1, most - sink)
    passed = jax.random.randint(jax.random.fold_in(own_key, 1), (couples,), 0, 1 << 20) % (room + 1)
    lengths = lengths.at[1:1 + 2 * couples:2].set(giver - passed).at[2:2 + 2 * couples:2].set(sink + passed)
    return lengths[jax.random.permutation(jax.random.fold_in(own_key, 2), amount)]


def gaussian(key, shape, scale, bound, cuts=(), held_as=jnp.bfloat16):
    entries = jax.random.normal(key, shape, jnp.float32) * scale
    if len(cuts) > 0:
        entries = levels(key, shape, cuts, -0.22, 0.18) * entries
    return jnp.clip(entries, min=-bound, max=bound).astype(held_as)


def setup_inputs(seed: int = 0) -> dict:
    key_list = jax.random.split(jax.random.key(seed), 23)
    encoder_input = gaussian(key_list[0], (TOKENS, D), 1.0, 6.0, ((0, 32),))
    decoder_copy = gaussian(key_list[1], (TOKENS, D), 1.0, 6.0, ((0, 32),))
    decoder_target = gaussian(key_list[2], (TOKENS, D), 1.0, 6.0, ((0, 32),))
    decoder_cotangent = gaussian(key_list[3], (TOKENS, D), 1.0, 6.0, ((0, 32),))
    source_segments = jax.vmap(lambda own: jnp.searchsorted(jnp.cumsum(ragged(own, SEGS, TOK_DEV, SEG_MOST, 1)), jnp.arange(TOK_DEV), side="right"))(jax.random.split(key_list[4], ROWS)).reshape((ROWS, TOK_DEV)).astype(jnp.int32)
    target_segments = jax.vmap(lambda own: jnp.searchsorted(jnp.cumsum(ragged(own, SEGS, TOK_DEV, SEG_MOST, 1)), jnp.arange(TOK_DEV), side="right"))(jax.random.split(key_list[5], ROWS)).reshape((ROWS, TOK_DEV)).astype(jnp.int32)
    glance_mask = set_ends((jax.random.randint(key_list[6], (ROWS, TOK_DEV), 0, 5) < 2).astype(jnp.int32), jax.random.fold_in(key_list[6], 1), 0, 1)
    attention_in = draw_attention_in(jax.random.fold_in(key_list[22], 71), 0)
    attention_out = draw_attention_out(jax.random.fold_in(key_list[22], 71), 0)
    feed_in = draw_feed_in(jax.random.fold_in(key_list[22], 71), 0)
    feed_out = draw_feed_out(jax.random.fold_in(key_list[22], 71), 0)
    norm_params = draw_norm_params(jax.random.fold_in(key_list[22], 71), 0)
    attention_in_first = draw_attention_in_first(jax.random.fold_in(key_list[22], 71), 0)
    attention_out_first = draw_attention_out_first(jax.random.fold_in(key_list[22], 71), 0)
    feed_in_first = draw_feed_in_first(jax.random.fold_in(key_list[22], 71), 0)
    feed_out_first = draw_feed_out_first(jax.random.fold_in(key_list[22], 71), 0)
    norm_params_first = draw_norm_params_first(jax.random.fold_in(key_list[22], 71), 0)
    attention_in_second = draw_attention_in_second(jax.random.fold_in(key_list[22], 71), 0)
    attention_out_second = draw_attention_out_second(jax.random.fold_in(key_list[22], 71), 0)
    feed_in_second = draw_feed_in_second(jax.random.fold_in(key_list[22], 71), 0)
    feed_out_second = draw_feed_out_second(jax.random.fold_in(key_list[22], 71), 0)
    norm_params_second = draw_norm_params_second(jax.random.fold_in(key_list[22], 71), 0)
    return {"encoder_input": encoder_input, "decoder_copy": decoder_copy, "decoder_target": decoder_target, "decoder_cotangent": decoder_cotangent, "source_segments": source_segments, "target_segments": target_segments, "glance_mask": glance_mask, "attention_in": attention_in, "attention_out": attention_out, "feed_in": feed_in, "feed_out": feed_out, "norm_params": norm_params, "attention_in_first": attention_in_first, "attention_out_first": attention_out_first, "feed_in_first": feed_in_first, "feed_out_first": feed_out_first, "norm_params_first": norm_params_first, "attention_in_second": attention_in_second, "attention_out_second": attention_out_second, "feed_in_second": feed_in_second, "feed_out_second": feed_out_second, "norm_params_second": norm_params_second}


norm_eps = 1e-05
beta_one = 0.9
beta_two = 0.98
adam_eps = 1e-08
weight_decay = 0.01
rate_matrix = 0.1
rate_norm = 0.5
clip_bound = 1.0
masked_score = -1e+30

@jax.custom_vjp
def low(v):
    return lax.optimization_barrier(v.astype(jnp.bfloat16)).astype(jnp.float32)

@jax.custom_vjp
def low_back(v):
    return v

def low_keep(v):
    return (low(v), None)

def low_pass(kept, grad):
    return (grad,)

def back_keep(v):
    return (v, None)

def back_low(kept, grad):
    return (low(grad),)
low.defvjp(low_keep, low_pass)
low_back.defvjp(back_keep, back_low)

def matmul(operand, weights):
    return jnp.dot(operand, weights, precision=lax.Precision.HIGHEST, preferred_element_type=jnp.float32)

def rounded_both(values):
    return low_back(low(values))

def layer_norm(totals, norm_gain, norm_shift):
    centred = totals - lax.optimization_barrier(jnp.mean(totals, axis=-1, keepdims=True))
    spread = lax.optimization_barrier(jnp.mean(centred * centred, axis=-1, keepdims=True))
    return centred * lax.rsqrt(spread + norm_eps) * norm_gain + norm_shift

def attention(query_rows, key_rows, weights_query, weights_key, weights_value, weights_out, query_segments, key_segments):
    length_query = query_rows.shape[0]
    length_key = key_rows.shape[0]
    queries = rounded_both(matmul(query_rows, weights_query)).reshape(length_query, HEADS, HEAD_DIM)
    keys_all = rounded_both(matmul(key_rows, weights_key)).reshape(length_key, HEADS, HEAD_DIM)
    values_all = rounded_both(matmul(key_rows, weights_value)).reshape(length_key, HEADS, HEAD_DIM)
    scores = jnp.einsum('qhd,khd->hqk', queries, keys_all, precision=lax.Precision.HIGHEST) * HEAD_DIM ** (-0.5)
    scores = low_back(scores)
    allowed = query_segments[:, None] == key_segments[None, :]
    scores = jnp.where(allowed[None], scores, masked_score)
    attention_probs = low(jax.nn.softmax(scores, axis=-1))
    context = jnp.einsum('hqk,khd->qhd', attention_probs, values_all, precision=lax.Precision.HIGHEST)
    context = rounded_both(context.reshape(length_query, HEADS * HEAD_DIM))
    return low_back(matmul(context, weights_out))

def feed_forward(rows_low, weights_first, weights_second):
    pre_values = low_back(matmul(rows_low, weights_first))
    hidden_values = low(jax.nn.gelu(pre_values))
    return low_back(matmul(hidden_values, weights_second))

def row_forward(params, encoder_row, decoder_row, source_row, target_row):
    attention_in, attention_out, feed_in, feed_out, norm_params = params
    branch = attention(encoder_row, encoder_row, attention_in[0], attention_in[1], attention_in[2], attention_out[0], source_row, source_row)
    first_norm = layer_norm(encoder_row + branch, norm_params[0, 0], norm_params[0, 1])
    branch = feed_forward(low(first_norm), feed_in[0], feed_out[0])
    second_norm = layer_norm(first_norm + branch, norm_params[1, 0], norm_params[1, 1])
    memory = low(second_norm)
    branch = attention(decoder_row, decoder_row, attention_in[3], attention_in[4], attention_in[5], attention_out[1], target_row, target_row)
    third_norm = layer_norm(decoder_row + branch, norm_params[2, 0], norm_params[2, 1])
    branch = attention(low(third_norm), memory, attention_in[6], attention_in[7], attention_in[8], attention_out[2], target_row, source_row)
    fourth_norm = layer_norm(third_norm + branch, norm_params[3, 0], norm_params[3, 1])
    branch = feed_forward(low(fourth_norm), feed_in[1], feed_out[1])
    fifth_norm = layer_norm(fourth_norm + branch, norm_params[4, 0], norm_params[4, 1])
    return (memory, fifth_norm)

def adam_step(weights, first, second, grads, rate, decay):
    first_new = beta_one * first + (1.0 - beta_one) * grads
    second_new = beta_two * second + (1.0 - beta_two) * grads * grads
    first_hat = first_new / (1.0 - beta_one ** STEP)
    second_hat = second_new / (1.0 - beta_two ** STEP)
    weights_new = weights - rate * (first_hat / (jnp.sqrt(second_hat) + adam_eps) + decay * weights)
    return (weights_new, first_new, second_new)

def reference(encoder_input, decoder_copy, decoder_target, decoder_cotangent, source_segments, target_segments, glance_mask, attention_in, attention_out, feed_in, feed_out, norm_params, attention_in_first, attention_out_first, feed_in_first, feed_out_first, norm_params_first, attention_in_second, attention_out_second, feed_in_second, feed_out_second, norm_params_second):
    masters = (attention_in, attention_out, feed_in, feed_out, norm_params)
    params = tuple((low(weights) for weights in masters))
    shape_rows = (ROWS, TOK_DEV, D)
    encoder_rows = encoder_input.astype(jnp.float32).reshape(shape_rows)
    picked = (glance_mask == 1)[..., None]
    decoder_rows = jnp.where(picked, decoder_target.astype(jnp.float32).reshape(shape_rows), decoder_copy.astype(jnp.float32).reshape(shape_rows))
    cotangent_rows = decoder_cotangent.astype(jnp.float32).reshape(shape_rows)

    def one_row(summed, inputs_row):
        encoder_row, decoder_row, cotangent_row, source_row, target_row = inputs_row

        def forward(weights_all, encoder_values, decoder_values):
            return row_forward(weights_all, encoder_values, decoder_values, source_row, target_row)
        outputs, pullback = jax.vjp(forward, params, encoder_row, decoder_row)
        weight_grads, encoder_grad, decoder_grad = pullback((jnp.zeros_like(outputs[0]), cotangent_row))
        summed = jax.tree.map(jnp.add, summed, weight_grads)
        return (summed, (outputs[0], outputs[1], encoder_grad, decoder_grad))
    initial = tuple((jnp.zeros_like(weights) for weights in params))
    grads, stacked = lax.scan(one_row, initial, (encoder_rows, decoder_rows, cotangent_rows, source_segments, target_segments))
    shape_flat = (TOKENS, D)
    encoder_output = stacked[0].reshape(shape_flat).astype(jnp.bfloat16)
    decoder_output = stacked[1].reshape(shape_flat).astype(jnp.bfloat16)
    encoder_input_grad = stacked[2].reshape(shape_flat)
    decoder_input_grad = stacked[3].reshape(shape_flat)
    squares = jnp.float32(0.0)
    for grad_part in grads:
        squares = squares + jnp.sum(grad_part * grad_part)
    grad_norm = jnp.sqrt(squares)
    factor = clip_bound / jnp.maximum(grad_norm, clip_bound)
    firsts = (attention_in_first, attention_out_first, feed_in_first, feed_out_first, norm_params_first)
    seconds = (attention_in_second, attention_out_second, feed_in_second, feed_out_second, norm_params_second)
    results = []
    for number in range(5):
        rate = rate_norm if number == 4 else rate_matrix
        decay = 0.0 if number == 4 else weight_decay
        results.append(adam_step(masters[number], firsts[number], seconds[number], grads[number] * factor, rate, decay))
    return (encoder_output, decoder_output, encoder_input_grad, decoder_input_grad, grad_norm, results[0][0], results[1][0], results[2][0], results[3][0], results[4][0], results[0][1], results[1][1], results[2][1], results[3][1], results[4][1], results[0][2], results[1][2], results[2][2], results[3][2], results[4][2])
```

```python
import functools

import jax
import jax.numpy as jnp
from jax import lax
from jax.experimental import pallas as pl
from jax.experimental.pallas import tpu as pltpu
from jax.sharding import Mesh
from jax.sharding import PartitionSpec as P

HEAD_DIM = 64
STEP = 10
BLOCK = 128
PAIR = 2 * HEAD_DIM

norm_eps = 1e-05
beta_one = 0.9
beta_two = 0.98
adam_eps = 1e-08
weight_decay = 0.01
rate_matrix = 0.1
rate_norm = 0.5
clip_bound = 1.0
masked_score = -1e30
score_scale = HEAD_DIM ** (-0.5)
gelu_a = 0.7978845608028654
gelu_b = 0.044715

F32 = jnp.float32
BF16 = jnp.bfloat16
ANY = pl.ANY
SMEM = pltpu.SMEM
VMEM = pltpu.VMEM

NN = (((1,), (0,)), ((), ()))
NT = (((1,), (1,)), ((), ()))


def mm(a, b, dims=NN):
    return lax.dot_general(a, b, dims, preferred_element_type=F32)


def vmem(count=1):
    return [pl.BlockSpec(memory_space=VMEM)] * count


def params(mib):
    return pltpu.CompilerParams(vmem_limit_bytes=mib * 1024 * 1024)


def shaped(shape, dtype):
    return jax.ShapeDtypeStruct(shape, dtype)


def normalize(total):
    centred = total - jnp.mean(total, axis=-1, keepdims=True)
    spread = jnp.mean(centred * centred, axis=-1, keepdims=True)
    rstd = lax.rsqrt(spread + norm_eps)
    return centred * rstd, rstd


def norm_backward(grad_out, xhat, rstd, gain):
    scaled = grad_out * gain
    first = jnp.mean(scaled, axis=-1, keepdims=True)
    second = jnp.mean(scaled * xhat, axis=-1, keepdims=True)
    return rstd * (scaled - first - xhat * second)


def norm_param_grads(grad_out, xhat):
    return (
        jnp.sum(grad_out * xhat, axis=0, keepdims=True),
        jnp.sum(grad_out, axis=0, keepdims=True),
    )


def half_masks():
    lane = lax.broadcasted_iota(jnp.int32, (1, PAIR), 1)
    low = jnp.where(lane < HEAD_DIM, 1.0, 0.0).astype(BF16)
    high = jnp.where(lane < HEAD_DIM, 0.0, 1.0).astype(BF16)
    return low, high


def stack_pair(values, masks):
    return jnp.concatenate([values * masks[0], values * masks[1]], axis=0)


def weight_copies(w_hbm, w_vmem, sems):
    blocks, depth, width = w_hbm.shape
    part = width // 4
    copies = []
    for kind in range(4):
        copies.append([])
        for block in range(blocks):
            copies[kind].append(
                pltpu.make_async_copy(
                    w_hbm.at[block, :, pl.ds(kind * part, part)],
                    w_vmem.at[:, pl.ds((kind * blocks + block) * part, part)],
                    sems.at[kind, block],
                )
            )
    return copies


def grad_copies(dw_vmem, dw_hbm, sems):
    blocks, depth, width = dw_hbm.shape
    part = width // 4
    copies = []
    for kind in range(4):
        copies.append([])
        for block in range(blocks):
            copies[kind].append(
                pltpu.make_async_copy(
                    dw_vmem.at[:, pl.ds((kind * blocks + block) * part, part)],
                    dw_hbm.at[block, :, pl.ds(kind * part, part)],
                    sems.at[kind, block],
                )
            )
    return copies


def start_all(groups):
    for group in groups:
        for copy in group:
            copy.start()


def wait_all(group):
    for copy in group:
        copy.wait()


def self_forward_kernel(
    x_ref, segq_ref, segk_ref, w_hbm, norm_ref,
    xhat_ref, rstd_ref, q_ref, k_ref, v_ref, ctx_ref, pt_ref,
    w_vmem, vt_s, ctxt_s, sems,
):
    copies = weight_copies(w_hbm, w_vmem, sems)
    start_all([copies[1], copies[2], copies[0], copies[3]])
    rows, width = q_ref.shape
    blocks, pairs = rows // BLOCK, width // PAIR
    window = 3 * BLOCK
    wait_all(copies[1])
    wait_all(copies[2])
    kv = mm(x_ref[...], w_vmem[:, width : 3 * width]).astype(BF16)
    k_ref[...] = kv[:, :width]
    v_ref[...] = kv[:, width:]
    vt_s[...] = kv[:, width:].T
    wait_all(copies[0])
    q = mm(x_ref[BLOCK : BLOCK + rows, :], w_vmem[:, :width]).astype(BF16)
    q_ref[...] = q * jnp.asarray(score_scale, BF16)
    masks = half_masks()
    for block in range(blocks):
        at = pl.ds(block * BLOCK, BLOCK)
        keys_at = pl.ds(block * BLOCK, window)
        allowed = segk_ref[keys_at, :] == segq_ref[block : block + 1, :]
        for pair in range(pairs):
            cols = pl.ds(pair * PAIR, PAIR)
            stacked = stack_pair(q_ref[at, cols], masks)
            scores = mm(k_ref[keys_at, cols], stacked, NT)
            scores = jnp.where(allowed, scores, masked_score)
            highest = jnp.max(scores, axis=0, keepdims=True)
            raised = jnp.exp(scores - highest)
            total = jnp.sum(raised, axis=0, keepdims=True)
            probs = (raised * (1.0 / total)).astype(BF16)
            pt_ref[block * pairs + pair] = probs
            context = mm(vt_s[cols, keys_at], probs).astype(BF16)
            ctxt_s[pl.ds(pair * PAIR, HEAD_DIM), at] = context[:HEAD_DIM, :BLOCK]
            ctxt_s[pl.ds(pair * PAIR + HEAD_DIM, HEAD_DIM), at] = context[HEAD_DIM:, BLOCK:]
    context = ctxt_s[...].T
    ctx_ref[...] = context
    wait_all(copies[3])
    branch = mm(context, w_vmem[:, 3 * width :], NT)
    xhat, rstd = normalize(x_ref[BLOCK : BLOCK + rows, :].astype(F32) + branch)
    xhat_ref[...] = xhat
    rstd_ref[...] = rstd


def self_forward(x, segq, segk, weights, norm):
    keys, width = x.shape
    rows = keys - 2 * BLOCK
    blocks, pairs = rows // BLOCK, width // PAIR
    return pl.pallas_call(
        self_forward_kernel,
        out_shape=(
            shaped((rows, width), F32),
            shaped((rows, 1), F32),
            shaped((rows, width), BF16),
            shaped((keys, width), BF16),
            shaped((keys, width), BF16),
            shaped((rows, width), BF16),
            shaped((blocks * pairs, 3 * BLOCK, 2 * BLOCK), BF16),
        ),
        in_specs=vmem(3) + [pl.BlockSpec(memory_space=ANY)] + vmem(1),
        out_specs=tuple(vmem(7)),
        scratch_shapes=[
            pltpu.VMEM((width, 4 * width), BF16),
            pltpu.VMEM((width, keys), BF16),
            pltpu.VMEM((width, rows), BF16),
            pltpu.SemaphoreType.DMA((4, weights.shape[0])),
        ],
        compiler_params=params(32),
        name="self_forward",
    )(x, segq, segk, weights, norm)


def self_backward_kernel(
    dy_ref, xhat_ref, rstd_ref, norm_ref, w_hbm, x_ref, q_ref, k_ref, v_ref, ctx_ref, pt_ref,
    dx_ref, dnorm_ref, dw_hbm,
    w_vmem, dw_s, dctx_s, kt_s, dqt_s, dkv_s, sems, out_sems,
):
    copies = weight_copies(w_hbm, w_vmem, sems)
    start_all([copies[3], copies[0], copies[1], copies[2]])
    out_copies = grad_copies(dw_s, dw_hbm, out_sems)
    rows, width = q_ref.shape
    blocks, pairs = rows // BLOCK, width // PAIR
    window = 3 * BLOCK
    masks = half_masks()
    dy = dy_ref[...]
    xhat = xhat_ref[...]
    dgain, dshift = norm_param_grads(dy, xhat)
    dnorm_ref[0:1, :] = dgain
    dnorm_ref[1:2, :] = dshift
    dtotal = norm_backward(dy, xhat, rstd_ref[...], norm_ref[0:1, :])
    low = dtotal.astype(BF16)
    wait_all(copies[3])
    dctx_s[...] = mm(low, w_vmem[:, 3 * width :]).astype(BF16)
    dw_s[:, 3 * width :] = mm(low.T, ctx_ref[...]).astype(BF16)
    start_all([out_copies[3]])
    kt_s[...] = k_ref[...].T
    dkv_s[...] = jnp.zeros_like(dkv_s)
    for block in range(blocks):
        at = pl.ds(block * BLOCK, BLOCK)
        keys_at = pl.ds(block * BLOCK, window)
        for pair in range(pairs):
            cols = pl.ds(pair * PAIR, PAIR)
            dstacked = stack_pair(dctx_s[at, cols], masks)
            qstacked = stack_pair(q_ref[at, cols], masks)
            probs_low = pt_ref[block * pairs + pair]
            probs = probs_low.astype(F32)
            dprobs = mm(v_ref[keys_at, cols], dstacked, NT)
            delta = jnp.sum(probs * dprobs, axis=0, keepdims=True)
            dscores = (probs * (dprobs - delta)).astype(BF16)
            dkv_s[keys_at, cols] += mm(dscores, qstacked)
            dkv_s[keys_at, pl.ds(width + pair * PAIR, PAIR)] += mm(probs_low, dstacked)
            dqt = mm(kt_s[cols, keys_at], dscores) * score_scale
            dqt = dqt.astype(BF16)
            dqt_s[pl.ds(pair * PAIR, HEAD_DIM), at] = dqt[:HEAD_DIM, :BLOCK]
            dqt_s[pl.ds(pair * PAIR + HEAD_DIM, HEAD_DIM), at] = dqt[HEAD_DIM:, BLOCK:]
    dq = dqt_s[...].T
    dkv = dkv_s[...].astype(BF16)
    xt = x_ref[...].T
    dw_s[:, width : 3 * width] = mm(xt, dkv).astype(BF16)
    start_all([out_copies[1], out_copies[2]])
    dw_s[:, :width] = mm(xt[:, BLOCK : BLOCK + rows], dq).astype(BF16)
    start_all([out_copies[0]])
    wait_all(copies[1])
    wait_all(copies[2])
    dx_ref[...] = mm(dkv, w_vmem[:, width : 3 * width], NT)
    wait_all(copies[0])
    dx_ref[BLOCK : BLOCK + rows, :] += dtotal + mm(dq, w_vmem[:, :width], NT)
    for group in out_copies:
        wait_all(group)


def self_backward(dy, xhat, rstd, norm, weights, x, saved):
    keys, width = x.shape
    rows = keys - 2 * BLOCK
    mp = weights.shape[0]
    return pl.pallas_call(
        self_backward_kernel,
        out_shape=(
            shaped((keys, width), F32),
            shaped((2, width), F32),
            shaped(weights.shape, BF16),
        ),
        in_specs=vmem(4) + [pl.BlockSpec(memory_space=ANY)] + vmem(6),
        out_specs=(*vmem(2), pl.BlockSpec(memory_space=ANY)),
        scratch_shapes=[
            pltpu.VMEM((width, 4 * width), BF16),
            pltpu.VMEM((width, 4 * width), BF16),
            pltpu.VMEM((rows, width), BF16),
            pltpu.VMEM((width, keys), BF16),
            pltpu.VMEM((width, rows), BF16),
            pltpu.VMEM((keys, 2 * width), F32),
            pltpu.SemaphoreType.DMA((4, mp)),
            pltpu.SemaphoreType.DMA((4, mp)),
        ],
        compiler_params=params(40),
        name="self_backward",
    )(dy, xhat, rstd, norm, weights, x, *saved)


def cross_forward_kernel(
    range_ref, xin_ref, norm_in_ref, m_ref, segq_ref, segk_ref, w_hbm,
    xhat_ref, rstd_ref, q_ref, k_ref, v_ref, ctx_ref, lse_ref,
    w_vmem, vt_s, s_s, acc_s, ctxt_s, sems,
):
    copies = weight_copies(w_hbm, w_vmem, sems)
    start_all([copies[0], copies[1], copies[2], copies[3]])
    rows, width = q_ref.shape
    blocks, pairs = rows // BLOCK, width // PAIR
    masks = half_masks()
    inputs = xin_ref[...] * norm_in_ref[0:1, :] + norm_in_ref[1:2, :]
    wait_all(copies[0])
    q = mm(inputs.astype(BF16), w_vmem[:, :width]).astype(BF16)
    q_ref[...] = q * jnp.asarray(score_scale, BF16)
    wait_all(copies[1])
    wait_all(copies[2])

    @pl.loop(range_ref[0], range_ref[2 * blocks - 1])
    def _(key_block):
        keys_at = pl.ds(pl.multiple_of(key_block * BLOCK, BLOCK), BLOCK)
        kv = mm(m_ref[keys_at, :], w_vmem[:, width : 3 * width]).astype(BF16)
        k_ref[keys_at, :] = kv[:, :width]
        v_ref[keys_at, :] = kv[:, width:]
        vt_s[:, keys_at] = kv[:, width:].T

    for block in range(blocks):
        at = pl.ds(block * BLOCK, BLOCK)
        first, last = range_ref[2 * block], range_ref[2 * block + 1]
        stacked = [stack_pair(q_ref[at, pl.ds(p * PAIR, PAIR)], masks) for p in range(pairs)]
        segq = segq_ref[block : block + 1, :]

        def scan_scores(key_block, highest):
            keys_at = pl.ds(pl.multiple_of(key_block * BLOCK, BLOCK), BLOCK)
            allowed = segk_ref[keys_at, :] == segq
            result = []
            for pair in range(pairs):
                scores = mm(k_ref[keys_at, pl.ds(pair * PAIR, PAIR)], stacked[pair], NT)
                scores = jnp.where(allowed, scores, masked_score)
                s_s[pair, keys_at, :] = scores
                result.append(
                    jnp.maximum(highest[pair], jnp.max(scores, axis=0, keepdims=True))
                )
            return tuple(result)

        start = tuple(jnp.full((1, 2 * BLOCK), masked_score, F32) for _ in range(pairs))
        highest = lax.fori_loop(first, last, scan_scores, start)
        acc_s[...] = jnp.zeros_like(acc_s)

        def scan_context(key_block, sums):
            keys_at = pl.ds(pl.multiple_of(key_block * BLOCK, BLOCK), BLOCK)
            result = []
            for pair in range(pairs):
                raised = jnp.exp(s_s[pair, keys_at, :] - highest[pair])
                result.append(sums[pair] + jnp.sum(raised, axis=0, keepdims=True))
                acc_s[pair] += mm(vt_s[pl.ds(pair * PAIR, PAIR), keys_at], raised.astype(BF16))
            return tuple(result)

        start = tuple(jnp.zeros((1, 2 * BLOCK), F32) for _ in range(pairs))
        sums = lax.fori_loop(first, last, scan_context, start)
        for pair in range(pairs):
            context = (acc_s[pair] * (1.0 / sums[pair])).astype(BF16)
            ctxt_s[pl.ds(pair * PAIR, HEAD_DIM), at] = context[:HEAD_DIM, :BLOCK]
            ctxt_s[pl.ds(pair * PAIR + HEAD_DIM, HEAD_DIM), at] = context[HEAD_DIM:, BLOCK:]
            row = block * pairs + pair
            lse_ref[row : row + 1, :] = highest[pair] + jnp.log(sums[pair])
    context = ctxt_s[...].T
    ctx_ref[...] = context
    wait_all(copies[3])
    branch = mm(context, w_vmem[:, 3 * width :], NT)
    xhat, rstd = normalize(inputs + branch)
    xhat_ref[...] = xhat
    rstd_ref[...] = rstd


def cross_forward(ranges, xin, norm_in, memory, segq, segk, weights):
    rows, width = xin.shape
    keys = memory.shape[0]
    blocks, pairs = rows // BLOCK, width // PAIR
    return pl.pallas_call(
        cross_forward_kernel,
        out_shape=(
            shaped((rows, width), F32),
            shaped((rows, 1), F32),
            shaped((rows, width), BF16),
            shaped((keys, width), BF16),
            shaped((keys, width), BF16),
            shaped((rows, width), BF16),
            shaped((blocks * pairs, 2 * BLOCK), F32),
        ),
        in_specs=[pl.BlockSpec(memory_space=SMEM)]
        + vmem(5)
        + [pl.BlockSpec(memory_space=ANY)],
        out_specs=tuple(vmem(7)),
        scratch_shapes=[
            pltpu.VMEM((width, 4 * width), BF16),
            pltpu.VMEM((width, keys), BF16),
            pltpu.VMEM((pairs, keys, 2 * BLOCK), F32),
            pltpu.VMEM((pairs, PAIR, 2 * BLOCK), F32),
            pltpu.VMEM((width, rows), BF16),
            pltpu.SemaphoreType.DMA((4, weights.shape[0])),
        ],
        compiler_params=params(40),
        name="cross_forward",
    )(ranges, xin, norm_in, memory, segq, segk, weights)


def cross_backward_kernel(
    range_ref, dy_ref, xhat_ref, rstd_ref, norm_ref, xin_ref, norm_in_ref, m_ref,
    segq_ref, segk_ref, q_ref, k_ref, v_ref, ctx_ref, lse_ref, w_hbm,
    dx_ref, dm_ref, dnorm_ref, dw_hbm,
    w_vmem, dw_s, dctx_s, kt_s, dqt_acc, dqt_s, dkv_s, dwkv_s, sems, out_sems,
):
    copies = weight_copies(w_hbm, w_vmem, sems)
    start_all([copies[3], copies[0], copies[1], copies[2]])
    out_copies = grad_copies(dw_s, dw_hbm, out_sems)
    rows, width = q_ref.shape
    blocks, pairs = rows // BLOCK, width // PAIR
    heads_here = width // HEAD_DIM
    masks = half_masks()
    dy = dy_ref[...]
    xhat = xhat_ref[...]
    dgain, dshift = norm_param_grads(dy, xhat)
    dnorm_ref[0:1, :] = dgain
    dnorm_ref[1:2, :] = dshift
    dtotal = norm_backward(dy, xhat, rstd_ref[...], norm_ref[0:1, :])
    low = dtotal.astype(BF16)
    wait_all(copies[3])
    dctx = mm(low, w_vmem[:, 3 * width :]).astype(BF16)
    dctx_s[...] = dctx
    dw_s[:, 3 * width :] = mm(low.T, ctx_ref[...]).astype(BF16)
    start_all([out_copies[3]])
    products = (dctx.astype(F32) * ctx_ref[...].astype(F32)).T
    deltas = [
        jnp.sum(products[h * HEAD_DIM : (h + 1) * HEAD_DIM, :], axis=0, keepdims=True)
        for h in range(heads_here)
    ]
    everything_first, everything_last = range_ref[0], range_ref[2 * blocks - 1]

    @pl.loop(everything_first, everything_last)
    def _(key_block):
        keys_at = pl.ds(pl.multiple_of(key_block * BLOCK, BLOCK), BLOCK)
        kt_s[:, keys_at] = k_ref[keys_at, :].T
        dkv_s[keys_at, :] = jnp.zeros((BLOCK, 2 * width), F32)

    for block in range(blocks):
        at = pl.ds(block * BLOCK, BLOCK)
        lanes = slice(block * BLOCK, (block + 1) * BLOCK)
        first, last = range_ref[2 * block], range_ref[2 * block + 1]
        qstacked = [stack_pair(q_ref[at, pl.ds(p * PAIR, PAIR)], masks) for p in range(pairs)]
        dstacked = [stack_pair(dctx_s[at, pl.ds(p * PAIR, PAIR)], masks) for p in range(pairs)]
        delta = [
            jnp.concatenate([deltas[2 * p][:, lanes], deltas[2 * p + 1][:, lanes]], axis=1)
            for p in range(pairs)
        ]
        segq = segq_ref[block : block + 1, :]
        dqt_acc[...] = jnp.zeros_like(dqt_acc)

        @pl.loop(first, last)
        def _(key_block):
            keys_at = pl.ds(pl.multiple_of(key_block * BLOCK, BLOCK), BLOCK)
            allowed = segk_ref[keys_at, :] == segq
            for pair in range(pairs):
                cols = pl.ds(pair * PAIR, PAIR)
                row = block * pairs + pair
                scores = mm(k_ref[keys_at, cols], qstacked[pair], NT)
                scores = jnp.where(allowed, scores, masked_score)
                probs = jnp.exp(scores - lse_ref[row : row + 1, :])
                dprobs = mm(v_ref[keys_at, cols], dstacked[pair], NT)
                dscores = (probs * (dprobs - delta[pair])).astype(BF16)
                dkv_s[keys_at, cols] += mm(dscores, qstacked[pair])
                dkv_s[keys_at, pl.ds(width + pair * PAIR, PAIR)] += mm(
                    probs.astype(BF16), dstacked[pair]
                )
                dqt_acc[pair] += mm(kt_s[cols, keys_at], dscores)

        for pair in range(pairs):
            dqt = (dqt_acc[pair] * score_scale).astype(BF16)
            dqt_s[pl.ds(pair * PAIR, HEAD_DIM), at] = dqt[:HEAD_DIM, :BLOCK]
            dqt_s[pl.ds(pair * PAIR + HEAD_DIM, HEAD_DIM), at] = dqt[HEAD_DIM:, BLOCK:]
    dq = dqt_s[...].T
    inputs = (xin_ref[...] * norm_in_ref[0:1, :] + norm_in_ref[1:2, :]).astype(BF16)
    dw_s[:, :width] = mm(inputs.T, dq).astype(BF16)
    start_all([out_copies[0]])
    wait_all(copies[0])
    dx_ref[...] = dtotal + mm(dq, w_vmem[:, :width], NT)
    wait_all(copies[1])
    wait_all(copies[2])
    dm_ref[...] = jnp.zeros_like(dm_ref)
    dwkv_s[...] = jnp.zeros_like(dwkv_s)

    @pl.loop(everything_first, everything_last)
    def _(key_block):
        keys_at = pl.ds(pl.multiple_of(key_block * BLOCK, BLOCK), BLOCK)
        dkv = dkv_s[keys_at, :].astype(BF16)
        dm_ref[keys_at, :] = mm(dkv, w_vmem[:, width : 3 * width], NT).astype(BF16)
        dwkv_s[...] += mm(m_ref[keys_at, :].T, dkv)

    dw_s[:, width : 3 * width] = dwkv_s[...].astype(BF16)
    start_all([out_copies[1], out_copies[2]])
    for group in out_copies:
        wait_all(group)


def cross_backward(ranges, dy, xhat, rstd, norm, xin, norm_in, memory, segq, segk, saved, weights):
    rows, width = xin.shape
    keys = memory.shape[0]
    pairs = width // PAIR
    mp = weights.shape[0]
    return pl.pallas_call(
        cross_backward_kernel,
        out_shape=(
            shaped((rows, width), F32),
            shaped((keys, width), BF16),
            shaped((2, width), F32),
            shaped(weights.shape, BF16),
        ),
        in_specs=[pl.BlockSpec(memory_space=SMEM)]
        + vmem(14)
        + [pl.BlockSpec(memory_space=ANY)],
        out_specs=(*vmem(3), pl.BlockSpec(memory_space=ANY)),
        scratch_shapes=[
            pltpu.VMEM((width, 4 * width), BF16),
            pltpu.VMEM((width, 4 * width), BF16),
            pltpu.VMEM((rows, width), BF16),
            pltpu.VMEM((width, keys), BF16),
            pltpu.VMEM((pairs, PAIR, 2 * BLOCK), F32),
            pltpu.VMEM((width, rows), BF16),
            pltpu.VMEM((keys, 2 * width), F32),
            pltpu.VMEM((width, 2 * width), F32),
            pltpu.SemaphoreType.DMA((4, mp)),
            pltpu.SemaphoreType.DMA((4, mp)),
        ],
        compiler_params=params(48),
        name="cross_backward",
    )(ranges, dy, xhat, rstd, norm, xin, norm_in, memory, segq, segk, *saved, weights)


def feed_forward_kernel(
    xin_ref, norm_in_ref, norm_ref, w_ref,
    xhat_ref, rstd_ref, out_ref, hidden_ref, slope_ref,
    low_s, acc_s,
):
    step = pl.program_id(0)
    half = w_ref.shape[2] // 2

    @pl.when(step == 0)
    def _():
        inputs = xin_ref[...] * norm_in_ref[0:1, :] + norm_in_ref[1:2, :]
        low_s[...] = inputs.astype(BF16)
        acc_s[...] = inputs

    pre = mm(low_s[...], w_ref[0, :, :half])
    square = pre * pre
    tanh = jnp.tanh(gelu_a * pre * (1.0 + gelu_b * square))
    cdf = 0.5 + 0.5 * tanh
    hidden = (pre * cdf).astype(BF16)
    hidden_ref[...] = hidden
    slope = cdf + (0.5 * gelu_a) * pre * (1.0 - tanh * tanh) * (1.0 + (3.0 * gelu_b) * square)
    slope_ref[...] = slope.astype(BF16)
    acc_s[...] += mm(hidden, w_ref[0, :, half:], NT)

    @pl.when(step == pl.num_programs(0) - 1)
    def _():
        xhat, rstd = normalize(acc_s[...])
        xhat_ref[...] = xhat
        rstd_ref[...] = rstd
        out_ref[...] = (xhat * norm_ref[0:1, :] + norm_ref[1:2, :]).astype(BF16)


def feed_forward(xin, norm_in, norm, weights):
    rows, width = xin.shape
    mp, _, both = weights.shape
    half = both // 2
    whole = pl.BlockSpec((rows, width), lambda i: (0, 0))
    two = pl.BlockSpec((2, width), lambda i: (0, 0))
    part = pl.BlockSpec((rows, half), lambda i: (0, i))
    return pl.pallas_call(
        feed_forward_kernel,
        grid=(mp,),
        out_shape=(
            shaped((rows, width), F32),
            shaped((rows, 1), F32),
            shaped((rows, width), BF16),
            shaped((rows, mp * half), BF16),
            shaped((rows, mp * half), BF16),
        ),
        in_specs=[whole, two, two, pl.BlockSpec((1, width, both), lambda i: (i, 0, 0))],
        out_specs=(whole, pl.BlockSpec((rows, 1), lambda i: (0, 0)), whole, part, part),
        scratch_shapes=[pltpu.VMEM((rows, width), BF16), pltpu.VMEM((rows, width), F32)],
        compiler_params=params(32),
        name="feed_forward",
    )(xin, norm_in, norm, weights)


def feed_backward_kernel(
    dy_ref, xhat_ref, rstd_ref, norm_ref, xin_ref, norm_in_ref, w_ref, hidden_ref, slope_ref,
    dx_ref, dnorm_ref, dw_ref,
    low_s, lowt_s, xt_s,
):
    step = pl.program_id(0)
    half = w_ref.shape[2] // 2

    @pl.when(step == 0)
    def _():
        dy = dy_ref[...].astype(F32)
        xhat = xhat_ref[...]
        dgain, dshift = norm_param_grads(dy, xhat)
        dnorm_ref[0:1, :] = dgain
        dnorm_ref[1:2, :] = dshift
        dtotal = norm_backward(dy, xhat, rstd_ref[...], norm_ref[0:1, :])
        dx_ref[...] = dtotal
        low = dtotal.astype(BF16)
        low_s[...] = low
        lowt_s[...] = low.T
        inputs = xin_ref[...] * norm_in_ref[0:1, :] + norm_in_ref[1:2, :]
        xt_s[...] = inputs.astype(BF16).T

    dhidden = mm(low_s[...], w_ref[0, :, half:])
    dpre = (dhidden * slope_ref[...].astype(F32)).astype(BF16)
    dw_ref[0, :, :half] = mm(xt_s[...], dpre).astype(BF16)
    dw_ref[0, :, half:] = mm(lowt_s[...], hidden_ref[...]).astype(BF16)
    dx_ref[...] += mm(dpre, w_ref[0, :, :half], NT)


def feed_backward(dy, xhat, rstd, norm, xin, norm_in, weights, hidden, slope):
    rows, width = xin.shape
    mp, _, both = weights.shape
    half = both // 2
    whole = pl.BlockSpec((rows, width), lambda i: (0, 0))
    two = pl.BlockSpec((2, width), lambda i: (0, 0))
    part = pl.BlockSpec((rows, half), lambda i: (0, i))
    blocks = pl.BlockSpec((1, width, both), lambda i: (i, 0, 0))
    return pl.pallas_call(
        feed_backward_kernel,
        grid=(mp,),
        out_shape=(
            shaped((rows, width), F32),
            shaped((2, width), F32),
            shaped(weights.shape, BF16),
        ),
        in_specs=[
            whole, whole, pl.BlockSpec((rows, 1), lambda i: (0, 0)), two, whole, two,
            blocks, part, part,
        ],
        out_specs=(whole, two, blocks),
        scratch_shapes=[
            pltpu.VMEM((rows, width), BF16),
            pltpu.VMEM((width, rows), BF16),
            pltpu.VMEM((width, rows), BF16),
        ],
        compiler_params=params(32),
        name="feed_backward",
    )(dy, xhat, rstd, norm, xin, norm_in, weights, hidden, slope)


DP = ("z", "x")
MP = ("y", "c")
ALL = ("z", "x", "y", "c")


def gather_weights(shard):
    gathered = lax.all_gather(shard, MP + DP, axis=0, tiled=True)
    blocks = lax.axis_size(MP)
    return gathered.reshape(blocks, gathered.shape[0] // blocks, shard.shape[1])


def scatter_grads(grads):
    part = lax.psum_scatter(grads, MP, scatter_dimension=0, tiled=True)
    return lax.psum_scatter(part[0], DP, scatter_dimension=0, tiled=True)


def shift_rows(values, step):
    count = lax.axis_size(MP)
    pairs = [(i, i + step) for i in range(count) if 0 <= i + step < count]
    return lax.ppermute(values, MP, pairs)


def with_halos(values):
    before = shift_rows(values[-BLOCK:], 1)
    after = shift_rows(values[:BLOCK], -1)
    return jnp.concatenate([before, values, after], axis=0)


def add_halos(values):
    rows = values.shape[0] - 2 * BLOCK
    own = values[BLOCK : BLOCK + rows]
    after = shift_rows(values[:BLOCK], -1)
    before = shift_rows(values[BLOCK + rows :], 1)
    spread = jnp.pad(before, ((0, rows - BLOCK), (0, 0))) + jnp.pad(
        after, ((rows - BLOCK, 0), (0, 0))
    )
    return own + spread


def adam_step(weights, first, second, grads, rate, decay):
    first_new = beta_one * first + (1.0 - beta_one) * grads
    second_new = beta_two * second + (1.0 - beta_two) * grads * grads
    first_hat = first_new / (1.0 - beta_one**STEP)
    second_hat = second_new / (1.0 - beta_two**STEP)
    weights_new = weights - rate * (first_hat / (jnp.sqrt(second_hat) + adam_eps) + decay * weights)
    return (weights_new, first_new, second_new)


def on_device(
    encoder_input, decoder_copy, decoder_target, decoder_cotangent,
    source_segments, target_segments, glance_mask,
    attention_in, attention_out, feed_in, feed_out, norm_params,
    attention_in_first, attention_out_first, feed_in_first, feed_out_first, norm_params_first,
    attention_in_second, attention_out_second, feed_in_second, feed_out_second, norm_params_second,
):
    rows, width = encoder_input.shape
    length = source_segments.shape[1]
    masters = (attention_in, attention_out, feed_in, feed_out, norm_params)

    picked = glance_mask[0] == 1
    decoder_input = jnp.where(picked[:, None], decoder_target, decoder_copy)
    encoder_x = with_halos(encoder_input)
    decoder_x = with_halos(decoder_input)

    def attention_shard(number):
        parts = [attention_in[3 * number + kind] for kind in range(3)]
        return jnp.concatenate(parts + [attention_out[number].T], axis=1).astype(BF16)

    def feed_shard(number):
        return jnp.concatenate([feed_in[number], feed_out[number].T], axis=1).astype(BF16)

    norms = lax.all_gather(norm_params.astype(BF16), DP, axis=2, tiled=True).astype(F32)
    w_enc = gather_weights(attention_shard(0))
    w_enc_feed = gather_weights(feed_shard(0))
    w_self = gather_weights(attention_shard(1))
    w_cross = gather_weights(attention_shard(2))
    w_dec_feed = gather_weights(feed_shard(1))

    position = lax.axis_index(MP) * rows
    blocks = rows // BLOCK

    def query_segments(row):
        own = lax.dynamic_slice(row, (position,), (rows,)).reshape(blocks, BLOCK)
        return jnp.concatenate([own, own], axis=1)

    def key_segments(row):
        padded = jnp.pad(row, (BLOCK, BLOCK), constant_values=-1)
        return lax.dynamic_slice(padded, (position,), (rows + 2 * BLOCK,))[:, None]

    source_row, target_row = source_segments[0], target_segments[0]
    source_q, target_q = query_segments(source_row), query_segments(target_row)
    source_k, target_k = key_segments(source_row), key_segments(target_row)
    lowest, highest = target_q[:, 0], target_q[:, BLOCK - 1]
    first_key = jnp.sum((source_row[None, :] < lowest[:, None]).astype(jnp.int32), axis=1)
    last_key = jnp.sum((source_row[None, :] <= highest[:, None]).astype(jnp.int32), axis=1)
    ranges = jnp.stack([first_key // BLOCK, (last_key + BLOCK - 1) // BLOCK], axis=1)
    ranges = ranges.astype(jnp.int32).reshape(2 * blocks)

    xhat0, rstd0, *enc_saved = self_forward(encoder_x, source_q, source_k, w_enc, norms[0])
    xhat1, rstd1, encoder_output, enc_hidden, enc_slope = feed_forward(
        xhat0, norms[0], norms[1], w_enc_feed
    )
    memory = lax.all_gather(encoder_output, MP, axis=0, tiled=True)
    xhat2, rstd2, *self_saved = self_forward(decoder_x, target_q, target_k, w_self, norms[2])
    xhat3, rstd3, *cross_saved = cross_forward(
        ranges, xhat2, norms[2], memory, target_q, source_row[:, None], w_cross
    )
    xhat4, rstd4, decoder_output, dec_hidden, dec_slope = feed_forward(
        xhat3, norms[3], norms[4], w_dec_feed
    )

    d4, dnorm4, dw_dec_feed = feed_backward(
        decoder_cotangent, xhat4, rstd4, norms[4], xhat3, norms[3], w_dec_feed, dec_hidden, dec_slope
    )
    g_dec_feed = scatter_grads(dw_dec_feed)
    d3, dmemory, dnorm3, dw_cross = cross_backward(
        ranges, d4, xhat3, rstd3, norms[3], xhat2, norms[2], memory,
        target_q, source_row[:, None], cross_saved, w_cross,
    )
    dmemory = lax.psum_scatter(dmemory, MP, scatter_dimension=0, tiled=True)
    g_cross = scatter_grads(dw_cross)
    dx_dec, dnorm2, dw_self = self_backward(
        d3, xhat2, rstd2, norms[2], w_self, decoder_x, self_saved
    )
    g_self = scatter_grads(dw_self)
    d1, dnorm1, dw_enc_feed = feed_backward(
        dmemory, xhat1, rstd1, norms[1], xhat0, norms[0], w_enc_feed, enc_hidden, enc_slope
    )
    g_enc_feed = scatter_grads(dw_enc_feed)
    dx_enc, dnorm0, dw_enc = self_backward(
        d1, xhat0, rstd0, norms[0], w_enc, encoder_x, enc_saved
    )
    g_enc = scatter_grads(dw_enc)
    decoder_input_grad = add_halos(dx_dec)
    encoder_input_grad = add_halos(dx_enc)

    dnorms = lax.psum(jnp.stack([dnorm0, dnorm1, dnorm2, dnorm3, dnorm4]), MP)
    g_norms = lax.psum_scatter(dnorms, DP, scatter_dimension=2, tiled=True)

    attention_parts = [g.astype(F32) for g in (g_enc, g_self, g_cross)]
    feed_parts = [g.astype(F32) for g in (g_enc_feed, g_dec_feed)]
    squares = sum(jnp.sum(g * g) for g in attention_parts + feed_parts)
    squares = squares + jnp.sum(g_norms * g_norms) / lax.axis_size(MP)
    grad_norm = jnp.sqrt(lax.psum(squares, ALL))
    factor = clip_bound / jnp.maximum(grad_norm, clip_bound)

    part = attention_in.shape[2]
    half = feed_in.shape[2]
    g_in = jnp.stack(
        [g[:, kind * part : (kind + 1) * part] for g in attention_parts for kind in range(3)]
    )
    g_out = jnp.stack([g[:, 3 * part :].T for g in attention_parts])
    g_first = jnp.stack([g[:, :half] for g in feed_parts])
    g_second = jnp.stack([g[:, half:].T for g in feed_parts])
    reduced = (g_in, g_out, g_first, g_second, g_norms)
    firsts = (
        attention_in_first, attention_out_first, feed_in_first, feed_out_first, norm_params_first,
    )
    seconds = (
        attention_in_second, attention_out_second, feed_in_second, feed_out_second,
        norm_params_second,
    )
    results = []
    for number in range(5):
        rate = rate_norm if number == 4 else rate_matrix
        decay = 0.0 if number == 4 else weight_decay
        results.append(
            adam_step(
                masters[number], firsts[number], seconds[number], reduced[number] * factor, rate, decay
            )
        )
    return (
        encoder_output,
        decoder_output,
        encoder_input_grad,
        decoder_input_grad,
        grad_norm,
        *(result[0] for result in results),
        *(result[1] for result in results),
        *(result[2] for result in results),
    )


def solution(mesh):
    dp, mp = mesh.shape["dp"], mesh.shape["mp"]
    fine = Mesh(mesh.devices.reshape(dp // 2, 2, mp // 2, 2), ALL)
    tokens = P(ALL, None)
    columns = P(None, DP, MP)
    turned = P(None, MP, DP)
    states = (columns, turned, columns, turned, P(None, None, DP))
    return jax.shard_map(
        on_device,
        mesh=fine,
        in_specs=(
            *((tokens,) * 4),
            P(DP, None),
            P(DP, None),
            P(DP, MP),
            *states,
            *states,
            *states,
        ),
        out_specs=(*((tokens,) * 4), P(), *states, *states, *states),
        check_vma=False,
    )
```

```python
import functools

import jax
import jax.numpy as jnp
from jax import lax
from jax.experimental import pallas as pl
from jax.experimental.pallas import tpu as pltpu
from jax.sharding import Mesh
from jax.sharding import PartitionSpec as P

HEAD_DIM = 64
STEP = 10
BLOCK = 128
PAIR = 2 * HEAD_DIM

norm_eps = 1e-05
beta_one = 0.9
beta_two = 0.98
adam_eps = 1e-08
weight_decay = 0.01
rate_matrix = 0.1
rate_norm = 0.5
clip_bound = 1.0
masked_score = -1e30
score_scale = HEAD_DIM ** (-0.5)
gelu_a = 0.7978845608028654
gelu_b = 0.044715

F32 = jnp.float32
BF16 = jnp.bfloat16
ANY = pl.ANY
SMEM = pltpu.SMEM
VMEM = pltpu.VMEM

NN = (((1,), (0,)), ((), ()))
NT = (((1,), (1,)), ((), ()))


def mm(a, b, dims=NN):
    return lax.dot_general(a, b, dims, preferred_element_type=F32)


def vmem(count):
    return [pl.BlockSpec(memory_space=VMEM)] * count


def smem(count):
    return [pl.BlockSpec(memory_space=SMEM)] * count


def hbm(count):
    return [pl.BlockSpec(memory_space=ANY)] * count


def params(mib=60):
    return pltpu.CompilerParams(vmem_limit_bytes=mib * 1024 * 1024)


def shaped(shape, dtype):
    return jax.ShapeDtypeStruct(shape, dtype)


def normalize(total):
    centred = total - jnp.mean(total, axis=-1, keepdims=True)
    spread = jnp.mean(centred * centred, axis=-1, keepdims=True)
    rstd = lax.rsqrt(spread + norm_eps)
    return centred * rstd, rstd


def norm_backward(grad_out, xhat, rstd, gain):
    scaled = grad_out * gain
    first = jnp.mean(scaled, axis=-1, keepdims=True)
    second = jnp.mean(scaled * xhat, axis=-1, keepdims=True)
    return rstd * (scaled - first - xhat * second)


def norm_param_grads(grad_out, xhat):
    return (
        jnp.sum(grad_out * xhat, axis=0, keepdims=True),
        jnp.sum(grad_out, axis=0, keepdims=True),
    )


def half_masks():
    lane = lax.broadcasted_iota(jnp.int32, (1, PAIR), 1)
    low = jnp.where(lane < HEAD_DIM, 1.0, 0.0).astype(BF16)
    high = jnp.where(lane < HEAD_DIM, 0.0, 1.0).astype(BF16)
    return low, high


def stack_pair(values, masks):
    return jnp.concatenate([values * masks[0], values * masks[1]], axis=0)


SLAB = 64


def slots(member):
    side, row = member % 2, member // 2
    return [(side, (2 * row + x) * 4 + z, 2 * z + x) for x in range(2) for z in range(4)]


def slab_rows(me_ref, block):
    return pl.ds(pl.multiple_of((me_ref[0] ^ block) * SLAB, SLAB), SLAB)


def weight_copies(me_ref, pieces, offset, w_vmem, sems):
    width = w_vmem.shape[2]
    copies = []
    for member in range(4):
        copies.append(
            [
                pltpu.make_async_copy(
                    pieces[side].at[slot, :, pl.ds(offset, width)],
                    w_vmem.at[member, slab_rows(me_ref, block), :],
                    sems.at[member, block],
                )
                for side, slot, block in slots(member)
            ]
        )
    return copies


def grad_copies(me_ref, dw_vmem, pieces, offset, sems):
    width = dw_vmem.shape[2]
    copies = []
    for member in range(4):
        copies.append(
            [
                pltpu.make_async_copy(
                    dw_vmem.at[member, slab_rows(me_ref, block), :],
                    pieces[side].at[slot, :, pl.ds(offset, width)],
                    sems.at[member, block],
                )
                for side, slot, block in slots(member)
            ]
        )
    return copies


def start_all(groups):
    for group in groups:
        for copy in group:
            copy.start()


def wait_all(group):
    for copy in group:
        copy.wait()


def spread_kinds(w_vmem, w_flat, member):
    part = w_vmem.shape[2] // 4
    for kind in range(4):
        w_flat[:, pl.ds((kind * 4 + member) * part, part)] = w_vmem[
            member, :, kind * part : (kind + 1) * part
        ]


def store_kind(dw_vmem, kind, grads):
    part = dw_vmem.shape[2] // 4
    for member in range(4):
        dw_vmem[member, :, kind * part : (kind + 1) * part] = grads[
            :, member * part : (member + 1) * part
        ].astype(BF16)


def self_forward_kernel(
    offset, me_ref, x_ref, segq_ref, segk_ref, own_hbm, sib_hbm,
    xhat_ref, rstd_ref, q_ref, k_ref, v_ref, ctx_ref, pt_ref,
    w_vmem, w_s, vt_s, ctxt_s, sems,
):
    copies = weight_copies(me_ref, (own_hbm, sib_hbm), offset, w_vmem, sems)
    start_all(copies)
    rows, width = q_ref.shape
    blocks, pairs = rows // BLOCK, width // PAIR
    window = 3 * BLOCK
    for member in range(4):
        wait_all(copies[member])
        spread_kinds(w_vmem, w_s, member)
    kv = mm(x_ref[...], w_s[:, width : 3 * width]).astype(BF16)
    k_ref[...] = kv[:, :width]
    v_ref[...] = kv[:, width:]
    vt_s[...] = kv[:, width:].T
    q = mm(x_ref[BLOCK : BLOCK + rows, :], w_s[:, :width]).astype(BF16)
    q_ref[...] = q * jnp.asarray(score_scale, BF16)
    masks = half_masks()
    for block in range(blocks):
        at = pl.ds(block * BLOCK, BLOCK)
        keys_at = pl.ds(block * BLOCK, window)
        allowed = segk_ref[keys_at, :] == segq_ref[block : block + 1, :]
        for pair in range(pairs):
            cols = pl.ds(pair * PAIR, PAIR)
            stacked = stack_pair(q_ref[at, cols], masks)
            scores = mm(k_ref[keys_at, cols], stacked, NT)
            scores = jnp.where(allowed, scores, masked_score)
            highest = jnp.max(scores, axis=0, keepdims=True)
            raised = jnp.exp(scores - highest)
            total = jnp.sum(raised, axis=0, keepdims=True)
            probs = (raised * (1.0 / total)).astype(BF16)
            pt_ref[block * pairs + pair] = probs
            context = mm(vt_s[cols, keys_at], probs).astype(BF16)
            ctxt_s[pl.ds(pair * PAIR, HEAD_DIM), at] = context[:HEAD_DIM, :BLOCK]
            ctxt_s[pl.ds(pair * PAIR + HEAD_DIM, HEAD_DIM), at] = context[HEAD_DIM:, BLOCK:]
    context = ctxt_s[...].T
    ctx_ref[...] = context
    branch = mm(context, w_s[:, 3 * width :], NT)
    xhat, rstd = normalize(x_ref[BLOCK : BLOCK + rows, :].astype(F32) + branch)
    xhat_ref[...] = xhat
    rstd_ref[...] = rstd


def self_forward(me, x, segq, segk, weights):
    (own, sib), offset = weights
    keys, width = x.shape
    rows = keys - 2 * BLOCK
    blocks, pairs = rows // BLOCK, width // PAIR
    return pl.pallas_call(
        functools.partial(self_forward_kernel, offset),
        out_shape=(
            shaped((rows, width), F32),
            shaped((rows, 1), F32),
            shaped((rows, width), BF16),
            shaped((keys, width), BF16),
            shaped((keys, width), BF16),
            shaped((rows, width), BF16),
            shaped((blocks * pairs, 3 * BLOCK, 2 * BLOCK), BF16),
        ),
        in_specs=smem(1) + vmem(3) + hbm(2),
        out_specs=tuple(vmem(7)),
        scratch_shapes=[
            pltpu.VMEM((4, width, width), BF16),
            pltpu.VMEM((width, 4 * width), BF16),
            pltpu.VMEM((width, keys), BF16),
            pltpu.VMEM((width, rows), BF16),
            pltpu.SemaphoreType.DMA((4, width // SLAB)),
        ],
        compiler_params=params(),
        name="self_forward",
    )(me, x, segq, segk, own, sib)


def self_backward_kernel(
    offset, out_offset, k_norm, prior, me_ref, dy_ref, xhat_ref, rstd_ref, norms_ref, x_ref,
    q_ref, k_ref, v_ref, ctx_ref, pt_ref, own_hbm, sib_hbm, *rest,
):
    rest = rest[prior:]
    dx_ref, before_ref, after_ref, dnorm_ref, keep_hbm, send_hbm = rest[:6]
    w_vmem, w_s, dw_s, dctx_s, kt_s, dqt_s, dkv_s, sems, out_sems = rest[6:]
    copies = weight_copies(me_ref, (own_hbm, sib_hbm), offset, w_vmem, sems)
    start_all(copies)
    out_copies = grad_copies(me_ref, dw_s, (keep_hbm, send_hbm), out_offset, out_sems)
    rows, width = q_ref.shape
    blocks, pairs = rows // BLOCK, width // PAIR
    window = 3 * BLOCK
    masks = half_masks()
    dy = dy_ref[...]
    xhat = xhat_ref[...]
    dgain, dshift = norm_param_grads(dy, xhat)
    dnorm_ref[0:1, :] = dgain
    dnorm_ref[1:2, :] = dshift
    dtotal = norm_backward(dy, xhat, rstd_ref[...], norms_ref[2 * k_norm : 2 * k_norm + 1, :])
    low = dtotal.astype(BF16)
    for member in range(4):
        wait_all(copies[member])
        spread_kinds(w_vmem, w_s, member)
    dctx_s[...] = mm(low, w_s[:, 3 * width :]).astype(BF16)
    store_kind(dw_s, 3, mm(low.T, ctx_ref[...]))
    kt_s[...] = k_ref[...].T
    dkv_s[...] = jnp.zeros_like(dkv_s)
    for block in range(blocks):
        at = pl.ds(block * BLOCK, BLOCK)
        keys_at = pl.ds(block * BLOCK, window)
        for pair in range(pairs):
            cols = pl.ds(pair * PAIR, PAIR)
            dstacked = stack_pair(dctx_s[at, cols], masks)
            qstacked = stack_pair(q_ref[at, cols], masks)
            probs_low = pt_ref[block * pairs + pair]
            probs = probs_low.astype(F32)
            dprobs = mm(v_ref[keys_at, cols], dstacked, NT)
            delta = jnp.sum(probs * dprobs, axis=0, keepdims=True)
            dscores = (probs * (dprobs - delta)).astype(BF16)
            dkv_s[keys_at, cols] += mm(dscores, qstacked)
            dkv_s[keys_at, pl.ds(width + pair * PAIR, PAIR)] += mm(probs_low, dstacked)
            dqt = mm(kt_s[cols, keys_at], dscores) * score_scale
            dqt = dqt.astype(BF16)
            dqt_s[pl.ds(pair * PAIR, HEAD_DIM), at] = dqt[:HEAD_DIM, :BLOCK]
            dqt_s[pl.ds(pair * PAIR + HEAD_DIM, HEAD_DIM), at] = dqt[HEAD_DIM:, BLOCK:]
    dq = dqt_s[...].T
    dkv = dkv_s[...].astype(BF16)
    xt = x_ref[...].T
    store_kind(dw_s, 0, mm(xt[:, BLOCK : BLOCK + rows], dq))
    store_kind(dw_s, 1, mm(xt, dkv[:, :width]))
    store_kind(dw_s, 2, mm(xt, dkv[:, width:]))
    start_all(out_copies)
    dx = mm(dkv, w_s[:, width : 3 * width], NT)
    before_ref[...] = dx[:BLOCK]
    after_ref[...] = dx[BLOCK + rows :]
    dx_ref[...] = dx[BLOCK : BLOCK + rows] + dtotal + mm(dq, w_s[:, :width], NT)
    for group in out_copies:
        wait_all(group)


def self_backward(me, dy, xhat, rstd, norms, k_norm, x, saved, weights, grads):
    (own, sib), offset = weights
    prior, out_offset, out_width = grads
    keys, width = x.shape
    rows = keys - 2 * BLOCK
    piece = shaped((16, SLAB, out_width), BF16)
    return pl.pallas_call(
        functools.partial(self_backward_kernel, offset, out_offset, k_norm, len(prior)),
        out_shape=(
            shaped((rows, width), F32),
            shaped((BLOCK, width), F32),
            shaped((BLOCK, width), F32),
            shaped((2, width), F32),
            piece,
            piece,
        ),
        in_specs=smem(1) + vmem(10) + hbm(2 + len(prior)),
        out_specs=(*vmem(4), *hbm(2)),
        input_output_aliases={13 + i: 4 + i for i in range(len(prior))},
        scratch_shapes=[
            pltpu.VMEM((4, width, width), BF16),
            pltpu.VMEM((width, 4 * width), BF16),
            pltpu.VMEM((4, width, width), BF16),
            pltpu.VMEM((rows, width), BF16),
            pltpu.VMEM((width, keys), BF16),
            pltpu.VMEM((width, rows), BF16),
            pltpu.VMEM((keys, 2 * width), F32),
            pltpu.SemaphoreType.DMA((4, width // SLAB)),
            pltpu.SemaphoreType.DMA((4, width // SLAB)),
        ],
        compiler_params=params(),
        name="self_backward",
    )(me, dy, xhat, rstd, norms, x, *saved, own, sib, *prior)


def memory_copies(me_ref, pieces, m_s, sems):
    rows = pieces[0].shape[0]
    return [
        pltpu.make_async_copy(
            piece,
            m_s.at[pl.ds(pl.multiple_of((me_ref[1] ^ member) * rows, rows), rows), :],
            sems.at[member],
        )
        for member, piece in enumerate(pieces)
    ]


def cross_forward_kernel(
    offset, k_in, me_ref, range_ref, xin_ref, norms_ref, segq_ref, segk_ref,
    m0_hbm, m1_hbm, m2_hbm, m3_hbm, own_hbm, sib_hbm,
    xhat_ref, rstd_ref, q_ref, k_ref, v_ref, ctx_ref, lse_ref,
    m_s, w_vmem, w_s, vt_s, s_s, acc_s, ctxt_s, sems, m_sems,
):
    copies = weight_copies(me_ref, (own_hbm, sib_hbm), offset, w_vmem, sems)
    start_all(copies)
    m_copies = memory_copies(me_ref, (m0_hbm, m1_hbm, m2_hbm, m3_hbm), m_s, m_sems)
    start_all([m_copies])
    rows, width = q_ref.shape
    blocks, pairs = rows // BLOCK, width // PAIR
    masks = half_masks()
    gain, shift = norms_ref[2 * k_in : 2 * k_in + 1, :], norms_ref[2 * k_in + 1 : 2 * k_in + 2, :]
    inputs = xin_ref[...] * gain + shift
    for member in range(4):
        wait_all(copies[member])
        spread_kinds(w_vmem, w_s, member)
    q = mm(inputs.astype(BF16), w_s[:, :width]).astype(BF16)
    q_ref[...] = q * jnp.asarray(score_scale, BF16)
    wait_all(m_copies)

    @pl.loop(range_ref[0], range_ref[2 * blocks - 1])
    def _(key_block):
        keys_at = pl.ds(pl.multiple_of(key_block * BLOCK, BLOCK), BLOCK)
        kv = mm(m_s[keys_at, :], w_s[:, width : 3 * width]).astype(BF16)
        k_ref[keys_at, :] = kv[:, :width]
        v_ref[keys_at, :] = kv[:, width:]
        vt_s[:, keys_at] = kv[:, width:].T

    for block in range(blocks):
        at = pl.ds(block * BLOCK, BLOCK)
        first, last = range_ref[2 * block], range_ref[2 * block + 1]
        stacked = [stack_pair(q_ref[at, pl.ds(p * PAIR, PAIR)], masks) for p in range(pairs)]
        segq = segq_ref[block : block + 1, :]

        def scan_scores(key_block, highest):
            keys_at = pl.ds(pl.multiple_of(key_block * BLOCK, BLOCK), BLOCK)
            allowed = segk_ref[keys_at, :] == segq
            result = []
            for pair in range(pairs):
                scores = mm(k_ref[keys_at, pl.ds(pair * PAIR, PAIR)], stacked[pair], NT)
                scores = jnp.where(allowed, scores, masked_score)
                s_s[pair, keys_at, :] = scores
                result.append(
                    jnp.maximum(highest[pair], jnp.max(scores, axis=0, keepdims=True))
                )
            return tuple(result)

        start = tuple(jnp.full((1, 2 * BLOCK), masked_score, F32) for _ in range(pairs))
        highest = lax.fori_loop(first, last, scan_scores, start)
        acc_s[...] = jnp.zeros_like(acc_s)

        def scan_context(key_block, sums):
            keys_at = pl.ds(pl.multiple_of(key_block * BLOCK, BLOCK), BLOCK)
            result = []
            for pair in range(pairs):
                raised = jnp.exp(s_s[pair, keys_at, :] - highest[pair])
                result.append(sums[pair] + jnp.sum(raised, axis=0, keepdims=True))
                acc_s[pair] += mm(vt_s[pl.ds(pair * PAIR, PAIR), keys_at], raised.astype(BF16))
            return tuple(result)

        start = tuple(jnp.zeros((1, 2 * BLOCK), F32) for _ in range(pairs))
        sums = lax.fori_loop(first, last, scan_context, start)
        for pair in range(pairs):
            context = (acc_s[pair] * (1.0 / sums[pair])).astype(BF16)
            ctxt_s[pl.ds(pair * PAIR, HEAD_DIM), at] = context[:HEAD_DIM, :BLOCK]
            ctxt_s[pl.ds(pair * PAIR + HEAD_DIM, HEAD_DIM), at] = context[HEAD_DIM:, BLOCK:]
            row = block * pairs + pair
            lse_ref[row : row + 1, :] = highest[pair] + jnp.log(sums[pair])
    context = ctxt_s[...].T
    ctx_ref[...] = context
    branch = mm(context, w_s[:, 3 * width :], NT)
    xhat, rstd = normalize(inputs + branch)
    xhat_ref[...] = xhat
    rstd_ref[...] = rstd


def cross_forward(me, ranges, xin, norms, k_in, segq, segk, memory, weights):
    (own, sib), offset = weights
    rows, width = xin.shape
    keys = 4 * rows
    blocks, pairs = rows // BLOCK, width // PAIR
    return pl.pallas_call(
        functools.partial(cross_forward_kernel, offset, k_in),
        out_shape=(
            shaped((rows, width), F32),
            shaped((rows, 1), F32),
            shaped((rows, width), BF16),
            shaped((keys, width), BF16),
            shaped((keys, width), BF16),
            shaped((rows, width), BF16),
            shaped((blocks * pairs, 2 * BLOCK), F32),
        ),
        in_specs=smem(2) + vmem(4) + hbm(6),
        out_specs=tuple(vmem(7)),
        scratch_shapes=[
            pltpu.VMEM((keys, width), BF16),
            pltpu.VMEM((4, width, width), BF16),
            pltpu.VMEM((width, 4 * width), BF16),
            pltpu.VMEM((width, keys), BF16),
            pltpu.VMEM((pairs, keys, 2 * BLOCK), F32),
            pltpu.VMEM((pairs, PAIR, 2 * BLOCK), F32),
            pltpu.VMEM((width, rows), BF16),
            pltpu.SemaphoreType.DMA((4, width // SLAB)),
            pltpu.SemaphoreType.DMA((4,)),
        ],
        compiler_params=params(),
        name="cross_forward",
    )(me, ranges, xin, norms, segq, segk, *memory, own, sib)


def cross_backward_kernel(
    offset, out_offset, k_norm, k_in, prior, me_ref, range_ref, dy_ref, xhat_ref, rstd_ref,
    norms_ref, xin_ref, segq_ref, segk_ref, q_ref, k_ref, v_ref, ctx_ref, lse_ref,
    m0_hbm, m1_hbm, m2_hbm, m3_hbm, own_hbm, sib_hbm, *rest,
):
    rest = rest[prior:]
    dx_ref, dnorm_ref, dm_keep, dm_send, keep_hbm, send_hbm = rest[:6]
    (
        m_s, w_vmem, w_s, dw_s, dctx_s, kt_s, dqt_acc, dqt_s, dkv_s, dwkv_s, dm_s,
        sems, out_sems, m_sems, dm_sems,
    ) = rest[6:]
    copies = weight_copies(me_ref, (own_hbm, sib_hbm), offset, w_vmem, sems)
    start_all(copies)
    m_copies = memory_copies(me_ref, (m0_hbm, m1_hbm, m2_hbm, m3_hbm), m_s, m_sems)
    start_all([m_copies])
    out_copies = grad_copies(me_ref, dw_s, (keep_hbm, send_hbm), out_offset, out_sems)
    rows, width = q_ref.shape
    blocks, pairs = rows // BLOCK, width // PAIR
    heads_here = width // HEAD_DIM
    masks = half_masks()
    dy = dy_ref[...]
    xhat = xhat_ref[...]
    dgain, dshift = norm_param_grads(dy, xhat)
    dnorm_ref[0:1, :] = dgain
    dnorm_ref[1:2, :] = dshift
    dtotal = norm_backward(dy, xhat, rstd_ref[...], norms_ref[2 * k_norm : 2 * k_norm + 1, :])
    low = dtotal.astype(BF16)
    for member in range(4):
        wait_all(copies[member])
        spread_kinds(w_vmem, w_s, member)
    dctx = mm(low, w_s[:, 3 * width :]).astype(BF16)
    dctx_s[...] = dctx
    store_kind(dw_s, 3, mm(low.T, ctx_ref[...]))
    products = (dctx.astype(F32) * ctx_ref[...].astype(F32)).T
    deltas = [
        jnp.sum(products[h * HEAD_DIM : (h + 1) * HEAD_DIM, :], axis=0, keepdims=True)
        for h in range(heads_here)
    ]
    everything_first, everything_last = range_ref[0], range_ref[2 * blocks - 1]

    @pl.loop(everything_first, everything_last)
    def _(key_block):
        keys_at = pl.ds(pl.multiple_of(key_block * BLOCK, BLOCK), BLOCK)
        kt_s[:, keys_at] = k_ref[keys_at, :].T
        dkv_s[keys_at, :] = jnp.zeros((BLOCK, 2 * width), F32)

    for block in range(blocks):
        at = pl.ds(block * BLOCK, BLOCK)
        lanes = slice(block * BLOCK, (block + 1) * BLOCK)
        first, last = range_ref[2 * block], range_ref[2 * block + 1]
        qstacked = [stack_pair(q_ref[at, pl.ds(p * PAIR, PAIR)], masks) for p in range(pairs)]
        dstacked = [stack_pair(dctx_s[at, pl.ds(p * PAIR, PAIR)], masks) for p in range(pairs)]
        delta = [
            jnp.concatenate([deltas[2 * p][:, lanes], deltas[2 * p + 1][:, lanes]], axis=1)
            for p in range(pairs)
        ]
        segq = segq_ref[block : block + 1, :]
        dqt_acc[...] = jnp.zeros_like(dqt_acc)

        @pl.loop(first, last)
        def _(key_block):
            keys_at = pl.ds(pl.multiple_of(key_block * BLOCK, BLOCK), BLOCK)
            allowed = segk_ref[keys_at, :] == segq
            for pair in range(pairs):
                cols = pl.ds(pair * PAIR, PAIR)
                row = block * pairs + pair
                scores = mm(k_ref[keys_at, cols], qstacked[pair], NT)
                scores = jnp.where(allowed, scores, masked_score)
                probs = jnp.exp(scores - lse_ref[row : row + 1, :])
                dprobs = mm(v_ref[keys_at, cols], dstacked[pair], NT)
                dscores = (probs * (dprobs - delta[pair])).astype(BF16)
                dkv_s[keys_at, cols] += mm(dscores, qstacked[pair])
                dkv_s[keys_at, pl.ds(width + pair * PAIR, PAIR)] += mm(
                    probs.astype(BF16), dstacked[pair]
                )
                dqt_acc[pair] += mm(kt_s[cols, keys_at], dscores)

        for pair in range(pairs):
            dqt = (dqt_acc[pair] * score_scale).astype(BF16)
            dqt_s[pl.ds(pair * PAIR, HEAD_DIM), at] = dqt[:HEAD_DIM, :BLOCK]
            dqt_s[pl.ds(pair * PAIR + HEAD_DIM, HEAD_DIM), at] = dqt[HEAD_DIM:, BLOCK:]
    dq = dqt_s[...].T
    gain, shift = norms_ref[2 * k_in : 2 * k_in + 1, :], norms_ref[2 * k_in + 1 : 2 * k_in + 2, :]
    inputs = (xin_ref[...] * gain + shift).astype(BF16)
    store_kind(dw_s, 0, mm(inputs.T, dq))
    dx_ref[...] = dtotal + mm(dq, w_s[:, :width], NT)
    dm_s[...] = jnp.zeros_like(dm_s)
    dwkv_s[...] = jnp.zeros_like(dwkv_s)
    wait_all(m_copies)

    @pl.loop(everything_first, everything_last)
    def _(key_block):
        keys_at = pl.ds(pl.multiple_of(key_block * BLOCK, BLOCK), BLOCK)
        dkv = dkv_s[keys_at, :].astype(BF16)
        dm_s[keys_at, :] = mm(dkv, w_s[:, width : 3 * width], NT).astype(BF16)
        dwkv_s[...] += mm(m_s[keys_at, :].T, dkv)

    dm_copies = [
        pltpu.make_async_copy(
            dm_s.at[pl.ds(pl.multiple_of((me_ref[1] ^ member) * rows, rows), rows), :],
            (dm_keep, dm_send)[member % 2].at[member // 2],
            dm_sems.at[member],
        )
        for member in range(4)
    ]
    start_all([dm_copies])
    store_kind(dw_s, 1, dwkv_s[:, :width])
    store_kind(dw_s, 2, dwkv_s[:, width:])
    start_all(out_copies)
    wait_all(dm_copies)
    for group in out_copies:
        wait_all(group)


def cross_backward(
    me, ranges, dy, xhat, rstd, norms, k_norm, xin, k_in, segq, segk, saved, memory, weights, grads
):
    (own, sib), offset = weights
    prior, out_offset, out_width = grads
    rows, width = xin.shape
    keys = 4 * rows
    pairs = width // PAIR
    piece = shaped((16, SLAB, out_width), BF16)
    half = shaped((2, rows, width), BF16)
    return pl.pallas_call(
        functools.partial(cross_backward_kernel, offset, out_offset, k_norm, k_in, len(prior)),
        out_shape=(shaped((rows, width), F32), shaped((2, width), F32), half, half, piece, piece),
        in_specs=smem(2) + vmem(12) + hbm(6 + len(prior)),
        out_specs=(*vmem(2), *hbm(4)),
        input_output_aliases={20 + i: 4 + i for i in range(len(prior))},
        scratch_shapes=[
            pltpu.VMEM((keys, width), BF16),
            pltpu.VMEM((4, width, width), BF16),
            pltpu.VMEM((width, 4 * width), BF16),
            pltpu.VMEM((4, width, width), BF16),
            pltpu.VMEM((rows, width), BF16),
            pltpu.VMEM((width, keys), BF16),
            pltpu.VMEM((pairs, PAIR, 2 * BLOCK), F32),
            pltpu.VMEM((width, rows), BF16),
            pltpu.VMEM((keys, 2 * width), F32),
            pltpu.VMEM((width, 2 * width), F32),
            pltpu.VMEM((keys, width), BF16),
            pltpu.SemaphoreType.DMA((4, width // SLAB)),
            pltpu.SemaphoreType.DMA((4, width // SLAB)),
            pltpu.SemaphoreType.DMA((4,)),
            pltpu.SemaphoreType.DMA((4,)),
        ],
        compiler_params=params(),
        name="cross_backward",
    )(me, ranges, dy, xhat, rstd, norms, xin, segq, segk, *saved, *memory, own, sib, *prior)


def gelu_and_slope(pre):
    square = pre * pre
    tanh = jnp.tanh(gelu_a * pre * (1.0 + gelu_b * square))
    cdf = 0.5 + 0.5 * tanh
    slope = cdf + (0.5 * gelu_a) * pre * (1.0 - tanh * tanh) * (1.0 + (3.0 * gelu_b) * square)
    return (pre * cdf).astype(BF16), slope.astype(BF16)


def feed_members_forward(low, acc_s, w_vmem, copies, hidden_ref, slope_ref):
    half = w_vmem.shape[2] // 2
    for member in range(4):
        wait_all(copies[member])
        hidden, slope = gelu_and_slope(mm(low, w_vmem[member, :, :half]))
        hidden_ref[member] = hidden
        slope_ref[member] = slope
        acc_s[...] += mm(hidden, w_vmem[member, :, half:], NT)


def feed_members_backward(
    low, x_low, dx_ref, w_vmem, copies, hidden_ref, slope_ref, dw_s, out_copies
):
    half = w_vmem.shape[2] // 2
    lowt = low.T
    xt = x_low.T
    for member in range(4):
        if copies is not None:
            wait_all(copies[member])
        dhidden = mm(low, w_vmem[member, :, half:])
        dpre = (dhidden * slope_ref[member].astype(F32)).astype(BF16)
        dw_s[member, :, :half] = mm(xt, dpre).astype(BF16)
        dw_s[member, :, half:] = mm(lowt, hidden_ref[member]).astype(BF16)
        start_all([out_copies[member]])
        dx_ref[...] += mm(dpre, w_vmem[member, :, :half], NT)
    for group in out_copies:
        wait_all(group)


def feed_forward_kernel(
    offset, norm_offset, k_in, k_out, me_ref, xin_ref, own_hbm, sib_hbm, norm_own_hbm,
    xhat_ref, rstd_ref, out_ref, hidden_ref, slope_ref, norms_ref,
    w_vmem, norm_s, acc_s, sems, norm_sems,
):
    copies = weight_copies(me_ref, (own_hbm, sib_hbm), offset, w_vmem, sems)
    norm_copies = [
        pltpu.make_async_copy(
            norm_own_hbm.at[slot, :, pl.ds(norm_offset, BLOCK)],
            norm_s.at[slab_rows(me_ref, block), :],
            norm_sems.at[block],
        )
        for side, slot, block in slots(0)
    ]
    start_all([norm_copies] + copies)
    wait_all(norm_copies)
    norms = norm_s[...].astype(F32).T[: norms_ref.shape[0], :]
    norms_ref[...] = norms
    inputs = xin_ref[...] * norms[2 * k_in : 2 * k_in + 1] + norms[2 * k_in + 1 : 2 * k_in + 2]
    acc_s[...] = inputs
    feed_members_forward(inputs.astype(BF16), acc_s, w_vmem, copies, hidden_ref, slope_ref)
    xhat, rstd = normalize(acc_s[...])
    xhat_ref[...] = xhat
    rstd_ref[...] = rstd
    normed = xhat * norms[2 * k_out : 2 * k_out + 1] + norms[2 * k_out + 1 : 2 * k_out + 2]
    out_ref[...] = normed.astype(BF16)


def feed_forward(me, xin, k_in, k_out, weights, norm_piece):
    (own, sib), offset = weights
    (norm_own, _), norm_offset = norm_piece
    rows, width = xin.shape
    part = shaped((4, rows, width), BF16)
    return pl.pallas_call(
        functools.partial(feed_forward_kernel, offset, norm_offset, k_in, k_out),
        out_shape=(
            shaped((rows, width), F32),
            shaped((rows, 1), F32),
            shaped((rows, width), BF16),
            part,
            part,
            shaped((16, width), F32),
        ),
        in_specs=smem(1) + vmem(1) + hbm(3),
        out_specs=tuple(vmem(6)),
        scratch_shapes=[
            pltpu.VMEM((4, width, 2 * width), BF16),
            pltpu.VMEM((width, BLOCK), BF16),
            pltpu.VMEM((rows, width), F32),
            pltpu.SemaphoreType.DMA((4, width // SLAB)),
            pltpu.SemaphoreType.DMA((width // SLAB,)),
        ],
        compiler_params=params(),
        name="feed_forward",
    )(me, xin, own, sib, norm_own)


def feed_backward_kernel(
    offset, out_offset, k_in, k_out, prior, me_ref, dy_ref, xhat_ref, rstd_ref, norms_ref, xin_ref,
    hidden_ref, slope_ref, own_hbm, sib_hbm, *rest,
):
    rest = rest[prior:]
    dx_ref, dnorm_ref, keep_hbm, send_hbm, w_vmem, dw_s, sems, out_sems = rest
    copies = weight_copies(me_ref, (own_hbm, sib_hbm), offset, w_vmem, sems)
    start_all(copies)
    out_copies = grad_copies(me_ref, dw_s, (keep_hbm, send_hbm), out_offset, out_sems)
    dy = dy_ref[...].astype(F32)
    xhat = xhat_ref[...]
    dgain, dshift = norm_param_grads(dy, xhat)
    dnorm_ref[0:1, :] = dgain
    dnorm_ref[1:2, :] = dshift
    dtotal = norm_backward(dy, xhat, rstd_ref[...], norms_ref[2 * k_out : 2 * k_out + 1, :])
    dx_ref[...] = dtotal
    gain, shift = norms_ref[2 * k_in : 2 * k_in + 1, :], norms_ref[2 * k_in + 1 : 2 * k_in + 2, :]
    inputs = (xin_ref[...] * gain + shift).astype(BF16)
    feed_members_backward(
        dtotal.astype(BF16), inputs, dx_ref, w_vmem, copies, hidden_ref, slope_ref, dw_s, out_copies
    )


def feed_backward(me, dy, xhat, rstd, norms, xin, k_in, k_out, hidden, slope, weights, grads):
    (own, sib), offset = weights
    prior, out_offset, out_width = grads
    rows, width = xin.shape
    piece = shaped((16, SLAB, out_width), BF16)
    return pl.pallas_call(
        functools.partial(feed_backward_kernel, offset, out_offset, k_in, k_out, len(prior)),
        out_shape=(shaped((rows, width), F32), shaped((2, width), F32), piece, piece),
        in_specs=smem(1) + vmem(7) + hbm(2 + len(prior)),
        out_specs=(*vmem(2), *hbm(2)),
        input_output_aliases={10 + i: 2 + i for i in range(len(prior))},
        scratch_shapes=[
            pltpu.VMEM((4, width, 2 * width), BF16),
            pltpu.VMEM((4, width, 2 * width), BF16),
            pltpu.SemaphoreType.DMA((4, width // SLAB)),
            pltpu.SemaphoreType.DMA((4, width // SLAB)),
        ],
        compiler_params=params(),
        name="feed_backward",
    )(me, dy, xhat, rstd, norms, xin, hidden, slope, own, sib, *prior)


def feed_turn_kernel(
    offset, out_offset, k_in, k_out, me_ref, xin_ref, norms_ref, dy_ref, own_hbm, sib_hbm,
    out_ref, dx_ref, dnorm_ref, keep_hbm, send_hbm,
    w_vmem, dw_s, hidden_s, slope_s, sems, out_sems,
):
    copies = weight_copies(me_ref, (own_hbm, sib_hbm), offset, w_vmem, sems)
    start_all(copies)
    out_copies = grad_copies(me_ref, dw_s, (keep_hbm, send_hbm), out_offset, out_sems)
    gain, shift = norms_ref[2 * k_in : 2 * k_in + 1, :], norms_ref[2 * k_in + 1 : 2 * k_in + 2, :]
    inputs = xin_ref[...] * gain + shift
    dx_ref[...] = inputs
    low = inputs.astype(BF16)
    feed_members_forward(low, dx_ref, w_vmem, copies, hidden_s, slope_s)
    xhat, rstd = normalize(dx_ref[...])
    gain = norms_ref[2 * k_out : 2 * k_out + 1, :]
    out_ref[...] = (xhat * gain + norms_ref[2 * k_out + 1 : 2 * k_out + 2, :]).astype(BF16)
    dy = dy_ref[...].astype(F32)
    dgain, dshift = norm_param_grads(dy, xhat)
    dnorm_ref[0:1, :] = dgain
    dnorm_ref[1:2, :] = dshift
    dtotal = norm_backward(dy, xhat, rstd, gain)
    dx_ref[...] = dtotal
    feed_members_backward(
        dtotal.astype(BF16), low, dx_ref, w_vmem, None, hidden_s, slope_s, dw_s, out_copies
    )


def feed_turn(me, xin, norms, k_in, k_out, dy, weights, grads):
    (own, sib), offset = weights
    _, out_offset, out_width = grads
    rows, width = xin.shape
    piece = shaped((16, SLAB, out_width), BF16)
    return pl.pallas_call(
        functools.partial(feed_turn_kernel, offset, out_offset, k_in, k_out),
        out_shape=(
            shaped((rows, width), BF16),
            shaped((rows, width), F32),
            shaped((2, width), F32),
            piece,
            piece,
        ),
        in_specs=smem(1) + vmem(3) + hbm(2),
        out_specs=(*vmem(3), *hbm(2)),
        scratch_shapes=[
            pltpu.VMEM((4, width, 2 * width), BF16),
            pltpu.VMEM((4, width, 2 * width), BF16),
            pltpu.VMEM((4, rows, width), BF16),
            pltpu.VMEM((4, rows, width), BF16),
            pltpu.SemaphoreType.DMA((4, width // SLAB)),
            pltpu.SemaphoreType.DMA((4, width // SLAB)),
        ],
        compiler_params=params(),
        name="feed_turn",
    )(me, xin, norms, dy, own, sib)


DP = ("z", "x")
MP = ("y", "c")
ALL = ("z", "x", "y", "c")


def is_cube():
    return tuple(lax.axis_size(axis) for axis in ALL) == (4, 2, 2, 2)


def swap(values, axis, distance=1):
    return lax.ppermute(values, axis, [(i, i ^ distance) for i in range(lax.axis_size(axis))])


def gather_pieces(shard):
    if not is_cube():
        whole = lax.all_gather(shard, MP + DP, axis=0, tiled=True)
        whole = whole.reshape(2, 2, 4, 2, SLAB, shard.shape[1])
        whole = whole.transpose(1, 0, 3, 2, 4, 5)
        whole = whole.reshape(2, 16, SLAB, shard.shape[1])
        return whole[0], whole[1]
    lines = jnp.stack([shard] + [swap(shard, "z", k) for k in (1, 2, 3)])
    over_x, over_y = swap(lines, "x"), swap(lines, "y")
    far_one, far_two = swap(over_y[:2], "x"), swap(over_x[2:], "y")
    own = jnp.concatenate([lines, over_x, over_y, far_one, far_two], axis=0)
    return own, swap(own, "c")


def add(*terms):
    return sum(term.astype(F32) for term in terms)


def reduce_pieces(keep, send):
    if not is_cube():
        whole = jnp.stack([keep, send]).reshape(2, 2, 2, 4, SLAB, keep.shape[2])
        whole = whole.transpose(1, 0, 3, 2, 4, 5).reshape(4, 8 * SLAB, keep.shape[2])
        part = lax.psum_scatter(whole, MP, scatter_dimension=0, tiled=True)
        part = lax.psum_scatter(part[0], DP, scatter_dimension=0, tiled=True)
        return part.astype(F32)
    got = swap(send, "c")
    far_one = swap(add(keep[12:14], got[12:14]).astype(BF16), "x")
    far_two = swap(add(keep[14:16], got[14:16]).astype(BF16), "y")
    to_x = jnp.concatenate(
        [add(keep[4:6], got[4:6]).astype(BF16), add(keep[6:8], got[6:8], far_two).astype(BF16)]
    )
    to_y = jnp.concatenate(
        [add(keep[8:10], got[8:10], far_one).astype(BF16), add(keep[10:12], got[10:12]).astype(BF16)]
    )
    from_x, from_y = swap(to_x, "x"), swap(to_y, "y")
    lines = [
        add(keep[k], got[k], from_x[k], from_y[k]).astype(F32 if k == 0 else BF16) for k in range(4)
    ]
    return add(lines[0], *(swap(lines[k], "z", k) for k in (1, 2, 3)))


def sum_all(values):
    if not is_cube():
        return lax.psum(values, ALL)
    for axis, distance in (("c", 1), ("y", 1), ("x", 1), ("z", 1), ("z", 2)):
        values = values + swap(values, axis, distance)
    return values


def gather_memory(values):
    if not is_cube():
        whole = lax.all_gather(values, MP, axis=0, tiled=False)
        return tuple(whole[k] for k in range(4))
    over_y, over_c = swap(values, "y"), swap(values, "c")
    return (values, over_c, over_y, swap(over_y, "c"))


def reduce_memory(keep, send):
    if not is_cube():
        whole = jnp.stack([keep[0], send[0], keep[1], send[1]])
        return lax.psum_scatter(whole, MP, scatter_dimension=0, tiled=True)[0].astype(F32)
    got = swap(send, "c")
    over_y = swap(add(keep[1], got[1]).astype(BF16), "y")
    return add(keep[0], got[0], over_y)


def shift_rows(values, step):
    count = lax.axis_size(MP)
    pairs = [(i, i + step) for i in range(count) if 0 <= i + step < count]
    return lax.ppermute(values, MP, pairs)


def with_halos(first, second):
    before = shift_rows(jnp.concatenate([first[-BLOCK:], second[-BLOCK:]]), 1)
    after = shift_rows(jnp.concatenate([first[:BLOCK], second[:BLOCK]]), -1)
    return (
        jnp.concatenate([before[:BLOCK], first, after[:BLOCK]]),
        jnp.concatenate([before[BLOCK:], second, after[BLOCK:]]),
    )


def add_halos(values, before, after):
    rows = values.shape[0]
    return (
        values
        + jnp.pad(before, ((0, rows - BLOCK), (0, 0)))
        + jnp.pad(after, ((rows - BLOCK, 0), (0, 0)))
    )


def adam_step(weights, first, second, grads, rate, decay):
    first_new = beta_one * first + (1.0 - beta_one) * grads
    second_new = beta_two * second + (1.0 - beta_two) * grads * grads
    first_hat = first_new / (1.0 - beta_one**STEP)
    second_hat = second_new / (1.0 - beta_two**STEP)
    weights_new = weights - rate * (first_hat / (jnp.sqrt(second_hat) + adam_eps) + decay * weights)
    return (weights_new, first_new, second_new)


GATHERS = (("enc",), ("enc_feed", "norms", "self"), ("cross",), ("dec_feed",))
REDUCES = (("dec_feed",), ("cross", "self"), ("enc_feed",), ("enc",))


def on_device(
    encoder_input, decoder_copy, decoder_target, decoder_cotangent,
    source_segments, target_segments, glance_mask,
    attention_in, attention_out, feed_in, feed_out, norm_params,
    attention_in_first, attention_out_first, feed_in_first, feed_out_first, norm_params_first,
    attention_in_second, attention_out_second, feed_in_second, feed_out_second, norm_params_second,
):
    rows, width = encoder_input.shape
    part, half = attention_in.shape[2], feed_in.shape[2]
    masters = (attention_in, attention_out, feed_in, feed_out, norm_params)

    def attention_shard(number):
        kinds = [attention_in[3 * number + kind] for kind in range(3)]
        return jnp.concatenate(kinds + [attention_out[number].T], axis=1)

    def feed_shard(number):
        return jnp.concatenate([feed_in[number], feed_out[number].T], axis=1)

    norm_columns = norm_params.reshape(10, -1).T
    shards = {
        "enc": attention_shard(0),
        "enc_feed": feed_shard(0),
        "norms": jnp.pad(norm_columns, ((0, 0), (0, BLOCK - 10))),
        "self": attention_shard(1),
        "cross": attention_shard(2),
        "dec_feed": feed_shard(1),
    }
    weights = {}
    for group in GATHERS:
        joined = jnp.concatenate([shards[name].astype(BF16) for name in group], axis=1)
        pieces = gather_pieces(joined)
        offset = 0
        for name in group:
            weights[name] = (pieces, offset)
            offset += shards[name].shape[1]

    picked = glance_mask[0] == 1
    decoder_input = jnp.where(picked[:, None], decoder_target, decoder_copy)
    encoder_x, decoder_x = with_halos(encoder_input, decoder_input)

    member = lax.axis_index(MP)
    position = member * rows
    blocks = rows // BLOCK
    me = jnp.stack([lax.axis_index(DP), member]) if is_cube() else jnp.zeros((2,), jnp.int32)
    me = me.astype(jnp.int32)

    def query_segments(row):
        own = lax.dynamic_slice(row, (position,), (rows,)).reshape(blocks, BLOCK)
        return jnp.concatenate([own, own], axis=1)

    def key_segments(row):
        padded = jnp.pad(row, (BLOCK, BLOCK), constant_values=-1)
        return lax.dynamic_slice(padded, (position,), (rows + 2 * BLOCK,))[:, None]

    source_row, target_row = source_segments[0], target_segments[0]
    source_q, target_q = query_segments(source_row), query_segments(target_row)
    source_k, target_k = key_segments(source_row), key_segments(target_row)
    lowest, highest = target_q[:, 0], target_q[:, BLOCK - 1]
    first_key = jnp.sum((source_row[None, :] < lowest[:, None]).astype(jnp.int32), axis=1)
    last_key = jnp.sum((source_row[None, :] <= highest[:, None]).astype(jnp.int32), axis=1)
    ranges = jnp.stack([first_key // BLOCK, (last_key + BLOCK - 1) // BLOCK], axis=1)
    ranges = ranges.astype(jnp.int32).reshape(2 * blocks)
    source_column = source_row[:, None]

    grads, buffers = {}, {}
    for group in REDUCES:
        offset = 0
        total = sum(shards[name].shape[1] for name in group)
        for name in group:
            grads[name] = (group, offset, total)
            offset += shards[name].shape[1]

    def target(name):
        group, offset, total = grads[name]
        return (buffers.get(group, ()), offset, total)

    def keep_grads(name, pieces):
        buffers[grads[name][0]] = tuple(pieces)

    reduced_groups = {}

    def finish(name):
        group = grads[name][0]
        reduced_groups[group] = reduce_pieces(*buffers[group])

    xhat0, rstd0, *enc_saved = self_forward(me, encoder_x, source_q, source_k, weights["enc"])
    xhat1, rstd1, encoder_output, enc_hidden, enc_slope, norms = feed_forward(
        me, xhat0, 0, 1, weights["enc_feed"], weights["norms"]
    )
    memory = gather_memory(encoder_output)
    xhat2, rstd2, *self_saved = self_forward(me, decoder_x, target_q, target_k, weights["self"])
    xhat3, rstd3, *cross_saved = cross_forward(
        me, ranges, xhat2, norms, 2, target_q, source_column, memory, weights["cross"]
    )
    decoder_output, d4, dnorm4, *pieces = feed_turn(
        me, xhat3, norms, 3, 4, decoder_cotangent, weights["dec_feed"], target("dec_feed")
    )
    keep_grads("dec_feed", pieces)
    finish("dec_feed")

    d3, dnorm3, dm_keep, dm_send, *pieces = cross_backward(
        me, ranges, d4, xhat3, rstd3, norms, 3, xhat2, 2, target_q, source_column, cross_saved,
        memory, weights["cross"], target("cross"),
    )
    keep_grads("cross", pieces)
    dmemory = reduce_memory(dm_keep, dm_send)
    dx_dec, before_dec, after_dec, dnorm2, *pieces = self_backward(
        me, d3, xhat2, rstd2, norms, 2, decoder_x, self_saved, weights["self"], target("self")
    )
    keep_grads("self", pieces)
    finish("self")
    d1, dnorm1, *pieces = feed_backward(
        me, dmemory, xhat1, rstd1, norms, xhat0, 0, 1, enc_hidden, enc_slope,
        weights["enc_feed"], target("enc_feed"),
    )
    keep_grads("enc_feed", pieces)
    finish("enc_feed")
    dx_enc, before_enc, after_enc, dnorm0, *pieces = self_backward(
        me, d1, xhat0, rstd0, norms, 0, encoder_x, enc_saved, weights["enc"], target("enc")
    )
    keep_grads("enc", pieces)
    finish("enc")
    before = shift_rows(jnp.concatenate([after_enc, after_dec]), 1)
    after = shift_rows(jnp.concatenate([before_enc, before_dec]), -1)
    encoder_input_grad = add_halos(dx_enc, before[:BLOCK], after[:BLOCK])
    decoder_input_grad = add_halos(dx_dec, before[BLOCK:], after[BLOCK:])

    reduced = {}
    for group, values in reduced_groups.items():
        for name in group:
            offset = grads[name][1]
            reduced[name] = values[:, offset : offset + shards[name].shape[1]]
    squares = sum(jnp.sum(values * values) for values in reduced_groups.values())
    payload = jnp.concatenate(
        [dnorm0, dnorm1, dnorm2, dnorm3, dnorm4, jnp.broadcast_to(squares, (1, width))]
    )
    payload = sum_all(payload)
    g_all = payload[:10]
    grad_norm = jnp.sqrt(payload[10, 0] + jnp.sum(g_all * g_all))
    factor = clip_bound / jnp.maximum(grad_norm, clip_bound)
    own_columns = norm_params.shape[2]
    g_norms = lax.dynamic_slice(g_all, (0, lax.axis_index(DP) * own_columns), (10, own_columns))

    attention_parts = [reduced[name] for name in ("enc", "self", "cross")]
    feed_parts = [reduced[name] for name in ("enc_feed", "dec_feed")]
    g_in = jnp.stack(
        [g[:, kind * part : (kind + 1) * part] for g in attention_parts for kind in range(3)]
    )
    g_out = jnp.stack([g[:, 3 * part :].T for g in attention_parts])
    g_first = jnp.stack([g[:, :half] for g in feed_parts])
    g_second = jnp.stack([g[:, half:].T for g in feed_parts])
    all_grads = (g_in, g_out, g_first, g_second, g_norms.reshape(norm_params.shape))
    firsts = (
        attention_in_first, attention_out_first, feed_in_first, feed_out_first, norm_params_first,
    )
    seconds = (
        attention_in_second, attention_out_second, feed_in_second, feed_out_second,
        norm_params_second,
    )
    results = []
    for number in range(5):
        rate = rate_norm if number == 4 else rate_matrix
        decay = 0.0 if number == 4 else weight_decay
        results.append(
            adam_step(
                masters[number],
                firsts[number],
                seconds[number],
                all_grads[number] * factor,
                rate,
                decay,
            )
        )
    return (
        encoder_output,
        decoder_output,
        encoder_input_grad,
        decoder_input_grad,
        grad_norm,
        *(result[0] for result in results),
        *(result[1] for result in results),
        *(result[2] for result in results),
    )


def solution(mesh):
    dp, mp = mesh.shape["dp"], mesh.shape["mp"]
    fine = Mesh(mesh.devices.reshape(dp // 2, 2, mp // 2, 2), ALL)
    tokens = P(ALL, None)
    columns = P(None, DP, MP)
    turned = P(None, MP, DP)
    states = (columns, turned, columns, turned, P(None, None, DP))
    return jax.shard_map(
        on_device,
        mesh=fine,
        in_specs=(
            *((tokens,) * 4),
            P(DP, None),
            P(DP, None),
            P(DP, MP),
            *states,
            *states,
            *states,
        ),
        out_specs=(*((tokens,) * 4), P(), *states, *states, *states),
        check_vma=False,
    )
```

```python
import functools

import jax
import jax.numpy as jnp
from jax import lax
from jax.experimental import pallas as pl
from jax.experimental.pallas import tpu as pltpu
from jax.sharding import Mesh
from jax.sharding import PartitionSpec as P

HEAD_DIM = 64
STEP = 10
BLOCK = 128
PAIR = 2 * HEAD_DIM

norm_eps = 1e-05
beta_one = 0.9
beta_two = 0.98
adam_eps = 1e-08
weight_decay = 0.01
rate_matrix = 0.1
rate_norm = 0.5
clip_bound = 1.0
masked_score = -1e30
score_scale = HEAD_DIM ** (-0.5)
gelu_a = 0.7978845608028654
gelu_b = 0.044715

F32 = jnp.float32
BF16 = jnp.bfloat16
ANY = pl.ANY
SMEM = pltpu.SMEM
VMEM = pltpu.VMEM

NN = (((1,), (0,)), ((), ()))
NT = (((1,), (1,)), ((), ()))


def mm(a, b, dims=NN):
    return lax.dot_general(a, b, dims, preferred_element_type=F32)


def vmem(count):
    return [pl.BlockSpec(memory_space=VMEM)] * count


def smem(count):
    return [pl.BlockSpec(memory_space=SMEM)] * count


def hbm(count):
    return [pl.BlockSpec(memory_space=ANY)] * count


def cost(microseconds):
    return pl.CostEstimate(
        flops=int(microseconds * 1.15e9), bytes_accessed=int(microseconds * 3.6e6), transcendentals=0
    )


def params(mib=60):
    return pltpu.CompilerParams(vmem_limit_bytes=mib * 1024 * 1024)


def shaped(shape, dtype):
    return jax.ShapeDtypeStruct(shape, dtype)


def normalize(total):
    centred = total - jnp.mean(total, axis=-1, keepdims=True)
    spread = jnp.mean(centred * centred, axis=-1, keepdims=True)
    rstd = lax.rsqrt(spread + norm_eps)
    return centred * rstd, rstd


def norm_backward(grad_out, xhat, rstd, gain):
    scaled = grad_out * gain
    first = jnp.mean(scaled, axis=-1, keepdims=True)
    second = jnp.mean(scaled * xhat, axis=-1, keepdims=True)
    return rstd * (scaled - first - xhat * second)


def norm_param_grads(grad_out, xhat):
    return (
        jnp.sum(grad_out * xhat, axis=0, keepdims=True),
        jnp.sum(grad_out, axis=0, keepdims=True),
    )


def half_masks():
    lane = lax.broadcasted_iota(jnp.int32, (1, PAIR), 1)
    low = jnp.where(lane < HEAD_DIM, 1.0, 0.0).astype(BF16)
    high = jnp.where(lane < HEAD_DIM, 0.0, 1.0).astype(BF16)
    return low, high


def stack_pair(values, masks):
    return jnp.concatenate([values * masks[0], values * masks[1]], axis=0)


SLAB = 64
PIECES = (4, 4, 4, 2, 2)


def slab_shape(width):
    return (4, 2, SLAB, width)


def flat(values):
    return values.reshape(values.shape[0] * values.shape[1] * values.shape[2], values.shape[3])


def weight_copies(me_ref, pieces, offset, w_vmem, sems):
    width = w_vmem.shape[4]
    columns = pl.ds(offset, width)
    copies = []
    for member in range(4):
        side, row = member % 2, member // 2
        group = []
        for x in range(2):
            number = 2 * row + x
            if side == 1 and len(pieces) == len(PIECES) + 1:
                parts = [(pieces[-1].at[pl.ds(4 * number, 4)], 0, 4)]
            elif number < 3:
                parts = [(pieces[side * len(PIECES) + number], 0, 4)]
            else:
                parts = [(pieces[side * len(PIECES) + 3 + k], 2 * k, 2) for k in range(2)]
            for part, start, count in parts:
                group.append(
                    pltpu.make_async_copy(
                        part.at[:, :, columns],
                        w_vmem.at[member, pl.ds(start, count), me_ref[1] ^ x],
                        sems.at[member, 2 * x + start // 2],
                    )
                )
        copies.append(group)
    return copies


def grad_copies(me_ref, dw_vmem, pieces, offset, sems):
    columns = pl.ds(offset, dw_vmem.shape[4])
    return [
        [
            pltpu.make_async_copy(
                dw_vmem.at[member, :, me_ref[1] ^ x],
                pieces[member % 2].at[pl.ds(4 * (2 * (member // 2) + x), 4), :, columns],
                sems.at[member, x],
            )
            for x in range(2)
        ]
        for member in range(4)
    ]


def start_all(groups):
    for group in groups:
        for copy in group:
            copy.start()


def wait_all(group):
    for copy in group:
        copy.wait()


class Inputs:
    def __init__(self, sources, places, sems):
        self.places = places
        self.copies = [
            pltpu.make_async_copy(source, place, sems.at[number])
            for number, (source, place) in enumerate(zip(sources, places))
        ]
        self.waited = set()

    def start(self, *numbers):
        for number in numbers:
            self.copies[number].start()

    def __getitem__(self, number):
        if number not in self.waited:
            self.waited.add(number)
            self.copies[number].wait()
        return self.places[number]


class Outputs:
    def __init__(self, places, targets, sems):
        self.places = places
        self.copies = [
            pltpu.make_async_copy(place, target, sems.at[number])
            for number, (place, target) in enumerate(zip(places, targets))
        ]

    def __getitem__(self, number):
        return self.places[number]

    def send(self, *numbers):
        for number in numbers:
            self.copies[number].start()

    def finish(self):
        wait_all(self.copies)


def staged(
    body, name, me, others, inputs, pieces, outputs, direct=(), scratch=(), prior=(), microseconds=10
):
    scalars = (me, *others)
    counts = (len(scalars), len(inputs), len(pieces), len(prior), len(outputs), len(direct))

    def kernel(*refs):
        parts, at = [], 0
        for count in counts:
            parts.append(refs[at : at + count])
            at += count
        scalar_refs, sources, piece_refs, _, targets, direct_refs = parts
        rest = refs[at:]
        in_places, rest = rest[: len(inputs)], rest[len(inputs) :]
        out_places, rest = rest[: len(outputs)], rest[len(outputs) :]
        in_sems, out_sems, rest = rest[0], rest[1], rest[2:]
        body(
            scalar_refs,
            Inputs(sources, in_places, in_sems),
            piece_refs,
            Outputs(out_places, targets, out_sems),
            direct_refs,
            *rest,
        )

    first_prior = len(scalars) + len(inputs) + len(pieces)
    return pl.pallas_call(
        kernel,
        out_shape=(*outputs, *direct),
        in_specs=smem(len(scalars)) + hbm(len(inputs) + len(pieces) + len(prior)),
        out_specs=tuple(hbm(len(outputs) + len(direct))),
        input_output_aliases={first_prior + i: len(outputs) + i for i in range(len(prior))},
        scratch_shapes=[
            *(pltpu.VMEM(array.shape, array.dtype) for array in inputs),
            *(pltpu.VMEM(array.shape, array.dtype) for array in outputs),
            pltpu.SemaphoreType.DMA((max(len(inputs), 1),)),
            pltpu.SemaphoreType.DMA((max(len(outputs), 1),)),
            *scratch,
        ],
        compiler_params=params(),
        cost_estimate=cost(microseconds),
        name=name,
    )(*scalars, *inputs, *pieces, *prior)


def weight_scratch(width):
    return [pltpu.VMEM((4, *slab_shape(width)), BF16), pltpu.SemaphoreType.DMA((4, 4))]


def grad_scratch(width):
    return [pltpu.VMEM((4, *slab_shape(width)), BF16), pltpu.SemaphoreType.DMA((4, 2))]


def spread_kinds(w_vmem, w_flat, member):
    part = w_vmem.shape[4] // 4
    for kind in range(4):
        w_flat[:, pl.ds((kind * 4 + member) * part, part)] = flat(
            w_vmem[member, :, :, :, kind * part : (kind + 1) * part]
        )


def store_kind(dw_vmem, kind, grads):
    part = dw_vmem.shape[4] // 4
    for member in range(4):
        dw_vmem[member, :, :, :, kind * part : (kind + 1) * part] = (
            grads[:, member * part : (member + 1) * part].astype(BF16).reshape(slab_shape(part))
        )


def self_forward(me, x, segq, segk, weights):
    pieces, offset = weights
    keys, width = x.shape
    rows = keys - 2 * BLOCK
    blocks, pairs = rows // BLOCK, width // PAIR
    window = 3 * BLOCK

    def body(scalars, ins, piece_refs, outs, direct, w_vmem, w_sems, w_s, vt_s, ctxt_s):
        ins.start(0)
        copies = weight_copies(scalars[0], piece_refs, offset, w_vmem, w_sems)
        start_all(copies)
        ins.start(1, 2)
        xhat_o, rstd_o, q_o, k_o, v_o, ctx_o, pt_o = outs.places
        for member in range(4):
            wait_all(copies[member])
            spread_kinds(w_vmem, w_s, member)
        x_ref = ins[0]
        kv = mm(x_ref[...], w_s[:, width : 3 * width]).astype(BF16)
        k_o[...] = kv[:, :width]
        v_o[...] = kv[:, width:]
        outs.send(3, 4)
        vt_s[...] = kv[:, width:].T
        q = mm(x_ref[BLOCK : BLOCK + rows, :], w_s[:, :width]).astype(BF16)
        q_o[...] = q * jnp.asarray(score_scale, BF16)
        outs.send(2)
        masks = half_masks()
        segq_ref, segk_ref = ins[1], ins[2]
        for block in range(blocks):
            at = pl.ds(block * BLOCK, BLOCK)
            keys_at = pl.ds(block * BLOCK, window)
            allowed = segk_ref[keys_at, :] == segq_ref[block : block + 1, :]
            for pair in range(pairs):
                cols = pl.ds(pair * PAIR, PAIR)
                stacked = stack_pair(q_o[at, cols], masks)
                scores = mm(k_o[keys_at, cols], stacked, NT)
                scores = jnp.where(allowed, scores, masked_score)
                highest = jnp.max(scores, axis=0, keepdims=True)
                raised = jnp.exp(scores - highest)
                total = jnp.sum(raised, axis=0, keepdims=True)
                probs = (raised * (1.0 / total)).astype(BF16)
                pt_o[block * pairs + pair] = probs
                context = mm(vt_s[cols, keys_at], probs).astype(BF16)
                ctxt_s[pl.ds(pair * PAIR, HEAD_DIM), at] = context[:HEAD_DIM, :BLOCK]
                ctxt_s[pl.ds(pair * PAIR + HEAD_DIM, HEAD_DIM), at] = context[HEAD_DIM:, BLOCK:]
        outs.send(6)
        context = ctxt_s[...].T
        ctx_o[...] = context
        outs.send(5)
        branch = mm(context, w_s[:, 3 * width :], NT)
        xhat, rstd = normalize(x_ref[BLOCK : BLOCK + rows, :].astype(F32) + branch)
        xhat_o[...] = xhat
        rstd_o[...] = rstd
        outs.send(0, 1)
        outs.finish()

    return staged(
        body,
        "self_forward",
        me,
        (),
        (x, segq, segk),
        pieces,
        (
            shaped((rows, width), F32),
            shaped((rows, 1), F32),
            shaped((rows, width), BF16),
            shaped((keys, width), BF16),
            shaped((keys, width), BF16),
            shaped((rows, width), BF16),
            shaped((blocks * pairs, window, 2 * BLOCK), BF16),
        ),
        scratch=(
            *weight_scratch(width),
            pltpu.VMEM((width, 4 * width), BF16),
            pltpu.VMEM((width, keys), BF16),
            pltpu.VMEM((width, rows), BF16),
        ),
        microseconds=9,
    )


def self_backward(me, dy, xhat, rstd, norms, k_norm, x, saved, weights, grads):
    pieces, offset = weights
    prior, out_offset, out_width = grads
    keys, width = x.shape
    rows = keys - 2 * BLOCK
    blocks, pairs = rows // BLOCK, width // PAIR
    window = 3 * BLOCK

    def body(
        scalars, ins, piece_refs, outs, direct,
        w_vmem, w_sems, dw_s, dw_sems, w_s, dctx_s, kt_s, dqt_s, dkv_s,
    ):
        copies = weight_copies(scalars[0], piece_refs, offset, w_vmem, w_sems)
        ins.start(0, 1, 2, 3)
        start_all(copies)
        ins.start(8, 6, 7, 9, 5, 4)
        out_copies = grad_copies(scalars[0], dw_s, direct, out_offset, dw_sems)
        dx_o, before_o, after_o, dnorm_o = outs.places
        dy_ref, xhat_ref, rstd_ref, norms_ref = ins[0], ins[1], ins[2], ins[3]
        masks = half_masks()
        dy = dy_ref[...]
        xhat = xhat_ref[...]
        dgain, dshift = norm_param_grads(dy, xhat)
        dnorm_o[0:1, :] = dgain
        dnorm_o[1:2, :] = dshift
        outs.send(3)
        dtotal = norm_backward(dy, xhat, rstd_ref[...], norms_ref[2 * k_norm : 2 * k_norm + 1, :])
        low = dtotal.astype(BF16)
        for member in range(4):
            wait_all(copies[member])
            spread_kinds(w_vmem, w_s, member)
        dctx_s[...] = mm(low, w_s[:, 3 * width :]).astype(BF16)
        store_kind(dw_s, 3, mm(low.T, ins[8][...]))
        kt_s[...] = ins[6][...].T
        dkv_s[...] = jnp.zeros_like(dkv_s)
        q_ref, v_ref, pt_ref = ins[5], ins[7], ins[9]
        for block in range(blocks):
            at = pl.ds(block * BLOCK, BLOCK)
            keys_at = pl.ds(block * BLOCK, window)
            for pair in range(pairs):
                cols = pl.ds(pair * PAIR, PAIR)
                dstacked = stack_pair(dctx_s[at, cols], masks)
                qstacked = stack_pair(q_ref[at, cols], masks)
                probs_low = pt_ref[block * pairs + pair]
                probs = probs_low.astype(F32)
                dprobs = mm(v_ref[keys_at, cols], dstacked, NT)
                delta = jnp.sum(probs * dprobs, axis=0, keepdims=True)
                dscores = (probs * (dprobs - delta)).astype(BF16)
                dkv_s[keys_at, cols] += mm(dscores, qstacked)
                dkv_s[keys_at, pl.ds(width + pair * PAIR, PAIR)] += mm(probs_low, dstacked)
                dqt = mm(kt_s[cols, keys_at], dscores) * score_scale
                dqt = dqt.astype(BF16)
                dqt_s[pl.ds(pair * PAIR, HEAD_DIM), at] = dqt[:HEAD_DIM, :BLOCK]
                dqt_s[pl.ds(pair * PAIR + HEAD_DIM, HEAD_DIM), at] = dqt[HEAD_DIM:, BLOCK:]
        dq = dqt_s[...].T
        dkv = dkv_s[...].astype(BF16)
        xt = ins[4][...].T
        store_kind(dw_s, 0, mm(xt[:, BLOCK : BLOCK + rows], dq))
        store_kind(dw_s, 1, mm(xt, dkv[:, :width]))
        store_kind(dw_s, 2, mm(xt, dkv[:, width:]))
        start_all(out_copies)
        dx = mm(dkv, w_s[:, width : 3 * width], NT)
        before_o[...] = dx[:BLOCK]
        after_o[...] = dx[BLOCK + rows :]
        dx_o[...] = dx[BLOCK : BLOCK + rows] + dtotal + mm(dq, w_s[:, :width], NT)
        outs.send(0, 1, 2)
        outs.finish()
        for group in out_copies:
            wait_all(group)

    piece = shaped((16, SLAB, out_width), BF16)
    return staged(
        body,
        "self_backward",
        me,
        (),
        (dy, xhat, rstd, norms, x, *saved),
        pieces,
        (
            shaped((rows, width), F32),
            shaped((BLOCK, width), F32),
            shaped((BLOCK, width), F32),
            shaped((2, width), F32),
        ),
        direct=(piece, piece),
        scratch=(
            *weight_scratch(width),
            *grad_scratch(width),
            pltpu.VMEM((width, 4 * width), BF16),
            pltpu.VMEM((rows, width), BF16),
            pltpu.VMEM((width, keys), BF16),
            pltpu.VMEM((width, rows), BF16),
            pltpu.VMEM((keys, 2 * width), F32),
        ),
        prior=prior,
        microseconds=12,
    )


def memory_copies(member_ref, pieces, m_s, sems):
    rows = pieces[0].shape[0]
    return [
        pltpu.make_async_copy(
            piece,
            m_s.at[pl.ds(pl.multiple_of((member_ref[2] ^ member) * rows, rows), rows), :],
            sems.at[member],
        )
        for member, piece in enumerate(pieces)
    ]


def cross_forward(me, ranges, xin, norms, k_in, segq, segk, memory, weights):
    pieces, offset = weights
    rows, width = xin.shape
    keys = 4 * rows
    blocks, pairs = rows // BLOCK, width // PAIR

    def body(
        scalars, ins, piece_refs, outs, direct,
        w_vmem, w_sems, m_sems, m_s, w_s, vt_s, s_s, acc_s, ctxt_s,
    ):
        me_ref, range_ref = scalars
        ins.start(0, 1)
        copies = weight_copies(me_ref, piece_refs[4:], offset, w_vmem, w_sems)
        start_all(copies)
        m_copies = memory_copies(me_ref, piece_refs[:4], m_s, m_sems)
        start_all([m_copies])
        ins.start(2, 3)
        xhat_o, rstd_o, q_o, k_o, v_o, ctx_o, lse_o = outs.places
        masks = half_masks()
        xin_ref, norms_ref = ins[0], ins[1]
        gain = norms_ref[2 * k_in : 2 * k_in + 1, :]
        shift = norms_ref[2 * k_in + 1 : 2 * k_in + 2, :]
        inputs = xin_ref[...] * gain + shift
        for member in range(4):
            wait_all(copies[member])
            spread_kinds(w_vmem, w_s, member)
        q = mm(inputs.astype(BF16), w_s[:, :width]).astype(BF16)
        q_o[...] = q * jnp.asarray(score_scale, BF16)
        outs.send(2)
        wait_all(m_copies)

        @pl.loop(range_ref[0], range_ref[2 * blocks - 1])
        def _(key_block):
            keys_at = pl.ds(pl.multiple_of(key_block * BLOCK, BLOCK), BLOCK)
            kv = mm(m_s[keys_at, :], w_s[:, width : 3 * width]).astype(BF16)
            k_o[keys_at, :] = kv[:, :width]
            v_o[keys_at, :] = kv[:, width:]
            vt_s[:, keys_at] = kv[:, width:].T

        outs.send(3, 4)
        segq_ref, segk_ref = ins[2], ins[3]
        for block in range(blocks):
            at = pl.ds(block * BLOCK, BLOCK)
            first, last = range_ref[2 * block], range_ref[2 * block + 1]
            stacked = [stack_pair(q_o[at, pl.ds(p * PAIR, PAIR)], masks) for p in range(pairs)]
            segq_row = segq_ref[block : block + 1, :]

            def scan_scores(key_block, highest):
                keys_at = pl.ds(pl.multiple_of(key_block * BLOCK, BLOCK), BLOCK)
                allowed = segk_ref[keys_at, :] == segq_row
                result = []
                for pair in range(pairs):
                    scores = mm(k_o[keys_at, pl.ds(pair * PAIR, PAIR)], stacked[pair], NT)
                    scores = jnp.where(allowed, scores, masked_score)
                    s_s[pair, keys_at, :] = scores
                    result.append(
                        jnp.maximum(highest[pair], jnp.max(scores, axis=0, keepdims=True))
                    )
                return tuple(result)

            start = tuple(jnp.full((1, 2 * BLOCK), masked_score, F32) for _ in range(pairs))
            highest = lax.fori_loop(first, last, scan_scores, start)
            acc_s[...] = jnp.zeros_like(acc_s)

            def scan_context(key_block, sums):
                keys_at = pl.ds(pl.multiple_of(key_block * BLOCK, BLOCK), BLOCK)
                result = []
                for pair in range(pairs):
                    raised = jnp.exp(s_s[pair, keys_at, :] - highest[pair])
                    result.append(sums[pair] + jnp.sum(raised, axis=0, keepdims=True))
                    acc_s[pair] += mm(vt_s[pl.ds(pair * PAIR, PAIR), keys_at], raised.astype(BF16))
                return tuple(result)

            start = tuple(jnp.zeros((1, 2 * BLOCK), F32) for _ in range(pairs))
            sums = lax.fori_loop(first, last, scan_context, start)
            for pair in range(pairs):
                context = (acc_s[pair] * (1.0 / sums[pair])).astype(BF16)
                ctxt_s[pl.ds(pair * PAIR, HEAD_DIM), at] = context[:HEAD_DIM, :BLOCK]
                ctxt_s[pl.ds(pair * PAIR + HEAD_DIM, HEAD_DIM), at] = context[HEAD_DIM:, BLOCK:]
                row = block * pairs + pair
                lse_o[row : row + 1, :] = highest[pair] + jnp.log(sums[pair])
        context = ctxt_s[...].T
        ctx_o[...] = context
        outs.send(5, 6)
        branch = mm(context, w_s[:, 3 * width :], NT)
        xhat, rstd = normalize(inputs + branch)
        xhat_o[...] = xhat
        rstd_o[...] = rstd
        outs.send(0, 1)
        outs.finish()

    return staged(
        body,
        "cross_forward",
        me,
        (ranges,),
        (xin, norms, segq, segk),
        (*memory, *pieces),
        (
            shaped((rows, width), F32),
            shaped((rows, 1), F32),
            shaped((rows, width), BF16),
            shaped((keys, width), BF16),
            shaped((keys, width), BF16),
            shaped((rows, width), BF16),
            shaped((blocks * pairs, 2 * BLOCK), F32),
        ),
        scratch=(
            *weight_scratch(width),
            pltpu.SemaphoreType.DMA((4,)),
            pltpu.VMEM((keys, width), BF16),
            pltpu.VMEM((width, 4 * width), BF16),
            pltpu.VMEM((width, keys), BF16),
            pltpu.VMEM((pairs, keys, 2 * BLOCK), F32),
            pltpu.VMEM((pairs, PAIR, 2 * BLOCK), F32),
            pltpu.VMEM((width, rows), BF16),
        ),
        microseconds=10,
    )


def cross_backward(
    me, ranges, dy, xhat, rstd, norms, k_norm, xin, k_in, segq, segk, saved, memory, weights, grads
):
    pieces, offset = weights
    prior, out_offset, out_width = grads
    rows, width = xin.shape
    keys = 4 * rows
    blocks, pairs = rows // BLOCK, width // PAIR
    heads_here = width // HEAD_DIM

    def body(
        scalars, ins, piece_refs, outs, direct,
        w_vmem, w_sems, dw_s, dw_sems, m_sems, dm_sems,
        m_s, w_s, dctx_s, kt_s, dqt_acc, dqt_s, dkv_s, dwkv_s, dm_s,
    ):
        me_ref, range_ref = scalars
        ins.start(0, 1, 2, 3)
        copies = weight_copies(me_ref, piece_refs[4:], offset, w_vmem, w_sems)
        start_all(copies)
        ins.start(10, 8, 9, 7, 11, 5, 6, 4)
        m_copies = memory_copies(me_ref, piece_refs[:4], m_s, m_sems)
        start_all([m_copies])
        out_copies = grad_copies(me_ref, dw_s, direct[:2], out_offset, dw_sems)
        dm_keep, dm_send = direct[2:]
        dx_o, dnorm_o = outs.places
        dy_ref, xhat_ref, rstd_ref, norms_ref = ins[0], ins[1], ins[2], ins[3]
        masks = half_masks()
        dy = dy_ref[...]
        xhat = xhat_ref[...]
        dgain, dshift = norm_param_grads(dy, xhat)
        dnorm_o[0:1, :] = dgain
        dnorm_o[1:2, :] = dshift
        outs.send(1)
        dtotal = norm_backward(dy, xhat, rstd_ref[...], norms_ref[2 * k_norm : 2 * k_norm + 1, :])
        low = dtotal.astype(BF16)
        for member in range(4):
            wait_all(copies[member])
            spread_kinds(w_vmem, w_s, member)
        dctx = mm(low, w_s[:, 3 * width :]).astype(BF16)
        dctx_s[...] = dctx
        context = ins[10][...]
        store_kind(dw_s, 3, mm(low.T, context))
        products = (dctx.astype(F32) * context.astype(F32)).T
        deltas = [
            jnp.sum(products[h * HEAD_DIM : (h + 1) * HEAD_DIM, :], axis=0, keepdims=True)
            for h in range(heads_here)
        ]
        everything_first, everything_last = range_ref[0], range_ref[2 * blocks - 1]
        k_ref, v_ref, q_ref, lse_ref = ins[8], ins[9], ins[7], ins[11]
        segq_ref, segk_ref = ins[5], ins[6]

        @pl.loop(everything_first, everything_last)
        def _(key_block):
            keys_at = pl.ds(pl.multiple_of(key_block * BLOCK, BLOCK), BLOCK)
            kt_s[:, keys_at] = k_ref[keys_at, :].T
            dkv_s[keys_at, :] = jnp.zeros((BLOCK, 2 * width), F32)

        for block in range(blocks):
            at = pl.ds(block * BLOCK, BLOCK)
            lanes = slice(block * BLOCK, (block + 1) * BLOCK)
            first, last = range_ref[2 * block], range_ref[2 * block + 1]
            qstacked = [stack_pair(q_ref[at, pl.ds(p * PAIR, PAIR)], masks) for p in range(pairs)]
            dstacked = [stack_pair(dctx_s[at, pl.ds(p * PAIR, PAIR)], masks) for p in range(pairs)]
            delta = [
                jnp.concatenate([deltas[2 * p][:, lanes], deltas[2 * p + 1][:, lanes]], axis=1)
                for p in range(pairs)
            ]
            segq_row = segq_ref[block : block + 1, :]
            dqt_acc[...] = jnp.zeros_like(dqt_acc)

            @pl.loop(first, last)
            def _(key_block):
                keys_at = pl.ds(pl.multiple_of(key_block * BLOCK, BLOCK), BLOCK)
                allowed = segk_ref[keys_at, :] == segq_row
                for pair in range(pairs):
                    cols = pl.ds(pair * PAIR, PAIR)
                    row = block * pairs + pair
                    scores = mm(k_ref[keys_at, cols], qstacked[pair], NT)
                    scores = jnp.where(allowed, scores, masked_score)
                    probs = jnp.exp(scores - lse_ref[row : row + 1, :])
                    dprobs = mm(v_ref[keys_at, cols], dstacked[pair], NT)
                    dscores = (probs * (dprobs - delta[pair])).astype(BF16)
                    dkv_s[keys_at, cols] += mm(dscores, qstacked[pair])
                    dkv_s[keys_at, pl.ds(width + pair * PAIR, PAIR)] += mm(
                        probs.astype(BF16), dstacked[pair]
                    )
                    dqt_acc[pair] += mm(kt_s[cols, keys_at], dscores)

            for pair in range(pairs):
                dqt = (dqt_acc[pair] * score_scale).astype(BF16)
                dqt_s[pl.ds(pair * PAIR, HEAD_DIM), at] = dqt[:HEAD_DIM, :BLOCK]
                dqt_s[pl.ds(pair * PAIR + HEAD_DIM, HEAD_DIM), at] = dqt[HEAD_DIM:, BLOCK:]
        dq = dqt_s[...].T
        gain = norms_ref[2 * k_in : 2 * k_in + 1, :]
        shift = norms_ref[2 * k_in + 1 : 2 * k_in + 2, :]
        inputs = (ins[4][...] * gain + shift).astype(BF16)
        store_kind(dw_s, 0, mm(inputs.T, dq))
        dx_o[...] = dtotal + mm(dq, w_s[:, :width], NT)
        outs.send(0)
        dm_s[...] = jnp.zeros_like(dm_s)
        dwkv_s[...] = jnp.zeros_like(dwkv_s)
        wait_all(m_copies)

        @pl.loop(everything_first, everything_last)
        def _(key_block):
            keys_at = pl.ds(pl.multiple_of(key_block * BLOCK, BLOCK), BLOCK)
            dkv = dkv_s[keys_at, :].astype(BF16)
            dm_s[keys_at, :] = mm(dkv, w_s[:, width : 3 * width], NT).astype(BF16)
            dwkv_s[...] += mm(m_s[keys_at, :].T, dkv)

        dm_copies = [
            pltpu.make_async_copy(
                dm_s.at[pl.ds(pl.multiple_of((me_ref[2] ^ member) * rows, rows), rows), :],
                (dm_keep, dm_send)[member % 2].at[member // 2],
                dm_sems.at[member],
            )
            for member in range(4)
        ]
        start_all([dm_copies])
        store_kind(dw_s, 1, dwkv_s[:, :width])
        store_kind(dw_s, 2, dwkv_s[:, width:])
        start_all(out_copies)
        outs.finish()
        wait_all(dm_copies)
        for group in out_copies:
            wait_all(group)

    piece = shaped((16, SLAB, out_width), BF16)
    half = shaped((2, rows, width), BF16)
    return staged(
        body,
        "cross_backward",
        me,
        (ranges,),
        (dy, xhat, rstd, norms, xin, segq, segk, *saved),
        (*memory, *pieces),
        (shaped((rows, width), F32), shaped((2, width), F32)),
        direct=(piece, piece, half, half),
        scratch=(
            *weight_scratch(width),
            *grad_scratch(width),
            pltpu.SemaphoreType.DMA((4,)),
            pltpu.SemaphoreType.DMA((4,)),
            pltpu.VMEM((keys, width), BF16),
            pltpu.VMEM((width, 4 * width), BF16),
            pltpu.VMEM((rows, width), BF16),
            pltpu.VMEM((width, keys), BF16),
            pltpu.VMEM((pairs, PAIR, 2 * BLOCK), F32),
            pltpu.VMEM((width, rows), BF16),
            pltpu.VMEM((keys, 2 * width), F32),
            pltpu.VMEM((width, 2 * width), F32),
            pltpu.VMEM((keys, width), BF16),
        ),
        prior=prior,
        microseconds=18,
    )


def gelu_and_slope(pre):
    square = pre * pre
    half = 0.5 * pre
    tanh = jnp.tanh(pre * (gelu_a + (gelu_a * gelu_b) * square))
    cdf = 0.5 + 0.5 * tanh
    slope = cdf + half * (1.0 - tanh * tanh) * (gelu_a + (3.0 * gelu_a * gelu_b) * square)
    return (pre * cdf).astype(BF16), slope.astype(BF16)


def feed_members_forward(low, acc_s, w_vmem, copies, hidden_refs, slope_refs, sent):
    half = w_vmem.shape[4] // 2
    for member in range(4):
        wait_all(copies[member])
        hidden, slope = gelu_and_slope(mm(low, flat(w_vmem[member, :, :, :, :half])))
        hidden_refs[member][...] = hidden
        slope_refs[member][...] = slope
        sent(member)
        acc_s[...] += mm(hidden, flat(w_vmem[member, :, :, :, half:]), NT)


def feed_members_backward(
    low, x_low, dx_ref, w_vmem, copies, hidden_refs, slope_refs, dw_s, out_copies
):
    half = w_vmem.shape[4] // 2
    lowt = low.T
    xt = x_low.T
    for member in range(4):
        if copies is not None:
            wait_all(copies[member])
        dhidden = mm(low, flat(w_vmem[member, :, :, :, half:]))
        dpre = (dhidden * slope_refs[member][...].astype(F32)).astype(BF16)
        dw_s[member, :, :, :, :half] = mm(xt, dpre).astype(BF16).reshape(slab_shape(half))
        dw_s[member, :, :, :, half:] = (
            mm(lowt, hidden_refs[member][...]).astype(BF16).reshape(slab_shape(half))
        )
        start_all([out_copies[member]])
        dx_ref[...] += mm(dpre, flat(w_vmem[member, :, :, :, :half]), NT)


def feed_forward(me, xin, k_in, k_out, weights, norm_piece):
    pieces, offset = weights
    norm_pieces, norm_offset = norm_piece
    rows, width = xin.shape

    def body(
        scalars, ins, piece_refs, outs, direct, w_vmem, w_sems, norm_s, norm_sems, acc_s
    ):
        ins.start(0)
        norm_copies = weight_copies(scalars[0], piece_refs, norm_offset, norm_s, norm_sems)[0]
        start_all([norm_copies])
        copies = weight_copies(scalars[0], piece_refs, offset, w_vmem, w_sems)
        start_all(copies)
        xhat_o, rstd_o, out_o, norms_o = outs.places[:4]
        wait_all(norm_copies)
        norms = flat(norm_s[0]).astype(F32).T[: norms_o.shape[0], :]
        norms_o[...] = norms
        outs.send(3)
        inputs = ins[0][...] * norms[2 * k_in : 2 * k_in + 1] + norms[2 * k_in + 1 : 2 * k_in + 2]
        acc_s[...] = inputs
        hidden, slope = outs.places[4:8], outs.places[8:]
        feed_members_forward(
            inputs.astype(BF16), acc_s, w_vmem, copies, hidden, slope,
            lambda member: outs.send(4 + member, 8 + member),
        )
        xhat, rstd = normalize(acc_s[...])
        xhat_o[...] = xhat
        rstd_o[...] = rstd
        normed = xhat * norms[2 * k_out : 2 * k_out + 1] + norms[2 * k_out + 1 : 2 * k_out + 2]
        out_o[...] = normed.astype(BF16)
        outs.send(0, 1, 2)
        outs.finish()

    part = shaped((rows, width), BF16)
    xhat, rstd, out, norms, *parts = staged(
        body,
        "feed_forward",
        me,
        (),
        (xin,),
        pieces,
        (
            shaped((rows, width), F32),
            shaped((rows, 1), F32),
            part,
            shaped((16, width), F32),
            *((part,) * 8),
        ),
        scratch=(
            *weight_scratch(2 * width),
            pltpu.VMEM((4, *slab_shape(BLOCK)), BF16),
            pltpu.SemaphoreType.DMA((4, 4)),
            pltpu.VMEM((rows, width), F32),
        ),
        microseconds=8,
    )
    return xhat, rstd, out, tuple(parts[:4]), tuple(parts[4:]), norms


def feed_backward(me, dy, xhat, rstd, norms, xin, k_in, k_out, hidden, slope, weights, grads):
    pieces, offset = weights
    prior, out_offset, out_width = grads
    rows, width = xin.shape

    def body(scalars, ins, piece_refs, outs, direct, w_vmem, w_sems, dw_s, dw_sems):
        ins.start(0, 1, 2, 3, 4)
        copies = weight_copies(scalars[0], piece_refs, offset, w_vmem, w_sems)
        for member in range(4):
            start_all([copies[member]])
            ins.start(9 + member, 5 + member)
        out_copies = grad_copies(scalars[0], dw_s, direct, out_offset, dw_sems)
        dx_o, dnorm_o = outs.places
        dy = ins[0][...].astype(F32)
        xhat = ins[1][...]
        norms_ref = ins[3]
        dgain, dshift = norm_param_grads(dy, xhat)
        dnorm_o[0:1, :] = dgain
        dnorm_o[1:2, :] = dshift
        outs.send(1)
        dtotal = norm_backward(dy, xhat, ins[2][...], norms_ref[2 * k_out : 2 * k_out + 1, :])
        dx_o[...] = dtotal
        gain = norms_ref[2 * k_in : 2 * k_in + 1, :]
        shift = norms_ref[2 * k_in + 1 : 2 * k_in + 2, :]
        inputs = (ins[4][...] * gain + shift).astype(BF16)
        feed_members_backward(
            dtotal.astype(BF16), inputs, dx_o, w_vmem, copies,
            Late(ins, 5), Late(ins, 9), dw_s, out_copies,
        )
        outs.send(0)
        outs.finish()
        for group in out_copies:
            wait_all(group)

    piece = shaped((16, SLAB, out_width), BF16)
    return staged(
        body,
        "feed_backward",
        me,
        (),
        (dy, xhat, rstd, norms, xin, *hidden, *slope),
        pieces,
        (shaped((rows, width), F32), shaped((2, width), F32)),
        direct=(piece, piece),
        scratch=(*weight_scratch(2 * width), *grad_scratch(2 * width)),
        prior=prior,
        microseconds=9,
    )


class Late:
    def __init__(self, ins, base):
        self.ins, self.base = ins, base

    def __getitem__(self, number):
        return self.ins[self.base + number]


def feed_turn(me, xin, norms, k_in, k_out, dy, weights, grads):
    pieces, offset = weights
    _, out_offset, out_width = grads
    rows, width = xin.shape

    def body(
        scalars, ins, piece_refs, outs, direct, w_vmem, w_sems, dw_s, dw_sems, hidden_s, slope_s
    ):
        ins.start(0, 1)
        copies = weight_copies(scalars[0], piece_refs, offset, w_vmem, w_sems)
        start_all(copies)
        ins.start(2)
        out_copies = grad_copies(scalars[0], dw_s, direct, out_offset, dw_sems)
        out_o, dx_o, dnorm_o = outs.places
        xin_ref, norms_ref = ins[0], ins[1]
        gain = norms_ref[2 * k_in : 2 * k_in + 1, :]
        shift = norms_ref[2 * k_in + 1 : 2 * k_in + 2, :]
        inputs = xin_ref[...] * gain + shift
        dx_o[...] = inputs
        low = inputs.astype(BF16)
        hidden = [hidden_s.at[member] for member in range(4)]
        slope = [slope_s.at[member] for member in range(4)]
        feed_members_forward(low, dx_o, w_vmem, copies, hidden, slope, lambda member: None)
        xhat, rstd = normalize(dx_o[...])
        gain = norms_ref[2 * k_out : 2 * k_out + 1, :]
        out_o[...] = (xhat * gain + norms_ref[2 * k_out + 1 : 2 * k_out + 2, :]).astype(BF16)
        outs.send(0)
        dy = ins[2][...].astype(F32)
        dgain, dshift = norm_param_grads(dy, xhat)
        dnorm_o[0:1, :] = dgain
        dnorm_o[1:2, :] = dshift
        outs.send(2)
        dtotal = norm_backward(dy, xhat, rstd, gain)
        dx_o[...] = dtotal
        feed_members_backward(
            dtotal.astype(BF16), low, dx_o, w_vmem, None, hidden, slope, dw_s, out_copies
        )
        outs.send(1)
        outs.finish()
        for group in out_copies:
            wait_all(group)

    piece = shaped((16, SLAB, out_width), BF16)
    return staged(
        body,
        "feed_turn",
        me,
        (),
        (xin, norms, dy),
        pieces,
        (shaped((rows, width), BF16), shaped((rows, width), F32), shaped((2, width), F32)),
        direct=(piece, piece),
        scratch=(
            *weight_scratch(2 * width),
            *grad_scratch(2 * width),
            pltpu.VMEM((4, rows, width), BF16),
            pltpu.VMEM((4, rows, width), BF16),
        ),
        microseconds=12,
    )


DP = ("z", "x")
MP = ("y", "c")
ALL = ("z", "x", "y", "c")


def is_cube():
    return tuple(lax.axis_size(axis) for axis in ALL) == (4, 2, 2, 2)


def swap(values, axis, distance=1):
    return lax.ppermute(values, axis, [(i, i ^ distance) for i in range(lax.axis_size(axis))])


def add(*terms):
    return sum(term.astype(F32) for term in terms)


def low_add(*terms):
    return add(*terms).astype(BF16)


def place_of(me_ref, at):
    return me_ref[0] ^ at[1] if isinstance(at, tuple) else at


def sum_kernel(sources, jobs, me_ref, *refs):
    inputs, outputs = refs[: len(sources)], refs[len(sources) : len(sources) + len(jobs)]
    places, sems = refs[len(sources) + len(jobs) : -1], refs[-1]
    copies = [
        pltpu.make_async_copy(ref.at[pl.ds(start, count)], place, sems.at[number])
        for number, (ref, place, (start, count)) in enumerate(zip(inputs, places, sources))
    ]
    start_all([copies])
    waited = set()
    for out, (_, slabs, turned) in zip(outputs, jobs):
        for at, terms in enumerate(slabs):
            at = ("z", at) if turned else at
            total = None
            for number, source_at in terms:
                if number not in waited:
                    waited.add(number)
                    copies[number].wait()
                value = places[number][place_of(me_ref, source_at)]
                if len(terms) > 1:
                    value = value.astype(F32)
                total = value if total is None else total + value
            out[place_of(me_ref, at) if turned else at] = total.astype(out.dtype)


def sum_slabs(me, requests):
    arrays, sources, jobs = [], [], []
    for request_sources, request_jobs in requests:
        base = len(arrays)
        for array, start, count in request_sources:
            arrays.append(array)
            sources.append((start, count))
        for dtype, slabs, *turned in request_jobs:
            shape = request_sources[0][0].shape[1:]
            moved = tuple(tuple((base + number, at) for number, at in terms) for terms in slabs)
            jobs.append((shaped((len(slabs), *shape), dtype), moved, bool(turned)))
    results = pl.pallas_call(
        functools.partial(sum_kernel, tuple(sources), tuple(jobs)),
        out_shape=tuple(job[0] for job in jobs),
        in_specs=smem(1) + hbm(len(arrays)),
        out_specs=tuple(vmem(len(jobs))),
        scratch_shapes=[
            *(
                pltpu.VMEM((count, *array.shape[1:]), array.dtype)
                for array, (_, count) in zip(arrays, sources)
            ),
            pltpu.SemaphoreType.DMA((len(arrays),)),
        ],
        compiler_params=params(),
        cost_estimate=cost(2),
        name="sum_slabs",
    )(me, *arrays)
    split, at = [], 0
    for _, request_jobs in requests:
        split.append(results[at : at + len(request_jobs)])
        at += len(request_jobs)
    return split


def gather_stages(shard, joined=False):
    if not is_cube():
        whole = lax.all_gather(shard, MP + DP, axis=0, tiled=True)
        whole = whole.reshape(2, 2, 4, 2, SLAB, shard.shape[1])
        whole = whole.transpose(1, 0, 3, 2, 4, 5)
        whole = whole.reshape(2, 16, SLAB, shard.shape[1])
        pieces = []
        for side in range(2):
            pieces += [whole[side, 0:4], whole[side, 4:8], whole[side, 8:12]]
            pieces += [whole[side, 12:14], whole[side, 14:16]]
        for _ in range(4):
            yield ()
        return tuple(pieces)
    over_z = yield tuple((shard, "z", k) for k in (1, 2, 3))
    (lines,) = yield (
        tuple((piece[None], 0, 1) for piece in (shard, *over_z)),
        ((BF16, tuple(((k, 0),) for k in range(4)), True),),
    )
    over_x, over_y = yield ((lines, "x", 1), (lines, "y", 1))
    if joined:
        far_one, far_two = yield ((over_y[:2], "x", 1), (over_x[2:], "y", 1))
        own = (lines, over_x, over_y, far_one, far_two)
        (whole,) = yield (
            tuple((piece, 0, piece.shape[0]) for piece in own),
            (
                (
                    BF16,
                    tuple(
                        ((number, at),) for number in range(5) for at in range(PIECES[number])
                    ),
                ),
            ),
        )
        (sib,) = yield ((whole, "c", 1),)
        return (*own, sib)
    far_one, far_two, lines_c, over_x_c, over_y_c = yield (
        (over_y[:2], "x", 1),
        (over_x[2:], "y", 1),
        (lines, "c", 1),
        (over_x, "c", 1),
        (over_y, "c", 1),
    )
    far_one_c, far_two_c = yield ((far_one, "c", 1), (far_two, "c", 1))
    return (
        lines, over_x, over_y, far_one, far_two,
        lines_c, over_x_c, over_y_c, far_one_c, far_two_c,
    )


def reduce_stages(keep, send):
    if not is_cube():
        whole = jnp.stack([keep, send]).reshape(2, 2, 2, 4, SLAB, keep.shape[2])
        whole = whole.transpose(1, 0, 3, 2, 4, 5).reshape(4, 8 * SLAB, keep.shape[2])
        part = lax.psum_scatter(whole, MP, scatter_dimension=0, tiled=True)
        part = lax.psum_scatter(part[0], DP, scatter_dimension=0, tiled=True)
        for _ in range(4):
            yield ()
        return part.astype(F32)
    (got,) = yield ((send, "c", 1),)
    far_one, far_two = yield (
        ((keep, 12, 4), (got, 12, 4)),
        tuple(
            (BF16, tuple(((0, 2 * half + k), (1, 2 * half + k)) for k in range(2)))
            for half in range(2)
        ),
    )
    far_one, far_two = yield ((far_one, "x", 1), (far_two, "y", 1))
    to_x, to_y = yield (
        ((keep, 4, 8), (got, 4, 8), (far_one, 0, 2), (far_two, 0, 2)),
        (
            (BF16, tuple(((0, k), (1, k)) + (((3, k - 2),) if k >= 2 else ()) for k in range(4))),
            (BF16, tuple(((0, k + 4), (1, k + 4)) + (((2, k),) if k < 2 else ()) for k in range(4))),
        ),
    )
    from_x, from_y = yield ((to_x, "x", 1), (to_y, "y", 1))
    lines = yield (
        ((keep, 0, 4), (got, 0, 4), (from_x, 0, 4), (from_y, 0, 4)),
        tuple(
            (F32 if k == 0 else BF16, (tuple((source, ("z", k)) for source in range(4)),))
            for k in range(4)
        ),
    )
    over_z = yield tuple((lines[k], "z", k) for k in (1, 2, 3))
    return add(lines[0][0], *(piece[0] for piece in over_z))


def memory_stages(values):
    if not is_cube():
        whole = lax.all_gather(values, MP, axis=0, tiled=False)
        for _ in range(2):
            yield ()
        return tuple(whole[k] for k in range(4))
    over_y, over_c = yield ((values, "y", 1), (values, "c", 1))
    (over_both,) = yield ((over_y, "c", 1),)
    return (values, over_c, over_y, over_both)


def memory_grad_stages(keep, send):
    if not is_cube():
        whole = jnp.stack([keep[0], send[0], keep[1], send[1]])
        whole = lax.psum_scatter(whole, MP, scatter_dimension=0, tiled=True)[0].astype(F32)
        for _ in range(2):
            yield ()
        return whole
    (got,) = yield ((send, "c", 1),)
    (over_y,) = yield ((low_add(keep[1], got[1]), "y", 1),)
    return add(keep[0], got[0], over_y)


class Flow:
    def __init__(self, me, token):
        self.me = me
        self.moving = {}
        self.ended = {}
        self.token = token

    def sync(self, names, *values, begin=(), hold=()):
        arrived = [self.moving[name][1] for name in names]
        held = [self.moving[name][1] for name in hold]
        arrived, held, values, token = lax.optimization_barrier(
            (arrived, held, values, self.token)
        )
        for name, result in zip(hold, held):
            self.moving[name] = (self.moving[name][0], result)
        to_send, asked = {}, {}
        begun = [(name, stages, None) for name, stages in begin]
        moved = [(name, self.moving[name][0], result) for name, result in zip(names, arrived)]

        def move(name, stages, result):
            try:
                wanted = stages.send(result)
            except StopIteration as end:
                self.ended[name] = end.value
                self.moving.pop(name, None)
                return
            if wanted and isinstance(wanted[0][0], tuple):
                asked[name] = (stages, wanted)
            else:
                to_send[name] = (stages, wanted)

        for job in moved + begun:
            move(*job)
        if asked:
            names = list(asked)
            sums = sum_slabs(self.me, [asked[name][1] for name in names])
            for name, result in zip(names, sums):
                move(name, asked[name][0], result)
        operands = [[job[0] for job in jobs] for _, jobs in to_send.values()]
        operands, values, self.token = lax.optimization_barrier((operands, values, token))
        for sending, (name, (stages, jobs)) in zip(operands, to_send.items()):
            results = [
                swap(operand, axis, distance) if axis else shift_rows(operand, distance)
                for operand, (_, axis, distance) in zip(sending, jobs)
            ]
            self.moving[name] = (stages, results)
        return values


def sum_all(values):
    if not is_cube():
        return lax.psum(values, ALL)
    values = values + swap(values, "c")
    half = (values + swap(values, "y"))
    values = half + swap(half, "x")
    one, two, three = (swap(values, "z", k) for k in (1, 2, 3))
    near, far = values + one, two + three
    return near + far


def shift_rows(values, step):
    count = lax.axis_size(MP)
    pairs = [(i, i + step) for i in range(count) if 0 <= i + step < count]
    return lax.ppermute(values, MP, pairs)


def halo_stages(before, after):
    return (yield ((before, None, 1), (after, None, -1)))


def add_halos(values, before, after):
    rows = values.shape[0]
    return (
        values
        + jnp.pad(before, ((0, rows - BLOCK), (0, 0)))
        + jnp.pad(after, ((rows - BLOCK, 0), (0, 0)))
    )


def adam_step(weights, first, second, grads, rate, decay):
    first_new = beta_one * first + (1.0 - beta_one) * grads
    second_new = beta_two * second + (1.0 - beta_two) * grads * grads
    first_hat = first_new / (1.0 - beta_one**STEP)
    second_hat = second_new / (1.0 - beta_two**STEP)
    weights_new = weights - rate * (first_hat / (jnp.sqrt(second_hat) + adam_eps) + decay * weights)
    return (weights_new, first_new, second_new)


GATHERS = (("enc", "enc_feed", "norms", "self"), ("cross", "dec_feed"))
REDUCES = (("dec_feed",), ("cross", "self"), ("enc_feed",), ("enc",))


def on_device(
    encoder_input, decoder_copy, decoder_target, decoder_cotangent,
    source_segments, target_segments, glance_mask,
    attention_in, attention_out, feed_in, feed_out, norm_params,
    attention_in_first, attention_out_first, feed_in_first, feed_out_first, norm_params_first,
    attention_in_second, attention_out_second, feed_in_second, feed_out_second, norm_params_second,
):
    rows, width = encoder_input.shape
    part, half = attention_in.shape[2], feed_in.shape[2]
    masters = (attention_in, attention_out, feed_in, feed_out, norm_params)

    def attention_shard(number):
        kinds = [attention_in[3 * number + kind] for kind in range(3)]
        return jnp.concatenate(kinds + [attention_out[number].T], axis=1)

    def feed_shard(number):
        return jnp.concatenate([feed_in[number], feed_out[number].T], axis=1)

    norm_columns = norm_params.reshape(10, -1).T
    shards = {
        "enc": attention_shard(0),
        "enc_feed": feed_shard(0),
        "norms": jnp.pad(norm_columns, ((0, 0), (0, BLOCK - 10))),
        "self": attention_shard(1),
        "cross": attention_shard(2),
        "dec_feed": feed_shard(1),
    }
    shard_groups, weight_places = [], {}
    for group in GATHERS:
        shard_groups.append(
            jnp.concatenate([shards[name].astype(BF16) for name in group], axis=1)
        )
        offset = 0
        for name in group:
            weight_places[name] = (group, offset)
            offset += shards[name].shape[1]

    def weights(name):
        group, offset = weight_places[name]
        return (flow.ended[group], offset)

    picked = glance_mask[0] == 1
    decoder_input = jnp.where(picked[:, None], decoder_target, decoder_copy)
    last_rows = jnp.concatenate([encoder_input[-BLOCK:], decoder_input[-BLOCK:]])
    first_rows = jnp.concatenate([encoder_input[:BLOCK], decoder_input[:BLOCK]])

    member = lax.axis_index(MP)
    position = member * rows
    blocks = rows // BLOCK
    here = [lax.axis_index("z"), lax.axis_index("x"), member]
    me = jnp.stack(here) if is_cube() else jnp.zeros((3,), jnp.int32)
    me = me.astype(jnp.int32)
    flow = Flow(me, jnp.zeros((8, BLOCK), F32) + norm_params[0, 0, 0])

    def query_segments(row):
        own = lax.dynamic_slice(row, (position,), (rows,)).reshape(blocks, BLOCK)
        return jnp.concatenate([own, own], axis=1)

    def key_segments(row):
        padded = jnp.pad(row, (BLOCK, BLOCK), constant_values=-1)
        return lax.dynamic_slice(padded, (position,), (rows + 2 * BLOCK,))[:, None]

    source_row, target_row = source_segments[0], target_segments[0]
    source_q, target_q = query_segments(source_row), query_segments(target_row)
    source_k, target_k = key_segments(source_row), key_segments(target_row)
    lowest, highest = target_q[:, 0], target_q[:, BLOCK - 1]
    first_key = jnp.sum((source_row[None, :] < lowest[:, None]).astype(jnp.int32), axis=1)
    last_key = jnp.sum((source_row[None, :] <= highest[:, None]).astype(jnp.int32), axis=1)
    ranges = jnp.stack([first_key // BLOCK, (last_key + BLOCK - 1) // BLOCK], axis=1)
    ranges = ranges.astype(jnp.int32).reshape(2 * blocks)
    source_column = source_row[:, None]

    grads, buffers = {}, {}
    for group in REDUCES:
        offset = 0
        total = sum(shards[name].shape[1] for name in group)
        for name in group:
            grads[name] = (group, offset, total)
            offset += shards[name].shape[1]

    def target(name):
        group, offset, total = grads[name]
        return (buffers.get(group, ()), offset, total)

    def keep_grads(name, pieces):
        buffers[grads[name][0]] = tuple(pieces)

    early, late = GATHERS
    last_rows, first_rows, shard_late = flow.sync(
        [], last_rows, first_rows, shard_groups[1], begin=[(early, gather_stages(shard_groups[0]))]
    )
    source_k, target_k, shard_late = flow.sync(
        [], source_k, target_k, shard_late, begin=[("halo", halo_stages(last_rows, first_rows))]
    )
    source_k, target_k, shard_late = flow.sync(["halo"], source_k, target_k, shard_late)
    before, after = flow.ended["halo"]
    encoder_x = jnp.concatenate([before[:BLOCK], encoder_input, after[:BLOCK]])
    decoder_x = jnp.concatenate([before[BLOCK:], decoder_input, after[BLOCK:]])
    encoder_x, decoder_x = flow.sync(
        [early], encoder_x, decoder_x, begin=[(late, gather_stages(shard_late))]
    )
    flow.sync([early], hold=[late])
    encoder_x, decoder_x = flow.sync([early], encoder_x, decoder_x)
    encoder_x, decoder_x = flow.sync([early, late], encoder_x, decoder_x)

    xhat0, rstd0, *enc_saved = self_forward(me, encoder_x, source_q, source_k, weights("enc"))
    xhat1, rstd1, encoder_output, enc_hidden, enc_slope, norms = feed_forward(
        me, xhat0, 0, 1, weights("enc_feed"), weights("norms")
    )
    encoder_output, decoder_x = flow.sync([late], encoder_output, decoder_x)
    (decoder_x,) = flow.sync([], decoder_x, begin=[("memory", memory_stages(encoder_output))])
    xhat2, rstd2, *self_saved = self_forward(me, decoder_x, target_q, target_k, weights("self"))
    (xhat2,) = flow.sync([late, "memory"], xhat2)
    (xhat2,) = flow.sync([late, "memory"], xhat2)
    memory = flow.ended["memory"]
    xhat3, rstd3, *cross_saved = cross_forward(
        me, ranges, xhat2, norms, 2, target_q, source_column, memory, weights("cross")
    )
    decoder_output, d4, dnorm4, *pieces = feed_turn(
        me, xhat3, norms, 3, 4, decoder_cotangent, weights("dec_feed"), target("dec_feed")
    )

    r_dec_feed, r_cross_self, r_enc_feed, r_enc = REDUCES
    (d4,) = flow.sync([], d4, begin=[(r_dec_feed, reduce_stages(*pieces))])
    d3, dnorm3, *pieces, dm_keep, dm_send = cross_backward(
        me, ranges, d4, xhat3, rstd3, norms, 3, xhat2, 2, target_q, source_column, cross_saved,
        memory, weights("cross"), target("cross"),
    )
    keep_grads("cross", pieces)
    (d3,) = flow.sync(
        [r_dec_feed], d3, begin=[("memory_grad", memory_grad_stages(dm_keep, dm_send))]
    )
    (d3,) = flow.sync(["memory_grad"], d3)
    dx_dec, before_dec, after_dec, dnorm2, *pieces = self_backward(
        me, d3, xhat2, rstd2, norms, 2, decoder_x, self_saved, weights("self"), target("self")
    )
    (dx_dec,) = flow.sync(
        [r_dec_feed, "memory_grad"], dx_dec, begin=[(r_cross_self, reduce_stages(*pieces))]
    )
    dmemory, dx_dec = lax.optimization_barrier((flow.ended["memory_grad"], dx_dec))
    d1, dnorm1, *pieces = feed_backward(
        me, dmemory, xhat1, rstd1, norms, xhat0, 0, 1, enc_hidden, enc_slope,
        weights("enc_feed"), target("enc_feed"),
    )
    (d1,) = flow.sync(
        [r_dec_feed, r_cross_self], d1, begin=[(r_enc_feed, reduce_stages(*pieces))]
    )
    dx_enc, before_enc, after_enc, dnorm0, *pieces = self_backward(
        me, d1, xhat0, rstd0, norms, 0, encoder_x, enc_saved, weights("enc"), target("enc")
    )
    (dx_enc,) = flow.sync(
        [r_dec_feed, r_cross_self, r_enc_feed], dx_enc, begin=[(r_enc, reduce_stages(*pieces))]
    )
    to_after, to_before = flow.sync(
        [r_cross_self, r_enc_feed, r_enc],
        jnp.concatenate([after_enc, after_dec]),
        jnp.concatenate([before_enc, before_dec]),
    )
    to_after, to_before = flow.sync([r_cross_self, r_enc_feed, r_enc], to_after, to_before)
    flow.sync([r_enc_feed, r_enc], begin=[("grad_halo", halo_stages(to_after, to_before))])
    flow.sync([r_enc, "grad_halo"])
    before, after = flow.ended["grad_halo"]
    encoder_input_grad = add_halos(dx_enc, before[:BLOCK], after[:BLOCK])
    decoder_input_grad = add_halos(dx_dec, before[BLOCK:], after[BLOCK:])
    reduced_groups = {group: flow.ended[group] for group in REDUCES}
    reduced = {}
    for group, values in reduced_groups.items():
        for name in group:
            offset = grads[name][1]
            reduced[name] = values[:, offset : offset + shards[name].shape[1]]
    squares = sum(jnp.sum(values * values) for values in reduced_groups.values())
    payload = jnp.concatenate(
        [dnorm0, dnorm1, dnorm2, dnorm3, dnorm4, jnp.broadcast_to(squares, (1, width))]
    )
    payload = sum_all(payload)
    g_all = payload[:10]
    grad_norm = jnp.sqrt(payload[10, 0] + jnp.sum(g_all * g_all))
    factor = clip_bound / jnp.maximum(grad_norm, clip_bound)
    own_columns = norm_params.shape[2]
    g_norms = lax.dynamic_slice(g_all, (0, lax.axis_index(DP) * own_columns), (10, own_columns))

    attention_parts = [reduced[name] for name in ("enc", "self", "cross")]
    feed_parts = [reduced[name] for name in ("enc_feed", "dec_feed")]
    g_in = jnp.stack(
        [g[:, kind * part : (kind + 1) * part] for g in attention_parts for kind in range(3)]
    )
    g_out = jnp.stack([g[:, 3 * part :].T for g in attention_parts])
    g_first = jnp.stack([g[:, :half] for g in feed_parts])
    g_second = jnp.stack([g[:, half:].T for g in feed_parts])
    all_grads = (g_in, g_out, g_first, g_second, g_norms.reshape(norm_params.shape))
    firsts = (
        attention_in_first, attention_out_first, feed_in_first, feed_out_first, norm_params_first,
    )
    seconds = (
        attention_in_second, attention_out_second, feed_in_second, feed_out_second,
        norm_params_second,
    )
    results = []
    for number in range(5):
        rate = rate_norm if number == 4 else rate_matrix
        decay = 0.0 if number == 4 else weight_decay
        results.append(
            adam_step(
                masters[number],
                firsts[number],
                seconds[number],
                all_grads[number] * factor,
                rate,
                decay,
            )
        )
    return (
        encoder_output,
        decoder_output,
        encoder_input_grad,
        decoder_input_grad,
        grad_norm,
        *(result[0] for result in results),
        *(result[1] for result in results),
        *(result[2] for result in results),
    )


def solution(mesh):
    dp, mp = mesh.shape["dp"], mesh.shape["mp"]
    fine = Mesh(mesh.devices.reshape(dp // 2, 2, mp // 2, 2), ALL)
    tokens = P(ALL, None)
    columns = P(None, DP, MP)
    turned = P(None, MP, DP)
    states = (columns, turned, columns, turned, P(None, None, DP))
    return jax.shard_map(
        on_device,
        mesh=fine,
        in_specs=(
            *((tokens,) * 4),
            P(DP, None),
            P(DP, None),
            P(DP, MP),
            *states,
            *states,
            *states,
        ),
        out_specs=(*((tokens,) * 4), P(), *states, *states, *states),
        check_vma=False,
    )
```

```python
import functools

import jax
import jax.numpy as jnp
from jax import lax
from jax.experimental import pallas as pl
from jax.experimental.pallas import tpu as pltpu
from jax.sharding import Mesh
from jax.sharding import PartitionSpec as P

HEAD_DIM = 64
STEP = 10
BLOCK = 128
PAIR = 2 * HEAD_DIM

norm_eps = 1e-05
beta_one = 0.9
beta_two = 0.98
adam_eps = 1e-08
weight_decay = 0.01
rate_matrix = 0.1
rate_norm = 0.5
clip_bound = 1.0
masked_score = -1e30
score_scale = HEAD_DIM ** (-0.5)
gelu_a = 0.7978845608028654
gelu_b = 0.044715

F32 = jnp.float32
BF16 = jnp.bfloat16
ANY = pl.ANY
SMEM = pltpu.SMEM
VMEM = pltpu.VMEM

NN = (((1,), (0,)), ((), ()))
NT = (((1,), (1,)), ((), ()))


def mm(a, b, dims=NN):
    return lax.dot_general(a, b, dims, preferred_element_type=F32)


def vmem(count):
    return [pl.BlockSpec(memory_space=VMEM)] * count


def smem(count):
    return [pl.BlockSpec(memory_space=SMEM)] * count


def hbm(count):
    return [pl.BlockSpec(memory_space=ANY)] * count


def cost(microseconds):
    return pl.CostEstimate(
        flops=int(microseconds * 1.15e9), bytes_accessed=int(microseconds * 3.6e6), transcendentals=0
    )


def params(mib=12):
    return pltpu.CompilerParams(vmem_limit_bytes=mib * 1024 * 1024)


LIMITS = {
    "self_forward": 14,
    "self_backward": 22,
    "cross_forward": 24,
    "cross_backward": 32,
    "feed_forward": 16,
    "feed_backward": 24,
    "end_norm": 10,
}


def shaped(shape, dtype):
    return jax.ShapeDtypeStruct(shape, dtype)


def normalize(total):
    centred = total - jnp.mean(total, axis=-1, keepdims=True)
    spread = jnp.mean(centred * centred, axis=-1, keepdims=True)
    rstd = lax.rsqrt(spread + norm_eps)
    return centred * rstd, rstd


def norm_backward(grad_out, xhat, rstd, gain):
    scaled = grad_out * gain
    first = jnp.mean(scaled, axis=-1, keepdims=True)
    second = jnp.mean(scaled * xhat, axis=-1, keepdims=True)
    return rstd * (scaled - first - xhat * second)


def norm_param_grads(grad_out, xhat):
    return (
        jnp.sum(grad_out * xhat, axis=0, keepdims=True),
        jnp.sum(grad_out, axis=0, keepdims=True),
    )


def half_masks():
    lane = lax.broadcasted_iota(jnp.int32, (1, PAIR), 1)
    low = jnp.where(lane < HEAD_DIM, 1.0, 0.0).astype(BF16)
    high = jnp.where(lane < HEAD_DIM, 0.0, 1.0).astype(BF16)
    return low, high


def stack_pair(values, masks):
    return jnp.concatenate([values * masks[0], values * masks[1]], axis=0)


SLAB = 64
PIECES = (4, 4, 4, 2, 2)
ROWS_OF = {"encoder": 0, "decoder": 1, "cotangent": 2}


def slab_shape(width):
    return (4, 2, SLAB, width)


def flat(values):
    return values.reshape(values.shape[0] * values.shape[1] * values.shape[2], values.shape[3])


def weight_copies(me_ref, pieces, offset, w_vmem, sems):
    columns = pl.ds(offset, w_vmem.shape[4])
    copies = []
    for member in range(2):
        group = []
        for x in range(2):
            number = 2 * member + x
            parts = [(pieces[number], 0, 4)] if number < 3 else [(pieces[3], 0, 2), (pieces[4], 2, 2)]
            for part, start, count in parts:
                group.append(
                    pltpu.make_async_copy(
                        part.at[:, :, columns],
                        w_vmem.at[member, pl.ds(start, count), me_ref[1] ^ x],
                        sems.at[member, 2 * x + start // 2],
                    )
                )
        copies.append(group)
    return copies


def grad_copies(me_ref, dw_vmem, targets, sems):
    return [
        [
            pltpu.make_async_copy(
                dw_vmem.at[member, :, me_ref[1] ^ x], targets[2 * member + x], sems.at[member, x]
            )
            for x in range(2)
        ]
        for member in range(2)
    ]


def start_all(groups):
    for group in groups:
        for copy in group:
            copy.start()


def wait_all(group):
    for copy in group:
        copy.wait()


def row_at(start, count):
    return pl.ds(pl.multiple_of(start, BLOCK), count)


def chip_copies(me_ref, own, sib, place, first, sems):
    rows = own.shape[0]
    return [
        pltpu.make_async_copy(own, place.at[row_at(first + me_ref[4] * rows, rows)], sems.at[0]),
        pltpu.make_async_copy(
            sib, place.at[row_at(first + (1 - me_ref[4]) * rows, rows)], sems.at[1]
        ),
    ]


def halo_place(me_ref, place, side):
    far = place.shape[0] - BLOCK
    return row_at((side ^ me_ref[3]) * far, BLOCK)


def haloed_copies(me_ref, refs, which, place, sems):
    own, sib, halo = refs
    rows = (place.shape[0] - 2 * BLOCK) // 2
    copies = chip_copies(
        me_ref,
        own.at[pl.ds(which * rows, rows)],
        sib.at[pl.ds(which * rows, rows)],
        place,
        BLOCK,
        sems,
    )
    place[halo_place(me_ref, place, 0), :] = jnp.zeros((BLOCK, place.shape[1]), BF16)
    copies.append(
        pltpu.make_async_copy(
            halo.at[pl.ds(which * BLOCK, BLOCK)],
            place.at[halo_place(me_ref, place, 1)],
            sems.at[2],
        )
    )
    return copies


class Inputs:
    def __init__(self, sources, places, sems):
        self.places = places
        self.copies = [
            pltpu.make_async_copy(source, place, sems.at[number])
            for number, (source, place) in enumerate(zip(sources, places))
        ]
        self.waited = set()

    def start(self, *numbers):
        for number in numbers:
            self.copies[number].start()

    def __getitem__(self, number):
        if number not in self.waited:
            self.waited.add(number)
            self.copies[number].wait()
        return self.places[number]


class Late:
    def __init__(self, ins, base):
        self.ins, self.base = ins, base

    def __getitem__(self, number):
        return self.ins[self.base + number]


class Outputs:
    def __init__(self, places, targets, sems):
        self.places = places
        self.copies = [
            pltpu.make_async_copy(place, target, sems.at[number])
            for number, (place, target) in enumerate(zip(places, targets))
        ]

    def __getitem__(self, number):
        return self.places[number]

    def send(self, *numbers):
        for number in numbers:
            self.copies[number].start()

    def finish(self):
        wait_all(self.copies)


def staged(
    body, name, me, others, inputs, raw, outputs, direct=(), scratch=(), microseconds=10
):
    scalars = (me, *others)
    counts = (len(scalars), len(inputs), len(raw), len(outputs), len(direct))

    def kernel(*refs):
        parts, at = [], 0
        for count in counts:
            parts.append(refs[at : at + count])
            at += count
        scalar_refs, sources, raw_refs, targets, direct_refs = parts
        rest = refs[at:]
        in_places, rest = rest[: len(inputs)], rest[len(inputs) :]
        out_places, rest = rest[: len(outputs)], rest[len(outputs) :]
        in_sems, out_sems, rest = rest[0], rest[1], rest[2:]
        body(
            scalar_refs,
            Inputs(sources, in_places, in_sems),
            raw_refs,
            Outputs(out_places, targets, out_sems),
            direct_refs,
            *rest,
        )

    return pl.pallas_call(
        kernel,
        out_shape=(*outputs, *direct),
        in_specs=smem(len(scalars)) + hbm(len(inputs) + len(raw)),
        out_specs=tuple(hbm(len(outputs) + len(direct))),
        scratch_shapes=[
            *(pltpu.VMEM(array.shape, array.dtype) for array in inputs),
            *(pltpu.VMEM(array.shape, array.dtype) for array in outputs),
            pltpu.SemaphoreType.DMA((max(len(inputs), 1),)),
            pltpu.SemaphoreType.DMA((max(len(outputs), 1),)),
            *scratch,
        ],
        compiler_params=params(LIMITS[name]),
        cost_estimate=cost(microseconds),
        name=name,
    )(*scalars, *inputs, *raw)


def weight_scratch(width):
    return [pltpu.VMEM((2, *slab_shape(width)), BF16), pltpu.SemaphoreType.DMA((2, 4))]


def grad_scratch(width):
    return [pltpu.VMEM((2, *slab_shape(width)), BF16), pltpu.SemaphoreType.DMA((2, 2))]


def grad_pieces(width):
    return (shaped((4, SLAB, width), BF16),) * 4


def spread_kinds(w_vmem, w_flat, member):
    part = w_vmem.shape[4] // 4
    for kind in range(4):
        w_flat[:, pl.ds((kind * 2 + member) * part, part)] = flat(
            w_vmem[member, :, :, :, kind * part : (kind + 1) * part]
        )


def store_kind(dw_vmem, kind, grads):
    part = dw_vmem.shape[4] // 4
    for member in range(2):
        dw_vmem[member, :, :, :, kind * part : (kind + 1) * part] = (
            grads[:, member * part : (member + 1) * part].astype(BF16).reshape(slab_shape(part))
        )


def gain_of(norms, number):
    return norms[2 * number : 2 * number + 1, :]


def shift_of(norms, number):
    return norms[2 * number + 1 : 2 * number + 2, :]


def both(own_ref, sib_ref):
    return own_ref[...].astype(F32) + sib_ref[...].astype(F32)


def store_norm_grads(outs, number, dy, xhat):
    dgain, dshift = norm_param_grads(dy, xhat)
    outs[number][0:1, :] = dgain
    outs[number][1:2, :] = dshift
    outs.send(number)


def lanes_at(block):
    return pl.ds(pl.multiple_of(block * BLOCK, BLOCK), BLOCK)


def store_halves(target, at, pair, values):
    target[pl.ds(pair * PAIR, HEAD_DIM), at] = values[:HEAD_DIM, :BLOCK]
    target[pl.ds(pair * PAIR + HEAD_DIM, HEAD_DIM), at] = values[HEAD_DIM:, BLOCK:]


def self_forward(me, chip, which, segk, weights):
    pieces, offset = weights
    width = chip[0].shape[1]
    rows = 2 * (chip[0].shape[0] // 3)
    keys = rows + 2 * BLOCK
    here = width // 2
    blocks, pairs, window = rows // BLOCK, here // PAIR, 3 * BLOCK

    def body(scalars, ins, raw, outs, direct, w_vmem, w_sems, x_sems, x_s, w_s, vt_s, ctxt_s):
        me_ref = scalars[0]
        x_copies = haloed_copies(me_ref, raw[:3], which, x_s, x_sems)
        start_all([x_copies])
        copies = weight_copies(me_ref, raw[3:], offset, w_vmem, w_sems)
        start_all(copies)
        ins.start(0)
        part_o, q_o, k_o, v_o, ctx_o, pt_o = outs.places
        segments = ins[0][...]
        columns = segments.T
        for member in range(2):
            wait_all(copies[member])
            spread_kinds(w_vmem, w_s, member)
        wait_all(x_copies)
        kv = mm(x_s[...], w_s[:, here : 3 * here]).astype(BF16)
        k_o[...] = kv[:, :here]
        v_o[...] = kv[:, here:]
        outs.send(2, 3)
        vt_s[...] = kv[:, here:].T
        q = mm(x_s[BLOCK : BLOCK + rows, :], w_s[:, :here]).astype(BF16)
        q_o[...] = q * jnp.asarray(score_scale, BF16)
        outs.send(1)
        masks = half_masks()
        for block in range(blocks):
            at = pl.ds(block * BLOCK, BLOCK)
            keys_at = pl.ds(block * BLOCK, window)
            column = jnp.concatenate([columns[:, block + k : block + k + 1] for k in range(3)])
            row = segments[block + 1 : block + 2, :]
            allowed = column == jnp.concatenate([row, row], axis=1)
            for pair in range(pairs):
                cols = pl.ds(pair * PAIR, PAIR)
                stacked = stack_pair(q_o[at, cols], masks)
                scores = mm(k_o[keys_at, cols], stacked, NT)
                scores = jnp.where(allowed, scores, masked_score)
                highest = jnp.max(scores, axis=0, keepdims=True)
                raised = jnp.exp(scores - highest)
                total = jnp.sum(raised, axis=0, keepdims=True)
                probs = (raised * (1.0 / total)).astype(BF16)
                pt_o[block * pairs + pair] = probs
                store_halves(ctxt_s, at, pair, mm(vt_s[cols, keys_at], probs).astype(BF16))
        outs.send(5)
        context = ctxt_s[...].T
        ctx_o[...] = context
        outs.send(4)
        part_o[...] = mm(context, w_s[:, 3 * here :], NT).astype(BF16)
        outs.send(0)
        outs.finish()

    part, *saved = staged(
        body,
        "self_forward",
        me,
        (),
        (segk,),
        (*chip, *pieces),
        (
            shaped((rows, width), BF16),
            shaped((rows, here), BF16),
            shaped((keys, here), BF16),
            shaped((keys, here), BF16),
            shaped((rows, here), BF16),
            shaped((blocks * pairs, window, 2 * BLOCK), BF16),
        ),
        scratch=(
            *weight_scratch(width),
            pltpu.SemaphoreType.DMA((3,)),
            pltpu.VMEM((keys, width), BF16),
            pltpu.VMEM((width, 4 * here), BF16),
            pltpu.VMEM((here, keys), BF16),
            pltpu.VMEM((here, rows), BF16),
        ),
        microseconds=9,
    )
    return part, saved


def self_backward(me, dy, xhat, rstd, norms, k_norm, chip, which, saved, weights):
    pieces, offset = weights
    rows, width = xhat.shape
    keys = rows + 2 * BLOCK
    own = rows // 2
    here = width // 2
    blocks, pairs, window = rows // BLOCK, here // PAIR, 3 * BLOCK

    def body(
        scalars, ins, raw, outs, direct,
        w_vmem, w_sems, dw_s, dw_sems, x_sems, dx_sems,
        x_s, w_s, dctx_s, kt_s, dqt_s, dkv_s, dx_s, dtotal_s,
    ):
        me_ref = scalars[0]
        ins.start(0, 1, 2, 3, 4, 5)
        copies = weight_copies(me_ref, raw[3:], offset, w_vmem, w_sems)
        start_all(copies)
        ins.start(9, 7, 8, 10, 6)
        x_copies = haloed_copies(me_ref, raw[:3], which, x_s, x_sems)
        start_all([x_copies])
        out_copies = grad_copies(me_ref, dw_s, direct[:4], dw_sems)
        dtotal_o, keep_o, send_o = direct[4:]
        masks = half_masks()
        dy = ins[0][...] + both(ins[1], ins[2])
        xhat = ins[3][...]
        store_norm_grads(outs, 0, dy, xhat)
        dtotal = norm_backward(dy, xhat, ins[4][...], gain_of(ins[5], k_norm))
        dtotal_s[...] = dtotal
        low = dtotal.astype(BF16)
        for member in range(2):
            wait_all(copies[member])
            spread_kinds(w_vmem, w_s, member)
        dctx_s[...] = mm(low, w_s[:, 3 * here :]).astype(BF16)
        store_kind(dw_s, 3, mm(low.T, ins[9][...]))
        kt_s[...] = ins[7][...].T
        dkv_s[...] = jnp.zeros_like(dkv_s)
        q_ref, v_ref, pt_ref = ins[6], ins[8], ins[10]
        for block in range(blocks):
            at = pl.ds(block * BLOCK, BLOCK)
            keys_at = pl.ds(block * BLOCK, window)
            for pair in range(pairs):
                cols = pl.ds(pair * PAIR, PAIR)
                dstacked = stack_pair(dctx_s[at, cols], masks)
                qstacked = stack_pair(q_ref[at, cols], masks)
                probs_low = pt_ref[block * pairs + pair]
                probs = probs_low.astype(F32)
                dprobs = mm(v_ref[keys_at, cols], dstacked, NT)
                delta = jnp.sum(probs * dprobs, axis=0, keepdims=True)
                dscores = (probs * (dprobs - delta)).astype(BF16)
                dkv_s[keys_at, cols] += mm(dscores, qstacked)
                dkv_s[keys_at, pl.ds(here + pair * PAIR, PAIR)] += mm(probs_low, dstacked)
                dqt = mm(kt_s[cols, keys_at], dscores) * score_scale
                store_halves(dqt_s, at, pair, dqt.astype(BF16))
        dq = dqt_s[...].T
        dkv = dkv_s[...].astype(BF16)
        wait_all(x_copies)
        xt = x_s[...].T
        store_kind(dw_s, 0, mm(xt[:, BLOCK : BLOCK + rows], dq))
        dw = mm(xt, dkv)
        store_kind(dw_s, 1, dw[:, :here])
        store_kind(dw_s, 2, dw[:, here:])
        start_all(out_copies)
        dx_s[...] = mm(dkv, w_s[:, here : 3 * here], NT).astype(BF16)
        middle = pl.ds(BLOCK, rows)
        dx_s[middle, :] = (dx_s[middle, :].astype(F32) + mm(dq, w_s[:, :here], NT)).astype(BF16)
        first = me_ref[4] * own
        other = (1 - me_ref[4]) * own
        halo = halo_place(me_ref, dx_s, 1)
        moves = [
            (dtotal_s.at[row_at(first, own)], dtotal_o),
            (dx_s.at[row_at(BLOCK + first, own)], keep_o.at[pl.ds(0, own)]),
            (dx_s.at[halo], keep_o.at[pl.ds(own, BLOCK)]),
            (dx_s.at[row_at(BLOCK + other, own)], send_o.at[pl.ds(0, own)]),
            (dx_s.at[halo], send_o.at[pl.ds(own, BLOCK)]),
        ]
        dx_copies = [
            pltpu.make_async_copy(source, target, dx_sems.at[number])
            for number, (source, target) in enumerate(moves)
        ]
        start_all([dx_copies])
        outs.finish()
        wait_all(dx_copies)
        for group in out_copies:
            wait_all(group)

    swapped = shaped((own + BLOCK, width), BF16)
    dnorm, *results = staged(
        body,
        "self_backward",
        me,
        (),
        (*dy, xhat, rstd, norms, *saved),
        (*chip, *pieces),
        (shaped((2, width), F32),),
        direct=(*grad_pieces(width), shaped((own, width), F32), swapped, swapped),
        scratch=(
            *weight_scratch(width),
            *grad_scratch(width),
            pltpu.SemaphoreType.DMA((3,)),
            pltpu.SemaphoreType.DMA((5,)),
            pltpu.VMEM((keys, width), BF16),
            pltpu.VMEM((width, 4 * here), BF16),
            pltpu.VMEM((rows, here), BF16),
            pltpu.VMEM((here, keys), BF16),
            pltpu.VMEM((here, rows), BF16),
            pltpu.VMEM((keys, 2 * here), F32),
            pltpu.VMEM((keys, width), BF16),
            pltpu.VMEM((rows, width), F32),
        ),
        microseconds=12,
    )
    return dnorm, results[:4], results[4], results[5], results[6]


def memory_copies(me_ref, pieces, m_s, sems):
    rows = pieces[0].shape[0]
    return [
        pltpu.make_async_copy(
            piece, m_s.at[row_at((me_ref[2] ^ member) * rows, rows)], sems.at[member]
        )
        for member, piece in enumerate(pieces)
    ]


WINDOW = 3 * BLOCK


def chunk_range(range_ref, blocks):
    size = WINDOW // BLOCK
    return range_ref[0] // size, (range_ref[2 * blocks - 1] + size - 1) // size


def fresh_keys(start, last_start):
    key = lax.broadcasted_iota(jnp.int32, (WINDOW, 1), 0)
    return key >= (start - jnp.minimum(start, last_start)) * BLOCK


def cross_forward(me, ranges, chip, which, part_own, part_sib, norms, k_in, segq, segk, memory, weights):
    pieces, offset = weights
    rows, width = part_own.shape
    own = rows // 2
    here = width // 2
    keys = 2 * rows
    blocks, pairs = rows // BLOCK, here // PAIR

    def body(
        scalars, ins, raw, outs, direct,
        w_vmem, w_sems, x_sems, m_sems, x_s, m_s, w_s, vt_s, acc_s, ctxt_s, seg_s, stat_s,
    ):
        me_ref, range_ref = scalars
        x_copies = chip_copies(
            me_ref,
            raw[0].at[pl.ds(which * own, own)],
            raw[1].at[pl.ds(which * own, own)],
            x_s,
            0,
            x_sems,
        )
        start_all([x_copies])
        ins.start(0, 1, 2)
        copies = weight_copies(me_ref, raw[6:], offset, w_vmem, w_sems)
        start_all(copies)
        m_copies = memory_copies(me_ref, raw[2:6], m_s, m_sems)
        start_all([m_copies])
        ins.start(3, 4)
        part_o, xhat_o, rstd_o, q_o, k_o, v_o, ctx_o, lse_o = outs.places
        masks = half_masks()
        wait_all(x_copies)
        xhat, rstd = normalize(x_s[...].astype(F32) + both(ins[0], ins[1]))
        xhat_o[...] = xhat
        rstd_o[...] = rstd
        outs.send(1, 2)
        inputs = xhat * gain_of(ins[2], k_in) + shift_of(ins[2], k_in)
        for member in range(2):
            wait_all(copies[member])
            spread_kinds(w_vmem, w_s, member)
        q = mm(inputs.astype(BF16), w_s[:, :here]).astype(BF16)
        q_o[...] = q * jnp.asarray(score_scale, BF16)
        outs.send(3)
        ins[3]
        columns = ins[4][...].T
        for block in range(keys // BLOCK):
            seg_s[pl.ds(block * BLOCK, BLOCK), :] = columns[:, block : block + 1]
        wait_all(m_copies)

        @pl.loop(*chunk_range(range_ref, blocks))
        def _(chunk):
            keys_at = row_at(chunk * WINDOW, WINDOW)
            kv = mm(m_s[keys_at, :], w_s[:, here : 3 * here]).astype(BF16)
            k_o[keys_at, :] = kv[:, :here]
            v_o[keys_at, :] = kv[:, here:]
            vt_s[:, keys_at] = kv[:, here:].T

        outs.send(4, 5)
        size = WINDOW // BLOCK
        last_start = (chunk_range(range_ref, blocks)[1] - 1) * size

        @pl.loop(0, blocks)
        def _(block):
            at = lanes_at(block)
            first, last = range_ref[2 * block], range_ref[2 * block + 1]
            row = ins[3][pl.ds(block + 1, 1), :]
            segq_row = jnp.concatenate([row, row], axis=1)

            def window_scores(start):
                keys_at = row_at(start * BLOCK, WINDOW)
                allowed = seg_s[keys_at, :] == segq_row
                result = []
                for pair in range(pairs):
                    cols = pl.ds(pair * PAIR, PAIR)
                    scores = mm(k_o[keys_at, cols], stack_pair(q_o[at, cols], masks), NT)
                    result.append(jnp.where(allowed, scores, masked_score))
                return keys_at, result

            keys_at, scores = window_scores(jnp.minimum(first, last_start))
            for pair in range(pairs):
                highest = jnp.max(scores[pair], axis=0, keepdims=True)
                raised = jnp.exp(scores[pair] - highest)
                total = jnp.sum(raised, axis=0, keepdims=True)
                acc_s[pair] = mm(vt_s[pl.ds(pair * PAIR, PAIR), keys_at], raised.astype(BF16))
                stat_s[2 * pair : 2 * pair + 1, :] = highest
                stat_s[2 * pair + 1 : 2 * pair + 2, :] = total

            @pl.loop(1, (last - first + size - 1) // size)
            def _(number):
                start = first + number * size
                keys_at, scores = window_scores(jnp.minimum(start, last_start))
                fresh = fresh_keys(start, last_start)
                for pair in range(pairs):
                    kept = jnp.where(fresh, scores[pair], masked_score)
                    before = stat_s[2 * pair : 2 * pair + 1, :]
                    highest = jnp.maximum(before, jnp.max(kept, axis=0, keepdims=True))
                    shrink = jnp.exp(before - highest)
                    raised = jnp.where(kept > 0.5 * masked_score, jnp.exp(kept - highest), 0.0)
                    acc_s[pair] = acc_s[pair] * shrink + mm(
                        vt_s[pl.ds(pair * PAIR, PAIR), keys_at], raised.astype(BF16)
                    )
                    stat_s[2 * pair : 2 * pair + 1, :] = highest
                    stat_s[2 * pair + 1 : 2 * pair + 2, :] = stat_s[
                        2 * pair + 1 : 2 * pair + 2, :
                    ] * shrink + jnp.sum(raised, axis=0, keepdims=True)

            for pair in range(pairs):
                total = stat_s[2 * pair + 1 : 2 * pair + 2, :]
                store_halves(ctxt_s, at, pair, (acc_s[pair] * (1.0 / total)).astype(BF16))
                lse_o[pl.ds(block * pairs + pair, 1), :] = stat_s[
                    2 * pair : 2 * pair + 1, :
                ] + jnp.log(total)

        context = ctxt_s[...].T
        ctx_o[...] = context
        outs.send(6, 7)
        part_o[...] = mm(context, w_s[:, 3 * here :], NT).astype(BF16)
        outs.send(0)
        outs.finish()

    part, xhat, rstd, *saved = staged(
        body,
        "cross_forward",
        me,
        (ranges,),
        (part_own, part_sib, norms, segq, segk),
        (*chip[:2], *memory, *pieces),
        (
            shaped((rows, width), BF16),
            shaped((rows, width), F32),
            shaped((rows, 1), F32),
            shaped((rows, here), BF16),
            shaped((keys, here), BF16),
            shaped((keys, here), BF16),
            shaped((rows, here), BF16),
            shaped((blocks * pairs, 2 * BLOCK), F32),
        ),
        scratch=(
            *weight_scratch(width),
            pltpu.SemaphoreType.DMA((2,)),
            pltpu.SemaphoreType.DMA((4,)),
            pltpu.VMEM((rows, width), BF16),
            pltpu.VMEM((keys, width), BF16),
            pltpu.VMEM((width, 4 * here), BF16),
            pltpu.VMEM((here, keys), BF16),
            pltpu.VMEM((pairs, PAIR, 2 * BLOCK), F32),
            pltpu.VMEM((here, rows), BF16),
            pltpu.VMEM((keys, 1), F32),
            pltpu.VMEM((8, 2 * BLOCK), F32),
        ),
        microseconds=10,
    )
    return part, xhat, rstd, saved


def cross_backward(
    me, ranges, dy, xhat, rstd, norms, k_norm, xin, k_in, segq, segk, saved, memory, weights
):
    pieces, offset = weights
    rows, width = xhat.shape
    half = rows // 2
    here = width // 2
    keys = 2 * rows
    blocks, pairs = rows // BLOCK, here // PAIR
    heads_here = here // HEAD_DIM

    def body(
        scalars, ins, raw, outs, direct,
        w_vmem, w_sems, dw_s, dw_sems, m_sems, dm_sems,
        m_s, w_s, dctx_s, kt_s, dqt_acc, dqt_s, dkv_s, dwkv_s, dm_s, seg_s, delta_s,
    ):
        me_ref, range_ref = scalars
        ins.start(0, 1, 2, 3, 4, 5)
        copies = weight_copies(me_ref, raw[4:], offset, w_vmem, w_sems)
        start_all(copies)
        ins.start(12, 10, 11, 9, 13, 7, 8, 6)
        m_copies = memory_copies(me_ref, raw[:4], m_s, m_sems)
        start_all([m_copies])
        out_copies = grad_copies(me_ref, dw_s, direct[:4], dw_sems)
        dm_keep, dm_send = direct[4:]
        part_o, dtotal_o, dnorm_o = outs.places
        norms_ref = ins[5]
        masks = half_masks()
        dy = ins[0][...] + both(ins[1], ins[2])
        xhat = ins[3][...]
        store_norm_grads(outs, 2, dy, xhat)
        dtotal = norm_backward(dy, xhat, ins[4][...], gain_of(norms_ref, k_norm))
        dtotal_o[...] = dtotal
        outs.send(1)
        low = dtotal.astype(BF16)
        for member in range(2):
            wait_all(copies[member])
            spread_kinds(w_vmem, w_s, member)
        dctx = mm(low, w_s[:, 3 * here :]).astype(BF16)
        dctx_s[...] = dctx
        context = ins[12][...]
        store_kind(dw_s, 3, mm(low.T, context))
        products = (dctx.astype(F32) * context.astype(F32)).T
        for head in range(heads_here):
            delta_s[head : head + 1, :] = jnp.sum(
                products[head * HEAD_DIM : (head + 1) * HEAD_DIM, :], axis=0, keepdims=True
            )
        k_ref, v_ref, q_ref, lse_ref = ins[10], ins[11], ins[9], ins[13]
        ins[7]
        columns = ins[8][...].T
        for block in range(keys // BLOCK):
            seg_s[pl.ds(block * BLOCK, BLOCK), :] = columns[:, block : block + 1]

        @pl.loop(*chunk_range(range_ref, blocks))
        def _(chunk):
            keys_at = row_at(chunk * WINDOW, WINDOW)
            kt_s[:, keys_at] = k_ref[keys_at, :].T
            dkv_s[keys_at, :] = jnp.zeros((WINDOW, 2 * here), F32)

        size = WINDOW // BLOCK
        last_start = (chunk_range(range_ref, blocks)[1] - 1) * size

        @pl.loop(0, blocks)
        def _(block):
            at = lanes_at(block)
            first, last = range_ref[2 * block], range_ref[2 * block + 1]
            row = ins[7][pl.ds(block + 1, 1), :]
            segq_row = jnp.concatenate([row, row], axis=1)
            dqt_acc[...] = jnp.zeros_like(dqt_acc)

            @pl.loop(0, (last - first + size - 1) // size)
            def _(number):
                start = first + number * size
                keys_at = row_at(jnp.minimum(start, last_start) * BLOCK, WINDOW)
                allowed = jnp.logical_and(
                    seg_s[keys_at, :] == segq_row, fresh_keys(start, last_start)
                )
                for pair in range(pairs):
                    cols = pl.ds(pair * PAIR, PAIR)
                    qstacked = stack_pair(q_ref[at, cols], masks)
                    dstacked = stack_pair(dctx_s[at, cols], masks)
                    delta = jnp.concatenate(
                        [delta_s[2 * pair : 2 * pair + 1, at], delta_s[2 * pair + 1 : 2 * pair + 2, at]],
                        axis=1,
                    )
                    scores = mm(k_ref[keys_at, cols], qstacked, NT)
                    scores = jnp.where(allowed, scores, masked_score)
                    probs = jnp.exp(scores - lse_ref[pl.ds(block * pairs + pair, 1), :])
                    dprobs = mm(v_ref[keys_at, cols], dstacked, NT)
                    dscores = (probs * (dprobs - delta)).astype(BF16)
                    dkv_s[keys_at, cols] += mm(dscores, qstacked)
                    dkv_s[keys_at, pl.ds(here + pair * PAIR, PAIR)] += mm(
                        probs.astype(BF16), dstacked
                    )
                    dqt_acc[pair] += mm(kt_s[cols, keys_at], dscores)

            for pair in range(pairs):
                store_halves(dqt_s, at, pair, (dqt_acc[pair] * score_scale).astype(BF16))

        dq = dqt_s[...].T
        part_o[...] = mm(dq, w_s[:, :here], NT).astype(BF16)
        outs.send(0)
        inputs = (ins[6][...] * gain_of(norms_ref, k_in) + shift_of(norms_ref, k_in)).astype(BF16)
        store_kind(dw_s, 0, mm(inputs.T, dq))
        dm_s[...] = jnp.zeros_like(dm_s)
        dwkv_s[...] = jnp.zeros_like(dwkv_s)
        wait_all(m_copies)

        @pl.loop(*chunk_range(range_ref, blocks))
        def _(chunk):
            keys_at = row_at(chunk * WINDOW, WINDOW)
            dkv = dkv_s[keys_at, :].astype(BF16)
            dm_s[keys_at, :] = mm(dkv, w_s[:, here : 3 * here], NT).astype(BF16)
            dwkv_s[...] += mm(m_s[keys_at, :].T, dkv)

        dm_copies = [
            pltpu.make_async_copy(
                dm_s.at[row_at((me_ref[2] ^ member) * half, half), :],
                (dm_keep, dm_send)[member % 2].at[member // 2],
                dm_sems.at[member],
            )
            for member in range(4)
        ]
        start_all([dm_copies])
        store_kind(dw_s, 1, dwkv_s[:, :here])
        store_kind(dw_s, 2, dwkv_s[:, here:])
        start_all(out_copies)
        outs.finish()
        wait_all(dm_copies)
        for group in out_copies:
            wait_all(group)

    halves = shaped((2, half, width), BF16)
    part, dtotal, dnorm, *results = staged(
        body,
        "cross_backward",
        me,
        (ranges,),
        (*dy, xhat, rstd, norms, xin, segq, segk, *saved),
        (*memory, *pieces),
        (shaped((rows, width), BF16), shaped((rows, width), F32), shaped((2, width), F32)),
        direct=(*grad_pieces(width), halves, halves),
        scratch=(
            *weight_scratch(width),
            *grad_scratch(width),
            pltpu.SemaphoreType.DMA((4,)),
            pltpu.SemaphoreType.DMA((4,)),
            pltpu.VMEM((keys, width), BF16),
            pltpu.VMEM((width, 4 * here), BF16),
            pltpu.VMEM((rows, here), BF16),
            pltpu.VMEM((here, keys), BF16),
            pltpu.VMEM((pairs, PAIR, 2 * BLOCK), F32),
            pltpu.VMEM((here, rows), BF16),
            pltpu.VMEM((keys, 2 * here), F32),
            pltpu.VMEM((width, 2 * here), F32),
            pltpu.VMEM((keys, width), BF16),
            pltpu.VMEM((keys, 1), F32),
            pltpu.VMEM((8, rows), F32),
        ),
        microseconds=16,
    )
    return dtotal, part, dnorm, results[:4], results[4], results[5]


def gelu_and_slope(pre):
    square = pre * pre
    half = 0.5 * pre
    tanh = jnp.tanh(pre * (gelu_a + (gelu_a * gelu_b) * square))
    cdf = 0.5 + 0.5 * tanh
    slope = cdf + half * (1.0 - tanh * tanh) * (gelu_a + (3.0 * gelu_a * gelu_b) * square)
    return (pre * cdf).astype(BF16), slope.astype(BF16)


def feed_forward(me, base, part_own, part_sib, k_norm, weights, norms, norm_piece=None):
    pieces, offset = weights
    rows, width = part_own.shape
    own = rows // 2
    first = norm_piece is not None
    raw = (*base[0][:2], *pieces) if first else pieces
    inputs = (part_own, part_sib) if first else (part_own, part_sib, norms, base[0])

    def body(scalars, ins, raw, outs, direct, w_vmem, w_sems, *rest):
        me_ref = scalars[0]
        part_o, xhat_o, rstd_o = outs.places[:3]
        hidden, slope = outs.places[3:5], outs.places[5:7]
        if first:
            norm_s, norm_sems, x_s, x_sems, acc_s = rest
            which = base[1]
            x_copies = chip_copies(
                me_ref,
                raw[0].at[pl.ds(which * own, own)],
                raw[1].at[pl.ds(which * own, own)],
                x_s,
                0,
                x_sems,
            )
            start_all([x_copies])
            raw = raw[2:]
            norm_copies = weight_copies(me_ref, raw, norm_piece[1], norm_s, norm_sems)[0]
            start_all([norm_copies])
        else:
            (acc_s,) = rest
        ins.start(*range(len(inputs)))
        copies = weight_copies(me_ref, raw, offset, w_vmem, w_sems)
        start_all(copies)
        if first:
            wait_all(norm_copies)
            norms_ref = outs[7]
            norms_ref[...] = flat(norm_s[0]).astype(F32).T[: norms_ref.shape[0], :]
            outs.send(7)
            wait_all(x_copies)
            before = x_s[...].astype(F32)
        else:
            norms_ref = ins[2]
            before = ins[3][...] * gain_of(norms_ref, base[1]) + shift_of(norms_ref, base[1])
        xhat, rstd = normalize(before + both(ins[0], ins[1]))
        xhat_o[...] = xhat
        rstd_o[...] = rstd
        outs.send(1, 2)
        low = (xhat * gain_of(norms_ref, k_norm) + shift_of(norms_ref, k_norm)).astype(BF16)
        half = w_vmem.shape[4] // 2
        for member in range(2):
            wait_all(copies[member])
            hidden_low, slope_low = gelu_and_slope(mm(low, flat(w_vmem[member, :, :, :, :half])))
            hidden[member][...] = hidden_low
            slope[member][...] = slope_low
            outs.send(3 + member, 5 + member)
            product = mm(hidden_low, flat(w_vmem[member, :, :, :, half:]), NT)
            if member == 0:
                acc_s[...] = product
            else:
                part_o[...] = (acc_s[...] + product).astype(BF16)
        outs.send(0)
        outs.finish()

    piece = shaped((rows, width), BF16)
    results = staged(
        body,
        "feed_forward",
        me,
        (),
        inputs,
        raw,
        (
            piece,
            shaped((rows, width), F32),
            shaped((rows, 1), F32),
            *((piece,) * 4),
            *((shaped((16, width), F32),) if first else ()),
        ),
        scratch=(
            *weight_scratch(2 * width),
            *(
                (
                    pltpu.VMEM((2, *slab_shape(BLOCK)), BF16),
                    pltpu.SemaphoreType.DMA((2, 4)),
                    pltpu.VMEM((rows, width), BF16),
                    pltpu.SemaphoreType.DMA((2,)),
                )
                if first
                else ()
            ),
            pltpu.VMEM((rows, width), F32),
        ),
        microseconds=7,
    )
    return results[0], results[1], results[2], results[3:5], results[5:7], *results[7:]


def end_norm(me, xhat_before, k_before, part_own, part_sib, norms, k_norm):
    rows, width = part_own.shape
    own = rows // 2

    def body(scalars, ins, raw, outs, direct, x_s, one_s, two_s, sems):
        at = row_at(scalars[0][4] * own, own)
        copies = [
            pltpu.make_async_copy(source.at[at], place, sems.at[number])
            for number, (source, place) in enumerate(zip(raw, (x_s, one_s, two_s)))
        ]
        start_all([copies])
        ins.start(0)
        wait_all(copies)
        before = x_s[...] * gain_of(ins[0], k_before) + shift_of(ins[0], k_before)
        xhat, _ = normalize(before + both(one_s, two_s))
        outs[0][...] = (xhat * gain_of(ins[0], k_norm) + shift_of(ins[0], k_norm)).astype(BF16)
        outs.send(0)
        outs.finish()

    (out,) = staged(
        body,
        "end_norm",
        me,
        (),
        (norms,),
        (xhat_before, part_own, part_sib),
        (shaped((own, width), BF16),),
        scratch=(
            pltpu.VMEM((own, width), F32),
            pltpu.VMEM((own, width), BF16),
            pltpu.VMEM((own, width), BF16),
            pltpu.SemaphoreType.DMA((3,)),
        ),
        microseconds=2,
    )
    return out


def feed_backward(me, dy, parts, xin, k_in, k_out, norms, hidden, slope, weights, turning):
    pieces, offset = weights
    (dy_own, dy_sib), which = dy
    rows, width = xin.shape
    own = rows // 2

    def body(
        scalars, ins, raw, outs, direct, w_vmem, w_sems, dw_s, dw_sems, dy_s, dy_sems, acc_s, *rest
    ):
        me_ref = scalars[0]
        ins.start(0, 1, 2, 3)
        dy_copies = chip_copies(
            me_ref,
            raw[0].at[pl.ds(which * own, own)],
            raw[1].at[pl.ds(which * own, own)],
            dy_s,
            0,
            dy_sems,
        )
        start_all([dy_copies])
        copies = weight_copies(me_ref, raw[2:], offset, w_vmem, w_sems)
        for member in range(2):
            start_all([copies[member]])
            ins.start(6 + member, 4 + member)
        out_copies = grad_copies(me_ref, dw_s, direct[:4], dw_sems)
        part_o, dtotal_o, dnorm_o = outs.places
        norms_ref = ins[1]
        inputs = ins[0][...] * gain_of(norms_ref, k_in) + shift_of(norms_ref, k_in)
        gain = gain_of(norms_ref, k_out)
        xhat, rstd = normalize(inputs + both(ins[2], ins[3]))
        if turning:
            out_s, out_sems = rest
            out_s[...] = (xhat * gain + shift_of(norms_ref, k_out)).astype(BF16)
            out_copy = pltpu.make_async_copy(
                out_s.at[row_at(me_ref[4] * own, own)], direct[4], out_sems.at[0]
            )
            out_copy.start()
        wait_all(dy_copies)
        dy = dy_s[...].astype(F32)
        store_norm_grads(outs, 2, dy, xhat)
        dtotal = norm_backward(dy, xhat, rstd, gain)
        dtotal_o[...] = dtotal
        outs.send(1)
        low = dtotal.astype(BF16)
        lowt = low.T
        xt = inputs.astype(BF16).T
        half = w_vmem.shape[4] // 2
        for member in range(2):
            wait_all(copies[member])
            dhidden = mm(low, flat(w_vmem[member, :, :, :, half:]))
            dpre = (dhidden * ins[6 + member][...].astype(F32)).astype(BF16)
            dw_s[member, :, :, :, :half] = mm(xt, dpre).astype(BF16).reshape(slab_shape(half))
            dw_s[member, :, :, :, half:] = (
                mm(lowt, ins[4 + member][...]).astype(BF16).reshape(slab_shape(half))
            )
            start_all([out_copies[member]])
            product = mm(dpre, flat(w_vmem[member, :, :, :, :half]), NT)
            if member == 0:
                acc_s[...] = product
            else:
                part_o[...] = (acc_s[...] + product).astype(BF16)
        outs.send(0)
        outs.finish()
        for group in out_copies:
            wait_all(group)
        if turning:
            out_copy.wait()

    part, dtotal, dnorm, *results = staged(
        body,
        "feed_backward",
        me,
        (),
        (xin, norms, *parts, *hidden, *slope),
        (dy_own, dy_sib, *pieces),
        (shaped((rows, width), BF16), shaped((rows, width), F32), shaped((2, width), F32)),
        direct=(
            *grad_pieces(2 * width),
            *((shaped((own, width), BF16),) if turning else ()),
        ),
        scratch=(
            *weight_scratch(2 * width),
            *grad_scratch(2 * width),
            pltpu.VMEM((rows, width), BF16),
            pltpu.SemaphoreType.DMA((2,)),
            pltpu.VMEM((rows, width), F32),
            *(
                (pltpu.VMEM((rows, width), BF16), pltpu.SemaphoreType.DMA((1,)))
                if turning
                else ()
            ),
        ),
        microseconds=9,
    )
    return dtotal, part, dnorm, results[:4], *results[4:]


DP = ("z", "x")
MP = ("y", "c")
ALL = ("z", "x", "y", "c")


def is_cube():
    return tuple(lax.axis_size(axis) for axis in ALL) == (4, 2, 2, 2)


def swap(values, axis, distance=1):
    count = lax.axis_size(axis)
    return lax.ppermute(values, axis, [(i, i ^ distance) for i in range(count)])


def add(*terms):
    return sum(term.astype(F32) for term in terms)


def low_add(*terms):
    return add(*terms).astype(BF16)


def place_of(me_ref, at):
    return me_ref[0] ^ at[1] if isinstance(at, tuple) else at


def sum_kernel(sources, jobs, me_ref, *refs):
    inputs, outputs = refs[: len(sources)], refs[len(sources) : len(sources) + len(jobs)]
    places, sems = refs[len(sources) + len(jobs) : -1], refs[-1]
    copies = [
        pltpu.make_async_copy(ref.at[pl.ds(start, count)], place, sems.at[number])
        for number, (ref, place, (start, count)) in enumerate(zip(inputs, places, sources))
    ]
    start_all([copies])
    waited = set()
    for out, (_, slabs, turned) in zip(outputs, jobs):
        for at, terms in enumerate(slabs):
            total = None
            for number, source_at in terms:
                if number not in waited:
                    waited.add(number)
                    copies[number].wait()
                value = places[number][place_of(me_ref, source_at)]
                if len(terms) > 1:
                    value = value.astype(F32)
                total = value if total is None else total + value
            out[place_of(me_ref, ("z", at)) if turned else at] = total.astype(out.dtype)


def sum_slabs(me, requests):
    arrays, sources, jobs = [], [], []
    for request_sources, request_jobs in requests:
        base = len(arrays)
        for array, start, count in request_sources:
            arrays.append(array)
            sources.append((start, count))
        for dtype, slabs, *turned in request_jobs:
            shape = request_sources[0][0].shape[1:]
            moved = tuple(tuple((base + number, at) for number, at in terms) for terms in slabs)
            jobs.append((shaped((len(slabs), *shape), dtype), moved, bool(turned)))
    results = pl.pallas_call(
        functools.partial(sum_kernel, tuple(sources), tuple(jobs)),
        out_shape=tuple(job[0] for job in jobs),
        in_specs=smem(1) + hbm(len(arrays)),
        out_specs=tuple(vmem(len(jobs))),
        scratch_shapes=[
            *(
                pltpu.VMEM((count, *array.shape[1:]), array.dtype)
                for array, (_, count) in zip(arrays, sources)
            ),
            pltpu.SemaphoreType.DMA((len(arrays),)),
        ],
        compiler_params=params(),
        cost_estimate=cost(2),
        name="sum_slabs",
    )(me, *arrays)
    split, at = [], 0
    for _, request_jobs in requests:
        split.append(results[at : at + len(request_jobs)])
        at += len(request_jobs)
    return split


def gather_stages(shard, gated=False):
    if not is_cube():
        whole = lax.all_gather(shard, ("y", *DP), axis=0, tiled=True)
        whole = whole.reshape(2, 4, 2, SLAB, shard.shape[1])
        pieces = (whole[0, :, 0], whole[0, :, 1], whole[1, :, 0], whole[1, :2, 1], whole[1, 2:, 1])
        for _ in range(4 if gated else 3):
            yield ()
        return pieces
    over_z = yield tuple((shard, "z", k) for k in (1, 2, 3))
    (lines,) = yield (
        tuple((piece[None], 0, 1) for piece in (shard, *over_z)),
        ((BF16, tuple(((k, 0),) for k in range(4)), True),),
    )
    if gated:
        yield ()
    over_x, over_y = yield ((lines, "x", 1), (lines, "y", 1))
    far_one, far_two = yield ((over_y[:2], "x", 1), (over_x[2:], "y", 1))
    return lines, over_x, over_y, far_one, far_two


def reduce_stages(own, to_x, to_y, to_far):
    if not is_cube():
        whole = jnp.stack([own, to_x, to_y, to_far])
        whole = whole.reshape(2, 2, 4, SLAB, own.shape[2])
        whole = whole.transpose(0, 2, 1, 3, 4).reshape(2, 8 * SLAB, own.shape[2])
        part = lax.psum_scatter(whole, "y", scatter_dimension=0, tiled=True)
        part = lax.psum_scatter(part[0], DP, scatter_dimension=0, tiled=True)
        for _ in range(2):
            yield ()
        return part.astype(F32)
    arrived = yield ((to_x, "x", 1), (to_y, "y", 1), (to_far, ("x", "y"), 3))
    lines = yield (
        tuple((array, 0, 4) for array in (own, *arrived)),
        tuple(
            (F32 if k == 0 else BF16, (tuple((source, ("z", k)) for source in range(4)),))
            for k in range(4)
        ),
    )
    over_z = yield tuple((lines[k], "z", k) for k in (1, 2, 3))
    return add(lines[0][0], *(piece[0] for piece in over_z))


def one_stage(*jobs):
    return (yield jobs)


def memory_stages(values):
    over_y, over_c = yield ((values, "y", 1), (values, "c", 1))
    (over_both,) = yield ((over_y, "c", 1),)
    return values, over_c, over_y, over_both


def memory_grad_stages(keep, send):
    (got,) = yield ((send, "c", 1),)
    (over_y,) = yield ((low_add(keep[1], got[1]), "y", 1),)
    own = low_add(keep[0], got[0], over_y)
    (sib,) = yield ((own, "c", 1),)
    return own, sib


class Flow:
    def __init__(self, me, token):
        self.me = me
        self.moving = {}
        self.ended = {}
        self.token = token

    def sync(self, names, *values, begin=(), hold=()):
        arrived = [self.moving[name][1] for name in names]
        held = [self.moving[name][1] for name in hold]
        arrived, held, values, token = lax.optimization_barrier(
            (arrived, held, values, self.token)
        )
        for name, result in zip(hold, held):
            self.moving[name] = (self.moving[name][0], result)
        to_send, asked = {}, {}
        begun = [(name, stages, None) for name, stages in begin]
        moved = [(name, self.moving[name][0], result) for name, result in zip(names, arrived)]

        def move(name, stages, result):
            try:
                wanted = stages.send(result)
            except StopIteration as end:
                self.ended[name] = end.value
                self.moving.pop(name, None)
                return
            if wanted and isinstance(wanted[0][0], tuple):
                asked[name] = (stages, wanted)
            else:
                to_send[name] = (stages, wanted)

        for job in moved + begun:
            move(*job)
        if asked:
            names = list(asked)
            sums = sum_slabs(self.me, [asked[name][1] for name in names])
            for name, result in zip(names, sums):
                move(name, asked[name][0], result)
        operands = [[job[0] for job in jobs] for _, jobs in to_send.values()]
        operands, values, self.token = lax.optimization_barrier((operands, values, token))
        for sending, (name, (stages, jobs)) in zip(operands, to_send.items()):
            results = [
                swap(operand, axis, distance)
                for operand, (_, axis, distance) in zip(sending, jobs)
            ]
            self.moving[name] = (stages, results)
        return values


def sum_all(values):
    if not is_cube():
        return lax.psum(values, ALL)
    values = values + swap(values, "c")
    one, two, three = swap(values, "y"), swap(values, "x"), swap(values, ("x", "y"), 3)
    values = (values + one) + (two + three)
    one, two, three = (swap(values, "z", k) for k in (1, 2, 3))
    return (values + one) + (two + three)


def adam_step(weights, first, second, grads, rate, decay):
    first_new = beta_one * first + (1.0 - beta_one) * grads
    second_new = beta_two * second + (1.0 - beta_two) * grads * grads
    first_hat = first_new / (1.0 - beta_one**STEP)
    second_hat = second_new / (1.0 - beta_two**STEP)
    weights_new = weights - rate * (first_hat / (jnp.sqrt(second_hat) + adam_eps) + decay * weights)
    return (weights_new, first_new, second_new)


GATHERS = (("enc", "enc_feed", "norms", "self"), ("cross",), ("dec_feed",))
REDUCES = ("dec_feed", "cross", "self", "enc_feed", "enc")


def on_device(
    encoder_input, decoder_copy, decoder_target, decoder_cotangent,
    source_segments, target_segments, glance_mask,
    attention_in, attention_out, feed_in, feed_out, norm_params,
    attention_in_first, attention_out_first, feed_in_first, feed_out_first, norm_params_first,
    attention_in_second, attention_out_second, feed_in_second, feed_out_second, norm_params_second,
):
    rows, width = encoder_input.shape
    length = source_segments.shape[1]
    part, half = attention_in.shape[2], feed_in.shape[2]
    masters = (attention_in, attention_out, feed_in, feed_out, norm_params)
    chip_y, core = lax.axis_index("y"), lax.axis_index("c")
    here = (lax.axis_index("z"), lax.axis_index("x")) if is_cube() else (0, 0)
    me = jnp.stack([jnp.int32(value) for value in (*here, 2 * chip_y + core, chip_y, core)])
    flow = Flow(me, jnp.zeros((8, BLOCK), F32) + norm_params[0, 0, 0])

    def attention_shard(number):
        kinds = [attention_in[3 * number + kind] for kind in range(3)]
        return jnp.concatenate(kinds + [attention_out[number].T], axis=1)

    def feed_shard(number):
        return jnp.concatenate([feed_in[number], feed_out[number].T], axis=1)

    norm_columns = norm_params.reshape(10, -1).T
    shards = {
        "enc": attention_shard(0),
        "enc_feed": feed_shard(0),
        "norms": jnp.pad(norm_columns, ((0, 0), (0, BLOCK - 10))),
        "self": attention_shard(1),
        "cross": attention_shard(2),
        "dec_feed": feed_shard(1),
    }
    shard_groups, weight_places = [], {}
    for group in GATHERS:
        shard_groups.append(
            jnp.concatenate([shards[name].astype(BF16) for name in group], axis=1)
        )
        offset = 0
        for name in group:
            weight_places[name] = (group, offset)
            offset += shards[name].shape[1]

    def weights(name):
        group, offset = weight_places[name]
        return (flow.ended[group], offset)

    picked = glance_mask[0] == 1
    decoder_input = jnp.where(picked[:, None], decoder_target, decoder_copy)
    own_rows = jnp.concatenate([encoder_input, decoder_input, decoder_cotangent])

    chip_rows = 2 * rows
    blocks = chip_rows // BLOCK
    source_row = source_segments[0].astype(F32)
    target_row = target_segments[0].astype(F32)

    def chip_segments(row):
        padded = jnp.pad(row, (BLOCK, BLOCK), constant_values=-1.0)
        own = lax.dynamic_slice(padded, (chip_y * chip_rows,), (chip_rows + 2 * BLOCK,))
        return own.reshape(blocks + 2, BLOCK)

    source_chip, target_chip = chip_segments(source_row), chip_segments(target_row)
    source_all = jnp.pad(source_row.reshape(length // BLOCK, BLOCK), ((0, 16 - length // BLOCK), (0, 0)))
    lowest, highest = target_chip[1:-1, 0], target_chip[1:-1, BLOCK - 1]
    first_key = jnp.sum((source_row[None, :] < lowest[:, None]).astype(jnp.int32), axis=1)
    last_key = jnp.sum((source_row[None, :] <= highest[:, None]).astype(jnp.int32), axis=1)
    ranges = jnp.stack([first_key // BLOCK, (last_key + BLOCK - 1) // BLOCK], axis=1)
    ranges = ranges.astype(jnp.int32).reshape(2 * blocks)

    early, cross, feed = GATHERS
    own_rows, shard_cross, shard_feed = flow.sync(
        [],
        own_rows,
        *shard_groups[1:],
        begin=[(early, gather_stages(shard_groups[0]))],
    )
    shard_cross, shard_feed = flow.sync(
        [], shard_cross, shard_feed, begin=[("rows", one_stage((own_rows, "c", 1)))]
    )
    own_rows, shard_cross, shard_feed = flow.sync(["rows"], own_rows, shard_cross, shard_feed)
    (sib_rows,) = flow.ended["rows"]

    def edge(which):
        last = jnp.where(core == 1, own_rows[(which + 1) * rows - BLOCK : (which + 1) * rows],
                         sib_rows[(which + 1) * rows - BLOCK : (which + 1) * rows])
        first = jnp.where(core == 0, own_rows[which * rows : which * rows + BLOCK],
                          sib_rows[which * rows : which * rows + BLOCK])
        return jnp.where(chip_y == 0, last, first)

    edges = jnp.concatenate([edge(0), edge(1)])
    shard_cross, shard_feed = flow.sync(
        [], shard_cross, shard_feed, begin=[("halo", one_stage((edges, "y", 1)))]
    )
    shard_cross, shard_feed = flow.sync(["halo"], shard_cross, shard_feed)
    chip = (own_rows, sib_rows, flow.ended["halo"][0])
    (shard_cross,) = flow.sync(
        [early], shard_cross, begin=[(feed, gather_stages(shard_feed, gated=True))]
    )
    chip, source_chip, target_chip, ranges, source_all, shard_cross = flow.sync(
        [early], chip, source_chip, target_chip, ranges, source_all, shard_cross, hold=[feed]
    )
    flow.sync([feed], begin=[(cross, gather_stages(shard_cross, gated=True))])
    flow.sync([cross])
    chip, source_chip = flow.sync([early, feed], chip, source_chip)

    enc, dec, cot = 0, 1, 2
    part0, enc_saved = self_forward(me, chip, enc, source_chip, weights("enc"))
    (part0,) = flow.sync([], part0, hold=[feed])
    (part0,) = flow.sync([cross], part0, begin=[("part0", one_stage((part0, "c", 1)))])
    (part0,) = flow.sync(["part0"], part0)
    part1, xhat0, rstd0, enc_hidden, enc_slope, norms = feed_forward(
        me, (chip, enc), part0, *flow.ended["part0"], 0, weights("enc_feed"), None, weights("norms")
    )
    (part1,) = flow.sync([], part1, hold=[cross])
    (part1,) = flow.sync([], part1, begin=[("part1", one_stage((part1, "c", 1)))])
    (part1,) = flow.sync(["part1", cross], part1)
    parts1 = (part1, *flow.ended["part1"])
    encoder_output = end_norm(me, xhat0, 0, *parts1, norms, 1)
    (encoder_output,) = flow.sync([cross], encoder_output)
    (target_chip,) = flow.sync(
        [], target_chip, begin=[("memory", memory_stages(encoder_output))]
    )
    part2, self_saved = self_forward(me, chip, dec, target_chip, weights("self"))
    (part2,) = flow.sync(["memory"], part2, begin=[("part2", one_stage((part2, "c", 1)))])
    (part2,) = flow.sync(["memory", "part2"], part2)
    (part2,) = flow.sync([feed], part2)
    memory = flow.ended["memory"]
    part3, xhat2, rstd2, cross_saved = cross_forward(
        me, ranges, chip, dec, part2, *flow.ended["part2"], norms, 2, target_chip, source_all,
        memory, weights("cross"),
    )
    (part3,) = flow.sync([feed], part3)
    (part3,) = flow.sync([], part3, begin=[("part3", one_stage((part3, "c", 1)))])
    (part3,) = flow.sync(["part3"], part3)
    part4, xhat3, rstd3, dec_hidden, dec_slope = feed_forward(
        me, (xhat2, 2), part3, *flow.ended["part3"], 3, weights("dec_feed"), norms
    )
    (part4,) = flow.sync([], part4, begin=[("part4", one_stage((part4, "c", 1)))])
    (part4,) = flow.sync(["part4"], part4)

    dtotal4, dpart4, dnorm4, pieces, decoder_output = feed_backward(
        me, (chip[:2], cot), (part4, *flow.ended["part4"]), xhat3, 3, 4, norms,
        dec_hidden, dec_slope, weights("dec_feed"), True,
    )
    (dtotal4,) = flow.sync([], dtotal4, begin=[("dpart4", one_stage((dpart4, "c", 1)))])
    (dtotal4,) = flow.sync(["dpart4"], dtotal4, begin=[("dec_feed", reduce_stages(*pieces))])
    dtotal3, dpart3, dnorm3, pieces, dm_keep, dm_send = cross_backward(
        me, ranges, (dtotal4, dpart4, *flow.ended["dpart4"]), xhat3, rstd3, norms, 3, xhat2, 2,
        target_chip, source_all, cross_saved, memory, weights("cross"),
    )
    dpart3, dtotal3, dm_keep, dm_send = flow.sync(
        [], dpart3, dtotal3, dm_keep, dm_send, hold=["dec_feed"]
    )
    dpart3, dtotal3 = flow.sync(
        [],
        dpart3,
        dtotal3,
        begin=[
            ("memory_grad", memory_grad_stages(dm_keep, dm_send)),
            ("dpart3", one_stage((dpart3, "c", 1))),
        ],
    )
    dpart3, dtotal3 = flow.sync(
        ["memory_grad", "dpart3"], dpart3, dtotal3, begin=[("cross", reduce_stages(*pieces))]
    )
    dnorm2, pieces, dtotal2, dec_keep, dec_send = self_backward(
        me, (dtotal3, dpart3, *flow.ended["dpart3"]), xhat2, rstd2, norms, 2, chip, dec,
        self_saved, weights("self"),
    )
    (dtotal2,) = flow.sync(["memory_grad"], dtotal2, hold=["cross"])
    (dtotal2,) = flow.sync(
        ["memory_grad", "dec_feed"], dtotal2, begin=[("self", reduce_stages(*pieces))]
    )
    dmemory = flow.ended["memory_grad"]
    dmemory, dtotal2 = lax.optimization_barrier((dmemory, dtotal2))
    dtotal1, dpart1, dnorm1, pieces = feed_backward(
        me, (dmemory, 0), parts1, xhat0, 0, 1, norms, enc_hidden, enc_slope,
        weights("enc_feed"), False,
    )
    dpart1, dtotal1 = flow.sync([], dpart1, dtotal1, hold=["self", "dec_feed"])
    (dtotal1,) = flow.sync([], dtotal1, begin=[("dpart1", one_stage((dpart1, "c", 1)))])
    (dtotal1,) = flow.sync(
        ["dpart1", "cross", "dec_feed", "self"],
        dtotal1,
        begin=[("enc_feed", reduce_stages(*pieces))],
    )
    dnorm0, pieces, dtotal0, enc_keep, enc_send = self_backward(
        me, (dtotal1, dpart1, *flow.ended["dpart1"]), xhat0, rstd0, norms, 0, chip, enc,
        enc_saved, weights("enc"),
    )
    both_send = jnp.concatenate([enc_send, dec_send])
    (both_send,) = flow.sync([], both_send, hold=["cross", "self", "enc_feed"])
    (both_send,) = flow.sync(
        ["enc_feed"], both_send, begin=[("enc", reduce_stages(*pieces))]
    )
    flow.sync([], begin=[("rows_grad", one_stage((both_send, "c", 1)))])
    flow.sync(["cross", "self", "rows_grad"], hold=["enc", "enc_feed"])
    (got,) = flow.ended["rows_grad"]
    swapped = rows + BLOCK
    enc_rows = add(enc_keep, got[:swapped])
    dec_rows = add(dec_keep, got[swapped:])
    halos = jnp.concatenate([enc_rows[rows:], dec_rows[rows:]])
    flow.sync(["enc"], begin=[("halo_grad", one_stage((halos, "y", 1)))])
    flow.sync(["enc_feed"])
    flow.sync(["enc", "halo_grad"])
    (halos,) = flow.ended["halo_grad"]
    at_start = jnp.logical_and(chip_y == 1, core == 0)
    at_end = jnp.logical_and(chip_y == 0, core == 1)

    def input_grad(dtotal, summed, halo):
        first = jnp.where(at_start, halo, 0.0)
        last = jnp.where(at_end, halo, 0.0)
        spread = jnp.concatenate([first, jnp.zeros((rows - 2 * BLOCK, width), F32), last])
        return dtotal + summed[:rows] + spread

    encoder_input_grad = input_grad(dtotal0, enc_rows, halos[:BLOCK])
    decoder_input_grad = input_grad(dtotal2, dec_rows, halos[BLOCK:])

    reduced = {name: flow.ended[name] for name in REDUCES}
    squares = sum(jnp.sum(values * values) for values in reduced.values())
    payload = jnp.concatenate(
        [
            0.5 * jnp.concatenate([dnorm0, dnorm1, dnorm2, dnorm3, dnorm4]),
            jnp.broadcast_to(squares, (1, width)),
        ]
    )
    payload = sum_all(payload)
    g_all = payload[:10]
    grad_norm = jnp.sqrt(payload[10, 0] + jnp.sum(g_all * g_all))
    factor = clip_bound / jnp.maximum(grad_norm, clip_bound)
    own_columns = norm_params.shape[2]
    g_norms = lax.dynamic_slice(g_all, (0, lax.axis_index(DP) * own_columns), (10, own_columns))

    attention_parts = [reduced[name] for name in ("enc", "self", "cross")]
    feed_parts = [reduced[name] for name in ("enc_feed", "dec_feed")]
    g_in = jnp.stack(
        [g[:, kind * part : (kind + 1) * part] for g in attention_parts for kind in range(3)]
    )
    g_out = jnp.stack([g[:, 3 * part :].T for g in attention_parts])
    g_first = jnp.stack([g[:, :half] for g in feed_parts])
    g_second = jnp.stack([g[:, half:].T for g in feed_parts])
    all_grads = (g_in, g_out, g_first, g_second, g_norms.reshape(norm_params.shape))
    firsts = (
        attention_in_first, attention_out_first, feed_in_first, feed_out_first, norm_params_first,
    )
    seconds = (
        attention_in_second, attention_out_second, feed_in_second, feed_out_second,
        norm_params_second,
    )
    results = []
    for number in range(5):
        rate = rate_norm if number == 4 else rate_matrix
        decay = 0.0 if number == 4 else weight_decay
        results.append(
            adam_step(
                masters[number],
                firsts[number],
                seconds[number],
                all_grads[number] * factor,
                rate,
                decay,
            )
        )
    return (
        encoder_output,
        decoder_output,
        encoder_input_grad,
        decoder_input_grad,
        grad_norm,
        *(result[0] for result in results),
        *(result[1] for result in results),
        *(result[2] for result in results),
    )


def solution(mesh):
    dp, mp = mesh.shape["dp"], mesh.shape["mp"]
    fine = Mesh(mesh.devices.reshape(dp // 2, 2, mp // 2, 2), ALL)
    tokens = P(ALL, None)
    columns = P(None, DP, MP)
    turned = P(None, MP, DP)
    states = (columns, turned, columns, turned, P(None, None, DP))
    return jax.shard_map(
        on_device,
        mesh=fine,
        in_specs=(
            *((tokens,) * 4),
            P(DP, None),
            P(DP, None),
            P(DP, MP),
            *states,
            *states,
            *states,
        ),
        out_specs=(*((tokens,) * 4), P(), *states, *states, *states),
        check_vma=False,
    )
```

```python
import functools

import jax
import jax.numpy as jnp
from jax import lax
from jax.experimental import pallas as pl
from jax.experimental.pallas import tpu as pltpu
from jax.sharding import Mesh
from jax.sharding import PartitionSpec as P

HEAD_DIM = 64
STEP = 10
BLOCK = 128
PAIR = 2 * HEAD_DIM

norm_eps = 1e-05
beta_one = 0.9
beta_two = 0.98
adam_eps = 1e-08
weight_decay = 0.01
rate_matrix = 0.1
rate_norm = 0.5
clip_bound = 1.0
masked_score = -1e30
score_scale = HEAD_DIM ** (-0.5)
gelu_a = 0.7978845608028654
gelu_b = 0.044715

F32 = jnp.float32
BF16 = jnp.bfloat16
ANY = pl.ANY
SMEM = pltpu.SMEM
VMEM = pltpu.VMEM

NN = (((1,), (0,)), ((), ()))
NT = (((1,), (1,)), ((), ()))


def mm(a, b, dims=NN):
    return lax.dot_general(a, b, dims, preferred_element_type=F32)


def vmem(count):
    return [pl.BlockSpec(memory_space=VMEM)] * count


def smem(count):
    return [pl.BlockSpec(memory_space=SMEM)] * count


def hbm(count):
    return [pl.BlockSpec(memory_space=ANY)] * count


def cost(microseconds):
    return pl.CostEstimate(
        flops=int(microseconds * 1.15e9), bytes_accessed=int(microseconds * 3.6e6), transcendentals=0
    )


def params(mib=12):
    return pltpu.CompilerParams(vmem_limit_bytes=mib * 1024 * 1024)


LIMITS = {
    "self_forward": 14,
    "self_backward": 22,
    "cross_forward": 24,
    "cross_backward": 32,
    "feed_forward": 16,
    "feed_backward": 24,
    "end_norm": 10,
}


def shaped(shape, dtype):
    return jax.ShapeDtypeStruct(shape, dtype)


def normalize(total):
    centred = total - jnp.mean(total, axis=-1, keepdims=True)
    spread = jnp.mean(centred * centred, axis=-1, keepdims=True)
    rstd = lax.rsqrt(spread + norm_eps)
    return centred * rstd, rstd


def norm_backward(grad_out, xhat, rstd, gain):
    scaled = grad_out * gain
    first = jnp.mean(scaled, axis=-1, keepdims=True)
    second = jnp.mean(scaled * xhat, axis=-1, keepdims=True)
    return rstd * (scaled - first - xhat * second)


def norm_param_grads(grad_out, xhat):
    return (
        jnp.sum(grad_out * xhat, axis=0, keepdims=True),
        jnp.sum(grad_out, axis=0, keepdims=True),
    )


def half_masks():
    lane = lax.broadcasted_iota(jnp.int32, (1, PAIR), 1)
    low = jnp.where(lane < HEAD_DIM, 1.0, 0.0).astype(BF16)
    high = jnp.where(lane < HEAD_DIM, 0.0, 1.0).astype(BF16)
    return low, high


def stack_pair(values, masks):
    return jnp.concatenate([values * masks[0], values * masks[1]], axis=0)


SLAB = 64
PIECES = (4, 4, 4, 2, 2)
ROWS_OF = {"encoder": 0, "decoder": 1, "cotangent": 2}


def slab_shape(width):
    return (4, 2, SLAB, width)


def flat(values):
    return values.reshape(values.shape[0] * values.shape[1] * values.shape[2], values.shape[3])


def weight_copies(me_ref, pieces, offset, w_vmem, sems):
    columns = pl.ds(offset, w_vmem.shape[4])
    copies = []
    for member in range(2):
        group = []
        for x in range(2):
            number = 2 * member + x
            parts = [(pieces[number], 0, 4)] if number < 3 else [(pieces[3], 0, 2), (pieces[4], 2, 2)]
            for part, start, count in parts:
                group.append(
                    pltpu.make_async_copy(
                        part.at[:, :, columns],
                        w_vmem.at[member, pl.ds(start, count), me_ref[1] ^ x],
                        sems.at[member, 2 * x + start // 2],
                    )
                )
        copies.append(group)
    return copies


def grad_copies(me_ref, dw_vmem, targets, sems):
    return [
        [
            pltpu.make_async_copy(
                dw_vmem.at[member, :, me_ref[1] ^ x], targets[2 * member + x], sems.at[member, x]
            )
            for x in range(2)
        ]
        for member in range(2)
    ]


def start_all(groups):
    for group in groups:
        for copy in group:
            copy.start()


def wait_all(group):
    for copy in group:
        copy.wait()


def row_at(start, count):
    return pl.ds(pl.multiple_of(start, BLOCK), count)


def chip_copies(me_ref, own, sib, place, first, sems):
    rows = own.shape[0]
    return [
        pltpu.make_async_copy(own, place.at[row_at(first + me_ref[4] * rows, rows)], sems.at[0]),
        pltpu.make_async_copy(
            sib, place.at[row_at(first + (1 - me_ref[4]) * rows, rows)], sems.at[1]
        ),
    ]


def halo_place(me_ref, place, side):
    far = place.shape[0] - BLOCK
    return row_at((side ^ me_ref[3]) * far, BLOCK)


def haloed_copies(me_ref, refs, which, place, sems):
    own, sib, halo = refs
    rows = (place.shape[0] - 2 * BLOCK) // 2
    copies = chip_copies(
        me_ref,
        own.at[pl.ds(which * rows, rows)],
        sib.at[pl.ds(which * rows, rows)],
        place,
        BLOCK,
        sems,
    )
    place[halo_place(me_ref, place, 0), :] = jnp.zeros((BLOCK, place.shape[1]), BF16)
    copies.append(
        pltpu.make_async_copy(
            halo.at[pl.ds(which * BLOCK, BLOCK)],
            place.at[halo_place(me_ref, place, 1)],
            sems.at[2],
        )
    )
    return copies


class Inputs:
    def __init__(self, sources, places, sems):
        self.places = places
        self.copies = [
            pltpu.make_async_copy(source, place, sems.at[number])
            for number, (source, place) in enumerate(zip(sources, places))
        ]
        self.waited = set()

    def start(self, *numbers):
        for number in numbers:
            self.copies[number].start()

    def __getitem__(self, number):
        if number not in self.waited:
            self.waited.add(number)
            self.copies[number].wait()
        return self.places[number]


class Late:
    def __init__(self, ins, base):
        self.ins, self.base = ins, base

    def __getitem__(self, number):
        return self.ins[self.base + number]


class Outputs:
    def __init__(self, places, targets, sems):
        self.places = places
        self.copies = [
            pltpu.make_async_copy(place, target, sems.at[number])
            for number, (place, target) in enumerate(zip(places, targets))
        ]

    def __getitem__(self, number):
        return self.places[number]

    def send(self, *numbers):
        for number in numbers:
            self.copies[number].start()

    def finish(self):
        wait_all(self.copies)


def staged(
    body, name, me, others, inputs, raw, outputs, direct=(), scratch=(), microseconds=10
):
    scalars = (me, *others)
    counts = (len(scalars), len(inputs), len(raw), len(outputs), len(direct))

    def kernel(*refs):
        parts, at = [], 0
        for count in counts:
            parts.append(refs[at : at + count])
            at += count
        scalar_refs, sources, raw_refs, targets, direct_refs = parts
        rest = refs[at:]
        in_places, rest = rest[: len(inputs)], rest[len(inputs) :]
        out_places, rest = rest[: len(outputs)], rest[len(outputs) :]
        in_sems, out_sems, rest = rest[0], rest[1], rest[2:]
        body(
            scalar_refs,
            Inputs(sources, in_places, in_sems),
            raw_refs,
            Outputs(out_places, targets, out_sems),
            direct_refs,
            *rest,
        )

    return pl.pallas_call(
        kernel,
        out_shape=(*outputs, *direct),
        in_specs=smem(len(scalars)) + hbm(len(inputs) + len(raw)),
        out_specs=tuple(hbm(len(outputs) + len(direct))),
        scratch_shapes=[
            *(pltpu.VMEM(array.shape, array.dtype) for array in inputs),
            *(pltpu.VMEM(array.shape, array.dtype) for array in outputs),
            pltpu.SemaphoreType.DMA((max(len(inputs), 1),)),
            pltpu.SemaphoreType.DMA((max(len(outputs), 1),)),
            *scratch,
        ],
        compiler_params=params(LIMITS[name]),
        cost_estimate=cost(microseconds),
        name=name,
    )(*scalars, *inputs, *raw)


def weight_scratch(width):
    return [pltpu.VMEM((2, *slab_shape(width)), BF16), pltpu.SemaphoreType.DMA((2, 4))]


def grad_scratch(width):
    return [pltpu.VMEM((2, *slab_shape(width)), BF16), pltpu.SemaphoreType.DMA((2, 2))]


def grad_pieces(width):
    return (shaped((4, SLAB, width), BF16),) * 4


def spread_kinds(w_vmem, w_flat, member):
    part = w_vmem.shape[4] // 4
    for kind in range(4):
        w_flat[:, pl.ds((kind * 2 + member) * part, part)] = flat(
            w_vmem[member, :, :, :, kind * part : (kind + 1) * part]
        )


def store_kind(dw_vmem, kind, grads):
    part = dw_vmem.shape[4] // 4
    for member in range(2):
        dw_vmem[member, :, :, :, kind * part : (kind + 1) * part] = (
            grads[:, member * part : (member + 1) * part].astype(BF16).reshape(slab_shape(part))
        )


def gain_of(norms, number):
    return norms[2 * number : 2 * number + 1, :]


def shift_of(norms, number):
    return norms[2 * number + 1 : 2 * number + 2, :]


def both(own_ref, sib_ref):
    return own_ref[...].astype(F32) + sib_ref[...].astype(F32)


def store_norm_grads(outs, number, dy, xhat):
    dgain, dshift = norm_param_grads(dy, xhat)
    outs[number][0:1, :] = dgain
    outs[number][1:2, :] = dshift
    outs.send(number)


def lanes_at(block):
    return pl.ds(pl.multiple_of(block * BLOCK, BLOCK), BLOCK)


def store_halves(target, at, pair, values):
    target[pl.ds(pair * PAIR, HEAD_DIM), at] = values[:HEAD_DIM, :BLOCK]
    target[pl.ds(pair * PAIR + HEAD_DIM, HEAD_DIM), at] = values[HEAD_DIM:, BLOCK:]


def self_forward(me, chip, which, segk, weights):
    pieces, offset = weights
    width = chip[0].shape[1]
    rows = 2 * (chip[0].shape[0] // 3)
    keys = rows + 2 * BLOCK
    here = width // 2
    blocks, pairs, window = rows // BLOCK, here // PAIR, 3 * BLOCK

    def body(scalars, ins, raw, outs, direct, w_vmem, w_sems, x_sems, x_s, w_s, vt_s, ctxt_s):
        me_ref = scalars[0]
        x_copies = haloed_copies(me_ref, raw[:3], which, x_s, x_sems)
        start_all([x_copies])
        copies = weight_copies(me_ref, raw[3:], offset, w_vmem, w_sems)
        start_all(copies)
        ins.start(0)
        part_o, q_o, k_o, v_o, ctx_o, pt_o = outs.places
        segments = ins[0][...]
        columns = segments.T
        for member in range(2):
            wait_all(copies[member])
            spread_kinds(w_vmem, w_s, member)
        wait_all(x_copies)
        kv = mm(x_s[...], w_s[:, here : 3 * here]).astype(BF16)
        k_o[...] = kv[:, :here]
        v_o[...] = kv[:, here:]
        outs.send(2, 3)
        vt_s[...] = kv[:, here:].T
        q = mm(x_s[BLOCK : BLOCK + rows, :], w_s[:, :here]).astype(BF16)
        q_o[...] = q * jnp.asarray(score_scale, BF16)
        outs.send(1)
        masks = half_masks()
        for block in range(blocks):
            at = pl.ds(block * BLOCK, BLOCK)
            keys_at = pl.ds(block * BLOCK, window)
            column = jnp.concatenate([columns[:, block + k : block + k + 1] for k in range(3)])
            row = segments[block + 1 : block + 2, :]
            allowed = column == jnp.concatenate([row, row], axis=1)
            for pair in range(pairs):
                cols = pl.ds(pair * PAIR, PAIR)
                stacked = stack_pair(q_o[at, cols], masks)
                scores = mm(k_o[keys_at, cols], stacked, NT)
                scores = jnp.where(allowed, scores, masked_score)
                highest = jnp.max(scores, axis=0, keepdims=True)
                raised = jnp.exp(scores - highest)
                total = jnp.sum(raised, axis=0, keepdims=True)
                probs = (raised * (1.0 / total)).astype(BF16)
                pt_o[block * pairs + pair] = probs
                store_halves(ctxt_s, at, pair, mm(vt_s[cols, keys_at], probs).astype(BF16))
        outs.send(5)
        context = ctxt_s[...].T
        ctx_o[...] = context
        outs.send(4)
        part_o[...] = mm(context, w_s[:, 3 * here :], NT).astype(BF16)
        outs.send(0)
        outs.finish()

    part, *saved = staged(
        body,
        "self_forward",
        me,
        (),
        (segk,),
        (*chip, *pieces),
        (
            shaped((rows, width), BF16),
            shaped((rows, here), BF16),
            shaped((keys, here), BF16),
            shaped((keys, here), BF16),
            shaped((rows, here), BF16),
            shaped((blocks * pairs, window, 2 * BLOCK), BF16),
        ),
        scratch=(
            *weight_scratch(width),
            pltpu.SemaphoreType.DMA((3,)),
            pltpu.VMEM((keys, width), BF16),
            pltpu.VMEM((width, 4 * here), BF16),
            pltpu.VMEM((here, keys), BF16),
            pltpu.VMEM((here, rows), BF16),
        ),
        microseconds=9,
    )
    return part, saved


def self_backward(me, dy, xhat, rstd, norms, k_norm, chip, which, saved, weights):
    pieces, offset = weights
    rows, width = xhat.shape
    keys = rows + 2 * BLOCK
    own = rows // 2
    here = width // 2
    blocks, pairs, window = rows // BLOCK, here // PAIR, 3 * BLOCK

    def body(
        scalars, ins, raw, outs, direct,
        w_vmem, w_sems, dw_s, dw_sems, x_sems, dx_sems,
        x_s, w_s, dctx_s, kt_s, dqt_s, dkv_s, dx_s, dtotal_s,
    ):
        me_ref = scalars[0]
        ins.start(0, 1, 2, 3, 4, 5)
        copies = weight_copies(me_ref, raw[3:], offset, w_vmem, w_sems)
        start_all(copies)
        ins.start(9, 7, 8, 10, 6)
        x_copies = haloed_copies(me_ref, raw[:3], which, x_s, x_sems)
        start_all([x_copies])
        out_copies = grad_copies(me_ref, dw_s, direct[:4], dw_sems)
        dtotal_o, keep_o, send_o = direct[4:]
        masks = half_masks()
        dy = ins[0][...] + both(ins[1], ins[2])
        xhat = ins[3][...]
        store_norm_grads(outs, 0, dy, xhat)
        dtotal = norm_backward(dy, xhat, ins[4][...], gain_of(ins[5], k_norm))
        dtotal_s[...] = dtotal
        low = dtotal.astype(BF16)
        for member in range(2):
            wait_all(copies[member])
            spread_kinds(w_vmem, w_s, member)
        dctx_s[...] = mm(low, w_s[:, 3 * here :]).astype(BF16)
        store_kind(dw_s, 3, mm(low.T, ins[9][...]))
        kt_s[...] = ins[7][...].T
        dkv_s[...] = jnp.zeros_like(dkv_s)
        q_ref, v_ref, pt_ref = ins[6], ins[8], ins[10]
        for block in range(blocks):
            at = pl.ds(block * BLOCK, BLOCK)
            keys_at = pl.ds(block * BLOCK, window)
            for pair in range(pairs):
                cols = pl.ds(pair * PAIR, PAIR)
                dstacked = stack_pair(dctx_s[at, cols], masks)
                qstacked = stack_pair(q_ref[at, cols], masks)
                probs_low = pt_ref[block * pairs + pair]
                probs = probs_low.astype(F32)
                dprobs = mm(v_ref[keys_at, cols], dstacked, NT)
                delta = jnp.sum(probs * dprobs, axis=0, keepdims=True)
                dscores = (probs * (dprobs - delta)).astype(BF16)
                dkv_s[keys_at, cols] += mm(dscores, qstacked)
                dkv_s[keys_at, pl.ds(here + pair * PAIR, PAIR)] += mm(probs_low, dstacked)
                dqt = mm(kt_s[cols, keys_at], dscores) * score_scale
                store_halves(dqt_s, at, pair, dqt.astype(BF16))
        dq = dqt_s[...].T
        dkv = dkv_s[...].astype(BF16)
        wait_all(x_copies)
        xt = x_s[...].T
        store_kind(dw_s, 0, mm(xt[:, BLOCK : BLOCK + rows], dq))
        dw = mm(xt, dkv)
        store_kind(dw_s, 1, dw[:, :here])
        store_kind(dw_s, 2, dw[:, here:])
        start_all(out_copies)
        dx_s[...] = mm(dkv, w_s[:, here : 3 * here], NT).astype(BF16)
        middle = pl.ds(BLOCK, rows)
        dx_s[middle, :] = (dx_s[middle, :].astype(F32) + mm(dq, w_s[:, :here], NT)).astype(BF16)
        first = me_ref[4] * own
        other = (1 - me_ref[4]) * own
        halo = halo_place(me_ref, dx_s, 1)
        moves = [
            (dtotal_s.at[row_at(first, own)], dtotal_o),
            (dx_s.at[row_at(BLOCK + first, own)], keep_o.at[pl.ds(0, own)]),
            (dx_s.at[halo], keep_o.at[pl.ds(own, BLOCK)]),
            (dx_s.at[row_at(BLOCK + other, own)], send_o.at[pl.ds(0, own)]),
            (dx_s.at[halo], send_o.at[pl.ds(own, BLOCK)]),
        ]
        dx_copies = [
            pltpu.make_async_copy(source, target, dx_sems.at[number])
            for number, (source, target) in enumerate(moves)
        ]
        start_all([dx_copies])
        outs.finish()
        wait_all(dx_copies)
        for group in out_copies:
            wait_all(group)

    swapped = shaped((own + BLOCK, width), BF16)
    dnorm, *results = staged(
        body,
        "self_backward",
        me,
        (),
        (*dy, xhat, rstd, norms, *saved),
        (*chip, *pieces),
        (shaped((2, width), F32),),
        direct=(*grad_pieces(width), shaped((own, width), F32), swapped, swapped),
        scratch=(
            *weight_scratch(width),
            *grad_scratch(width),
            pltpu.SemaphoreType.DMA((3,)),
            pltpu.SemaphoreType.DMA((5,)),
            pltpu.VMEM((keys, width), BF16),
            pltpu.VMEM((width, 4 * here), BF16),
            pltpu.VMEM((rows, here), BF16),
            pltpu.VMEM((here, keys), BF16),
            pltpu.VMEM((here, rows), BF16),
            pltpu.VMEM((keys, 2 * here), F32),
            pltpu.VMEM((keys, width), BF16),
            pltpu.VMEM((rows, width), F32),
        ),
        microseconds=12,
    )
    return dnorm, results[:4], results[4], results[5], results[6]


def memory_copies(me_ref, pieces, m_s, sems):
    rows = pieces[0].shape[0]
    return [
        pltpu.make_async_copy(
            piece, m_s.at[row_at((me_ref[2] ^ member) * rows, rows)], sems.at[member]
        )
        for member, piece in enumerate(pieces)
    ]


WINDOW = 3 * BLOCK


def chunk_range(range_ref, blocks):
    size = WINDOW // BLOCK
    return range_ref[0] // size, (range_ref[2 * blocks - 1] + size - 1) // size


def fresh_keys(start, last_start):
    key = lax.broadcasted_iota(jnp.int32, (WINDOW, 1), 0)
    return key >= (start - jnp.minimum(start, last_start)) * BLOCK


def cross_forward(me, ranges, chip, which, part_own, part_sib, norms, k_in, segq, segk, memory, weights):
    pieces, offset = weights
    rows, width = part_own.shape
    own = rows // 2
    here = width // 2
    keys = 2 * rows
    blocks, pairs = rows // BLOCK, here // PAIR

    def body(
        scalars, ins, raw, outs, direct,
        w_vmem, w_sems, x_sems, m_sems, x_s, m_s, w_s, vt_s, acc_s, ctxt_s, seg_s, stat_s,
    ):
        me_ref, range_ref = scalars
        x_copies = chip_copies(
            me_ref,
            raw[0].at[pl.ds(which * own, own)],
            raw[1].at[pl.ds(which * own, own)],
            x_s,
            0,
            x_sems,
        )
        start_all([x_copies])
        ins.start(0, 1, 2)
        copies = weight_copies(me_ref, raw[6:], offset, w_vmem, w_sems)
        start_all(copies)
        m_copies = memory_copies(me_ref, raw[2:6], m_s, m_sems)
        start_all([m_copies])
        ins.start(3, 4)
        part_o, xhat_o, rstd_o, q_o, k_o, v_o, ctx_o, lse_o = outs.places
        masks = half_masks()
        wait_all(x_copies)
        xhat, rstd = normalize(x_s[...].astype(F32) + both(ins[0], ins[1]))
        xhat_o[...] = xhat
        rstd_o[...] = rstd
        outs.send(1, 2)
        inputs = xhat * gain_of(ins[2], k_in) + shift_of(ins[2], k_in)
        for member in range(2):
            wait_all(copies[member])
            spread_kinds(w_vmem, w_s, member)
        q = mm(inputs.astype(BF16), w_s[:, :here]).astype(BF16)
        q_o[...] = q * jnp.asarray(score_scale, BF16)
        outs.send(3)
        ins[3]
        columns = ins[4][...].T
        for block in range(keys // BLOCK):
            seg_s[pl.ds(block * BLOCK, BLOCK), :] = columns[:, block : block + 1]
        wait_all(m_copies)

        @pl.loop(*chunk_range(range_ref, blocks))
        def _(chunk):
            keys_at = row_at(chunk * WINDOW, WINDOW)
            kv = mm(m_s[keys_at, :], w_s[:, here : 3 * here]).astype(BF16)
            k_o[keys_at, :] = kv[:, :here]
            v_o[keys_at, :] = kv[:, here:]
            vt_s[:, keys_at] = kv[:, here:].T

        outs.send(4, 5)
        size = WINDOW // BLOCK
        last_start = (chunk_range(range_ref, blocks)[1] - 1) * size

        @pl.loop(0, blocks)
        def _(block):
            at = lanes_at(block)
            first, last = range_ref[2 * block], range_ref[2 * block + 1]
            row = ins[3][pl.ds(block + 1, 1), :]
            segq_row = jnp.concatenate([row, row], axis=1)

            def window_scores(start):
                keys_at = row_at(start * BLOCK, WINDOW)
                allowed = seg_s[keys_at, :] == segq_row
                result = []
                for pair in range(pairs):
                    cols = pl.ds(pair * PAIR, PAIR)
                    scores = mm(k_o[keys_at, cols], stack_pair(q_o[at, cols], masks), NT)
                    result.append(jnp.where(allowed, scores, masked_score))
                return keys_at, result

            keys_at, scores = window_scores(jnp.minimum(first, last_start))
            for pair in range(pairs):
                highest = jnp.max(scores[pair], axis=0, keepdims=True)
                raised = jnp.exp(scores[pair] - highest)
                total = jnp.sum(raised, axis=0, keepdims=True)
                acc_s[pair] = mm(vt_s[pl.ds(pair * PAIR, PAIR), keys_at], raised.astype(BF16))
                stat_s[2 * pair : 2 * pair + 1, :] = highest
                stat_s[2 * pair + 1 : 2 * pair + 2, :] = total

            @pl.loop(1, (last - first + size - 1) // size)
            def _(number):
                start = first + number * size
                keys_at, scores = window_scores(jnp.minimum(start, last_start))
                fresh = fresh_keys(start, last_start)
                for pair in range(pairs):
                    kept = jnp.where(fresh, scores[pair], masked_score)
                    before = stat_s[2 * pair : 2 * pair + 1, :]
                    highest = jnp.maximum(before, jnp.max(kept, axis=0, keepdims=True))
                    shrink = jnp.exp(before - highest)
                    raised = jnp.where(kept > 0.5 * masked_score, jnp.exp(kept - highest), 0.0)
                    acc_s[pair] = acc_s[pair] * shrink + mm(
                        vt_s[pl.ds(pair * PAIR, PAIR), keys_at], raised.astype(BF16)
                    )
                    stat_s[2 * pair : 2 * pair + 1, :] = highest
                    stat_s[2 * pair + 1 : 2 * pair + 2, :] = stat_s[
                        2 * pair + 1 : 2 * pair + 2, :
                    ] * shrink + jnp.sum(raised, axis=0, keepdims=True)

            for pair in range(pairs):
                total = stat_s[2 * pair + 1 : 2 * pair + 2, :]
                store_halves(ctxt_s, at, pair, (acc_s[pair] * (1.0 / total)).astype(BF16))
                lse_o[pl.ds(block * pairs + pair, 1), :] = stat_s[
                    2 * pair : 2 * pair + 1, :
                ] + jnp.log(total)

        context = ctxt_s[...].T
        ctx_o[...] = context
        outs.send(6, 7)
        part_o[...] = mm(context, w_s[:, 3 * here :], NT).astype(BF16)
        outs.send(0)
        outs.finish()

    part, xhat, rstd, *saved = staged(
        body,
        "cross_forward",
        me,
        (ranges,),
        (part_own, part_sib, norms, segq, segk),
        (*chip[:2], *memory, *pieces),
        (
            shaped((rows, width), BF16),
            shaped((rows, width), F32),
            shaped((rows, 1), F32),
            shaped((rows, here), BF16),
            shaped((keys, here), BF16),
            shaped((keys, here), BF16),
            shaped((rows, here), BF16),
            shaped((blocks * pairs, 2 * BLOCK), F32),
        ),
        scratch=(
            *weight_scratch(width),
            pltpu.SemaphoreType.DMA((2,)),
            pltpu.SemaphoreType.DMA((4,)),
            pltpu.VMEM((rows, width), BF16),
            pltpu.VMEM((keys, width), BF16),
            pltpu.VMEM((width, 4 * here), BF16),
            pltpu.VMEM((here, keys), BF16),
            pltpu.VMEM((pairs, PAIR, 2 * BLOCK), F32),
            pltpu.VMEM((here, rows), BF16),
            pltpu.VMEM((keys, 1), F32),
            pltpu.VMEM((8, 2 * BLOCK), F32),
        ),
        microseconds=10,
    )
    return part, xhat, rstd, saved


def cross_backward(
    me, ranges, dy, xhat, rstd, norms, k_norm, xin, k_in, segq, segk, saved, memory, weights
):
    pieces, offset = weights
    rows, width = xhat.shape
    half = rows // 2
    here = width // 2
    keys = 2 * rows
    blocks, pairs = rows // BLOCK, here // PAIR
    heads_here = here // HEAD_DIM

    def body(
        scalars, ins, raw, outs, direct,
        w_vmem, w_sems, dw_s, dw_sems, m_sems, dm_sems,
        m_s, w_s, dctx_s, kt_s, dqt_acc, dqt_s, dkv_s, dwkv_s, dm_s, seg_s, delta_s,
    ):
        me_ref, range_ref = scalars
        ins.start(0, 1, 2, 3, 4, 5)
        copies = weight_copies(me_ref, raw[4:], offset, w_vmem, w_sems)
        start_all(copies)
        ins.start(12, 10, 11, 9, 13, 7, 8, 6)
        m_copies = memory_copies(me_ref, raw[:4], m_s, m_sems)
        start_all([m_copies])
        out_copies = grad_copies(me_ref, dw_s, direct[:4], dw_sems)
        dm_keep, dm_send = direct[4:]
        part_o, dtotal_o, dnorm_o = outs.places
        norms_ref = ins[5]
        masks = half_masks()
        dy = ins[0][...] + both(ins[1], ins[2])
        xhat = ins[3][...]
        store_norm_grads(outs, 2, dy, xhat)
        dtotal = norm_backward(dy, xhat, ins[4][...], gain_of(norms_ref, k_norm))
        dtotal_o[...] = dtotal
        outs.send(1)
        low = dtotal.astype(BF16)
        for member in range(2):
            wait_all(copies[member])
            spread_kinds(w_vmem, w_s, member)
        dctx = mm(low, w_s[:, 3 * here :]).astype(BF16)
        dctx_s[...] = dctx
        context = ins[12][...]
        store_kind(dw_s, 3, mm(low.T, context))
        products = (dctx.astype(F32) * context.astype(F32)).T
        for head in range(heads_here):
            delta_s[head : head + 1, :] = jnp.sum(
                products[head * HEAD_DIM : (head + 1) * HEAD_DIM, :], axis=0, keepdims=True
            )
        k_ref, v_ref, q_ref, lse_ref = ins[10], ins[11], ins[9], ins[13]
        ins[7]
        columns = ins[8][...].T
        for block in range(keys // BLOCK):
            seg_s[pl.ds(block * BLOCK, BLOCK), :] = columns[:, block : block + 1]

        @pl.loop(*chunk_range(range_ref, blocks))
        def _(chunk):
            keys_at = row_at(chunk * WINDOW, WINDOW)
            kt_s[:, keys_at] = k_ref[keys_at, :].T
            dkv_s[keys_at, :] = jnp.zeros((WINDOW, 2 * here), F32)

        size = WINDOW // BLOCK
        last_start = (chunk_range(range_ref, blocks)[1] - 1) * size

        @pl.loop(0, blocks)
        def _(block):
            at = lanes_at(block)
            first, last = range_ref[2 * block], range_ref[2 * block + 1]
            row = ins[7][pl.ds(block + 1, 1), :]
            segq_row = jnp.concatenate([row, row], axis=1)
            dqt_acc[...] = jnp.zeros_like(dqt_acc)

            @pl.loop(0, (last - first + size - 1) // size)
            def _(number):
                start = first + number * size
                keys_at = row_at(jnp.minimum(start, last_start) * BLOCK, WINDOW)
                allowed = jnp.logical_and(
                    seg_s[keys_at, :] == segq_row, fresh_keys(start, last_start)
                )
                for pair in range(pairs):
                    cols = pl.ds(pair * PAIR, PAIR)
                    qstacked = stack_pair(q_ref[at, cols], masks)
                    dstacked = stack_pair(dctx_s[at, cols], masks)
                    delta = jnp.concatenate(
                        [delta_s[2 * pair : 2 * pair + 1, at], delta_s[2 * pair + 1 : 2 * pair + 2, at]],
                        axis=1,
                    )
                    scores = mm(k_ref[keys_at, cols], qstacked, NT)
                    scores = jnp.where(allowed, scores, masked_score)
                    probs = jnp.exp(scores - lse_ref[pl.ds(block * pairs + pair, 1), :])
                    dprobs = mm(v_ref[keys_at, cols], dstacked, NT)
                    dscores = (probs * (dprobs - delta)).astype(BF16)
                    dkv_s[keys_at, cols] += mm(dscores, qstacked)
                    dkv_s[keys_at, pl.ds(here + pair * PAIR, PAIR)] += mm(
                        probs.astype(BF16), dstacked
                    )
                    dqt_acc[pair] += mm(kt_s[cols, keys_at], dscores)

            for pair in range(pairs):
                store_halves(dqt_s, at, pair, (dqt_acc[pair] * score_scale).astype(BF16))

        dq = dqt_s[...].T
        part_o[...] = mm(dq, w_s[:, :here], NT).astype(BF16)
        outs.send(0)
        inputs = (ins[6][...] * gain_of(norms_ref, k_in) + shift_of(norms_ref, k_in)).astype(BF16)
        store_kind(dw_s, 0, mm(inputs.T, dq))
        dm_s[...] = jnp.zeros_like(dm_s)
        dwkv_s[...] = jnp.zeros_like(dwkv_s)
        wait_all(m_copies)

        @pl.loop(*chunk_range(range_ref, blocks))
        def _(chunk):
            keys_at = row_at(chunk * WINDOW, WINDOW)
            dkv = dkv_s[keys_at, :].astype(BF16)
            dm_s[keys_at, :] = mm(dkv, w_s[:, here : 3 * here], NT).astype(BF16)
            dwkv_s[...] += mm(m_s[keys_at, :].T, dkv)

        dm_copies = [
            pltpu.make_async_copy(
                dm_s.at[row_at((me_ref[2] ^ member) * half, half), :],
                (dm_keep, dm_send)[member % 2].at[member // 2],
                dm_sems.at[member],
            )
            for member in range(4)
        ]
        start_all([dm_copies])
        store_kind(dw_s, 1, dwkv_s[:, :here])
        store_kind(dw_s, 2, dwkv_s[:, here:])
        start_all(out_copies)
        outs.finish()
        wait_all(dm_copies)
        for group in out_copies:
            wait_all(group)

    halves = shaped((2, half, width), BF16)
    part, dtotal, dnorm, *results = staged(
        body,
        "cross_backward",
        me,
        (ranges,),
        (*dy, xhat, rstd, norms, xin, segq, segk, *saved),
        (*memory, *pieces),
        (shaped((rows, width), BF16), shaped((rows, width), F32), shaped((2, width), F32)),
        direct=(*grad_pieces(width), halves, halves),
        scratch=(
            *weight_scratch(width),
            *grad_scratch(width),
            pltpu.SemaphoreType.DMA((4,)),
            pltpu.SemaphoreType.DMA((4,)),
            pltpu.VMEM((keys, width), BF16),
            pltpu.VMEM((width, 4 * here), BF16),
            pltpu.VMEM((rows, here), BF16),
            pltpu.VMEM((here, keys), BF16),
            pltpu.VMEM((pairs, PAIR, 2 * BLOCK), F32),
            pltpu.VMEM((here, rows), BF16),
            pltpu.VMEM((keys, 2 * here), F32),
            pltpu.VMEM((width, 2 * here), F32),
            pltpu.VMEM((keys, width), BF16),
            pltpu.VMEM((keys, 1), F32),
            pltpu.VMEM((8, rows), F32),
        ),
        microseconds=16,
    )
    return dtotal, part, dnorm, results[:4], results[4], results[5]


def gelu_and_slope(pre):
    square = pre * pre
    half = 0.5 * pre
    tanh = jnp.tanh(pre * (gelu_a + (gelu_a * gelu_b) * square))
    cdf = 0.5 + 0.5 * tanh
    slope = cdf + half * (1.0 - tanh * tanh) * (gelu_a + (3.0 * gelu_a * gelu_b) * square)
    return (pre * cdf).astype(BF16), slope.astype(BF16)


def feed_forward(me, base, part_own, part_sib, k_norm, weights, norms, norm_piece=None):
    pieces, offset = weights
    rows, width = part_own.shape
    own = rows // 2
    first = norm_piece is not None
    raw = (*base[0][:2], *pieces) if first else pieces
    inputs = (part_own, part_sib) if first else (part_own, part_sib, norms, base[0])

    def body(scalars, ins, raw, outs, direct, w_vmem, w_sems, *rest):
        me_ref = scalars[0]
        part_o, xhat_o, rstd_o = outs.places[:3]
        hidden, slope = outs.places[3:5], outs.places[5:7]
        if first:
            norm_s, norm_sems, x_s, x_sems, acc_s = rest
            which = base[1]
            x_copies = chip_copies(
                me_ref,
                raw[0].at[pl.ds(which * own, own)],
                raw[1].at[pl.ds(which * own, own)],
                x_s,
                0,
                x_sems,
            )
            start_all([x_copies])
            raw = raw[2:]
            norm_copies = weight_copies(me_ref, raw, norm_piece[1], norm_s, norm_sems)[0]
            start_all([norm_copies])
        else:
            (acc_s,) = rest
        ins.start(*range(len(inputs)))
        copies = weight_copies(me_ref, raw, offset, w_vmem, w_sems)
        start_all(copies)
        if first:
            wait_all(norm_copies)
            norms_ref = outs[7]
            norms_ref[...] = flat(norm_s[0]).astype(F32).T[: norms_ref.shape[0], :]
            outs.send(7)
            wait_all(x_copies)
            before = x_s[...].astype(F32)
        else:
            norms_ref = ins[2]
            before = ins[3][...] * gain_of(norms_ref, base[1]) + shift_of(norms_ref, base[1])
        xhat, rstd = normalize(before + both(ins[0], ins[1]))
        xhat_o[...] = xhat
        rstd_o[...] = rstd
        outs.send(1, 2)
        low = (xhat * gain_of(norms_ref, k_norm) + shift_of(norms_ref, k_norm)).astype(BF16)
        half = w_vmem.shape[4] // 2
        for member in range(2):
            wait_all(copies[member])
            hidden_low, slope_low = gelu_and_slope(mm(low, flat(w_vmem[member, :, :, :, :half])))
            hidden[member][...] = hidden_low
            slope[member][...] = slope_low
            outs.send(3 + member, 5 + member)
            product = mm(hidden_low, flat(w_vmem[member, :, :, :, half:]), NT)
            if member == 0:
                acc_s[...] = product
            else:
                part_o[...] = (acc_s[...] + product).astype(BF16)
        outs.send(0)
        outs.finish()

    piece = shaped((rows, width), BF16)
    results = staged(
        body,
        "feed_forward",
        me,
        (),
        inputs,
        raw,
        (
            piece,
            shaped((rows, width), F32),
            shaped((rows, 1), F32),
            *((piece,) * 4),
            *((shaped((16, width), F32),) if first else ()),
        ),
        scratch=(
            *weight_scratch(2 * width),
            *(
                (
                    pltpu.VMEM((2, *slab_shape(BLOCK)), BF16),
                    pltpu.SemaphoreType.DMA((2, 4)),
                    pltpu.VMEM((rows, width), BF16),
                    pltpu.SemaphoreType.DMA((2,)),
                )
                if first
                else ()
            ),
            pltpu.VMEM((rows, width), F32),
        ),
        microseconds=7,
    )
    return results[0], results[1], results[2], results[3:5], results[5:7], *results[7:]


def end_norm(me, xhat_before, k_before, part_own, part_sib, norms, k_norm):
    rows, width = part_own.shape
    own = rows // 2

    def body(scalars, ins, raw, outs, direct, x_s, one_s, two_s, sems):
        at = row_at(scalars[0][4] * own, own)
        copies = [
            pltpu.make_async_copy(source.at[at], place, sems.at[number])
            for number, (source, place) in enumerate(zip(raw, (x_s, one_s, two_s)))
        ]
        start_all([copies])
        ins.start(0)
        wait_all(copies)
        before = x_s[...] * gain_of(ins[0], k_before) + shift_of(ins[0], k_before)
        xhat, _ = normalize(before + both(one_s, two_s))
        outs[0][...] = (xhat * gain_of(ins[0], k_norm) + shift_of(ins[0], k_norm)).astype(BF16)
        outs.send(0)
        outs.finish()

    (out,) = staged(
        body,
        "end_norm",
        me,
        (),
        (norms,),
        (xhat_before, part_own, part_sib),
        (shaped((own, width), BF16),),
        scratch=(
            pltpu.VMEM((own, width), F32),
            pltpu.VMEM((own, width), BF16),
            pltpu.VMEM((own, width), BF16),
            pltpu.SemaphoreType.DMA((3,)),
        ),
        microseconds=2,
    )
    return out


def feed_backward(me, dy, parts, xin, k_in, k_out, norms, hidden, slope, weights, turning):
    pieces, offset = weights
    (dy_own, dy_sib), which = dy
    rows, width = xin.shape
    own = rows // 2

    def body(
        scalars, ins, raw, outs, direct, w_vmem, w_sems, dw_s, dw_sems, dy_s, dy_sems, acc_s, *rest
    ):
        me_ref = scalars[0]
        ins.start(0, 1, 2, 3)
        dy_copies = chip_copies(
            me_ref,
            raw[0].at[pl.ds(which * own, own)],
            raw[1].at[pl.ds(which * own, own)],
            dy_s,
            0,
            dy_sems,
        )
        start_all([dy_copies])
        copies = weight_copies(me_ref, raw[2:], offset, w_vmem, w_sems)
        for member in range(2):
            start_all([copies[member]])
            ins.start(6 + member, 4 + member)
        out_copies = grad_copies(me_ref, dw_s, direct[:4], dw_sems)
        part_o, dtotal_o, dnorm_o = outs.places
        norms_ref = ins[1]
        inputs = ins[0][...] * gain_of(norms_ref, k_in) + shift_of(norms_ref, k_in)
        gain = gain_of(norms_ref, k_out)
        xhat, rstd = normalize(inputs + both(ins[2], ins[3]))
        if turning:
            out_s, out_sems = rest
            out_s[...] = (xhat * gain + shift_of(norms_ref, k_out)).astype(BF16)
            out_copy = pltpu.make_async_copy(
                out_s.at[row_at(me_ref[4] * own, own)], direct[4], out_sems.at[0]
            )
            out_copy.start()
        wait_all(dy_copies)
        dy = dy_s[...].astype(F32)
        store_norm_grads(outs, 2, dy, xhat)
        dtotal = norm_backward(dy, xhat, rstd, gain)
        dtotal_o[...] = dtotal
        outs.send(1)
        low = dtotal.astype(BF16)
        lowt = low.T
        xt = inputs.astype(BF16).T
        half = w_vmem.shape[4] // 2
        for member in range(2):
            wait_all(copies[member])
            dhidden = mm(low, flat(w_vmem[member, :, :, :, half:]))
            dpre = (dhidden * ins[6 + member][...].astype(F32)).astype(BF16)
            dw_s[member, :, :, :, :half] = mm(xt, dpre).astype(BF16).reshape(slab_shape(half))
            dw_s[member, :, :, :, half:] = (
                mm(lowt, ins[4 + member][...]).astype(BF16).reshape(slab_shape(half))
            )
            start_all([out_copies[member]])
            product = mm(dpre, flat(w_vmem[member, :, :, :, :half]), NT)
            if member == 0:
                acc_s[...] = product
            else:
                part_o[...] = (acc_s[...] + product).astype(BF16)
        outs.send(0)
        outs.finish()
        for group in out_copies:
            wait_all(group)
        if turning:
            out_copy.wait()

    part, dtotal, dnorm, *results = staged(
        body,
        "feed_backward",
        me,
        (),
        (xin, norms, *parts, *hidden, *slope),
        (dy_own, dy_sib, *pieces),
        (shaped((rows, width), BF16), shaped((rows, width), F32), shaped((2, width), F32)),
        direct=(
            *grad_pieces(2 * width),
            *((shaped((own, width), BF16),) if turning else ()),
        ),
        scratch=(
            *weight_scratch(2 * width),
            *grad_scratch(2 * width),
            pltpu.VMEM((rows, width), BF16),
            pltpu.SemaphoreType.DMA((2,)),
            pltpu.VMEM((rows, width), F32),
            *(
                (pltpu.VMEM((rows, width), BF16), pltpu.SemaphoreType.DMA((1,)))
                if turning
                else ()
            ),
        ),
        microseconds=9,
    )
    return dtotal, part, dnorm, results[:4], *results[4:]


DP = ("z", "x")
MP = ("y", "c")
ALL = ("z", "x", "y", "c")


def is_cube():
    return tuple(lax.axis_size(axis) for axis in ALL) == (4, 2, 2, 2)


def swap(values, axis, distance=1):
    count = lax.axis_size(axis)
    return lax.ppermute(values, axis, [(i, i ^ distance) for i in range(count)])


def add(*terms):
    return sum(term.astype(F32) for term in terms)


def low_add(*terms):
    return add(*terms).astype(BF16)


def place_of(me_ref, at):
    return me_ref[0] ^ at[1] if isinstance(at, tuple) else at


def sum_kernel(sources, jobs, me_ref, *refs):
    inputs, outputs = refs[: len(sources)], refs[len(sources) : len(sources) + len(jobs)]
    places, sems = refs[len(sources) + len(jobs) : -1], refs[-1]
    copies = [
        pltpu.make_async_copy(ref.at[pl.ds(start, count)], place, sems.at[number])
        for number, (ref, place, (start, count)) in enumerate(zip(inputs, places, sources))
    ]
    start_all([copies])
    waited = set()
    for out, (_, slabs, turned, cut) in zip(outputs, jobs):
        for at, terms in enumerate(slabs):
            total = None
            for number, source_at in terms:
                if number not in waited:
                    waited.add(number)
                    copies[number].wait()
                value = places[number][place_of(me_ref, source_at), :, cut]
                if len(terms) > 1:
                    value = value.astype(F32)
                total = value if total is None else total + value
            out[place_of(me_ref, ("z", at)) if turned else at] = total.astype(out.dtype)


def sum_slabs(me, requests):
    arrays, sources, jobs = [], [], []
    for request_sources, request_jobs in requests:
        base = len(arrays)
        for array, start, count in request_sources:
            arrays.append(array)
            sources.append((start, count))
        for dtype, slabs, turned, cut in request_jobs:
            _, rows, width = request_sources[0][0].shape
            start, width = cut or (0, width)
            moved = tuple(tuple((base + number, at) for number, at in terms) for terms in slabs)
            out = shaped((len(slabs), rows, width), dtype)
            jobs.append((out, moved, turned, slice(start, start + width)))
    results = pl.pallas_call(
        functools.partial(sum_kernel, tuple(sources), tuple(jobs)),
        out_shape=tuple(job[0] for job in jobs),
        in_specs=smem(1) + hbm(len(arrays)),
        out_specs=tuple(vmem(len(jobs))),
        scratch_shapes=[
            *(
                pltpu.VMEM((count, *array.shape[1:]), array.dtype)
                for array, (_, count) in zip(arrays, sources)
            ),
            pltpu.SemaphoreType.DMA((len(arrays),)),
        ],
        compiler_params=params(),
        cost_estimate=cost(2),
        name="sum_slabs",
    )(me, *arrays)
    split, at = [], 0
    for _, request_jobs in requests:
        split.append(results[at : at + len(request_jobs)])
        at += len(request_jobs)
    return split


def gather_lines(shard, widths):
    starts = [sum(widths[:number]) for number in range(len(widths))]
    if not is_cube():
        yield ()
        return tuple(shard[:, at : at + width] for at, width in zip(starts, widths))
    over_z = yield tuple((shard, "z", k) for k in (1, 2, 3))
    return (
        yield (
            tuple((piece[None], 0, 1) for piece in (shard, *over_z)),
            tuple(
                (BF16, tuple(((k, 0),) for k in range(4)), True, cut) for cut in zip(starts, widths)
            ),
        )
    )


def gather_square(lines):
    if not is_cube():
        whole = lax.all_gather(lines, ("y", *DP), axis=0, tiled=True)
        whole = whole.reshape(2, 4, 2, SLAB, lines.shape[1])
        for _ in range(2):
            yield ()
        return (whole[0, :, 0], whole[0, :, 1], whole[1, :, 0], whole[1, :2, 1], whole[1, 2:, 1])
    over_x, over_y = yield ((lines, "x", 1), (lines, "y", 1))
    far_one, far_two = yield ((over_y[:2], "x", 1), (over_x[2:], "y", 1))
    return lines, over_x, over_y, far_one, far_two


def reduce_square(own, to_x, to_y, to_far):
    if not is_cube():
        yield ()
        return own, to_x, to_y, to_far
    arrived = yield ((to_x, "x", 1), (to_y, "y", 1), (to_far, ("x", "y"), 3))
    return (own, *arrived)


def reduce_lines(*groups):
    if not is_cube():
        sums = []
        for group in groups:
            whole = jnp.stack(group).reshape(2, 2, 4, SLAB, group[0].shape[2])
            whole = whole.transpose(0, 2, 1, 3, 4).reshape(2, 8 * SLAB, group[0].shape[2])
            part = lax.psum_scatter(whole, "y", scatter_dimension=0, tiled=True)
            sums.append(lax.psum_scatter(part[0], DP, scatter_dimension=0, tiled=True))
        yield ()
        sums = jnp.stack(sums).astype(F32)
        empty = jnp.zeros(sums.shape, BF16)
        return sums, (empty, empty, empty)
    lines = yield (
        tuple((array, 0, 4) for group in groups for array in group),
        tuple(
            (
                F32 if k == 0 else BF16,
                tuple(
                    tuple((4 * number + source, ("z", k)) for source in range(4))
                    for number in range(len(groups))
                ),
                False,
                None,
            )
            for k in range(4)
        ),
    )
    over_z = yield tuple((lines[k], "z", k) for k in (1, 2, 3))
    return lines[0], over_z


def finish_group(ended, number=0):
    own, over_z = ended
    return add(own[number], *(piece[number] for piece in over_z))


def one_stage(*jobs):
    return (yield jobs)


def memory_stages(values):
    over_y, over_c = yield ((values, "y", 1), (values, "c", 1))
    (over_both,) = yield ((over_y, "c", 1),)
    return values, over_c, over_y, over_both


def memory_grad_stages(keep, send):
    (got,) = yield ((send, "c", 1),)
    (over_y,) = yield ((low_add(keep[1], got[1]), "y", 1),)
    own = low_add(keep[0], got[0], over_y)
    (sib,) = yield ((own, "c", 1),)
    return own, sib


class Flow:
    def __init__(self, me, token):
        self.me = me
        self.moving = {}
        self.ended = {}
        self.token = token

    def sync(self, names, *values, begin=(), hold=()):
        arrived = [self.moving[name][1] for name in names]
        held = [self.moving[name][1] for name in hold]
        arrived, held, values, token = lax.optimization_barrier(
            (arrived, held, values, self.token)
        )
        for name, result in zip(hold, held):
            self.moving[name] = (self.moving[name][0], result)
        to_send, asked = {}, {}
        begun = [(name, stages, None) for name, stages in begin]
        moved = [(name, self.moving[name][0], result) for name, result in zip(names, arrived)]

        def move(name, stages, result):
            try:
                wanted = stages.send(result)
            except StopIteration as end:
                self.ended[name] = end.value
                self.moving.pop(name, None)
                return
            if wanted and isinstance(wanted[0][0], tuple):
                asked[name] = (stages, wanted)
            else:
                to_send[name] = (stages, wanted)

        for job in moved + begun:
            move(*job)
        if asked:
            names = list(asked)
            sums = sum_slabs(self.me, [asked[name][1] for name in names])
            for name, result in zip(names, sums):
                move(name, asked[name][0], result)
        operands = [[job[0] for job in jobs] for _, jobs in to_send.values()]
        operands, values, self.token = lax.optimization_barrier((operands, values, token))
        for sending, (name, (stages, jobs)) in zip(operands, to_send.items()):
            results = [
                swap(operand, axis, distance)
                for operand, (_, axis, distance) in zip(sending, jobs)
            ]
            self.moving[name] = (stages, results)
        return values


def sum_stages(values):
    if not is_cube():
        return (lax.psum(values, ALL), *((jnp.zeros_like(values),) * 3))
    values = values + swap(values, "c")
    one, two, three = swap(values, "y"), swap(values, "x"), swap(values, ("x", "y"), 3)
    values = (values + one) + (two + three)
    return (values, *(swap(values, "z", k) for k in (1, 2, 3)))


def pack(groups, widths, attention_in, attention_out, feed_in, feed_out, norm_columns):
    rows = attention_in.shape[1]
    inputs = (attention_in, attention_out, feed_in, feed_out, norm_columns)

    def kernel(*refs):
        sources, shards, places, sems = refs[:5], refs[5 : 5 + len(groups)], refs[-6:-1], refs[-1]
        ins = Inputs(sources, places, sems)
        ins.start(4, 0, 1, 2, 3)
        order = {"enc": 0, "self": 1, "cross": 2, "enc_feed": 0, "dec_feed": 1}
        for shard, names in zip(shards, groups):
            offset = 0
            for name in names:
                number = order.get(name)
                if name == "norms":
                    pieces = [ins[4][...]]
                elif name.endswith("feed"):
                    pieces = [ins[2][number], ins[3][number]]
                else:
                    pieces = [ins[0][3 * number + kind] for kind in range(3)] + [ins[1][number]]
                for piece in pieces:
                    shard[:, pl.ds(offset, piece.shape[1])] = piece.astype(BF16)
                    offset += piece.shape[1]

    return pl.pallas_call(
        kernel,
        out_shape=tuple(
            shaped((rows, sum(widths[name] for name in group)), BF16) for group in groups
        ),
        in_specs=hbm(5),
        out_specs=tuple(vmem(len(groups))),
        scratch_shapes=[
            *(pltpu.VMEM(array.shape, F32) for array in inputs),
            pltpu.SemaphoreType.DMA((5,)),
        ],
        compiler_params=params(60),
        cost_estimate=cost(2),
        name="pack",
    )(*inputs)


def close_kernel(*refs):
    own, far, others, norms = refs[0], refs[1:4], refs[4:8], refs[8:13]
    grad, payload = refs[13:]
    total = own[0] + sum(ref[0].astype(F32) for ref in far)
    grad[...] = total
    squares = jnp.sum(total * total)
    for other in others:
        squares = squares + jnp.sum(other[...] * other[...])
    for number, norm in enumerate(norms):
        payload[2 * number : 2 * number + 2, :] = 0.5 * norm[...]
    payload[10:, :] = jnp.full((payload.shape[0] - 10, payload.shape[1]), squares, F32)


def close(own, far, others, norms):
    return pl.pallas_call(
        close_kernel,
        out_shape=(shaped(own.shape[1:], F32), shaped((16, norms[0].shape[1]), F32)),
        in_specs=vmem(13),
        out_specs=tuple(vmem(2)),
        compiler_params=params(),
        cost_estimate=cost(2),
        name="close",
    )(own, *far, *others, *norms)


def adam_step(weights, first, second, grads, rate, decay):
    first_new = beta_one * first + (1.0 - beta_one) * grads
    second_new = beta_two * second + (1.0 - beta_two) * grads * grads
    first_hat = first_new / (1.0 - beta_one**STEP)
    second_hat = second_new / (1.0 - beta_two**STEP)
    weights_new = weights - rate * (first_hat / (jnp.sqrt(second_hat) + adam_eps) + decay * weights)
    return (weights_new, first_new, second_new)


def update_kernel(count, me_ref, *refs):
    sums, grads, refs = refs[:4], refs[4:9], refs[9:]
    masters, firsts, seconds = refs[:count], refs[count : 2 * count], refs[2 * count : 3 * count]
    refs = refs[3 * count :]
    news, new_firsts, new_seconds = refs[:count], refs[count : 2 * count], refs[2 * count : 3 * count]
    total_ref, norm_ref = refs[3 * count :]
    total = (sums[0][...] + sums[1][...]) + (sums[2][...] + sums[3][...])
    total_ref[...] = total
    norm_grads = total[:10]
    squares = total[10:11, :BLOCK] + jnp.sum(norm_grads * norm_grads)
    grad_norm = jnp.sqrt(squares)
    norm_ref[...] = grad_norm
    factor = clip_bound / jnp.maximum(grad_norm[:, :1], clip_bound)
    part = masters[0].shape[2]
    half = masters[2].shape[2]
    attention, feed = grads[:3], grads[3:]

    def step(number, at, grad, rate=rate_matrix, decay=weight_decay):
        results = adam_step(
            masters[number][at], firsts[number][at], seconds[number][at], grad * factor, rate, decay
        )
        for target, value in zip((news, new_firsts, new_seconds), results):
            target[number][at] = value

    for number in range(3):
        for kind in range(3):
            step(0, 3 * number + kind, attention[number][:, kind * part : (kind + 1) * part])
        step(1, number, attention[number][:, 3 * part :])
    for number in range(2):
        step(2, number, feed[number][:, :half])
        step(3, number, feed[number][:, half:])
    if count == 5:
        own = total_ref[:, pl.ds(pl.multiple_of(me_ref[0] * BLOCK, BLOCK), BLOCK)]
        columns = masters[4].shape[2]
        own = jnp.where(me_ref[1] == 0, own[:, :columns], own[:, columns:])
        for number in range(5):
            step(4, number, own[2 * number : 2 * number + 2], rate_norm, 0.0)


def update(me, sums, grads, masters, firsts, seconds):
    count = len(masters)
    states = (*masters, *firsts, *seconds)
    *results, total, grad_norm = pl.pallas_call(
        functools.partial(update_kernel, count),
        out_shape=(
            *(shaped(array.shape, F32) for array in states),
            shaped(sums[0].shape, F32),
            shaped((1, BLOCK), F32),
        ),
        in_specs=smem(1) + vmem(9 + len(states)),
        out_specs=tuple(vmem(len(states) + 2)),
        compiler_params=params(24),
        cost_estimate=cost(4),
        name="update",
    )(me, *sums, *grads, *states)
    split = [results[k * count : (k + 1) * count] for k in range(3)]
    return split, total, grad_norm[0, 0]


EARLY = ("enc", "enc_feed", "norms")
MIDDLE = ("self", "cross")
LATE = ("dec_feed",)


def on_device(
    encoder_input, decoder_copy, decoder_target, decoder_cotangent,
    source_segments, target_segments, glance_mask,
    attention_in, attention_out, feed_in, feed_out, norm_params,
    attention_in_first, attention_out_first, feed_in_first, feed_out_first, norm_params_first,
    attention_in_second, attention_out_second, feed_in_second, feed_out_second, norm_params_second,
):
    rows, width = encoder_input.shape
    length = source_segments.shape[1]
    part, half = attention_in.shape[2], feed_in.shape[2]
    chip_y, core = lax.axis_index("y"), lax.axis_index("c")
    here = (lax.axis_index("z"), lax.axis_index("x")) if is_cube() else (0, 0)
    me = jnp.stack([jnp.int32(value) for value in (*here, 2 * chip_y + core, chip_y, core)])
    flow = Flow(me, jnp.zeros((8, BLOCK), F32) + norm_params[0, 0, 0])

    def turned(array):
        return array.transpose(0, 2, 1)

    masters = (attention_in, turned(attention_out), feed_in, turned(feed_out), norm_params)
    firsts = (
        attention_in_first, turned(attention_out_first), feed_in_first, turned(feed_out_first),
        norm_params_first,
    )
    seconds = (
        attention_in_second, turned(attention_out_second), feed_in_second,
        turned(feed_out_second), norm_params_second,
    )
    norm_columns = jnp.pad(norm_params.reshape(10, -1).T, ((0, 0), (0, BLOCK - 10)))
    widths = {
        "enc": 4 * part, "self": 4 * part, "cross": 4 * part, "norms": BLOCK,
        "enc_feed": 2 * half, "dec_feed": 2 * half,
    }
    shard_early, shard_rest = pack((EARLY, MIDDLE + LATE), widths, *masters[:4], norm_columns)
    weight_places = {}
    for group in (EARLY, MIDDLE, LATE):
        offset = 0
        for name in group:
            weight_places[name] = (group, offset)
            offset += widths[name]

    def weights(name):
        group, offset = weight_places[name]
        return (flow.ended[group], offset)

    picked = glance_mask[0] == 1
    decoder_input = jnp.where(picked[:, None], decoder_target, decoder_copy)
    own_rows = jnp.concatenate([encoder_input, decoder_input, decoder_cotangent])

    chip_rows = 2 * rows
    blocks = chip_rows // BLOCK
    source_row = source_segments[0].astype(F32)
    target_row = target_segments[0].astype(F32)

    def chip_segments(row):
        padded = jnp.pad(row, (BLOCK, BLOCK), constant_values=-1.0)
        own = lax.dynamic_slice(padded, (chip_y * chip_rows,), (chip_rows + 2 * BLOCK,))
        return own.reshape(blocks + 2, BLOCK)

    source_chip, target_chip = chip_segments(source_row), chip_segments(target_row)
    source_all = jnp.pad(source_row.reshape(length // BLOCK, BLOCK), ((0, 16 - length // BLOCK), (0, 0)))
    lowest, highest = target_chip[1:-1, 0], target_chip[1:-1, BLOCK - 1]
    first_key = jnp.sum((source_row[None, :] < lowest[:, None]).astype(jnp.int32), axis=1)
    last_key = jnp.sum((source_row[None, :] <= highest[:, None]).astype(jnp.int32), axis=1)
    ranges = jnp.stack([first_key // BLOCK, (last_key + BLOCK - 1) // BLOCK], axis=1)
    ranges = ranges.astype(jnp.int32).reshape(2 * blocks)

    group_widths = [sum(widths[name] for name in group) for group in (EARLY, MIDDLE, LATE)]
    (shard_rest,) = flow.sync(
        [], shard_rest, begin=[("early_z", gather_lines(shard_early, group_widths[:1]))]
    )
    own_rows, shard_rest = flow.sync(["early_z"], own_rows, shard_rest)
    own_rows, shard_rest = flow.sync(
        [], own_rows, shard_rest, begin=[(EARLY, gather_square(*flow.ended["early_z"]))]
    )
    (own_rows,) = flow.sync(
        [],
        own_rows,
        begin=[
            ("rest_z", gather_lines(shard_rest, group_widths[1:])),
            ("rows", one_stage((own_rows, "c", 1))),
        ],
    )
    (own_rows,) = flow.sync(["rows"], own_rows)
    (sib_rows,) = flow.ended["rows"]

    def edge(which):
        last = jnp.where(core == 1, own_rows[(which + 1) * rows - BLOCK : (which + 1) * rows],
                         sib_rows[(which + 1) * rows - BLOCK : (which + 1) * rows])
        first = jnp.where(core == 0, own_rows[which * rows : which * rows + BLOCK],
                          sib_rows[which * rows : which * rows + BLOCK])
        return jnp.where(chip_y == 0, last, first)

    edges = jnp.concatenate([edge(0), edge(1)])
    edges, source_chip, target_chip, ranges, source_all = flow.sync(
        [], edges, source_chip, target_chip, ranges, source_all
    )
    (edges,) = flow.sync([EARLY], edges, hold=["rest_z"])
    flow.sync([], begin=[("halo", one_stage((edges, "y", 1)))])
    flow.sync(["rest_z"])
    lines_middle, lines_late = flow.ended["rest_z"]
    flow.sync([EARLY, "halo"])
    chip = (own_rows, sib_rows, flow.ended["halo"][0])
    chip, source_chip, lines_late = flow.sync(
        [], chip, source_chip, lines_late, begin=[(MIDDLE, gather_square(lines_middle))]
    )

    enc, dec, cot = 0, 1, 2
    part0, enc_saved = self_forward(me, chip, enc, source_chip, weights("enc"))
    (part0,) = flow.sync([], part0, hold=[MIDDLE])
    (part0,) = flow.sync([], part0, begin=[("part0", one_stage((part0, "c", 1)))])
    (part0,) = flow.sync(["part0", MIDDLE], part0)
    part1, xhat0, rstd0, enc_hidden, enc_slope, norms = feed_forward(
        me, (chip, enc), part0, *flow.ended["part0"], 0, weights("enc_feed"), None, weights("norms")
    )
    (part1,) = flow.sync([], part1, hold=[MIDDLE])
    (part1,) = flow.sync([], part1, begin=[("part1", one_stage((part1, "c", 1)))])
    (part1,) = flow.sync(["part1", MIDDLE], part1)
    parts1 = (part1, *flow.ended["part1"])
    encoder_output = end_norm(me, xhat0, 0, *parts1, norms, 1)
    (target_chip,) = flow.sync(
        [], target_chip, begin=[("memory", memory_stages(encoder_output))]
    )
    part2, self_saved = self_forward(me, chip, dec, target_chip, weights("self"))
    (part2,) = flow.sync(["memory"], part2, begin=[("part2", one_stage((part2, "c", 1)))])
    (part2,) = flow.sync(
        ["memory", "part2"], part2, begin=[(LATE, gather_square(lines_late))]
    )
    memory = flow.ended["memory"]
    part3, xhat2, rstd2, cross_saved = cross_forward(
        me, ranges, chip, dec, part2, *flow.ended["part2"], norms, 2, target_chip, source_all,
        memory, weights("cross"),
    )
    (part3,) = flow.sync([], part3, hold=[LATE])
    (part3,) = flow.sync([LATE], part3, begin=[("part3", one_stage((part3, "c", 1)))])
    (part3,) = flow.sync(["part3", LATE], part3)
    part4, xhat3, rstd3, dec_hidden, dec_slope = feed_forward(
        me, (xhat2, 2), part3, *flow.ended["part3"], 3, weights("dec_feed"), norms
    )
    (part4,) = flow.sync([], part4, begin=[("part4", one_stage((part4, "c", 1)))])
    (part4,) = flow.sync(["part4"], part4)

    dtotal4, dpart4, dnorm4, pieces, decoder_output = feed_backward(
        me, (chip[:2], cot), (part4, *flow.ended["part4"]), xhat3, 3, 4, norms,
        dec_hidden, dec_slope, weights("dec_feed"), True,
    )
    (dtotal4,) = flow.sync([], dtotal4, begin=[("dpart4", one_stage((dpart4, "c", 1)))])
    (dtotal4,) = flow.sync(["dpart4"], dtotal4, begin=[("dec_feed", reduce_square(*pieces))])
    dtotal3, dpart3, dnorm3, pieces, dm_keep, dm_send = cross_backward(
        me, ranges, (dtotal4, dpart4, *flow.ended["dpart4"]), xhat3, rstd3, norms, 3, xhat2, 2,
        target_chip, source_all, cross_saved, memory, weights("cross"),
    )
    dpart3, dtotal3, dm_keep, dm_send = flow.sync(
        [], dpart3, dtotal3, dm_keep, dm_send, hold=["dec_feed"]
    )
    dpart3, dtotal3 = flow.sync(
        [],
        dpart3,
        dtotal3,
        begin=[
            ("memory_grad", memory_grad_stages(dm_keep, dm_send)),
            ("dpart3", one_stage((dpart3, "c", 1))),
        ],
    )
    dpart3, dtotal3 = flow.sync(
        ["memory_grad", "dpart3", "dec_feed"],
        dpart3,
        dtotal3,
        begin=[("cross", reduce_square(*pieces))],
    )
    dnorm2, pieces, dtotal2, dec_keep, dec_send = self_backward(
        me, (dtotal3, dpart3, *flow.ended["dpart3"]), xhat2, rstd2, norms, 2, chip, dec,
        self_saved, weights("self"),
    )
    (dtotal2,) = flow.sync(["memory_grad"], dtotal2, hold=["cross"])
    (dtotal2,) = flow.sync(
        ["memory_grad", "cross"],
        dtotal2,
        begin=[
            ("dec_feed", reduce_lines(flow.ended["dec_feed"])),
            ("self", reduce_square(*pieces)),
        ],
    )
    dmemory = flow.ended["memory_grad"]
    dmemory, dtotal2 = lax.optimization_barrier((dmemory, dtotal2))
    dtotal1, dpart1, dnorm1, pieces = feed_backward(
        me, (dmemory, 0), parts1, xhat0, 0, 1, norms, enc_hidden, enc_slope,
        weights("enc_feed"), False,
    )
    dpart1, dtotal1 = flow.sync([], dpart1, dtotal1, hold=["self", "dec_feed"])
    (dtotal1,) = flow.sync([], dtotal1, begin=[("dpart1", one_stage((dpart1, "c", 1)))])
    (dtotal1,) = flow.sync(
        ["dpart1", "dec_feed", "self"], dtotal1, begin=[("enc_feed", reduce_square(*pieces))]
    )
    (dtotal1,) = flow.sync(
        [],
        dtotal1,
        begin=[("pair", reduce_lines(flow.ended["self"], flow.ended["cross"]))],
    )
    dnorm0, pieces, dtotal0, enc_keep, enc_send = self_backward(
        me, (dtotal1, dpart1, *flow.ended["dpart1"]), xhat0, rstd0, norms, 0, chip, enc,
        enc_saved, weights("enc"),
    )
    both_send = jnp.concatenate([enc_send, dec_send])
    (both_send,) = flow.sync(
        [], both_send, hold=["enc_feed", "pair"], begin=[("enc", reduce_square(*pieces))]
    )
    (both_send,) = flow.sync(["enc_feed", "pair"], both_send)
    (both_send,) = flow.sync(
        [], both_send, begin=[("enc_feed", reduce_lines(flow.ended["enc_feed"]))]
    )
    flow.sync([], begin=[("rows_grad", one_stage((both_send, "c", 1)))])
    flow.sync(["rows_grad"], hold=["enc", "enc_feed"])
    (got,) = flow.ended["rows_grad"]
    swapped = rows + BLOCK
    enc_rows = add(enc_keep, got[:swapped])
    dec_rows = add(dec_keep, got[swapped:])
    halos = jnp.concatenate([enc_rows[rows:], dec_rows[rows:]])
    flow.sync(["enc"])
    flow.sync(
        [],
        begin=[
            ("enc", reduce_lines(flow.ended["enc"])),
            ("halo_grad", one_stage((halos, "y", 1))),
        ],
    )
    flow.sync(["enc_feed"])
    others = [
        finish_group(flow.ended["pair"], 0),
        finish_group(flow.ended["pair"], 1),
        finish_group(flow.ended["enc_feed"]),
        finish_group(flow.ended["dec_feed"]),
    ]
    others = flow.sync(["halo_grad"], *others)
    flow.sync(["enc"])
    (halos,) = flow.ended["halo_grad"]
    at_start = jnp.logical_and(chip_y == 1, core == 0)
    at_end = jnp.logical_and(chip_y == 0, core == 1)

    def input_grad(dtotal, summed, halo):
        first = jnp.where(at_start, halo, 0.0)
        last = jnp.where(at_end, halo, 0.0)
        spread = jnp.concatenate([first, jnp.zeros((rows - 2 * BLOCK, width), F32), last])
        return dtotal + summed[:rows] + spread

    encoder_input_grad = input_grad(dtotal0, enc_rows, halos[:BLOCK])
    decoder_input_grad = input_grad(dtotal2, dec_rows, halos[BLOCK:])

    own_enc, far_enc = flow.ended["enc"]
    g_enc, payload = close(own_enc, far_enc, others, (dnorm0, dnorm1, dnorm2, dnorm3, dnorm4))
    sums = sum_stages(payload)
    grads = (g_enc, others[0], others[1], others[2], others[3])
    if norm_params.shape[2] == BLOCK // 2 and is_cube():
        split, total, grad_norm = update(me, sums, grads, masters, firsts, seconds)
        results = list(zip(*split))
    else:
        split, total, grad_norm = update(me, sums, grads, masters[:4], firsts[:4], seconds[:4])
        results = list(zip(*split))
        columns = norm_params.shape[2]
        g_norms = lax.dynamic_slice(total, (0, lax.axis_index(DP) * columns), (10, columns))
        factor = clip_bound / jnp.maximum(grad_norm, clip_bound)
        g_norms = g_norms.reshape(norm_params.shape) * factor
        results.append(
            adam_step(norm_params, norm_params_first, norm_params_second, g_norms, rate_norm, 0.0)
        )
    results = [
        tuple(turned(value) for value in result) if number in (1, 3) else result
        for number, result in enumerate(results)
    ]
    return (
        encoder_output,
        decoder_output,
        encoder_input_grad,
        decoder_input_grad,
        grad_norm,
        *(result[0] for result in results),
        *(result[1] for result in results),
        *(result[2] for result in results),
    )


def solution(mesh):
    dp, mp = mesh.shape["dp"], mesh.shape["mp"]
    fine = Mesh(mesh.devices.reshape(dp // 2, 2, mp // 2, 2), ALL)
    tokens = P(ALL, None)
    columns = P(None, DP, MP)
    turned = P(None, MP, DP)
    states = (columns, turned, columns, turned, P(None, None, DP))
    return jax.shard_map(
        on_device,
        mesh=fine,
        in_specs=(
            *((tokens,) * 4),
            P(DP, None),
            P(DP, None),
            P(DP, MP),
            *states,
            *states,
            *states,
        ),
        out_specs=(*((tokens,) * 4), P(), *states, *states, *states),
        check_vma=False,
    )
```

```python
import functools

import jax
import jax.numpy as jnp
from jax import lax
from jax.experimental import pallas as pl
from jax.experimental.pallas import tpu as pltpu
from jax.sharding import Mesh
from jax.sharding import PartitionSpec as P

HEAD_DIM = 64
STEP = 10
BLOCK = 128
PAIR = 2 * HEAD_DIM

norm_eps = 1e-05
beta_one = 0.9
beta_two = 0.98
adam_eps = 1e-08
weight_decay = 0.01
rate_matrix = 0.1
rate_norm = 0.5
clip_bound = 1.0
masked_score = -1e30
score_scale = HEAD_DIM ** (-0.5)
gelu_a = 0.7978845608028654
gelu_b = 0.044715

F32 = jnp.float32
BF16 = jnp.bfloat16
ANY = pl.ANY
SMEM = pltpu.SMEM
VMEM = pltpu.VMEM

NN = (((1,), (0,)), ((), ()))
NT = (((1,), (1,)), ((), ()))


def mm(a, b, dims=NN):
    return lax.dot_general(a, b, dims, preferred_element_type=F32)


def vmem(count):
    return [pl.BlockSpec(memory_space=VMEM)] * count


def smem(count):
    return [pl.BlockSpec(memory_space=SMEM)] * count


def hbm(count):
    return [pl.BlockSpec(memory_space=ANY)] * count


def cost(microseconds):
    return pl.CostEstimate(
        flops=int(microseconds * 2.3e7), bytes_accessed=int(microseconds * 7.2e4), transcendentals=0
    )


def params(mib=12):
    return pltpu.CompilerParams(vmem_limit_bytes=mib * 1024 * 1024)


LIMITS = {
    "self_forward": 14,
    "self_backward": 22,
    "cross_forward": 24,
    "cross_backward": 32,
    "feed_forward": 16,
    "feed_backward": 24,
    "end_norm": 10,
}


def shaped(shape, dtype):
    return jax.ShapeDtypeStruct(shape, dtype)


def normalize(total):
    centred = total - jnp.mean(total, axis=-1, keepdims=True)
    spread = jnp.mean(centred * centred, axis=-1, keepdims=True)
    rstd = lax.rsqrt(spread + norm_eps)
    return centred * rstd, rstd


def norm_backward(grad_out, xhat, rstd, gain):
    scaled = grad_out * gain
    first = jnp.mean(scaled, axis=-1, keepdims=True)
    second = jnp.mean(scaled * xhat, axis=-1, keepdims=True)
    return rstd * (scaled - first - xhat * second)


def norm_param_grads(grad_out, xhat):
    return (
        jnp.sum(grad_out * xhat, axis=0, keepdims=True),
        jnp.sum(grad_out, axis=0, keepdims=True),
    )


def half_masks():
    lane = lax.broadcasted_iota(jnp.int32, (1, PAIR), 1)
    low = jnp.where(lane < HEAD_DIM, 1.0, 0.0).astype(BF16)
    high = jnp.where(lane < HEAD_DIM, 0.0, 1.0).astype(BF16)
    return low, high


def stack_pair(values, masks):
    return jnp.concatenate([values * masks[0], values * masks[1]], axis=0)


SLAB = 64
PIECES = (4, 4, 4, 2, 2)
ROWS_OF = {"encoder": 0, "decoder": 1, "cotangent": 2}


def slab_shape(width):
    return (4, 2, SLAB, width)


def flat(values):
    return values.reshape(values.shape[0] * values.shape[1] * values.shape[2], values.shape[3])


def weight_copies(me_ref, pieces, offset, w_vmem, sems):
    columns = pl.ds(offset, w_vmem.shape[4])
    copies = []
    for member in range(2):
        group = []
        for x in range(2):
            number = 2 * member + x
            parts = [(pieces[number], 0, 4)] if number < 3 else [(pieces[3], 0, 2), (pieces[4], 2, 2)]
            for part, start, count in parts:
                group.append(
                    pltpu.make_async_copy(
                        part.at[:, :, columns],
                        w_vmem.at[member, pl.ds(start, count), me_ref[1] ^ x],
                        sems.at[member, 2 * x + start // 2],
                    )
                )
        copies.append(group)
    return copies


def grad_copies(me_ref, dw_vmem, targets, sems):
    return [
        [
            pltpu.make_async_copy(
                dw_vmem.at[member, :, me_ref[1] ^ x], targets[2 * member + x], sems.at[member, x]
            )
            for x in range(2)
        ]
        for member in range(2)
    ]


def start_all(groups):
    for group in groups:
        for copy in group:
            copy.start()


def wait_all(group):
    for copy in group:
        copy.wait()


def row_at(start, count):
    return pl.ds(pl.multiple_of(start, BLOCK), count)


def chip_copies(me_ref, own, sib, place, first, sems):
    rows = own.shape[0]
    return [
        pltpu.make_async_copy(own, place.at[row_at(first + me_ref[4] * rows, rows)], sems.at[0]),
        pltpu.make_async_copy(
            sib, place.at[row_at(first + (1 - me_ref[4]) * rows, rows)], sems.at[1]
        ),
    ]


def halo_place(me_ref, place, side):
    far = place.shape[0] - BLOCK
    return row_at((side ^ me_ref[3]) * far, BLOCK)


def haloed_copies(me_ref, refs, which, place, sems):
    own, sib, halo = refs
    rows = (place.shape[0] - 2 * BLOCK) // 2
    copies = chip_copies(
        me_ref,
        own.at[pl.ds(which * rows, rows)],
        sib.at[pl.ds(which * rows, rows)],
        place,
        BLOCK,
        sems,
    )
    place[halo_place(me_ref, place, 0), :] = jnp.zeros((BLOCK, place.shape[1]), BF16)
    copies.append(
        pltpu.make_async_copy(
            halo.at[pl.ds(which * BLOCK, BLOCK)],
            place.at[halo_place(me_ref, place, 1)],
            sems.at[2],
        )
    )
    return copies


class Inputs:
    def __init__(self, sources, places, sems):
        self.places = places
        self.copies = [
            pltpu.make_async_copy(source, place, sems.at[number])
            for number, (source, place) in enumerate(zip(sources, places))
        ]
        self.waited = set()

    def start(self, *numbers):
        for number in numbers:
            self.copies[number].start()

    def __getitem__(self, number):
        if number not in self.waited:
            self.waited.add(number)
            self.copies[number].wait()
        return self.places[number]


class Late:
    def __init__(self, ins, base):
        self.ins, self.base = ins, base

    def __getitem__(self, number):
        return self.ins[self.base + number]


class Outputs:
    def __init__(self, places, targets, sems):
        self.places = places
        self.copies = [
            pltpu.make_async_copy(place, target, sems.at[number])
            for number, (place, target) in enumerate(zip(places, targets))
        ]

    def __getitem__(self, number):
        return self.places[number]

    def send(self, *numbers):
        for number in numbers:
            self.copies[number].start()

    def finish(self):
        wait_all(self.copies)


def staged(
    body, name, me, others, inputs, raw, outputs, direct=(), scratch=(), microseconds=10
):
    scalars = (me, *others)
    counts = (len(scalars), len(inputs), len(raw), len(outputs), len(direct))

    def kernel(*refs):
        parts, at = [], 0
        for count in counts:
            parts.append(refs[at : at + count])
            at += count
        scalar_refs, sources, raw_refs, targets, direct_refs = parts
        rest = refs[at:]
        in_places, rest = rest[: len(inputs)], rest[len(inputs) :]
        out_places, rest = rest[: len(outputs)], rest[len(outputs) :]
        in_sems, out_sems, rest = rest[0], rest[1], rest[2:]
        body(
            scalar_refs,
            Inputs(sources, in_places, in_sems),
            raw_refs,
            Outputs(out_places, targets, out_sems),
            direct_refs,
            *rest,
        )

    return pl.pallas_call(
        kernel,
        out_shape=(*outputs, *direct),
        in_specs=smem(len(scalars)) + hbm(len(inputs) + len(raw)),
        out_specs=tuple(hbm(len(outputs) + len(direct))),
        scratch_shapes=[
            *(pltpu.VMEM(array.shape, array.dtype) for array in inputs),
            *(pltpu.VMEM(array.shape, array.dtype) for array in outputs),
            pltpu.SemaphoreType.DMA((max(len(inputs), 1),)),
            pltpu.SemaphoreType.DMA((max(len(outputs), 1),)),
            *scratch,
        ],
        compiler_params=params(LIMITS[name]),
        cost_estimate=cost(microseconds),
        name=name,
    )(*scalars, *inputs, *raw)


def weight_scratch(width):
    return [pltpu.VMEM((2, *slab_shape(width)), BF16), pltpu.SemaphoreType.DMA((2, 4))]


def grad_scratch(width):
    return [pltpu.VMEM((2, *slab_shape(width)), BF16), pltpu.SemaphoreType.DMA((2, 2))]


def grad_pieces(width):
    return (shaped((4, SLAB, width), BF16),) * 4


def spread_kinds(w_vmem, w_flat, member):
    part = w_vmem.shape[4] // 4
    for kind in range(4):
        w_flat[:, pl.ds((kind * 2 + member) * part, part)] = flat(
            w_vmem[member, :, :, :, kind * part : (kind + 1) * part]
        )


def store_kind(dw_vmem, kind, grads):
    part = dw_vmem.shape[4] // 4
    for member in range(2):
        dw_vmem[member, :, :, :, kind * part : (kind + 1) * part] = (
            grads[:, member * part : (member + 1) * part].astype(BF16).reshape(slab_shape(part))
        )


def gain_of(norms, number):
    return norms[2 * number : 2 * number + 1, :]


def shift_of(norms, number):
    return norms[2 * number + 1 : 2 * number + 2, :]


def both(own_ref, sib_ref):
    return own_ref[...].astype(F32) + sib_ref[...].astype(F32)


def store_norm_grads(outs, number, dy, xhat):
    dgain, dshift = norm_param_grads(dy, xhat)
    outs[number][0:1, :] = dgain
    outs[number][1:2, :] = dshift
    outs.send(number)


def lanes_at(block):
    return pl.ds(pl.multiple_of(block * BLOCK, BLOCK), BLOCK)


def store_halves(target, at, pair, values):
    target[pl.ds(pair * PAIR, HEAD_DIM), at] = values[:HEAD_DIM, :BLOCK]
    target[pl.ds(pair * PAIR + HEAD_DIM, HEAD_DIM), at] = values[HEAD_DIM:, BLOCK:]


def self_forward(me, chip, which, segk, weights):
    pieces, offset = weights
    width = chip[0].shape[1]
    rows = 2 * (chip[0].shape[0] // 3)
    keys = rows + 2 * BLOCK
    here = width // 2
    blocks, pairs, window = rows // BLOCK, here // PAIR, 3 * BLOCK

    def body(scalars, ins, raw, outs, direct, w_vmem, w_sems, x_sems, x_s, w_s, vt_s, ctxt_s):
        me_ref = scalars[0]
        x_copies = haloed_copies(me_ref, raw[:3], which, x_s, x_sems)
        start_all([x_copies])
        copies = weight_copies(me_ref, raw[3:], offset, w_vmem, w_sems)
        start_all(copies)
        ins.start(0)
        part_o, q_o, k_o, v_o, ctx_o, pt_o = outs.places
        segments = ins[0][...]
        columns = segments.T
        for member in range(2):
            wait_all(copies[member])
            spread_kinds(w_vmem, w_s, member)
        wait_all(x_copies)
        kv = mm(x_s[...], w_s[:, here : 3 * here]).astype(BF16)
        k_o[...] = kv[:, :here]
        v_o[...] = kv[:, here:]
        outs.send(2, 3)
        vt_s[...] = kv[:, here:].T
        q = mm(x_s[BLOCK : BLOCK + rows, :], w_s[:, :here]).astype(BF16)
        q_o[...] = q * jnp.asarray(score_scale, BF16)
        outs.send(1)
        masks = half_masks()
        for block in range(blocks):
            at = pl.ds(block * BLOCK, BLOCK)
            keys_at = pl.ds(block * BLOCK, window)
            column = jnp.concatenate([columns[:, block + k : block + k + 1] for k in range(3)])
            row = segments[block + 1 : block + 2, :]
            allowed = column == jnp.concatenate([row, row], axis=1)
            for pair in range(pairs):
                cols = pl.ds(pair * PAIR, PAIR)
                stacked = stack_pair(q_o[at, cols], masks)
                scores = mm(k_o[keys_at, cols], stacked, NT)
                scores = jnp.where(allowed, scores, masked_score)
                highest = jnp.max(scores, axis=0, keepdims=True)
                raised = jnp.exp(scores - highest)
                total = jnp.sum(raised, axis=0, keepdims=True)
                probs = (raised * (1.0 / total)).astype(BF16)
                pt_o[block * pairs + pair] = probs
                store_halves(ctxt_s, at, pair, mm(vt_s[cols, keys_at], probs).astype(BF16))
        outs.send(5)
        context = ctxt_s[...].T
        ctx_o[...] = context
        outs.send(4)
        part_o[...] = mm(context, w_s[:, 3 * here :], NT).astype(BF16)
        outs.send(0)
        outs.finish()

    part, *saved = staged(
        body,
        "self_forward",
        me,
        (),
        (segk,),
        (*chip, *pieces),
        (
            shaped((rows, width), BF16),
            shaped((rows, here), BF16),
            shaped((keys, here), BF16),
            shaped((keys, here), BF16),
            shaped((rows, here), BF16),
            shaped((blocks * pairs, window, 2 * BLOCK), BF16),
        ),
        scratch=(
            *weight_scratch(width),
            pltpu.SemaphoreType.DMA((3,)),
            pltpu.VMEM((keys, width), BF16),
            pltpu.VMEM((width, 4 * here), BF16),
            pltpu.VMEM((here, keys), BF16),
            pltpu.VMEM((here, rows), BF16),
        ),
        microseconds=9,
    )
    return part, saved


def self_backward(me, dy, xhat, rstd, norms, k_norm, chip, which, saved, weights):
    pieces, offset = weights
    rows, width = xhat.shape
    keys = rows + 2 * BLOCK
    own = rows // 2
    here = width // 2
    blocks, pairs, window = rows // BLOCK, here // PAIR, 3 * BLOCK

    def body(
        scalars, ins, raw, outs, direct,
        w_vmem, w_sems, dw_s, dw_sems, x_sems, dx_sems,
        x_s, w_s, dctx_s, kt_s, dqt_s, dkv_s, dx_s, dtotal_s,
    ):
        me_ref = scalars[0]
        ins.start(0, 1, 2, 3, 4, 5)
        copies = weight_copies(me_ref, raw[3:], offset, w_vmem, w_sems)
        start_all(copies)
        ins.start(9, 7, 8, 10, 6)
        x_copies = haloed_copies(me_ref, raw[:3], which, x_s, x_sems)
        start_all([x_copies])
        out_copies = grad_copies(me_ref, dw_s, direct[:4], dw_sems)
        dtotal_o, keep_o, send_o = direct[4:]
        masks = half_masks()
        dy = ins[0][...] + both(ins[1], ins[2])
        xhat = ins[3][...]
        store_norm_grads(outs, 0, dy, xhat)
        dtotal = norm_backward(dy, xhat, ins[4][...], gain_of(ins[5], k_norm))
        dtotal_s[...] = dtotal
        low = dtotal.astype(BF16)
        for member in range(2):
            wait_all(copies[member])
            spread_kinds(w_vmem, w_s, member)
        dctx_s[...] = mm(low, w_s[:, 3 * here :]).astype(BF16)
        store_kind(dw_s, 3, mm(low.T, ins[9][...]))
        kt_s[...] = ins[7][...].T
        dkv_s[...] = jnp.zeros_like(dkv_s)
        q_ref, v_ref, pt_ref = ins[6], ins[8], ins[10]
        for block in range(blocks):
            at = pl.ds(block * BLOCK, BLOCK)
            keys_at = pl.ds(block * BLOCK, window)
            for pair in range(pairs):
                cols = pl.ds(pair * PAIR, PAIR)
                dstacked = stack_pair(dctx_s[at, cols], masks)
                qstacked = stack_pair(q_ref[at, cols], masks)
                probs_low = pt_ref[block * pairs + pair]
                probs = probs_low.astype(F32)
                dprobs = mm(v_ref[keys_at, cols], dstacked, NT)
                delta = jnp.sum(probs * dprobs, axis=0, keepdims=True)
                dscores = (probs * (dprobs - delta)).astype(BF16)
                dkv_s[keys_at, cols] += mm(dscores, qstacked)
                dkv_s[keys_at, pl.ds(here + pair * PAIR, PAIR)] += mm(probs_low, dstacked)
                dqt = mm(kt_s[cols, keys_at], dscores) * score_scale
                store_halves(dqt_s, at, pair, dqt.astype(BF16))
        dq = dqt_s[...].T
        dkv = dkv_s[...].astype(BF16)
        wait_all(x_copies)
        xt = x_s[...].T
        store_kind(dw_s, 0, mm(xt[:, BLOCK : BLOCK + rows], dq))
        dw = mm(xt, dkv)
        store_kind(dw_s, 1, dw[:, :here])
        store_kind(dw_s, 2, dw[:, here:])
        start_all(out_copies)
        dx_s[...] = mm(dkv, w_s[:, here : 3 * here], NT).astype(BF16)
        middle = pl.ds(BLOCK, rows)
        dx_s[middle, :] = (dx_s[middle, :].astype(F32) + mm(dq, w_s[:, :here], NT)).astype(BF16)
        first = me_ref[4] * own
        other = (1 - me_ref[4]) * own
        halo = halo_place(me_ref, dx_s, 1)
        moves = [
            (dtotal_s.at[row_at(first, own)], dtotal_o),
            (dx_s.at[row_at(BLOCK + first, own)], keep_o.at[pl.ds(0, own)]),
            (dx_s.at[halo], keep_o.at[pl.ds(own, BLOCK)]),
            (dx_s.at[row_at(BLOCK + other, own)], send_o.at[pl.ds(0, own)]),
            (dx_s.at[halo], send_o.at[pl.ds(own, BLOCK)]),
        ]
        dx_copies = [
            pltpu.make_async_copy(source, target, dx_sems.at[number])
            for number, (source, target) in enumerate(moves)
        ]
        start_all([dx_copies])
        outs.finish()
        wait_all(dx_copies)
        for group in out_copies:
            wait_all(group)

    swapped = shaped((own + BLOCK, width), BF16)
    dnorm, *results = staged(
        body,
        "self_backward",
        me,
        (),
        (*dy, xhat, rstd, norms, *saved),
        (*chip, *pieces),
        (shaped((2, width), F32),),
        direct=(*grad_pieces(width), shaped((own, width), F32), swapped, swapped),
        scratch=(
            *weight_scratch(width),
            *grad_scratch(width),
            pltpu.SemaphoreType.DMA((3,)),
            pltpu.SemaphoreType.DMA((5,)),
            pltpu.VMEM((keys, width), BF16),
            pltpu.VMEM((width, 4 * here), BF16),
            pltpu.VMEM((rows, here), BF16),
            pltpu.VMEM((here, keys), BF16),
            pltpu.VMEM((here, rows), BF16),
            pltpu.VMEM((keys, 2 * here), F32),
            pltpu.VMEM((keys, width), BF16),
            pltpu.VMEM((rows, width), F32),
        ),
        microseconds=12,
    )
    return dnorm, results[:4], results[4], results[5], results[6]


def memory_copies(me_ref, pieces, m_s, sems):
    rows = pieces[0].shape[0]
    return [
        pltpu.make_async_copy(
            piece, m_s.at[row_at((me_ref[2] ^ member) * rows, rows)], sems.at[member]
        )
        for member, piece in enumerate(pieces)
    ]


WINDOW = 3 * BLOCK


def chunk_range(range_ref, blocks):
    size = WINDOW // BLOCK
    return range_ref[0] // size, (range_ref[2 * blocks - 1] + size - 1) // size


def fresh_keys(start, last_start):
    key = lax.broadcasted_iota(jnp.int32, (WINDOW, 1), 0)
    return key >= (start - jnp.minimum(start, last_start)) * BLOCK


def cross_forward(me, ranges, chip, which, part_own, part_sib, norms, k_in, segq, segk, memory, weights):
    pieces, offset = weights
    rows, width = part_own.shape
    own = rows // 2
    here = width // 2
    keys = 2 * rows
    blocks, pairs = rows // BLOCK, here // PAIR

    def body(
        scalars, ins, raw, outs, direct,
        w_vmem, w_sems, x_sems, m_sems, x_s, m_s, w_s, vt_s, acc_s, ctxt_s, seg_s, stat_s,
    ):
        me_ref, range_ref = scalars
        x_copies = chip_copies(
            me_ref,
            raw[0].at[pl.ds(which * own, own)],
            raw[1].at[pl.ds(which * own, own)],
            x_s,
            0,
            x_sems,
        )
        start_all([x_copies])
        ins.start(0, 1, 2)
        copies = weight_copies(me_ref, raw[6:], offset, w_vmem, w_sems)
        start_all(copies)
        m_copies = memory_copies(me_ref, raw[2:6], m_s, m_sems)
        start_all([m_copies])
        ins.start(3, 4)
        part_o, xhat_o, rstd_o, q_o, k_o, v_o, ctx_o, lse_o = outs.places
        masks = half_masks()
        wait_all(x_copies)
        xhat, rstd = normalize(x_s[...].astype(F32) + both(ins[0], ins[1]))
        xhat_o[...] = xhat
        rstd_o[...] = rstd
        outs.send(1, 2)
        inputs = xhat * gain_of(ins[2], k_in) + shift_of(ins[2], k_in)
        for member in range(2):
            wait_all(copies[member])
            spread_kinds(w_vmem, w_s, member)
        q = mm(inputs.astype(BF16), w_s[:, :here]).astype(BF16)
        q_o[...] = q * jnp.asarray(score_scale, BF16)
        outs.send(3)
        ins[3]
        columns = ins[4][...].T
        for block in range(keys // BLOCK):
            seg_s[pl.ds(block * BLOCK, BLOCK), :] = columns[:, block : block + 1]
        wait_all(m_copies)

        @pl.loop(*chunk_range(range_ref, blocks))
        def _(chunk):
            keys_at = row_at(chunk * WINDOW, WINDOW)
            kv = mm(m_s[keys_at, :], w_s[:, here : 3 * here]).astype(BF16)
            k_o[keys_at, :] = kv[:, :here]
            v_o[keys_at, :] = kv[:, here:]
            vt_s[:, keys_at] = kv[:, here:].T

        outs.send(4, 5)
        size = WINDOW // BLOCK
        last_start = (chunk_range(range_ref, blocks)[1] - 1) * size

        @pl.loop(0, blocks)
        def _(block):
            at = lanes_at(block)
            first, last = range_ref[2 * block], range_ref[2 * block + 1]
            row = ins[3][pl.ds(block + 1, 1), :]
            segq_row = jnp.concatenate([row, row], axis=1)

            def window_scores(start):
                keys_at = row_at(start * BLOCK, WINDOW)
                allowed = seg_s[keys_at, :] == segq_row
                result = []
                for pair in range(pairs):
                    cols = pl.ds(pair * PAIR, PAIR)
                    scores = mm(k_o[keys_at, cols], stack_pair(q_o[at, cols], masks), NT)
                    result.append(jnp.where(allowed, scores, masked_score))
                return keys_at, result

            keys_at, scores = window_scores(jnp.minimum(first, last_start))
            for pair in range(pairs):
                highest = jnp.max(scores[pair], axis=0, keepdims=True)
                raised = jnp.exp(scores[pair] - highest)
                total = jnp.sum(raised, axis=0, keepdims=True)
                acc_s[pair] = mm(vt_s[pl.ds(pair * PAIR, PAIR), keys_at], raised.astype(BF16))
                stat_s[2 * pair : 2 * pair + 1, :] = highest
                stat_s[2 * pair + 1 : 2 * pair + 2, :] = total

            @pl.loop(1, (last - first + size - 1) // size)
            def _(number):
                start = first + number * size
                keys_at, scores = window_scores(jnp.minimum(start, last_start))
                fresh = fresh_keys(start, last_start)
                for pair in range(pairs):
                    kept = jnp.where(fresh, scores[pair], masked_score)
                    before = stat_s[2 * pair : 2 * pair + 1, :]
                    highest = jnp.maximum(before, jnp.max(kept, axis=0, keepdims=True))
                    shrink = jnp.exp(before - highest)
                    raised = jnp.where(kept > 0.5 * masked_score, jnp.exp(kept - highest), 0.0)
                    acc_s[pair] = acc_s[pair] * shrink + mm(
                        vt_s[pl.ds(pair * PAIR, PAIR), keys_at], raised.astype(BF16)
                    )
                    stat_s[2 * pair : 2 * pair + 1, :] = highest
                    stat_s[2 * pair + 1 : 2 * pair + 2, :] = stat_s[
                        2 * pair + 1 : 2 * pair + 2, :
                    ] * shrink + jnp.sum(raised, axis=0, keepdims=True)

            for pair in range(pairs):
                total = stat_s[2 * pair + 1 : 2 * pair + 2, :]
                store_halves(ctxt_s, at, pair, (acc_s[pair] * (1.0 / total)).astype(BF16))
                lse_o[pl.ds(block * pairs + pair, 1), :] = stat_s[
                    2 * pair : 2 * pair + 1, :
                ] + jnp.log(total)

        context = ctxt_s[...].T
        ctx_o[...] = context
        outs.send(6, 7)
        part_o[...] = mm(context, w_s[:, 3 * here :], NT).astype(BF16)
        outs.send(0)
        outs.finish()

    part, xhat, rstd, *saved = staged(
        body,
        "cross_forward",
        me,
        (ranges,),
        (part_own, part_sib, norms, segq, segk),
        (*chip[:2], *memory, *pieces),
        (
            shaped((rows, width), BF16),
            shaped((rows, width), F32),
            shaped((rows, 1), F32),
            shaped((rows, here), BF16),
            shaped((keys, here), BF16),
            shaped((keys, here), BF16),
            shaped((rows, here), BF16),
            shaped((blocks * pairs, 2 * BLOCK), F32),
        ),
        scratch=(
            *weight_scratch(width),
            pltpu.SemaphoreType.DMA((2,)),
            pltpu.SemaphoreType.DMA((4,)),
            pltpu.VMEM((rows, width), BF16),
            pltpu.VMEM((keys, width), BF16),
            pltpu.VMEM((width, 4 * here), BF16),
            pltpu.VMEM((here, keys), BF16),
            pltpu.VMEM((pairs, PAIR, 2 * BLOCK), F32),
            pltpu.VMEM((here, rows), BF16),
            pltpu.VMEM((keys, 1), F32),
            pltpu.VMEM((8, 2 * BLOCK), F32),
        ),
        microseconds=10,
    )
    return part, xhat, rstd, saved


def cross_backward(
    me, ranges, dy, xhat, rstd, norms, k_norm, xin, k_in, segq, segk, saved, memory, weights
):
    pieces, offset = weights
    rows, width = xhat.shape
    half = rows // 2
    here = width // 2
    keys = 2 * rows
    blocks, pairs = rows // BLOCK, here // PAIR
    heads_here = here // HEAD_DIM

    def body(
        scalars, ins, raw, outs, direct,
        w_vmem, w_sems, dw_s, dw_sems, m_sems, dm_sems,
        m_s, w_s, dctx_s, kt_s, dqt_acc, dqt_s, dkv_s, dwkv_s, dm_s, seg_s, delta_s,
    ):
        me_ref, range_ref = scalars
        ins.start(0, 1, 2, 3, 4, 5)
        copies = weight_copies(me_ref, raw[4:], offset, w_vmem, w_sems)
        start_all(copies)
        ins.start(12, 10, 11, 9, 13, 7, 8, 6)
        m_copies = memory_copies(me_ref, raw[:4], m_s, m_sems)
        start_all([m_copies])
        out_copies = grad_copies(me_ref, dw_s, direct[:4], dw_sems)
        dm_keep, dm_send = direct[4:]
        part_o, dtotal_o, dnorm_o = outs.places
        norms_ref = ins[5]
        masks = half_masks()
        dy = ins[0][...] + both(ins[1], ins[2])
        xhat = ins[3][...]
        store_norm_grads(outs, 2, dy, xhat)
        dtotal = norm_backward(dy, xhat, ins[4][...], gain_of(norms_ref, k_norm))
        dtotal_o[...] = dtotal
        outs.send(1)
        low = dtotal.astype(BF16)
        for member in range(2):
            wait_all(copies[member])
            spread_kinds(w_vmem, w_s, member)
        dctx = mm(low, w_s[:, 3 * here :]).astype(BF16)
        dctx_s[...] = dctx
        context = ins[12][...]
        store_kind(dw_s, 3, mm(low.T, context))
        products = (dctx.astype(F32) * context.astype(F32)).T
        for head in range(heads_here):
            delta_s[head : head + 1, :] = jnp.sum(
                products[head * HEAD_DIM : (head + 1) * HEAD_DIM, :], axis=0, keepdims=True
            )
        k_ref, v_ref, q_ref, lse_ref = ins[10], ins[11], ins[9], ins[13]
        ins[7]
        columns = ins[8][...].T
        for block in range(keys // BLOCK):
            seg_s[pl.ds(block * BLOCK, BLOCK), :] = columns[:, block : block + 1]

        @pl.loop(*chunk_range(range_ref, blocks))
        def _(chunk):
            keys_at = row_at(chunk * WINDOW, WINDOW)
            kt_s[:, keys_at] = k_ref[keys_at, :].T
            dkv_s[keys_at, :] = jnp.zeros((WINDOW, 2 * here), F32)

        size = WINDOW // BLOCK
        last_start = (chunk_range(range_ref, blocks)[1] - 1) * size

        @pl.loop(0, blocks)
        def _(block):
            at = lanes_at(block)
            first, last = range_ref[2 * block], range_ref[2 * block + 1]
            row = ins[7][pl.ds(block + 1, 1), :]
            segq_row = jnp.concatenate([row, row], axis=1)
            dqt_acc[...] = jnp.zeros_like(dqt_acc)

            @pl.loop(0, (last - first + size - 1) // size)
            def _(number):
                start = first + number * size
                keys_at = row_at(jnp.minimum(start, last_start) * BLOCK, WINDOW)
                allowed = jnp.logical_and(
                    seg_s[keys_at, :] == segq_row, fresh_keys(start, last_start)
                )
                for pair in range(pairs):
                    cols = pl.ds(pair * PAIR, PAIR)
                    qstacked = stack_pair(q_ref[at, cols], masks)
                    dstacked = stack_pair(dctx_s[at, cols], masks)
                    delta = jnp.concatenate(
                        [delta_s[2 * pair : 2 * pair + 1, at], delta_s[2 * pair + 1 : 2 * pair + 2, at]],
                        axis=1,
                    )
                    scores = mm(k_ref[keys_at, cols], qstacked, NT)
                    scores = jnp.where(allowed, scores, masked_score)
                    probs = jnp.exp(scores - lse_ref[pl.ds(block * pairs + pair, 1), :])
                    dprobs = mm(v_ref[keys_at, cols], dstacked, NT)
                    dscores = (probs * (dprobs - delta)).astype(BF16)
                    dkv_s[keys_at, cols] += mm(dscores, qstacked)
                    dkv_s[keys_at, pl.ds(here + pair * PAIR, PAIR)] += mm(
                        probs.astype(BF16), dstacked
                    )
                    dqt_acc[pair] += mm(kt_s[cols, keys_at], dscores)

            for pair in range(pairs):
                store_halves(dqt_s, at, pair, (dqt_acc[pair] * score_scale).astype(BF16))

        dq = dqt_s[...].T
        part_o[...] = mm(dq, w_s[:, :here], NT).astype(BF16)
        outs.send(0)
        inputs = (ins[6][...] * gain_of(norms_ref, k_in) + shift_of(norms_ref, k_in)).astype(BF16)
        store_kind(dw_s, 0, mm(inputs.T, dq))
        dm_s[...] = jnp.zeros_like(dm_s)
        dwkv_s[...] = jnp.zeros_like(dwkv_s)
        wait_all(m_copies)

        @pl.loop(*chunk_range(range_ref, blocks))
        def _(chunk):
            keys_at = row_at(chunk * WINDOW, WINDOW)
            dkv = dkv_s[keys_at, :].astype(BF16)
            dm_s[keys_at, :] = mm(dkv, w_s[:, here : 3 * here], NT).astype(BF16)
            dwkv_s[...] += mm(m_s[keys_at, :].T, dkv)

        dm_copies = [
            pltpu.make_async_copy(
                dm_s.at[row_at((me_ref[2] ^ member) * half, half), :],
                (dm_keep, dm_send)[member % 2].at[member // 2],
                dm_sems.at[member],
            )
            for member in range(4)
        ]
        start_all([dm_copies])
        store_kind(dw_s, 1, dwkv_s[:, :here])
        store_kind(dw_s, 2, dwkv_s[:, here:])
        start_all(out_copies)
        outs.finish()
        wait_all(dm_copies)
        for group in out_copies:
            wait_all(group)

    halves = shaped((2, half, width), BF16)
    part, dtotal, dnorm, *results = staged(
        body,
        "cross_backward",
        me,
        (ranges,),
        (*dy, xhat, rstd, norms, xin, segq, segk, *saved),
        (*memory, *pieces),
        (shaped((rows, width), BF16), shaped((rows, width), F32), shaped((2, width), F32)),
        direct=(*grad_pieces(width), halves, halves),
        scratch=(
            *weight_scratch(width),
            *grad_scratch(width),
            pltpu.SemaphoreType.DMA((4,)),
            pltpu.SemaphoreType.DMA((4,)),
            pltpu.VMEM((keys, width), BF16),
            pltpu.VMEM((width, 4 * here), BF16),
            pltpu.VMEM((rows, here), BF16),
            pltpu.VMEM((here, keys), BF16),
            pltpu.VMEM((pairs, PAIR, 2 * BLOCK), F32),
            pltpu.VMEM((here, rows), BF16),
            pltpu.VMEM((keys, 2 * here), F32),
            pltpu.VMEM((width, 2 * here), F32),
            pltpu.VMEM((keys, width), BF16),
            pltpu.VMEM((keys, 1), F32),
            pltpu.VMEM((8, rows), F32),
        ),
        microseconds=16,
    )
    return dtotal, part, dnorm, results[:4], results[4], results[5]


def gelu_and_slope(pre):
    square = pre * pre
    half = 0.5 * pre
    tanh = jnp.tanh(pre * (gelu_a + (gelu_a * gelu_b) * square))
    cdf = 0.5 + 0.5 * tanh
    slope = cdf + half * (1.0 - tanh * tanh) * (gelu_a + (3.0 * gelu_a * gelu_b) * square)
    return (pre * cdf).astype(BF16), slope.astype(BF16)


def feed_forward(me, base, part_own, part_sib, k_norm, weights, norms, norm_piece=None):
    pieces, offset = weights
    rows, width = part_own.shape
    own = rows // 2
    first = norm_piece is not None
    raw = (*base[0][:2], *pieces) if first else pieces
    inputs = (part_own, part_sib) if first else (part_own, part_sib, norms, base[0])

    def body(scalars, ins, raw, outs, direct, w_vmem, w_sems, *rest):
        me_ref = scalars[0]
        part_o, xhat_o, rstd_o = outs.places[:3]
        hidden, slope = outs.places[3:5], outs.places[5:7]
        if first:
            norm_s, norm_sems, x_s, x_sems, acc_s = rest
            which = base[1]
            x_copies = chip_copies(
                me_ref,
                raw[0].at[pl.ds(which * own, own)],
                raw[1].at[pl.ds(which * own, own)],
                x_s,
                0,
                x_sems,
            )
            start_all([x_copies])
            raw = raw[2:]
            norm_copies = weight_copies(me_ref, raw, norm_piece[1], norm_s, norm_sems)[0]
            start_all([norm_copies])
        else:
            (acc_s,) = rest
        ins.start(*range(len(inputs)))
        copies = weight_copies(me_ref, raw, offset, w_vmem, w_sems)
        start_all(copies)
        if first:
            wait_all(norm_copies)
            norms_ref = outs[7]
            norms_ref[...] = flat(norm_s[0]).astype(F32).T[: norms_ref.shape[0], :]
            outs.send(7)
            wait_all(x_copies)
            before = x_s[...].astype(F32)
        else:
            norms_ref = ins[2]
            before = ins[3][...] * gain_of(norms_ref, base[1]) + shift_of(norms_ref, base[1])
        xhat, rstd = normalize(before + both(ins[0], ins[1]))
        xhat_o[...] = xhat
        rstd_o[...] = rstd
        outs.send(1, 2)
        low = (xhat * gain_of(norms_ref, k_norm) + shift_of(norms_ref, k_norm)).astype(BF16)
        half = w_vmem.shape[4] // 2
        for member in range(2):
            wait_all(copies[member])
            hidden_low, slope_low = gelu_and_slope(mm(low, flat(w_vmem[member, :, :, :, :half])))
            hidden[member][...] = hidden_low
            slope[member][...] = slope_low
            outs.send(3 + member, 5 + member)
            product = mm(hidden_low, flat(w_vmem[member, :, :, :, half:]), NT)
            if member == 0:
                acc_s[...] = product
            else:
                part_o[...] = (acc_s[...] + product).astype(BF16)
        outs.send(0)
        outs.finish()

    piece = shaped((rows, width), BF16)
    results = staged(
        body,
        "feed_forward",
        me,
        (),
        inputs,
        raw,
        (
            piece,
            shaped((rows, width), F32),
            shaped((rows, 1), F32),
            *((piece,) * 4),
            *((shaped((16, width), F32),) if first else ()),
        ),
        scratch=(
            *weight_scratch(2 * width),
            *(
                (
                    pltpu.VMEM((2, *slab_shape(BLOCK)), BF16),
                    pltpu.SemaphoreType.DMA((2, 4)),
                    pltpu.VMEM((rows, width), BF16),
                    pltpu.SemaphoreType.DMA((2,)),
                )
                if first
                else ()
            ),
            pltpu.VMEM((rows, width), F32),
        ),
        microseconds=7,
    )
    return results[0], results[1], results[2], results[3:5], results[5:7], *results[7:]


def end_norm(me, xhat_before, k_before, part_own, part_sib, norms, k_norm):
    rows, width = part_own.shape
    own = rows // 2

    def body(scalars, ins, raw, outs, direct, x_s, one_s, two_s, sems):
        at = row_at(scalars[0][4] * own, own)
        copies = [
            pltpu.make_async_copy(source.at[at], place, sems.at[number])
            for number, (source, place) in enumerate(zip(raw, (x_s, one_s, two_s)))
        ]
        start_all([copies])
        ins.start(0)
        wait_all(copies)
        before = x_s[...] * gain_of(ins[0], k_before) + shift_of(ins[0], k_before)
        xhat, _ = normalize(before + both(one_s, two_s))
        outs[0][...] = (xhat * gain_of(ins[0], k_norm) + shift_of(ins[0], k_norm)).astype(BF16)
        outs.send(0)
        outs.finish()

    (out,) = staged(
        body,
        "end_norm",
        me,
        (),
        (norms,),
        (xhat_before, part_own, part_sib),
        (shaped((own, width), BF16),),
        scratch=(
            pltpu.VMEM((own, width), F32),
            pltpu.VMEM((own, width), BF16),
            pltpu.VMEM((own, width), BF16),
            pltpu.SemaphoreType.DMA((3,)),
        ),
        microseconds=2,
    )
    return out


def feed_backward(me, dy, parts, xin, k_in, k_out, norms, hidden, slope, weights, turning):
    pieces, offset = weights
    (dy_own, dy_sib), which = dy
    rows, width = xin.shape
    own = rows // 2

    def body(
        scalars, ins, raw, outs, direct, w_vmem, w_sems, dw_s, dw_sems, dy_s, dy_sems, acc_s, *rest
    ):
        me_ref = scalars[0]
        ins.start(0, 1, 2, 3)
        dy_copies = chip_copies(
            me_ref,
            raw[0].at[pl.ds(which * own, own)],
            raw[1].at[pl.ds(which * own, own)],
            dy_s,
            0,
            dy_sems,
        )
        start_all([dy_copies])
        copies = weight_copies(me_ref, raw[2:], offset, w_vmem, w_sems)
        for member in range(2):
            start_all([copies[member]])
            ins.start(6 + member, 4 + member)
        out_copies = grad_copies(me_ref, dw_s, direct[:4], dw_sems)
        part_o, dtotal_o, dnorm_o = outs.places
        norms_ref = ins[1]
        inputs = ins[0][...] * gain_of(norms_ref, k_in) + shift_of(norms_ref, k_in)
        gain = gain_of(norms_ref, k_out)
        xhat, rstd = normalize(inputs + both(ins[2], ins[3]))
        if turning:
            out_s, out_sems = rest
            out_s[...] = (xhat * gain + shift_of(norms_ref, k_out)).astype(BF16)
            out_copy = pltpu.make_async_copy(
                out_s.at[row_at(me_ref[4] * own, own)], direct[4], out_sems.at[0]
            )
            out_copy.start()
        wait_all(dy_copies)
        dy = dy_s[...].astype(F32)
        store_norm_grads(outs, 2, dy, xhat)
        dtotal = norm_backward(dy, xhat, rstd, gain)
        dtotal_o[...] = dtotal
        outs.send(1)
        low = dtotal.astype(BF16)
        lowt = low.T
        xt = inputs.astype(BF16).T
        half = w_vmem.shape[4] // 2
        for member in range(2):
            wait_all(copies[member])
            dhidden = mm(low, flat(w_vmem[member, :, :, :, half:]))
            dpre = (dhidden * ins[6 + member][...].astype(F32)).astype(BF16)
            dw_s[member, :, :, :, :half] = mm(xt, dpre).astype(BF16).reshape(slab_shape(half))
            dw_s[member, :, :, :, half:] = (
                mm(lowt, ins[4 + member][...]).astype(BF16).reshape(slab_shape(half))
            )
            start_all([out_copies[member]])
            product = mm(dpre, flat(w_vmem[member, :, :, :, :half]), NT)
            if member == 0:
                acc_s[...] = product
            else:
                part_o[...] = (acc_s[...] + product).astype(BF16)
        outs.send(0)
        outs.finish()
        for group in out_copies:
            wait_all(group)
        if turning:
            out_copy.wait()

    part, dtotal, dnorm, *results = staged(
        body,
        "feed_backward",
        me,
        (),
        (xin, norms, *parts, *hidden, *slope),
        (dy_own, dy_sib, *pieces),
        (shaped((rows, width), BF16), shaped((rows, width), F32), shaped((2, width), F32)),
        direct=(
            *grad_pieces(2 * width),
            *((shaped((own, width), BF16),) if turning else ()),
        ),
        scratch=(
            *weight_scratch(2 * width),
            *grad_scratch(2 * width),
            pltpu.VMEM((rows, width), BF16),
            pltpu.SemaphoreType.DMA((2,)),
            pltpu.VMEM((rows, width), F32),
            *(
                (pltpu.VMEM((rows, width), BF16), pltpu.SemaphoreType.DMA((1,)))
                if turning
                else ()
            ),
        ),
        microseconds=9,
    )
    return dtotal, part, dnorm, results[:4], *results[4:]


DP = ("z", "x")
MP = ("y", "c")
ALL = ("z", "x", "y", "c")


def is_cube():
    return tuple(lax.axis_size(axis) for axis in ALL) == (4, 2, 2, 2)


def swap(values, axis, distance=1):
    count = lax.axis_size(axis)
    return lax.ppermute(values, axis, [(i, i ^ distance) for i in range(count)])


def add(*terms):
    return sum(term.astype(F32) for term in terms)


def low_add(*terms):
    return add(*terms).astype(BF16)


def place_of(me_ref, at):
    return me_ref[0] ^ at[1] if isinstance(at, tuple) else at


def sum_kernel(sources, jobs, me_ref, *refs):
    inputs, outputs = refs[: len(sources)], refs[len(sources) : len(sources) + len(jobs)]
    places, sems = refs[len(sources) + len(jobs) : -1], refs[-1]
    copies = [
        pltpu.make_async_copy(ref.at[pl.ds(start, count)], place, sems.at[number])
        for number, (ref, place, (start, count)) in enumerate(zip(inputs, places, sources))
    ]
    start_all([copies])
    waited = set()
    for out, (_, slabs, turned, cut) in zip(outputs, jobs):
        for at, terms in enumerate(slabs):
            total = None
            for number, source_at in terms:
                if number not in waited:
                    waited.add(number)
                    copies[number].wait()
                value = places[number][place_of(me_ref, source_at), :, cut]
                if len(terms) > 1:
                    value = value.astype(F32)
                total = value if total is None else total + value
            out[place_of(me_ref, ("z", at)) if turned else at] = total.astype(out.dtype)


def sum_slabs(me, requests):
    arrays, sources, jobs = [], [], []
    for request_sources, request_jobs in requests:
        base = len(arrays)
        for array, start, count in request_sources:
            arrays.append(array)
            sources.append((start, count))
        for dtype, slabs, turned, cut in request_jobs:
            _, rows, width = request_sources[0][0].shape
            start, width = cut or (0, width)
            moved = tuple(tuple((base + number, at) for number, at in terms) for terms in slabs)
            out = shaped((len(slabs), rows, width), dtype)
            jobs.append((out, moved, turned, slice(start, start + width)))
    results = pl.pallas_call(
        functools.partial(sum_kernel, tuple(sources), tuple(jobs)),
        out_shape=tuple(job[0] for job in jobs),
        in_specs=smem(1) + hbm(len(arrays)),
        out_specs=tuple(vmem(len(jobs))),
        scratch_shapes=[
            *(
                pltpu.VMEM((count, *array.shape[1:]), array.dtype)
                for array, (_, count) in zip(arrays, sources)
            ),
            pltpu.SemaphoreType.DMA((len(arrays),)),
        ],
        compiler_params=params(),
        cost_estimate=cost(2),
        name="sum_slabs",
    )(me, *arrays)
    split, at = [], 0
    for _, request_jobs in requests:
        split.append(results[at : at + len(request_jobs)])
        at += len(request_jobs)
    return split


def gather_lines(shard, widths):
    starts = [sum(widths[:number]) for number in range(len(widths))]
    if not is_cube():
        yield ()
        return tuple(shard[:, at : at + width] for at, width in zip(starts, widths))
    over_z = yield tuple((shard, "z", k) for k in (1, 2, 3))
    return (
        yield (
            tuple((piece[None], 0, 1) for piece in (shard, *over_z)),
            tuple(
                (BF16, tuple(((k, 0),) for k in range(4)), True, cut) for cut in zip(starts, widths)
            ),
        )
    )


def gather_square(lines):
    if not is_cube():
        whole = lax.all_gather(lines, ("y", *DP), axis=0, tiled=True)
        whole = whole.reshape(2, 4, 2, SLAB, lines.shape[1])
        for _ in range(2):
            yield ()
        return (whole[0, :, 0], whole[0, :, 1], whole[1, :, 0], whole[1, :2, 1], whole[1, 2:, 1])
    over_x, over_y = yield ((lines, "x", 1), (lines, "y", 1))
    far_one, far_two = yield ((over_y[:2], "x", 1), (over_x[2:], "y", 1))
    return lines, over_x, over_y, far_one, far_two


def reduce_square(own, to_x, to_y, to_far):
    if not is_cube():
        yield ()
        return own, to_x, to_y, to_far
    arrived = yield ((to_x, "x", 1), (to_y, "y", 1), (to_far, ("x", "y"), 3))
    return (own, *arrived)


def reduce_lines(*groups):
    if not is_cube():
        sums = []
        for group in groups:
            whole = jnp.stack(group).reshape(2, 2, 4, SLAB, group[0].shape[2])
            whole = whole.transpose(0, 2, 1, 3, 4).reshape(2, 8 * SLAB, group[0].shape[2])
            part = lax.psum_scatter(whole, "y", scatter_dimension=0, tiled=True)
            sums.append(lax.psum_scatter(part[0], DP, scatter_dimension=0, tiled=True))
        yield ()
        sums = jnp.stack(sums).astype(F32)
        empty = jnp.zeros(sums.shape, BF16)
        return sums, (empty, empty, empty)
    lines = yield (
        tuple((array, 0, 4) for group in groups for array in group),
        tuple(
            (
                F32 if k == 0 else BF16,
                tuple(
                    tuple((4 * number + source, ("z", k)) for source in range(4))
                    for number in range(len(groups))
                ),
                False,
                None,
            )
            for k in range(4)
        ),
    )
    over_z = yield tuple((lines[k], "z", k) for k in (1, 2, 3))
    return lines[0], over_z


def finish_group(ended, number=0):
    own, over_z = ended
    return add(own[number], *(piece[number] for piece in over_z))


def one_stage(*jobs):
    return (yield jobs)


def memory_stages(values):
    over_y, over_c = yield ((values, "y", 1), (values, "c", 1))
    (over_both,) = yield ((over_y, "c", 1),)
    return values, over_c, over_y, over_both


def memory_grad_stages(keep, send):
    (got,) = yield ((send, "c", 1),)
    (over_y,) = yield ((low_add(keep[1], got[1]), "y", 1),)
    own = low_add(keep[0], got[0], over_y)
    (sib,) = yield ((own, "c", 1),)
    return own, sib


class Flow:
    def __init__(self, me, token):
        self.me = me
        self.moving = {}
        self.ended = {}
        self.token = token

    def sync(self, names, *values, begin=(), hold=()):
        arrived = [self.moving[name][1] for name in names]
        held = [self.moving[name][1] for name in hold]
        arrived, held, values, token = lax.optimization_barrier(
            (arrived, held, values, self.token)
        )
        for name, result in zip(hold, held):
            self.moving[name] = (self.moving[name][0], result)
        to_send, asked = {}, {}
        begun = [(name, stages, None) for name, stages in begin]
        moved = [(name, self.moving[name][0], result) for name, result in zip(names, arrived)]

        def move(name, stages, result):
            try:
                wanted = stages.send(result)
            except StopIteration as end:
                self.ended[name] = end.value
                self.moving.pop(name, None)
                return
            if wanted and isinstance(wanted[0][0], tuple):
                asked[name] = (stages, wanted)
            else:
                to_send[name] = (stages, wanted)

        for job in moved + begun:
            move(*job)
        if asked:
            names = list(asked)
            sums = sum_slabs(self.me, [asked[name][1] for name in names])
            for name, result in zip(names, sums):
                move(name, asked[name][0], result)
        operands = [[job[0] for job in jobs] for _, jobs in to_send.values()]
        operands, values, self.token = lax.optimization_barrier((operands, values, token))
        for sending, (name, (stages, jobs)) in zip(operands, to_send.items()):
            results = [
                swap(operand, axis, distance)
                for operand, (_, axis, distance) in zip(sending, jobs)
            ]
            self.moving[name] = (stages, results)
        return values


def sum_stages(values):
    if not is_cube():
        return (lax.psum(values, ALL), *((jnp.zeros_like(values),) * 3))
    values = values + swap(values, "c")
    one, two, three = swap(values, "y"), swap(values, "x"), swap(values, ("x", "y"), 3)
    values = (values + one) + (two + three)
    return (values, *(swap(values, "z", k) for k in (1, 2, 3)))


def pack(groups, widths, attention_in, attention_out, feed_in, feed_out, norm_columns):
    rows = attention_in.shape[1]
    inputs = (attention_in, attention_out, feed_in, feed_out, norm_columns)

    def kernel(*refs):
        sources, shards, places, sems = refs[:5], refs[5 : 5 + len(groups)], refs[-6:-1], refs[-1]
        ins = Inputs(sources, places, sems)
        ins.start(4, 0, 1, 2, 3)
        order = {"enc": 0, "self": 1, "cross": 2, "enc_feed": 0, "dec_feed": 1}
        for shard, names in zip(shards, groups):
            offset = 0
            for name in names:
                number = order.get(name)
                if name == "norms":
                    pieces = [ins[4][...]]
                elif name.endswith("feed"):
                    pieces = [ins[2][number], ins[3][number]]
                else:
                    pieces = [ins[0][3 * number + kind] for kind in range(3)] + [ins[1][number]]
                for piece in pieces:
                    shard[:, pl.ds(offset, piece.shape[1])] = piece.astype(BF16)
                    offset += piece.shape[1]

    return pl.pallas_call(
        kernel,
        out_shape=tuple(
            shaped((rows, sum(widths[name] for name in group)), BF16) for group in groups
        ),
        in_specs=hbm(5),
        out_specs=tuple(vmem(len(groups))),
        scratch_shapes=[
            *(pltpu.VMEM(array.shape, F32) for array in inputs),
            pltpu.SemaphoreType.DMA((5,)),
        ],
        compiler_params=params(60),
        cost_estimate=cost(2),
        name="pack",
    )(*inputs)


def close_kernel(*refs):
    own, far, others, norms = refs[0], refs[1:4], refs[4:8], refs[8:13]
    grad, payload = refs[13:]
    total = own[0] + sum(ref[0].astype(F32) for ref in far)
    grad[...] = total
    squares = jnp.sum(total * total)
    for other in others:
        squares = squares + jnp.sum(other[...] * other[...])
    for number, norm in enumerate(norms):
        payload[2 * number : 2 * number + 2, :] = 0.5 * norm[...]
    payload[10:, :] = jnp.full((payload.shape[0] - 10, payload.shape[1]), squares, F32)


def close(own, far, others, norms):
    return pl.pallas_call(
        close_kernel,
        out_shape=(shaped(own.shape[1:], F32), shaped((16, norms[0].shape[1]), F32)),
        in_specs=vmem(13),
        out_specs=tuple(vmem(2)),
        compiler_params=params(),
        cost_estimate=cost(2),
        name="close",
    )(own, *far, *others, *norms)


def adam_step(weights, first, second, grads, rate, decay):
    first_new = beta_one * first + (1.0 - beta_one) * grads
    second_new = beta_two * second + (1.0 - beta_two) * grads * grads
    first_hat = first_new / (1.0 - beta_one**STEP)
    second_hat = second_new / (1.0 - beta_two**STEP)
    weights_new = weights - rate * (first_hat / (jnp.sqrt(second_hat) + adam_eps) + decay * weights)
    return (weights_new, first_new, second_new)


def update_kernel(count, me_ref, *refs):
    sums, grads, refs = refs[:4], refs[4:9], refs[9:]
    masters, firsts, seconds = refs[:count], refs[count : 2 * count], refs[2 * count : 3 * count]
    refs = refs[3 * count :]
    news, new_firsts, new_seconds = refs[:count], refs[count : 2 * count], refs[2 * count : 3 * count]
    total_ref, norm_ref = refs[3 * count :]
    total = (sums[0][...] + sums[1][...]) + (sums[2][...] + sums[3][...])
    total_ref[...] = total
    norm_grads = total[:10]
    squares = total[10:11, :BLOCK] + jnp.sum(norm_grads * norm_grads)
    grad_norm = jnp.sqrt(squares)
    norm_ref[...] = grad_norm
    factor = clip_bound / jnp.maximum(grad_norm[:, :1], clip_bound)
    part = masters[0].shape[2]
    half = masters[2].shape[2]
    attention, feed = grads[:3], grads[3:]

    def step(number, at, grad, rate=rate_matrix, decay=weight_decay):
        results = adam_step(
            masters[number][at], firsts[number][at], seconds[number][at], grad * factor, rate, decay
        )
        for target, value in zip((news, new_firsts, new_seconds), results):
            target[number][at] = value

    for number in range(3):
        for kind in range(3):
            step(0, 3 * number + kind, attention[number][:, kind * part : (kind + 1) * part])
        step(1, number, attention[number][:, 3 * part :])
    for number in range(2):
        step(2, number, feed[number][:, :half])
        step(3, number, feed[number][:, half:])
    if count == 5:
        own = total_ref[:, pl.ds(pl.multiple_of(me_ref[0] * BLOCK, BLOCK), BLOCK)]
        columns = masters[4].shape[2]
        own = jnp.where(me_ref[1] == 0, own[:, :columns], own[:, columns:])
        for number in range(5):
            step(4, number, own[2 * number : 2 * number + 2], rate_norm, 0.0)


def update(me, sums, grads, masters, firsts, seconds):
    count = len(masters)
    states = (*masters, *firsts, *seconds)
    *results, total, grad_norm = pl.pallas_call(
        functools.partial(update_kernel, count),
        out_shape=(
            *(shaped(array.shape, F32) for array in states),
            shaped(sums[0].shape, F32),
            shaped((1, BLOCK), F32),
        ),
        in_specs=smem(1) + vmem(9 + len(states)),
        out_specs=tuple(vmem(len(states) + 2)),
        compiler_params=params(24),
        cost_estimate=cost(4),
        name="update",
    )(me, *sums, *grads, *states)
    split = [results[k * count : (k + 1) * count] for k in range(3)]
    return split, total, grad_norm[0, 0]


EARLY = ("enc", "enc_feed", "norms")
MIDDLE = ("self", "cross")
LATE = ("dec_feed",)


def on_device(
    encoder_input, decoder_copy, decoder_target, decoder_cotangent,
    source_segments, target_segments, glance_mask,
    attention_in, attention_out, feed_in, feed_out, norm_params,
    attention_in_first, attention_out_first, feed_in_first, feed_out_first, norm_params_first,
    attention_in_second, attention_out_second, feed_in_second, feed_out_second, norm_params_second,
):
    rows, width = encoder_input.shape
    length = source_segments.shape[1]
    part, half = attention_in.shape[2], feed_in.shape[2]
    chip_y, core = lax.axis_index("y"), lax.axis_index("c")
    here = (lax.axis_index("z"), lax.axis_index("x")) if is_cube() else (0, 0)
    me = jnp.stack([jnp.int32(value) for value in (*here, 2 * chip_y + core, chip_y, core)])
    flow = Flow(me, jnp.zeros((8, BLOCK), F32) + norm_params[0, 0, 0])

    def turned(array):
        return array.transpose(0, 2, 1)

    masters = (attention_in, turned(attention_out), feed_in, turned(feed_out), norm_params)
    firsts = (
        attention_in_first, turned(attention_out_first), feed_in_first, turned(feed_out_first),
        norm_params_first,
    )
    seconds = (
        attention_in_second, turned(attention_out_second), feed_in_second,
        turned(feed_out_second), norm_params_second,
    )
    norm_columns = jnp.pad(norm_params.reshape(10, -1).T, ((0, 0), (0, BLOCK - 10)))
    widths = {
        "enc": 4 * part, "self": 4 * part, "cross": 4 * part, "norms": BLOCK,
        "enc_feed": 2 * half, "dec_feed": 2 * half,
    }
    shard_early, shard_rest = pack((EARLY, MIDDLE + LATE), widths, *masters[:4], norm_columns)
    weight_places = {}
    for group in (EARLY, MIDDLE, LATE):
        offset = 0
        for name in group:
            weight_places[name] = (group, offset)
            offset += widths[name]

    def weights(name):
        group, offset = weight_places[name]
        return (flow.ended[group], offset)

    picked = glance_mask[0] == 1
    decoder_input = jnp.where(picked[:, None], decoder_target, decoder_copy)
    own_rows = jnp.concatenate([encoder_input, decoder_input, decoder_cotangent])

    chip_rows = 2 * rows
    blocks = chip_rows // BLOCK
    source_row = source_segments[0].astype(F32)
    target_row = target_segments[0].astype(F32)

    def chip_segments(row):
        padded = jnp.pad(row, (BLOCK, BLOCK), constant_values=-1.0)
        own = lax.dynamic_slice(padded, (chip_y * chip_rows,), (chip_rows + 2 * BLOCK,))
        return own.reshape(blocks + 2, BLOCK)

    source_chip, target_chip = chip_segments(source_row), chip_segments(target_row)
    source_all = jnp.pad(source_row.reshape(length // BLOCK, BLOCK), ((0, 16 - length // BLOCK), (0, 0)))
    lowest, highest = target_chip[1:-1, 0], target_chip[1:-1, BLOCK - 1]
    first_key = jnp.sum((source_row[None, :] < lowest[:, None]).astype(jnp.int32), axis=1)
    last_key = jnp.sum((source_row[None, :] <= highest[:, None]).astype(jnp.int32), axis=1)
    ranges = jnp.stack([first_key // BLOCK, (last_key + BLOCK - 1) // BLOCK], axis=1)
    ranges = ranges.astype(jnp.int32).reshape(2 * blocks)

    group_widths = [sum(widths[name] for name in group) for group in (EARLY, MIDDLE, LATE)]
    (shard_rest,) = flow.sync(
        [], shard_rest, begin=[("early_z", gather_lines(shard_early, group_widths[:1]))]
    )
    own_rows, shard_rest = flow.sync(["early_z"], own_rows, shard_rest)
    own_rows, shard_rest = flow.sync(
        [], own_rows, shard_rest, begin=[(EARLY, gather_square(*flow.ended["early_z"]))]
    )
    (own_rows,) = flow.sync(
        [],
        own_rows,
        begin=[
            ("rest_z", gather_lines(shard_rest, group_widths[1:])),
            ("rows", one_stage((own_rows, "c", 1))),
        ],
    )
    (own_rows,) = flow.sync(["rows"], own_rows)
    (sib_rows,) = flow.ended["rows"]

    def edge(which):
        last = jnp.where(core == 1, own_rows[(which + 1) * rows - BLOCK : (which + 1) * rows],
                         sib_rows[(which + 1) * rows - BLOCK : (which + 1) * rows])
        first = jnp.where(core == 0, own_rows[which * rows : which * rows + BLOCK],
                          sib_rows[which * rows : which * rows + BLOCK])
        return jnp.where(chip_y == 0, last, first)

    edges = jnp.concatenate([edge(0), edge(1)])
    edges, source_chip, target_chip, ranges, source_all = flow.sync(
        [], edges, source_chip, target_chip, ranges, source_all
    )
    (edges,) = flow.sync([EARLY], edges, hold=["rest_z"])
    flow.sync([], begin=[("halo", one_stage((edges, "y", 1)))])
    flow.sync(["rest_z"])
    lines_middle, lines_late = flow.ended["rest_z"]
    flow.sync([EARLY, "halo"])
    chip = (own_rows, sib_rows, flow.ended["halo"][0])
    chip, source_chip, lines_late = flow.sync(
        [], chip, source_chip, lines_late, begin=[(MIDDLE, gather_square(lines_middle))]
    )

    enc, dec, cot = 0, 1, 2
    part0, enc_saved = self_forward(me, chip, enc, source_chip, weights("enc"))
    (part0,) = flow.sync([], part0, hold=[MIDDLE])
    (part0,) = flow.sync([], part0, begin=[("part0", one_stage((part0, "c", 1)))])
    (part0,) = flow.sync(["part0", MIDDLE], part0)
    part1, xhat0, rstd0, enc_hidden, enc_slope, norms = feed_forward(
        me, (chip, enc), part0, *flow.ended["part0"], 0, weights("enc_feed"), None, weights("norms")
    )
    (part1,) = flow.sync([], part1, hold=[MIDDLE])
    (part1,) = flow.sync([], part1, begin=[("part1", one_stage((part1, "c", 1)))])
    (part1,) = flow.sync(["part1", MIDDLE], part1)
    parts1 = (part1, *flow.ended["part1"])
    encoder_output = end_norm(me, xhat0, 0, *parts1, norms, 1)
    (target_chip,) = flow.sync(
        [], target_chip, begin=[("memory", memory_stages(encoder_output))]
    )
    part2, self_saved = self_forward(me, chip, dec, target_chip, weights("self"))
    (part2,) = flow.sync(["memory"], part2, begin=[("part2", one_stage((part2, "c", 1)))])
    (part2,) = flow.sync(
        ["memory", "part2"], part2, begin=[(LATE, gather_square(lines_late))]
    )
    memory = flow.ended["memory"]
    part3, xhat2, rstd2, cross_saved = cross_forward(
        me, ranges, chip, dec, part2, *flow.ended["part2"], norms, 2, target_chip, source_all,
        memory, weights("cross"),
    )
    (part3,) = flow.sync([], part3, hold=[LATE])
    (part3,) = flow.sync([LATE], part3, begin=[("part3", one_stage((part3, "c", 1)))])
    (part3,) = flow.sync(["part3", LATE], part3)
    part4, xhat3, rstd3, dec_hidden, dec_slope = feed_forward(
        me, (xhat2, 2), part3, *flow.ended["part3"], 3, weights("dec_feed"), norms
    )
    (part4,) = flow.sync([], part4, begin=[("part4", one_stage((part4, "c", 1)))])
    (part4,) = flow.sync(["part4"], part4)

    dtotal4, dpart4, dnorm4, pieces, decoder_output = feed_backward(
        me, (chip[:2], cot), (part4, *flow.ended["part4"]), xhat3, 3, 4, norms,
        dec_hidden, dec_slope, weights("dec_feed"), True,
    )
    (dtotal4,) = flow.sync([], dtotal4, begin=[("dpart4", one_stage((dpart4, "c", 1)))])
    (dtotal4,) = flow.sync(["dpart4"], dtotal4, begin=[("dec_feed", reduce_square(*pieces))])
    dtotal3, dpart3, dnorm3, pieces, dm_keep, dm_send = cross_backward(
        me, ranges, (dtotal4, dpart4, *flow.ended["dpart4"]), xhat3, rstd3, norms, 3, xhat2, 2,
        target_chip, source_all, cross_saved, memory, weights("cross"),
    )
    dpart3, dtotal3, dm_keep, dm_send = flow.sync(
        [], dpart3, dtotal3, dm_keep, dm_send, hold=["dec_feed"]
    )
    dpart3, dtotal3 = flow.sync(
        [],
        dpart3,
        dtotal3,
        begin=[
            ("memory_grad", memory_grad_stages(dm_keep, dm_send)),
            ("dpart3", one_stage((dpart3, "c", 1))),
        ],
    )
    dpart3, dtotal3 = flow.sync(
        ["memory_grad", "dpart3", "dec_feed"],
        dpart3,
        dtotal3,
        begin=[("cross", reduce_square(*pieces))],
    )
    dnorm2, pieces, dtotal2, dec_keep, dec_send = self_backward(
        me, (dtotal3, dpart3, *flow.ended["dpart3"]), xhat2, rstd2, norms, 2, chip, dec,
        self_saved, weights("self"),
    )
    (dtotal2,) = flow.sync(["memory_grad"], dtotal2, hold=["cross"])
    (dtotal2,) = flow.sync(
        ["memory_grad", "cross"],
        dtotal2,
        begin=[
            ("dec_feed", reduce_lines(flow.ended["dec_feed"])),
            ("self", reduce_square(*pieces)),
        ],
    )
    dmemory = flow.ended["memory_grad"]
    dmemory, dtotal2 = lax.optimization_barrier((dmemory, dtotal2))
    dtotal1, dpart1, dnorm1, pieces = feed_backward(
        me, (dmemory, 0), parts1, xhat0, 0, 1, norms, enc_hidden, enc_slope,
        weights("enc_feed"), False,
    )
    dpart1, dtotal1 = flow.sync([], dpart1, dtotal1, hold=["self", "dec_feed"])
    (dtotal1,) = flow.sync([], dtotal1, begin=[("dpart1", one_stage((dpart1, "c", 1)))])
    (dtotal1,) = flow.sync(
        ["dpart1", "dec_feed", "self"], dtotal1, begin=[("enc_feed", reduce_square(*pieces))]
    )
    (dtotal1,) = flow.sync(
        [],
        dtotal1,
        begin=[("pair", reduce_lines(flow.ended["self"], flow.ended["cross"]))],
    )
    dnorm0, pieces, dtotal0, enc_keep, enc_send = self_backward(
        me, (dtotal1, dpart1, *flow.ended["dpart1"]), xhat0, rstd0, norms, 0, chip, enc,
        enc_saved, weights("enc"),
    )
    both_send = jnp.concatenate([enc_send, dec_send])
    (both_send,) = flow.sync(
        [], both_send, hold=["enc_feed"], begin=[("enc", reduce_square(*pieces))]
    )
    (both_send,) = flow.sync(["enc_feed"], both_send)
    (both_send,) = flow.sync(
        [], both_send, begin=[("enc_feed", reduce_lines(flow.ended["enc_feed"]))]
    )
    (both_send,) = flow.sync(["pair"], both_send, hold=["enc", "enc_feed"])
    (both_send,) = flow.sync(["enc"], both_send)
    (both_send,) = flow.sync(
        [], both_send, begin=[("enc", reduce_lines(flow.ended["enc"]))]
    )
    flow.sync([], begin=[("rows_grad", one_stage((both_send, "c", 1)))])
    flow.sync(["rows_grad"])
    (got,) = flow.ended["rows_grad"]
    swapped = rows + BLOCK
    enc_rows = add(enc_keep, got[:swapped])
    dec_rows = add(dec_keep, got[swapped:])
    halos = jnp.concatenate([enc_rows[rows:], dec_rows[rows:]]).astype(BF16)
    flow.sync([], begin=[("halo_grad", one_stage((halos, "y", 1)))])
    flow.sync(["enc_feed"])
    others = [
        finish_group(flow.ended["pair"], 0),
        finish_group(flow.ended["pair"], 1),
        finish_group(flow.ended["enc_feed"]),
        finish_group(flow.ended["dec_feed"]),
    ]
    others = flow.sync(["halo_grad"], *others)
    flow.sync(["enc"])
    (halos,) = flow.ended["halo_grad"]
    at_start = jnp.logical_and(chip_y == 1, core == 0)
    at_end = jnp.logical_and(chip_y == 0, core == 1)

    def input_grad(dtotal, summed, halo):
        halo = halo.astype(F32)
        first = jnp.where(at_start, halo, 0.0)
        last = jnp.where(at_end, halo, 0.0)
        spread = jnp.concatenate([first, jnp.zeros((rows - 2 * BLOCK, width), F32), last])
        return dtotal + summed[:rows] + spread

    encoder_input_grad = input_grad(dtotal0, enc_rows, halos[:BLOCK])
    decoder_input_grad = input_grad(dtotal2, dec_rows, halos[BLOCK:])

    own_enc, far_enc = flow.ended["enc"]
    g_enc, payload = close(own_enc, far_enc, others, (dnorm0, dnorm1, dnorm2, dnorm3, dnorm4))
    sums = sum_stages(payload)
    grads = (g_enc, others[0], others[1], others[2], others[3])
    if norm_params.shape[2] == BLOCK // 2 and is_cube():
        split, total, grad_norm = update(me, sums, grads, masters, firsts, seconds)
        results = list(zip(*split))
    else:
        split, total, grad_norm = update(me, sums, grads, masters[:4], firsts[:4], seconds[:4])
        results = list(zip(*split))
        columns = norm_params.shape[2]
        g_norms = lax.dynamic_slice(total, (0, lax.axis_index(DP) * columns), (10, columns))
        factor = clip_bound / jnp.maximum(grad_norm, clip_bound)
        g_norms = g_norms.reshape(norm_params.shape) * factor
        results.append(
            adam_step(norm_params, norm_params_first, norm_params_second, g_norms, rate_norm, 0.0)
        )
    results = [
        tuple(turned(value) for value in result) if number in (1, 3) else result
        for number, result in enumerate(results)
    ]
    return (
        encoder_output,
        decoder_output,
        encoder_input_grad,
        decoder_input_grad,
        grad_norm,
        *(result[0] for result in results),
        *(result[1] for result in results),
        *(result[2] for result in results),
    )


def solution(mesh):
    dp, mp = mesh.shape["dp"], mesh.shape["mp"]
    fine = Mesh(mesh.devices.reshape(dp // 2, 2, mp // 2, 2), ALL)
    tokens = P(ALL, None)
    columns = P(None, DP, MP)
    turned = P(None, MP, DP)
    states = (columns, turned, columns, turned, P(None, None, DP))
    return jax.shard_map(
        on_device,
        mesh=fine,
        in_specs=(
            *((tokens,) * 4),
            P(DP, None),
            P(DP, None),
            P(DP, MP),
            *states,
            *states,
            *states,
        ),
        out_specs=(*((tokens,) * 4), P(), *states, *states, *states),
        check_vma=False,
    )
```

```python
import functools

import jax
import jax.numpy as jnp
from jax import lax
from jax.experimental import pallas as pl
from jax.experimental.pallas import tpu as pltpu
from jax.sharding import Mesh
from jax.sharding import PartitionSpec as P

HEAD_DIM = 64
STEP = 10
BLOCK = 128
PAIR = 2 * HEAD_DIM

norm_eps = 1e-05
beta_one = 0.9
beta_two = 0.98
adam_eps = 1e-08
weight_decay = 0.01
rate_matrix = 0.1
rate_norm = 0.5
clip_bound = 1.0
masked_score = -1e30
score_scale = HEAD_DIM ** (-0.5)
gelu_a = 0.7978845608028654
gelu_b = 0.044715

F32 = jnp.float32
BF16 = jnp.bfloat16
ANY = pl.ANY
SMEM = pltpu.SMEM
VMEM = pltpu.VMEM

NN = (((1,), (0,)), ((), ()))
NT = (((1,), (1,)), ((), ()))


def mm(a, b, dims=NN):
    return lax.dot_general(a, b, dims, preferred_element_type=F32)


def vmem(count):
    return [pl.BlockSpec(memory_space=VMEM)] * count


def smem(count):
    return [pl.BlockSpec(memory_space=SMEM)] * count


def hbm(count):
    return [pl.BlockSpec(memory_space=ANY)] * count


def cost(microseconds):
    return pl.CostEstimate(
        flops=int(microseconds * 2.3e7), bytes_accessed=int(microseconds * 7.2e4), transcendentals=0
    )


def params(mib=12):
    return pltpu.CompilerParams(vmem_limit_bytes=mib * 1024 * 1024)


LIMITS = {
    "self_forward": 14,
    "self_backward": 22,
    "cross_forward": 22,
    "cross_backward": 30,
    "feed_forward": 16,
    "feed_backward": 24,
    "end_norm": 10,
}


def shaped(shape, dtype):
    return jax.ShapeDtypeStruct(shape, dtype)


def normalize(total):
    centred = total - jnp.mean(total, axis=-1, keepdims=True)
    spread = jnp.mean(centred * centred, axis=-1, keepdims=True)
    rstd = lax.rsqrt(spread + norm_eps)
    return centred * rstd, rstd


def norm_backward(grad_out, xhat, rstd, gain):
    scaled = grad_out * gain
    first = jnp.mean(scaled, axis=-1, keepdims=True)
    second = jnp.mean(scaled * xhat, axis=-1, keepdims=True)
    return rstd * (scaled - first - xhat * second)


def norm_param_grads(grad_out, xhat):
    return (
        jnp.sum(grad_out * xhat, axis=0, keepdims=True),
        jnp.sum(grad_out, axis=0, keepdims=True),
    )


def half_masks():
    lane = lax.broadcasted_iota(jnp.int32, (1, PAIR), 1)
    low = jnp.where(lane < HEAD_DIM, 1.0, 0.0).astype(BF16)
    high = jnp.where(lane < HEAD_DIM, 0.0, 1.0).astype(BF16)
    return low, high


def stack_pair(values, masks):
    return jnp.concatenate([values * masks[0], values * masks[1]], axis=0)


SLAB = 64
PIECES = (4, 4, 4, 2, 2)
ROWS_OF = {"encoder": 0, "decoder": 1, "cotangent": 2}


def slab_shape(width):
    return (4, 2, SLAB, width)


def flat(values):
    return values.reshape(values.shape[0] * values.shape[1] * values.shape[2], values.shape[3])


def weight_copies(me_ref, pieces, offset, w_vmem, sems):
    columns = pl.ds(offset, w_vmem.shape[4])
    copies = []
    for member in range(2):
        group = []
        for x in range(2):
            number = 2 * member + x
            parts = [(pieces[number], 0, 4)] if number < 3 else [(pieces[3], 0, 2), (pieces[4], 2, 2)]
            for part, start, count in parts:
                group.append(
                    pltpu.make_async_copy(
                        part.at[:, :, columns],
                        w_vmem.at[member, pl.ds(start, count), me_ref[1] ^ x],
                        sems.at[member, 2 * x + start // 2],
                    )
                )
        copies.append(group)
    return copies


def grad_copies(me_ref, dw_vmem, targets, sems):
    return [
        [
            pltpu.make_async_copy(
                dw_vmem.at[member, :, me_ref[1] ^ x], targets[2 * member + x], sems.at[member, x]
            )
            for x in range(2)
        ]
        for member in range(2)
    ]


def start_all(groups):
    for group in groups:
        for copy in group:
            copy.start()


def wait_all(group):
    for copy in group:
        copy.wait()


def row_at(start, count):
    return pl.ds(pl.multiple_of(start, BLOCK), count)


def chip_copies(me_ref, own, sib, place, first, sems):
    rows = own.shape[0]
    return [
        pltpu.make_async_copy(own, place.at[row_at(first + me_ref[4] * rows, rows)], sems.at[0]),
        pltpu.make_async_copy(
            sib, place.at[row_at(first + (1 - me_ref[4]) * rows, rows)], sems.at[1]
        ),
    ]


def halo_place(me_ref, place, side):
    far = place.shape[0] - BLOCK
    return row_at((side ^ me_ref[3]) * far, BLOCK)


def haloed_copies(me_ref, refs, which, place, sems):
    own, sib, halo = refs
    rows = (place.shape[0] - 2 * BLOCK) // 2
    copies = chip_copies(
        me_ref,
        own.at[pl.ds(which * rows, rows)],
        sib.at[pl.ds(which * rows, rows)],
        place,
        BLOCK,
        sems,
    )
    place[halo_place(me_ref, place, 0), :] = jnp.zeros((BLOCK, place.shape[1]), BF16)
    copies.append(
        pltpu.make_async_copy(
            halo.at[pl.ds(which * BLOCK, BLOCK)],
            place.at[halo_place(me_ref, place, 1)],
            sems.at[2],
        )
    )
    return copies


class Inputs:
    def __init__(self, sources, places, sems):
        self.places = places
        self.copies = [
            pltpu.make_async_copy(source, place, sems.at[number])
            for number, (source, place) in enumerate(zip(sources, places))
        ]
        self.waited = set()

    def start(self, *numbers):
        for number in numbers:
            self.copies[number].start()

    def __getitem__(self, number):
        if number not in self.waited:
            self.waited.add(number)
            self.copies[number].wait()
        return self.places[number]


class Late:
    def __init__(self, ins, base):
        self.ins, self.base = ins, base

    def __getitem__(self, number):
        return self.ins[self.base + number]


class Outputs:
    def __init__(self, places, targets, sems):
        self.places = places
        self.copies = [
            pltpu.make_async_copy(place, target, sems.at[number])
            for number, (place, target) in enumerate(zip(places, targets))
        ]

    def __getitem__(self, number):
        return self.places[number]

    def send(self, *numbers):
        for number in numbers:
            self.copies[number].start()

    def finish(self):
        wait_all(self.copies)


def staged(
    body, name, me, others, inputs, raw, outputs, direct=(), scratch=(), microseconds=10
):
    scalars = (me, *others)
    counts = (len(scalars), len(inputs), len(raw), len(outputs), len(direct))

    def kernel(*refs):
        parts, at = [], 0
        for count in counts:
            parts.append(refs[at : at + count])
            at += count
        scalar_refs, sources, raw_refs, targets, direct_refs = parts
        rest = refs[at:]
        in_places, rest = rest[: len(inputs)], rest[len(inputs) :]
        out_places, rest = rest[: len(outputs)], rest[len(outputs) :]
        in_sems, out_sems, rest = rest[0], rest[1], rest[2:]
        body(
            scalar_refs,
            Inputs(sources, in_places, in_sems),
            raw_refs,
            Outputs(out_places, targets, out_sems),
            direct_refs,
            *rest,
        )

    return pl.pallas_call(
        kernel,
        out_shape=(*outputs, *direct),
        in_specs=smem(len(scalars)) + hbm(len(inputs) + len(raw)),
        out_specs=tuple(hbm(len(outputs) + len(direct))),
        scratch_shapes=[
            *(pltpu.VMEM(array.shape, array.dtype) for array in inputs),
            *(pltpu.VMEM(array.shape, array.dtype) for array in outputs),
            pltpu.SemaphoreType.DMA((max(len(inputs), 1),)),
            pltpu.SemaphoreType.DMA((max(len(outputs), 1),)),
            *scratch,
        ],
        compiler_params=params(LIMITS[name]),
        cost_estimate=cost(microseconds),
        name=name,
    )(*scalars, *inputs, *raw)


def weight_scratch(width):
    return [pltpu.VMEM((2, *slab_shape(width)), BF16), pltpu.SemaphoreType.DMA((2, 4))]


def grad_scratch(width):
    return [pltpu.VMEM((2, *slab_shape(width)), BF16), pltpu.SemaphoreType.DMA((2, 2))]


def grad_pieces(width):
    return (shaped((4, SLAB, width), BF16),) * 4


def spread_kinds(w_vmem, w_flat, member):
    part = w_vmem.shape[4] // 4
    for kind in range(4):
        w_flat[:, pl.ds((kind * 2 + member) * part, part)] = flat(
            w_vmem[member, :, :, :, kind * part : (kind + 1) * part]
        )


def store_kind(dw_vmem, kind, grads):
    part = dw_vmem.shape[4] // 4
    for member in range(2):
        dw_vmem[member, :, :, :, kind * part : (kind + 1) * part] = (
            grads[:, member * part : (member + 1) * part].astype(BF16).reshape(slab_shape(part))
        )


def gain_of(norms, number):
    return norms[2 * number : 2 * number + 1, :]


def shift_of(norms, number):
    return norms[2 * number + 1 : 2 * number + 2, :]


def both(own_ref, sib_ref):
    return own_ref[...].astype(F32) + sib_ref[...].astype(F32)


def store_norm_grads(outs, number, dy, xhat):
    dgain, dshift = norm_param_grads(dy, xhat)
    outs[number][0:1, :] = dgain
    outs[number][1:2, :] = dshift
    outs.send(number)


def lanes_at(block):
    return pl.ds(pl.multiple_of(block * BLOCK, BLOCK), BLOCK)


def store_halves(target, at, pair, values):
    target[pl.ds(pair * PAIR, HEAD_DIM), at] = values[:HEAD_DIM, :BLOCK]
    target[pl.ds(pair * PAIR + HEAD_DIM, HEAD_DIM), at] = values[HEAD_DIM:, BLOCK:]


def self_forward(me, chip, which, segk, weights):
    pieces, offset = weights
    width = chip[0].shape[1]
    rows = 2 * (chip[0].shape[0] // 3)
    keys = rows + 2 * BLOCK
    here = width // 2
    blocks, pairs, window = rows // BLOCK, here // PAIR, 3 * BLOCK

    def body(scalars, ins, raw, outs, direct, w_vmem, w_sems, x_sems, x_s, w_s, vt_s, ctxt_s):
        me_ref = scalars[0]
        x_copies = haloed_copies(me_ref, raw[:3], which, x_s, x_sems)
        start_all([x_copies])
        copies = weight_copies(me_ref, raw[3:], offset, w_vmem, w_sems)
        start_all(copies)
        ins.start(0)
        part_o, q_o, k_o, v_o, ctx_o, pt_o = outs.places
        segments = ins[0][...]
        columns = segments.T
        for member in range(2):
            wait_all(copies[member])
            spread_kinds(w_vmem, w_s, member)
        wait_all(x_copies)
        kv = mm(x_s[...], w_s[:, here : 3 * here]).astype(BF16)
        k_o[...] = kv[:, :here]
        v_o[...] = kv[:, here:]
        outs.send(2, 3)
        vt_s[...] = kv[:, here:].T
        q = mm(x_s[BLOCK : BLOCK + rows, :], w_s[:, :here]).astype(BF16)
        q_o[...] = q * jnp.asarray(score_scale, BF16)
        outs.send(1)
        masks = half_masks()
        for block in range(blocks):
            at = pl.ds(block * BLOCK, BLOCK)
            keys_at = pl.ds(block * BLOCK, window)
            column = jnp.concatenate([columns[:, block + k : block + k + 1] for k in range(3)])
            row = segments[block + 1 : block + 2, :]
            allowed = column == jnp.concatenate([row, row], axis=1)
            for pair in range(pairs):
                cols = pl.ds(pair * PAIR, PAIR)
                stacked = stack_pair(q_o[at, cols], masks)
                scores = mm(k_o[keys_at, cols], stacked, NT)
                scores = jnp.where(allowed, scores, masked_score)
                highest = jnp.max(scores, axis=0, keepdims=True)
                raised = jnp.exp(scores - highest)
                total = jnp.sum(raised, axis=0, keepdims=True)
                probs = (raised * (1.0 / total)).astype(BF16)
                pt_o[block * pairs + pair] = probs
                store_halves(ctxt_s, at, pair, mm(vt_s[cols, keys_at], probs).astype(BF16))
        outs.send(5)
        context = ctxt_s[...].T
        ctx_o[...] = context
        outs.send(4)
        part_o[...] = mm(context, w_s[:, 3 * here :], NT).astype(BF16)
        outs.send(0)
        outs.finish()

    part, *saved = staged(
        body,
        "self_forward",
        me,
        (),
        (segk,),
        (*chip, *pieces),
        (
            shaped((rows, width), BF16),
            shaped((rows, here), BF16),
            shaped((keys, here), BF16),
            shaped((keys, here), BF16),
            shaped((rows, here), BF16),
            shaped((blocks * pairs, window, 2 * BLOCK), BF16),
        ),
        scratch=(
            *weight_scratch(width),
            pltpu.SemaphoreType.DMA((3,)),
            pltpu.VMEM((keys, width), BF16),
            pltpu.VMEM((width, 4 * here), BF16),
            pltpu.VMEM((here, keys), BF16),
            pltpu.VMEM((here, rows), BF16),
        ),
        microseconds=9,
    )
    return part, saved


def self_backward(me, dy, xhat, rstd, norms, k_norm, chip, which, saved, weights):
    pieces, offset = weights
    rows, width = xhat.shape
    keys = rows + 2 * BLOCK
    own = rows // 2
    here = width // 2
    blocks, pairs, window = rows // BLOCK, here // PAIR, 3 * BLOCK

    def body(
        scalars, ins, raw, outs, direct,
        w_vmem, w_sems, dw_s, dw_sems, x_sems, dx_sems,
        x_s, w_s, dctx_s, kt_s, dqt_s, dkv_s, dx_s, dtotal_s,
    ):
        me_ref = scalars[0]
        ins.start(0, 1, 2, 3, 4, 5)
        copies = weight_copies(me_ref, raw[3:], offset, w_vmem, w_sems)
        start_all(copies)
        ins.start(9, 7, 8, 10, 6)
        x_copies = haloed_copies(me_ref, raw[:3], which, x_s, x_sems)
        start_all([x_copies])
        out_copies = grad_copies(me_ref, dw_s, direct[:4], dw_sems)
        dtotal_o, keep_o, send_o = direct[4:]
        masks = half_masks()
        dy = ins[0][...] + both(ins[1], ins[2])
        xhat = ins[3][...]
        store_norm_grads(outs, 0, dy, xhat)
        dtotal = norm_backward(dy, xhat, ins[4][...], gain_of(ins[5], k_norm))
        dtotal_s[...] = dtotal
        low = dtotal.astype(BF16)
        for member in range(2):
            wait_all(copies[member])
            spread_kinds(w_vmem, w_s, member)
        dctx_s[...] = mm(low, w_s[:, 3 * here :]).astype(BF16)
        store_kind(dw_s, 3, mm(low.T, ins[9][...]))
        kt_s[...] = ins[7][...].T
        dkv_s[...] = jnp.zeros_like(dkv_s)
        q_ref, v_ref, pt_ref = ins[6], ins[8], ins[10]
        for block in range(blocks):
            at = pl.ds(block * BLOCK, BLOCK)
            keys_at = pl.ds(block * BLOCK, window)
            for pair in range(pairs):
                cols = pl.ds(pair * PAIR, PAIR)
                dstacked = stack_pair(dctx_s[at, cols], masks)
                qstacked = stack_pair(q_ref[at, cols], masks)
                probs_low = pt_ref[block * pairs + pair]
                probs = probs_low.astype(F32)
                dprobs = mm(v_ref[keys_at, cols], dstacked, NT)
                delta = jnp.sum(probs * dprobs, axis=0, keepdims=True)
                dscores = (probs * (dprobs - delta)).astype(BF16)
                dkv_s[keys_at, cols] += mm(dscores, qstacked)
                dkv_s[keys_at, pl.ds(here + pair * PAIR, PAIR)] += mm(probs_low, dstacked)
                dqt = mm(kt_s[cols, keys_at], dscores) * score_scale
                store_halves(dqt_s, at, pair, dqt.astype(BF16))
        dq = dqt_s[...].T
        dkv = dkv_s[...].astype(BF16)
        wait_all(x_copies)
        xt = x_s[...].T
        store_kind(dw_s, 0, mm(xt[:, BLOCK : BLOCK + rows], dq))
        dw = mm(xt, dkv)
        store_kind(dw_s, 1, dw[:, :here])
        store_kind(dw_s, 2, dw[:, here:])
        start_all(out_copies)
        dx_s[...] = mm(dkv, w_s[:, here : 3 * here], NT).astype(BF16)
        middle = pl.ds(BLOCK, rows)
        dx_s[middle, :] = (dx_s[middle, :].astype(F32) + mm(dq, w_s[:, :here], NT)).astype(BF16)
        first = me_ref[4] * own
        other = (1 - me_ref[4]) * own
        halo = halo_place(me_ref, dx_s, 1)
        moves = [
            (dtotal_s.at[row_at(first, own)], dtotal_o),
            (dx_s.at[row_at(BLOCK + first, own)], keep_o.at[pl.ds(0, own)]),
            (dx_s.at[halo], keep_o.at[pl.ds(own, BLOCK)]),
            (dx_s.at[row_at(BLOCK + other, own)], send_o.at[pl.ds(0, own)]),
            (dx_s.at[halo], send_o.at[pl.ds(own, BLOCK)]),
        ]
        dx_copies = [
            pltpu.make_async_copy(source, target, dx_sems.at[number])
            for number, (source, target) in enumerate(moves)
        ]
        start_all([dx_copies])
        outs.finish()
        wait_all(dx_copies)
        for group in out_copies:
            wait_all(group)

    swapped = shaped((own + BLOCK, width), BF16)
    dnorm, *results = staged(
        body,
        "self_backward",
        me,
        (),
        (*dy, xhat, rstd, norms, *saved),
        (*chip, *pieces),
        (shaped((2, width), F32),),
        direct=(*grad_pieces(width), shaped((own, width), F32), swapped, swapped),
        scratch=(
            *weight_scratch(width),
            *grad_scratch(width),
            pltpu.SemaphoreType.DMA((3,)),
            pltpu.SemaphoreType.DMA((5,)),
            pltpu.VMEM((keys, width), BF16),
            pltpu.VMEM((width, 4 * here), BF16),
            pltpu.VMEM((rows, here), BF16),
            pltpu.VMEM((here, keys), BF16),
            pltpu.VMEM((here, rows), BF16),
            pltpu.VMEM((keys, 2 * here), F32),
            pltpu.VMEM((keys, width), BF16),
            pltpu.VMEM((rows, width), F32),
        ),
        microseconds=12,
    )
    return dnorm, results[:4], results[4], results[5], results[6]


def memory_copies(me_ref, pieces, m_s, sems):
    rows = pieces[0].shape[0]
    return [
        pltpu.make_async_copy(
            piece, m_s.at[row_at((me_ref[2] ^ member) * rows, rows)], sems.at[member]
        )
        for member, piece in enumerate(pieces)
    ]


WINDOW = 3 * BLOCK


def chunk_range(range_ref, blocks):
    size = WINDOW // BLOCK
    return range_ref[0] // size, (range_ref[2 * blocks - 1] + size - 1) // size


def fresh_keys(start, last_start):
    key = lax.broadcasted_iota(jnp.int32, (WINDOW, 1), 0)
    return key >= (start - jnp.minimum(start, last_start)) * BLOCK


def cross_forward(me, ranges, chip, which, part_own, part_sib, norms, k_in, segq, segk, memory, weights):
    pieces, offset = weights
    rows, width = part_own.shape
    own = rows // 2
    here = width // 2
    keys = 2 * rows
    blocks, pairs = rows // BLOCK, here // PAIR

    def body(
        scalars, ins, raw, outs, direct,
        w_vmem, w_sems, x_sems, m_sems, x_s, m_s, w_s, vt_s, acc_s, ctxt_s, seg_s, stat_s,
    ):
        me_ref, range_ref = scalars
        x_copies = chip_copies(
            me_ref,
            raw[0].at[pl.ds(which * own, own)],
            raw[1].at[pl.ds(which * own, own)],
            x_s,
            0,
            x_sems,
        )
        start_all([x_copies])
        ins.start(0, 1, 2)
        copies = weight_copies(me_ref, raw[6:], offset, w_vmem, w_sems)
        start_all(copies)
        m_copies = memory_copies(me_ref, raw[2:6], m_s, m_sems)
        start_all([m_copies])
        ins.start(3, 4)
        part_o, xhat_o, rstd_o, q_o, k_o, v_o, ctx_o, lse_o = outs.places
        masks = half_masks()
        wait_all(x_copies)
        xhat, rstd = normalize(x_s[...].astype(F32) + both(ins[0], ins[1]))
        xhat_o[...] = xhat
        rstd_o[...] = rstd
        outs.send(1, 2)
        inputs = xhat * gain_of(ins[2], k_in) + shift_of(ins[2], k_in)
        for member in range(2):
            wait_all(copies[member])
            spread_kinds(w_vmem, w_s, member)
        q = mm(inputs.astype(BF16), w_s[:, :here]).astype(BF16)
        q_o[...] = q * jnp.asarray(score_scale, BF16)
        outs.send(3)
        ins[3]
        columns = ins[4][...].T
        for block in range(keys // BLOCK):
            seg_s[pl.ds(block * BLOCK, BLOCK), :] = columns[:, block : block + 1]
        wait_all(m_copies)

        @pl.loop(*chunk_range(range_ref, blocks))
        def _(chunk):
            keys_at = row_at(chunk * WINDOW, WINDOW)
            kv = mm(m_s[keys_at, :], w_s[:, here : 3 * here]).astype(BF16)
            k_o[keys_at, :] = kv[:, :here]
            v_o[keys_at, :] = kv[:, here:]
            vt_s[:, keys_at] = kv[:, here:].T

        outs.send(4, 5)
        size = WINDOW // BLOCK
        last_start = (chunk_range(range_ref, blocks)[1] - 1) * size

        @pl.loop(0, blocks)
        def _(block):
            at = lanes_at(block)
            first, last = range_ref[2 * block], range_ref[2 * block + 1]
            row = ins[3][pl.ds(block + 1, 1), :]
            segq_row = jnp.concatenate([row, row], axis=1)

            def window_scores(start):
                keys_at = row_at(start * BLOCK, WINDOW)
                allowed = seg_s[keys_at, :] == segq_row
                result = []
                for pair in range(pairs):
                    cols = pl.ds(pair * PAIR, PAIR)
                    scores = mm(k_o[keys_at, cols], stack_pair(q_o[at, cols], masks), NT)
                    result.append(jnp.where(allowed, scores, masked_score))
                return keys_at, result

            keys_at, scores = window_scores(jnp.minimum(first, last_start))
            for pair in range(pairs):
                highest = jnp.max(scores[pair], axis=0, keepdims=True)
                raised = jnp.exp(scores[pair] - highest)
                total = jnp.sum(raised, axis=0, keepdims=True)
                acc_s[pair] = mm(vt_s[pl.ds(pair * PAIR, PAIR), keys_at], raised.astype(BF16))
                stat_s[2 * pair : 2 * pair + 1, :] = highest
                stat_s[2 * pair + 1 : 2 * pair + 2, :] = total

            @pl.loop(1, (last - first + size - 1) // size)
            def _(number):
                start = first + number * size
                keys_at, scores = window_scores(jnp.minimum(start, last_start))
                fresh = fresh_keys(start, last_start)
                for pair in range(pairs):
                    kept = jnp.where(fresh, scores[pair], masked_score)
                    before = stat_s[2 * pair : 2 * pair + 1, :]
                    highest = jnp.maximum(before, jnp.max(kept, axis=0, keepdims=True))
                    shrink = jnp.exp(before - highest)
                    raised = jnp.where(kept > 0.5 * masked_score, jnp.exp(kept - highest), 0.0)
                    acc_s[pair] = acc_s[pair] * shrink + mm(
                        vt_s[pl.ds(pair * PAIR, PAIR), keys_at], raised.astype(BF16)
                    )
                    stat_s[2 * pair : 2 * pair + 1, :] = highest
                    stat_s[2 * pair + 1 : 2 * pair + 2, :] = stat_s[
                        2 * pair + 1 : 2 * pair + 2, :
                    ] * shrink + jnp.sum(raised, axis=0, keepdims=True)

            for pair in range(pairs):
                total = stat_s[2 * pair + 1 : 2 * pair + 2, :]
                store_halves(ctxt_s, at, pair, (acc_s[pair] * (1.0 / total)).astype(BF16))
                lse_o[pl.ds(block * pairs + pair, 1), :] = stat_s[
                    2 * pair : 2 * pair + 1, :
                ] + jnp.log(total)

        context = ctxt_s[...].T
        ctx_o[...] = context
        outs.send(6, 7)
        part_o[...] = mm(context, w_s[:, 3 * here :], NT).astype(BF16)
        outs.send(0)
        outs.finish()

    part, xhat, rstd, *saved = staged(
        body,
        "cross_forward",
        me,
        (ranges,),
        (part_own, part_sib, norms, segq, segk),
        (*chip[:2], *memory, *pieces),
        (
            shaped((rows, width), BF16),
            shaped((rows, width), F32),
            shaped((rows, 1), F32),
            shaped((rows, here), BF16),
            shaped((keys, here), BF16),
            shaped((keys, here), BF16),
            shaped((rows, here), BF16),
            shaped((blocks * pairs, 2 * BLOCK), F32),
        ),
        scratch=(
            *weight_scratch(width),
            pltpu.SemaphoreType.DMA((2,)),
            pltpu.SemaphoreType.DMA((4,)),
            pltpu.VMEM((rows, width), BF16),
            pltpu.VMEM((keys, width), BF16),
            pltpu.VMEM((width, 4 * here), BF16),
            pltpu.VMEM((here, keys), BF16),
            pltpu.VMEM((pairs, PAIR, 2 * BLOCK), F32),
            pltpu.VMEM((here, rows), BF16),
            pltpu.VMEM((keys, 1), F32),
            pltpu.VMEM((8, 2 * BLOCK), F32),
        ),
        microseconds=10,
    )
    return part, xhat, rstd, saved


def cross_backward(
    me, ranges, dy, xhat, rstd, norms, k_norm, xin, k_in, segq, segk, saved, memory, weights
):
    pieces, offset = weights
    rows, width = xhat.shape
    half = rows // 2
    here = width // 2
    keys = 2 * rows
    blocks, pairs = rows // BLOCK, here // PAIR
    heads_here = here // HEAD_DIM

    def body(
        scalars, ins, raw, outs, direct,
        w_vmem, w_sems, dw_s, dw_sems, m_sems, dm_sems,
        m_s, w_s, dctx_s, kt_s, dqt_acc, dqt_s, dkv_s, dwkv_s, dm_s, seg_s, delta_s,
    ):
        me_ref, range_ref = scalars
        ins.start(0, 1, 2, 3, 4, 5)
        copies = weight_copies(me_ref, raw[4:], offset, w_vmem, w_sems)
        start_all(copies)
        ins.start(12, 10, 11, 9, 13, 7, 8, 6)
        m_copies = memory_copies(me_ref, raw[:4], m_s, m_sems)
        start_all([m_copies])
        out_copies = grad_copies(me_ref, dw_s, direct[:4], dw_sems)
        dm_keep, dm_send = direct[4:]
        part_o, dtotal_o, dnorm_o = outs.places
        norms_ref = ins[5]
        masks = half_masks()
        dy = ins[0][...] + both(ins[1], ins[2])
        xhat = ins[3][...]
        store_norm_grads(outs, 2, dy, xhat)
        dtotal = norm_backward(dy, xhat, ins[4][...], gain_of(norms_ref, k_norm))
        dtotal_o[...] = dtotal
        outs.send(1)
        low = dtotal.astype(BF16)
        for member in range(2):
            wait_all(copies[member])
            spread_kinds(w_vmem, w_s, member)
        dctx = mm(low, w_s[:, 3 * here :]).astype(BF16)
        dctx_s[...] = dctx
        context = ins[12][...]
        store_kind(dw_s, 3, mm(low.T, context))
        products = (dctx.astype(F32) * context.astype(F32)).T
        for head in range(heads_here):
            delta_s[head : head + 1, :] = jnp.sum(
                products[head * HEAD_DIM : (head + 1) * HEAD_DIM, :], axis=0, keepdims=True
            )
        k_ref, v_ref, q_ref, lse_ref = ins[10], ins[11], ins[9], ins[13]
        ins[7]
        columns = ins[8][...].T
        for block in range(keys // BLOCK):
            seg_s[pl.ds(block * BLOCK, BLOCK), :] = columns[:, block : block + 1]

        @pl.loop(*chunk_range(range_ref, blocks))
        def _(chunk):
            keys_at = row_at(chunk * WINDOW, WINDOW)
            kt_s[:, keys_at] = k_ref[keys_at, :].T
            dkv_s[keys_at, :] = jnp.zeros((WINDOW, 2 * here), F32)

        size = WINDOW // BLOCK
        last_start = (chunk_range(range_ref, blocks)[1] - 1) * size

        @pl.loop(0, blocks)
        def _(block):
            at = lanes_at(block)
            first, last = range_ref[2 * block], range_ref[2 * block + 1]
            row = ins[7][pl.ds(block + 1, 1), :]
            segq_row = jnp.concatenate([row, row], axis=1)
            dqt_acc[...] = jnp.zeros_like(dqt_acc)

            @pl.loop(0, (last - first + size - 1) // size)
            def _(number):
                start = first + number * size
                keys_at = row_at(jnp.minimum(start, last_start) * BLOCK, WINDOW)
                allowed = jnp.logical_and(
                    seg_s[keys_at, :] == segq_row, fresh_keys(start, last_start)
                )
                for pair in range(pairs):
                    cols = pl.ds(pair * PAIR, PAIR)
                    qstacked = stack_pair(q_ref[at, cols], masks)
                    dstacked = stack_pair(dctx_s[at, cols], masks)
                    delta = jnp.concatenate(
                        [delta_s[2 * pair : 2 * pair + 1, at], delta_s[2 * pair + 1 : 2 * pair + 2, at]],
                        axis=1,
                    )
                    scores = mm(k_ref[keys_at, cols], qstacked, NT)
                    scores = jnp.where(allowed, scores, masked_score)
                    probs = jnp.exp(scores - lse_ref[pl.ds(block * pairs + pair, 1), :])
                    dprobs = mm(v_ref[keys_at, cols], dstacked, NT)
                    dscores = (probs * (dprobs - delta)).astype(BF16)
                    dkv_s[keys_at, cols] += mm(dscores, qstacked)
                    dkv_s[keys_at, pl.ds(here + pair * PAIR, PAIR)] += mm(
                        probs.astype(BF16), dstacked
                    )
                    dqt_acc[pair] += mm(kt_s[cols, keys_at], dscores)

            for pair in range(pairs):
                store_halves(dqt_s, at, pair, (dqt_acc[pair] * score_scale).astype(BF16))

        dq = dqt_s[...].T
        part_o[...] = mm(dq, w_s[:, :here], NT).astype(BF16)
        outs.send(0)
        inputs = (ins[6][...] * gain_of(norms_ref, k_in) + shift_of(norms_ref, k_in)).astype(BF16)
        store_kind(dw_s, 0, mm(inputs.T, dq))
        dm_s[...] = jnp.zeros_like(dm_s)
        dwkv_s[...] = jnp.zeros_like(dwkv_s)
        wait_all(m_copies)

        @pl.loop(*chunk_range(range_ref, blocks))
        def _(chunk):
            keys_at = row_at(chunk * WINDOW, WINDOW)
            dkv = dkv_s[keys_at, :].astype(BF16)
            dm_s[keys_at, :] = mm(dkv, w_s[:, here : 3 * here], NT).astype(BF16)
            dwkv_s[...] += mm(m_s[keys_at, :].T, dkv)

        dm_copies = [
            pltpu.make_async_copy(
                dm_s.at[row_at((me_ref[2] ^ member) * half, half), :],
                (dm_keep, dm_send)[member % 2].at[member // 2],
                dm_sems.at[member],
            )
            for member in range(4)
        ]
        start_all([dm_copies])
        store_kind(dw_s, 1, dwkv_s[:, :here])
        store_kind(dw_s, 2, dwkv_s[:, here:])
        start_all(out_copies)
        outs.finish()
        wait_all(dm_copies)
        for group in out_copies:
            wait_all(group)

    halves = shaped((2, half, width), BF16)
    part, dtotal, dnorm, *results = staged(
        body,
        "cross_backward",
        me,
        (ranges,),
        (*dy, xhat, rstd, norms, xin, segq, segk, *saved),
        (*memory, *pieces),
        (shaped((rows, width), BF16), shaped((rows, width), F32), shaped((2, width), F32)),
        direct=(*grad_pieces(width), halves, halves),
        scratch=(
            *weight_scratch(width),
            *grad_scratch(width),
            pltpu.SemaphoreType.DMA((4,)),
            pltpu.SemaphoreType.DMA((4,)),
            pltpu.VMEM((keys, width), BF16),
            pltpu.VMEM((width, 4 * here), BF16),
            pltpu.VMEM((rows, here), BF16),
            pltpu.VMEM((here, keys), BF16),
            pltpu.VMEM((pairs, PAIR, 2 * BLOCK), F32),
            pltpu.VMEM((here, rows), BF16),
            pltpu.VMEM((keys, 2 * here), F32),
            pltpu.VMEM((width, 2 * here), F32),
            pltpu.VMEM((keys, width), BF16),
            pltpu.VMEM((keys, 1), F32),
            pltpu.VMEM((8, rows), F32),
        ),
        microseconds=16,
    )
    return dtotal, part, dnorm, results[:4], results[4], results[5]


def gelu_and_slope(pre):
    square = pre * pre
    half = 0.5 * pre
    tanh = jnp.tanh(pre * (gelu_a + (gelu_a * gelu_b) * square))
    cdf = 0.5 + 0.5 * tanh
    slope = cdf + half * (1.0 - tanh * tanh) * (gelu_a + (3.0 * gelu_a * gelu_b) * square)
    return (pre * cdf).astype(BF16), slope.astype(BF16)


def feed_forward(me, base, part_own, part_sib, k_norm, weights, norms, norm_piece=None):
    pieces, offset = weights
    rows, width = part_own.shape
    own = rows // 2
    first = norm_piece is not None
    raw = (*base[0][:2], *pieces) if first else pieces
    inputs = (part_own, part_sib) if first else (part_own, part_sib, norms, base[0])

    def body(scalars, ins, raw, outs, direct, w_vmem, w_sems, *rest):
        me_ref = scalars[0]
        part_o, xhat_o, rstd_o = outs.places[:3]
        hidden, slope = outs.places[3:5], outs.places[5:7]
        if first:
            norm_s, norm_sems, x_s, x_sems, acc_s = rest
            which = base[1]
            x_copies = chip_copies(
                me_ref,
                raw[0].at[pl.ds(which * own, own)],
                raw[1].at[pl.ds(which * own, own)],
                x_s,
                0,
                x_sems,
            )
            start_all([x_copies])
            raw = raw[2:]
            norm_copies = weight_copies(me_ref, raw, norm_piece[1], norm_s, norm_sems)[0]
            start_all([norm_copies])
        else:
            (acc_s,) = rest
        ins.start(*range(len(inputs)))
        copies = weight_copies(me_ref, raw, offset, w_vmem, w_sems)
        start_all(copies)
        if first:
            wait_all(norm_copies)
            norms_ref = outs[7]
            norms_ref[...] = flat(norm_s[0]).astype(F32).T[: norms_ref.shape[0], :]
            outs.send(7)
            wait_all(x_copies)
            before = x_s[...].astype(F32)
        else:
            norms_ref = ins[2]
            before = ins[3][...] * gain_of(norms_ref, base[1]) + shift_of(norms_ref, base[1])
        xhat, rstd = normalize(before + both(ins[0], ins[1]))
        xhat_o[...] = xhat
        rstd_o[...] = rstd
        outs.send(1, 2)
        low = (xhat * gain_of(norms_ref, k_norm) + shift_of(norms_ref, k_norm)).astype(BF16)
        half = w_vmem.shape[4] // 2
        for member in range(2):
            wait_all(copies[member])
            hidden_low, slope_low = gelu_and_slope(mm(low, flat(w_vmem[member, :, :, :, :half])))
            hidden[member][...] = hidden_low
            slope[member][...] = slope_low
            outs.send(3 + member, 5 + member)
            product = mm(hidden_low, flat(w_vmem[member, :, :, :, half:]), NT)
            if member == 0:
                acc_s[...] = product
            else:
                part_o[...] = (acc_s[...] + product).astype(BF16)
        outs.send(0)
        outs.finish()

    piece = shaped((rows, width), BF16)
    results = staged(
        body,
        "feed_forward",
        me,
        (),
        inputs,
        raw,
        (
            piece,
            shaped((rows, width), F32),
            shaped((rows, 1), F32),
            *((piece,) * 4),
            *((shaped((16, width), F32),) if first else ()),
        ),
        scratch=(
            *weight_scratch(2 * width),
            *(
                (
                    pltpu.VMEM((2, *slab_shape(BLOCK)), BF16),
                    pltpu.SemaphoreType.DMA((2, 4)),
                    pltpu.VMEM((rows, width), BF16),
                    pltpu.SemaphoreType.DMA((2,)),
                )
                if first
                else ()
            ),
            pltpu.VMEM((rows, width), F32),
        ),
        microseconds=7,
    )
    return results[0], results[1], results[2], results[3:5], results[5:7], *results[7:]


def end_norm(me, xhat_before, k_before, part_own, part_sib, norms, k_norm):
    rows, width = part_own.shape
    own = rows // 2

    def body(scalars, ins, raw, outs, direct, x_s, one_s, two_s, sems):
        at = row_at(scalars[0][4] * own, own)
        copies = [
            pltpu.make_async_copy(source.at[at], place, sems.at[number])
            for number, (source, place) in enumerate(zip(raw, (x_s, one_s, two_s)))
        ]
        start_all([copies])
        ins.start(0)
        wait_all(copies)
        before = x_s[...] * gain_of(ins[0], k_before) + shift_of(ins[0], k_before)
        xhat, _ = normalize(before + both(one_s, two_s))
        outs[0][...] = (xhat * gain_of(ins[0], k_norm) + shift_of(ins[0], k_norm)).astype(BF16)
        outs.send(0)
        outs.finish()

    (out,) = staged(
        body,
        "end_norm",
        me,
        (),
        (norms,),
        (xhat_before, part_own, part_sib),
        (shaped((own, width), BF16),),
        scratch=(
            pltpu.VMEM((own, width), F32),
            pltpu.VMEM((own, width), BF16),
            pltpu.VMEM((own, width), BF16),
            pltpu.SemaphoreType.DMA((3,)),
        ),
        microseconds=2,
    )
    return out


def feed_backward(me, dy, parts, xin, k_in, k_out, norms, hidden, slope, weights, turning):
    pieces, offset = weights
    (dy_own, dy_sib), which = dy
    rows, width = xin.shape
    own = rows // 2

    def body(
        scalars, ins, raw, outs, direct, w_vmem, w_sems, dw_s, dw_sems, dy_s, dy_sems, acc_s, *rest
    ):
        me_ref = scalars[0]
        ins.start(0, 1, 2, 3)
        dy_copies = chip_copies(
            me_ref,
            raw[0].at[pl.ds(which * own, own)],
            raw[1].at[pl.ds(which * own, own)],
            dy_s,
            0,
            dy_sems,
        )
        start_all([dy_copies])
        copies = weight_copies(me_ref, raw[2:], offset, w_vmem, w_sems)
        for member in range(2):
            start_all([copies[member]])
            ins.start(6 + member, 4 + member)
        out_copies = grad_copies(me_ref, dw_s, direct[:4], dw_sems)
        part_o, dtotal_o, dnorm_o = outs.places
        norms_ref = ins[1]
        inputs = ins[0][...] * gain_of(norms_ref, k_in) + shift_of(norms_ref, k_in)
        gain = gain_of(norms_ref, k_out)
        xhat, rstd = normalize(inputs + both(ins[2], ins[3]))
        if turning:
            out_s, out_sems = rest
            out_s[...] = (xhat * gain + shift_of(norms_ref, k_out)).astype(BF16)
            out_copy = pltpu.make_async_copy(
                out_s.at[row_at(me_ref[4] * own, own)], direct[4], out_sems.at[0]
            )
            out_copy.start()
        wait_all(dy_copies)
        dy = dy_s[...].astype(F32)
        store_norm_grads(outs, 2, dy, xhat)
        dtotal = norm_backward(dy, xhat, rstd, gain)
        dtotal_o[...] = dtotal
        outs.send(1)
        low = dtotal.astype(BF16)
        lowt = low.T
        xt = inputs.astype(BF16).T
        half = w_vmem.shape[4] // 2
        for member in range(2):
            wait_all(copies[member])
            dhidden = mm(low, flat(w_vmem[member, :, :, :, half:]))
            dpre = (dhidden * ins[6 + member][...].astype(F32)).astype(BF16)
            dw_s[member, :, :, :, :half] = mm(xt, dpre).astype(BF16).reshape(slab_shape(half))
            dw_s[member, :, :, :, half:] = (
                mm(lowt, ins[4 + member][...]).astype(BF16).reshape(slab_shape(half))
            )
            start_all([out_copies[member]])
            product = mm(dpre, flat(w_vmem[member, :, :, :, :half]), NT)
            if member == 0:
                acc_s[...] = product
            else:
                part_o[...] = (acc_s[...] + product).astype(BF16)
        outs.send(0)
        outs.finish()
        for group in out_copies:
            wait_all(group)
        if turning:
            out_copy.wait()

    part, dtotal, dnorm, *results = staged(
        body,
        "feed_backward",
        me,
        (),
        (xin, norms, *parts, *hidden, *slope),
        (dy_own, dy_sib, *pieces),
        (shaped((rows, width), BF16), shaped((rows, width), F32), shaped((2, width), F32)),
        direct=(
            *grad_pieces(2 * width),
            *((shaped((own, width), BF16),) if turning else ()),
        ),
        scratch=(
            *weight_scratch(2 * width),
            *grad_scratch(2 * width),
            pltpu.VMEM((rows, width), BF16),
            pltpu.SemaphoreType.DMA((2,)),
            pltpu.VMEM((rows, width), F32),
            *(
                (pltpu.VMEM((rows, width), BF16), pltpu.SemaphoreType.DMA((1,)))
                if turning
                else ()
            ),
        ),
        microseconds=9,
    )
    return dtotal, part, dnorm, results[:4], *results[4:]


DP = ("z", "x")
MP = ("y", "c")
ALL = ("z", "x", "y", "c")


def is_cube():
    return tuple(lax.axis_size(axis) for axis in ALL) == (4, 2, 2, 2)


def swap(values, axis, distance=1):
    count = lax.axis_size(axis)
    return lax.ppermute(values, axis, [(i, i ^ distance) for i in range(count)])


def add(*terms):
    return sum(term.astype(F32) for term in terms)


def low_add(*terms):
    return add(*terms).astype(BF16)


def place_of(me_ref, at):
    return me_ref[0] ^ at[1] if isinstance(at, tuple) else at


def sum_kernel(sources, jobs, me_ref, *refs):
    inputs, outputs = refs[: len(sources)], refs[len(sources) : len(sources) + len(jobs)]
    places, sems = refs[len(sources) + len(jobs) : -1], refs[-1]
    copies = [
        pltpu.make_async_copy(ref.at[pl.ds(start, count)], place, sems.at[number])
        for number, (ref, place, (start, count)) in enumerate(zip(inputs, places, sources))
    ]
    start_all([copies])
    waited = set()
    for out, (_, slabs, turned, cut) in zip(outputs, jobs):
        for at, terms in enumerate(slabs):
            total = None
            for number, source_at in terms:
                if number not in waited:
                    waited.add(number)
                    copies[number].wait()
                value = places[number][place_of(me_ref, source_at), :, cut]
                if len(terms) > 1:
                    value = value.astype(F32)
                total = value if total is None else total + value
            out[place_of(me_ref, ("z", at)) if turned else at] = total.astype(out.dtype)


def sum_slabs(me, requests):
    arrays, sources, jobs = [], [], []
    for request_sources, request_jobs in requests:
        base = len(arrays)
        for array, start, count in request_sources:
            arrays.append(array)
            sources.append((start, count))
        for dtype, slabs, turned, cut in request_jobs:
            _, rows, width = request_sources[0][0].shape
            start, width = cut or (0, width)
            moved = tuple(tuple((base + number, at) for number, at in terms) for terms in slabs)
            out = shaped((len(slabs), rows, width), dtype)
            jobs.append((out, moved, turned, slice(start, start + width)))
    results = pl.pallas_call(
        functools.partial(sum_kernel, tuple(sources), tuple(jobs)),
        out_shape=tuple(job[0] for job in jobs),
        in_specs=smem(1) + hbm(len(arrays)),
        out_specs=tuple(vmem(len(jobs))),
        scratch_shapes=[
            *(
                pltpu.VMEM((count, *array.shape[1:]), array.dtype)
                for array, (_, count) in zip(arrays, sources)
            ),
            pltpu.SemaphoreType.DMA((len(arrays),)),
        ],
        compiler_params=params(),
        cost_estimate=cost(2),
        name="sum_slabs",
    )(me, *arrays)
    split, at = [], 0
    for _, request_jobs in requests:
        split.append(results[at : at + len(request_jobs)])
        at += len(request_jobs)
    return split


def gather_lines(shard, widths):
    starts = [sum(widths[:number]) for number in range(len(widths))]
    if not is_cube():
        yield ()
        return tuple(shard[:, at : at + width] for at, width in zip(starts, widths))
    over_z = yield tuple((shard, "z", k) for k in (1, 2, 3))
    return (
        yield (
            tuple((piece[None], 0, 1) for piece in (shard, *over_z)),
            tuple(
                (BF16, tuple(((k, 0),) for k in range(4)), True, cut) for cut in zip(starts, widths)
            ),
        )
    )


def gather_square(lines):
    if not is_cube():
        whole = lax.all_gather(lines, ("y", *DP), axis=0, tiled=True)
        whole = whole.reshape(2, 4, 2, SLAB, lines.shape[1])
        for _ in range(2):
            yield ()
        return (whole[0, :, 0], whole[0, :, 1], whole[1, :, 0], whole[1, :2, 1], whole[1, 2:, 1])
    over_x, over_y = yield ((lines, "x", 1), (lines, "y", 1))
    far_one, far_two = yield ((over_y[:2], "x", 1), (over_x[2:], "y", 1))
    return lines, over_x, over_y, far_one, far_two


def reduce_square(own, to_x, to_y, to_far):
    if not is_cube():
        yield ()
        return own, to_x, to_y, to_far
    arrived = yield ((to_x, "x", 1), (to_y, "y", 1), (to_far, ("x", "y"), 3))
    return (own, *arrived)


def reduce_lines(*groups):
    if not is_cube():
        sums = []
        for group in groups:
            whole = jnp.stack(group).reshape(2, 2, 4, SLAB, group[0].shape[2])
            whole = whole.transpose(0, 2, 1, 3, 4).reshape(2, 8 * SLAB, group[0].shape[2])
            part = lax.psum_scatter(whole, "y", scatter_dimension=0, tiled=True)
            sums.append(lax.psum_scatter(part[0], DP, scatter_dimension=0, tiled=True))
        yield ()
        sums = jnp.stack(sums).astype(F32)
        empty = jnp.zeros(sums.shape, BF16)
        return sums, (empty, empty, empty)
    lines = yield (
        tuple((array, 0, 4) for group in groups for array in group),
        tuple(
            (
                F32 if k == 0 else BF16,
                tuple(
                    tuple((4 * number + source, ("z", k)) for source in range(4))
                    for number in range(len(groups))
                ),
                False,
                None,
            )
            for k in range(4)
        ),
    )
    over_z = yield tuple((lines[k], "z", k) for k in (1, 2, 3))
    return lines[0], over_z


def finish_group(ended, number=0):
    own, over_z = ended
    return add(own[number], *(piece[number] for piece in over_z))


def one_stage(*jobs):
    return (yield jobs)


def memory_stages(values):
    over_y, over_c = yield ((values, "y", 1), (values, "c", 1))
    (over_both,) = yield ((over_y, "c", 1),)
    return values, over_c, over_y, over_both


def memory_grad_stages(keep, send):
    (got,) = yield ((send, "c", 1),)
    (over_y,) = yield ((low_add(keep[1], got[1]), "y", 1),)
    own = low_add(keep[0], got[0], over_y)
    (sib,) = yield ((own, "c", 1),)
    return own, sib


class Flow:
    def __init__(self, me, token):
        self.me = me
        self.moving = {}
        self.ended = {}
        self.token = token

    def sync(self, names, *values, begin=(), hold=()):
        arrived = [self.moving[name][1] for name in names]
        held = [self.moving[name][1] for name in hold]
        arrived, held, values, token = lax.optimization_barrier(
            (arrived, held, values, self.token)
        )
        for name, result in zip(hold, held):
            self.moving[name] = (self.moving[name][0], result)
        to_send, asked = {}, {}
        begun = [(name, stages, None) for name, stages in begin]
        moved = [(name, self.moving[name][0], result) for name, result in zip(names, arrived)]

        def move(name, stages, result):
            try:
                wanted = stages.send(result)
            except StopIteration as end:
                self.ended[name] = end.value
                self.moving.pop(name, None)
                return
            if wanted and isinstance(wanted[0][0], tuple):
                asked[name] = (stages, wanted)
            else:
                to_send[name] = (stages, wanted)

        for job in moved + begun:
            move(*job)
        if asked:
            names = list(asked)
            sums = sum_slabs(self.me, [asked[name][1] for name in names])
            for name, result in zip(names, sums):
                move(name, asked[name][0], result)
        operands = [[job[0] for job in jobs] for _, jobs in to_send.values()]
        operands, values, self.token = lax.optimization_barrier((operands, values, token))
        for sending, (name, (stages, jobs)) in zip(operands, to_send.items()):
            results = [
                swap(operand, axis, distance)
                for operand, (_, axis, distance) in zip(sending, jobs)
            ]
            self.moving[name] = (stages, results)
        return values


def sum_stages(values):
    if not is_cube():
        return (lax.psum(values, ALL), *((jnp.zeros_like(values),) * 3))
    values = values + swap(values, "c")
    one, two, three = swap(values, "y"), swap(values, "x"), swap(values, ("x", "y"), 3)
    values = (values + one) + (two + three)
    return (values, *(swap(values, "z", k) for k in (1, 2, 3)))


def pack(groups, widths, attention_in, attention_out, feed_in, feed_out, norm_columns):
    rows = attention_in.shape[1]
    inputs = (attention_in, attention_out, feed_in, feed_out, norm_columns)

    def kernel(*refs):
        sources, shards, places, sems = refs[:5], refs[5 : 5 + len(groups)], refs[-6:-1], refs[-1]
        ins = Inputs(sources, places, sems)
        ins.start(4, 0, 1, 2, 3)
        order = {"enc": 0, "self": 1, "cross": 2, "enc_feed": 0, "dec_feed": 1}
        for shard, names in zip(shards, groups):
            offset = 0
            for name in names:
                number = order.get(name)
                if name == "norms":
                    pieces = [ins[4][...]]
                elif name.endswith("feed"):
                    pieces = [ins[2][number], ins[3][number]]
                else:
                    pieces = [ins[0][3 * number + kind] for kind in range(3)] + [ins[1][number]]
                for piece in pieces:
                    shard[:, pl.ds(offset, piece.shape[1])] = piece.astype(BF16)
                    offset += piece.shape[1]

    return pl.pallas_call(
        kernel,
        out_shape=tuple(
            shaped((rows, sum(widths[name] for name in group)), BF16) for group in groups
        ),
        in_specs=hbm(5),
        out_specs=tuple(vmem(len(groups))),
        scratch_shapes=[
            *(pltpu.VMEM(array.shape, F32) for array in inputs),
            pltpu.SemaphoreType.DMA((5,)),
        ],
        compiler_params=params(60),
        cost_estimate=cost(2),
        name="pack",
    )(*inputs)


def close_kernel(*refs):
    own, far, others, norms = refs[0], refs[1:4], refs[4:8], refs[8:13]
    grad, payload = refs[13:]
    total = own[0] + sum(ref[0].astype(F32) for ref in far)
    grad[...] = total
    squares = jnp.sum(total * total)
    for other in others:
        squares = squares + jnp.sum(other[...] * other[...])
    for number, norm in enumerate(norms):
        payload[2 * number : 2 * number + 2, :] = 0.5 * norm[...]
    payload[10:, :] = jnp.full((payload.shape[0] - 10, payload.shape[1]), squares, F32)


def close(own, far, others, norms):
    return pl.pallas_call(
        close_kernel,
        out_shape=(shaped(own.shape[1:], F32), shaped((16, norms[0].shape[1]), F32)),
        in_specs=vmem(13),
        out_specs=tuple(vmem(2)),
        compiler_params=params(),
        cost_estimate=cost(2),
        name="close",
    )(own, *far, *others, *norms)


def adam_step(weights, first, second, grads, rate, decay):
    first_new = beta_one * first + (1.0 - beta_one) * grads
    second_new = beta_two * second + (1.0 - beta_two) * grads * grads
    first_hat = first_new / (1.0 - beta_one**STEP)
    second_hat = second_new / (1.0 - beta_two**STEP)
    weights_new = weights - rate * (first_hat / (jnp.sqrt(second_hat) + adam_eps) + decay * weights)
    return (weights_new, first_new, second_new)


def update_kernel(count, me_ref, *refs):
    sums, grads, refs = refs[:4], refs[4:9], refs[9:]
    masters, firsts, seconds = refs[:count], refs[count : 2 * count], refs[2 * count : 3 * count]
    refs = refs[3 * count :]
    news, new_firsts, new_seconds = refs[:count], refs[count : 2 * count], refs[2 * count : 3 * count]
    total_ref, norm_ref = refs[3 * count :]
    total = (sums[0][...] + sums[1][...]) + (sums[2][...] + sums[3][...])
    total_ref[...] = total
    norm_grads = total[:10]
    squares = total[10:11, :BLOCK] + jnp.sum(norm_grads * norm_grads)
    grad_norm = jnp.sqrt(squares)
    norm_ref[...] = grad_norm
    factor = clip_bound / jnp.maximum(grad_norm[:, :1], clip_bound)
    part = masters[0].shape[2]
    half = masters[2].shape[2]
    attention, feed = grads[:3], grads[3:]

    def step(number, at, grad, rate=rate_matrix, decay=weight_decay):
        results = adam_step(
            masters[number][at], firsts[number][at], seconds[number][at], grad * factor, rate, decay
        )
        for target, value in zip((news, new_firsts, new_seconds), results):
            target[number][at] = value

    for number in range(3):
        for kind in range(3):
            step(0, 3 * number + kind, attention[number][:, kind * part : (kind + 1) * part])
        step(1, number, attention[number][:, 3 * part :])
    for number in range(2):
        step(2, number, feed[number][:, :half])
        step(3, number, feed[number][:, half:])
    if count == 5:
        own = total_ref[:, pl.ds(pl.multiple_of(me_ref[0] * BLOCK, BLOCK), BLOCK)]
        columns = masters[4].shape[2]
        own = jnp.where(me_ref[1] == 0, own[:, :columns], own[:, columns:])
        for number in range(5):
            step(4, number, own[2 * number : 2 * number + 2], rate_norm, 0.0)


def update(me, sums, grads, masters, firsts, seconds):
    count = len(masters)
    states = (*masters, *firsts, *seconds)
    *results, total, grad_norm = pl.pallas_call(
        functools.partial(update_kernel, count),
        out_shape=(
            *(shaped(array.shape, F32) for array in states),
            shaped(sums[0].shape, F32),
            shaped((1, BLOCK), F32),
        ),
        in_specs=smem(1) + vmem(9 + len(states)),
        out_specs=tuple(vmem(len(states) + 2)),
        compiler_params=params(24),
        cost_estimate=cost(4),
        name="update",
    )(me, *sums, *grads, *states)
    split = [results[k * count : (k + 1) * count] for k in range(3)]
    return split, total, grad_norm[0, 0]


EARLY = ("enc", "enc_feed", "norms")
MIDDLE = ("self", "cross")
LATE = ("dec_feed",)


def on_device(
    encoder_input, decoder_copy, decoder_target, decoder_cotangent,
    source_segments, target_segments, glance_mask,
    attention_in, attention_out, feed_in, feed_out, norm_params,
    attention_in_first, attention_out_first, feed_in_first, feed_out_first, norm_params_first,
    attention_in_second, attention_out_second, feed_in_second, feed_out_second, norm_params_second,
):
    rows, width = encoder_input.shape
    length = source_segments.shape[1]
    part, half = attention_in.shape[2], feed_in.shape[2]
    chip_y, core = lax.axis_index("y"), lax.axis_index("c")
    here = (lax.axis_index("z"), lax.axis_index("x")) if is_cube() else (0, 0)
    me = jnp.stack([jnp.int32(value) for value in (*here, 2 * chip_y + core, chip_y, core)])
    flow = Flow(me, jnp.zeros((8, BLOCK), F32) + norm_params[0, 0, 0])

    def turned(array):
        return array.transpose(0, 2, 1)

    masters = (attention_in, turned(attention_out), feed_in, turned(feed_out), norm_params)
    firsts = (
        attention_in_first, turned(attention_out_first), feed_in_first, turned(feed_out_first),
        norm_params_first,
    )
    seconds = (
        attention_in_second, turned(attention_out_second), feed_in_second,
        turned(feed_out_second), norm_params_second,
    )
    norm_columns = jnp.pad(norm_params.reshape(10, -1).T, ((0, 0), (0, BLOCK - 10)))
    widths = {
        "enc": 4 * part, "self": 4 * part, "cross": 4 * part, "norms": BLOCK,
        "enc_feed": 2 * half, "dec_feed": 2 * half,
    }
    shard_early, shard_rest, shard_late = pack((EARLY, MIDDLE, LATE), widths, *masters[:4], norm_columns)
    weight_places = {}
    for group in (EARLY, MIDDLE, LATE):
        offset = 0
        for name in group:
            weight_places[name] = (group, offset)
            offset += widths[name]

    def weights(name):
        group, offset = weight_places[name]
        return (flow.ended[group], offset)

    picked = glance_mask[0] == 1
    decoder_input = jnp.where(picked[:, None], decoder_target, decoder_copy)
    own_rows = jnp.concatenate([encoder_input, decoder_input, decoder_cotangent])

    chip_rows = 2 * rows
    blocks = chip_rows // BLOCK
    source_row = source_segments[0].astype(F32)
    target_row = target_segments[0].astype(F32)

    def chip_segments(row):
        padded = jnp.pad(row, (BLOCK, BLOCK), constant_values=-1.0)
        own = lax.dynamic_slice(padded, (chip_y * chip_rows,), (chip_rows + 2 * BLOCK,))
        return own.reshape(blocks + 2, BLOCK)

    source_chip, target_chip = chip_segments(source_row), chip_segments(target_row)
    source_all = jnp.pad(source_row.reshape(length // BLOCK, BLOCK), ((0, 16 - length // BLOCK), (0, 0)))
    lowest, highest = target_chip[1:-1, 0], target_chip[1:-1, BLOCK - 1]
    first_key = jnp.sum((source_row[None, :] < lowest[:, None]).astype(jnp.int32), axis=1)
    last_key = jnp.sum((source_row[None, :] <= highest[:, None]).astype(jnp.int32), axis=1)
    ranges = jnp.stack([first_key // BLOCK, (last_key + BLOCK - 1) // BLOCK], axis=1)
    ranges = ranges.astype(jnp.int32).reshape(2 * blocks)

    group_widths = [sum(widths[name] for name in group) for group in (EARLY, MIDDLE, LATE)]
    (shard_rest,) = flow.sync(
        [], shard_rest, begin=[("early_z", gather_lines(shard_early, group_widths[:1]))]
    )
    own_rows, shard_rest = flow.sync(["early_z"], own_rows, shard_rest)
    own_rows, shard_rest = flow.sync(
        [], own_rows, shard_rest, begin=[(EARLY, gather_square(*flow.ended["early_z"]))]
    )
    (own_rows,) = flow.sync(
        [],
        own_rows,
        begin=[
            ("rest_z", gather_lines(shard_rest, group_widths[1:2])),
            ("rows", one_stage((own_rows, "c", 1))),
        ],
    )
    (own_rows,) = flow.sync(["rows"], own_rows)
    (sib_rows,) = flow.ended["rows"]

    def edge(which):
        last = jnp.where(core == 1, own_rows[(which + 1) * rows - BLOCK : (which + 1) * rows],
                         sib_rows[(which + 1) * rows - BLOCK : (which + 1) * rows])
        first = jnp.where(core == 0, own_rows[which * rows : which * rows + BLOCK],
                          sib_rows[which * rows : which * rows + BLOCK])
        return jnp.where(chip_y == 0, last, first)

    edges = jnp.concatenate([edge(0), edge(1)])
    edges, source_chip, target_chip, ranges, source_all = flow.sync(
        [], edges, source_chip, target_chip, ranges, source_all
    )
    (edges,) = flow.sync([EARLY], edges, hold=["rest_z"])
    flow.sync([], begin=[("halo", one_stage((edges, "y", 1)))])
    flow.sync(["rest_z"])
    (lines_middle,) = flow.ended["rest_z"]
    flow.sync([EARLY, "halo"])
    chip = (own_rows, sib_rows, flow.ended["halo"][0])
    chip, source_chip, shard_late = flow.sync(
        [], chip, source_chip, shard_late, begin=[(MIDDLE, gather_square(lines_middle))]
    )
    chip, source_chip = flow.sync(
        [], chip, source_chip, begin=[("late_z", gather_lines(shard_late, group_widths[2:]))]
    )

    enc, dec, cot = 0, 1, 2
    part0, enc_saved = self_forward(me, chip, enc, source_chip, weights("enc"))
    (part0,) = flow.sync([], part0, hold=[MIDDLE, "late_z"])
    (part0,) = flow.sync([], part0, begin=[("part0", one_stage((part0, "c", 1)))])
    (part0,) = flow.sync(["part0", MIDDLE, "late_z"], part0)
    (lines_late,) = flow.ended["late_z"]
    part1, xhat0, rstd0, enc_hidden, enc_slope, norms = feed_forward(
        me, (chip, enc), part0, *flow.ended["part0"], 0, weights("enc_feed"), None, weights("norms")
    )
    (part1,) = flow.sync([], part1, hold=[MIDDLE])
    (part1,) = flow.sync([], part1, begin=[("part1", one_stage((part1, "c", 1)))])
    (part1,) = flow.sync(["part1", MIDDLE], part1)
    parts1 = (part1, *flow.ended["part1"])
    encoder_output = end_norm(me, xhat0, 0, *parts1, norms, 1)
    (target_chip,) = flow.sync(
        [], target_chip, begin=[("memory", memory_stages(encoder_output))]
    )
    part2, self_saved = self_forward(me, chip, dec, target_chip, weights("self"))
    (part2,) = flow.sync(["memory"], part2, begin=[("part2", one_stage((part2, "c", 1)))])
    (part2,) = flow.sync(
        ["memory", "part2"], part2, begin=[(LATE, gather_square(lines_late))]
    )
    memory = flow.ended["memory"]
    part3, xhat2, rstd2, cross_saved = cross_forward(
        me, ranges, chip, dec, part2, *flow.ended["part2"], norms, 2, target_chip, source_all,
        memory, weights("cross"),
    )
    (part3,) = flow.sync([], part3, hold=[LATE])
    (part3,) = flow.sync([LATE], part3, begin=[("part3", one_stage((part3, "c", 1)))])
    (part3,) = flow.sync(["part3", LATE], part3)
    part4, xhat3, rstd3, dec_hidden, dec_slope = feed_forward(
        me, (xhat2, 2), part3, *flow.ended["part3"], 3, weights("dec_feed"), norms
    )
    (part4,) = flow.sync([], part4, begin=[("part4", one_stage((part4, "c", 1)))])
    (part4,) = flow.sync(["part4"], part4)

    dtotal4, dpart4, dnorm4, pieces, decoder_output = feed_backward(
        me, (chip[:2], cot), (part4, *flow.ended["part4"]), xhat3, 3, 4, norms,
        dec_hidden, dec_slope, weights("dec_feed"), True,
    )
    (dtotal4,) = flow.sync([], dtotal4, begin=[("dpart4", one_stage((dpart4, "c", 1)))])
    (dtotal4,) = flow.sync(["dpart4"], dtotal4, begin=[("dec_feed", reduce_square(*pieces))])
    dtotal3, dpart3, dnorm3, pieces, dm_keep, dm_send = cross_backward(
        me, ranges, (dtotal4, dpart4, *flow.ended["dpart4"]), xhat3, rstd3, norms, 3, xhat2, 2,
        target_chip, source_all, cross_saved, memory, weights("cross"),
    )
    dpart3, dtotal3, dm_keep, dm_send = flow.sync(
        [], dpart3, dtotal3, dm_keep, dm_send, hold=["dec_feed"]
    )
    dpart3, dtotal3 = flow.sync(
        [],
        dpart3,
        dtotal3,
        begin=[
            ("memory_grad", memory_grad_stages(dm_keep, dm_send)),
            ("dpart3", one_stage((dpart3, "c", 1))),
        ],
    )
    dpart3, dtotal3 = flow.sync(
        ["memory_grad", "dpart3", "dec_feed"],
        dpart3,
        dtotal3,
        begin=[("cross", reduce_square(*pieces))],
    )
    dnorm2, pieces, dtotal2, dec_keep, dec_send = self_backward(
        me, (dtotal3, dpart3, *flow.ended["dpart3"]), xhat2, rstd2, norms, 2, chip, dec,
        self_saved, weights("self"),
    )
    (dtotal2,) = flow.sync(["memory_grad"], dtotal2, hold=["cross"])
    (dtotal2,) = flow.sync(
        ["memory_grad", "cross"],
        dtotal2,
        begin=[
            ("dec_feed", reduce_lines(flow.ended["dec_feed"])),
            ("self", reduce_square(*pieces)),
        ],
    )
    dmemory = flow.ended["memory_grad"]
    dmemory, dtotal2 = lax.optimization_barrier((dmemory, dtotal2))
    dtotal1, dpart1, dnorm1, pieces = feed_backward(
        me, (dmemory, 0), parts1, xhat0, 0, 1, norms, enc_hidden, enc_slope,
        weights("enc_feed"), False,
    )
    dpart1, dtotal1 = flow.sync([], dpart1, dtotal1, hold=["self", "dec_feed"])
    (dtotal1,) = flow.sync([], dtotal1, begin=[("dpart1", one_stage((dpart1, "c", 1)))])
    (dtotal1,) = flow.sync(
        ["dpart1", "dec_feed", "self"], dtotal1, begin=[("enc_feed", reduce_square(*pieces))]
    )
    (dtotal1,) = flow.sync(
        [],
        dtotal1,
        begin=[("pair", reduce_lines(flow.ended["self"], flow.ended["cross"]))],
    )
    dnorm0, pieces, dtotal0, enc_keep, enc_send = self_backward(
        me, (dtotal1, dpart1, *flow.ended["dpart1"]), xhat0, rstd0, norms, 0, chip, enc,
        enc_saved, weights("enc"),
    )
    both_send = jnp.concatenate([enc_send, dec_send])
    (both_send,) = flow.sync(
        [], both_send, hold=["enc_feed"], begin=[("enc", reduce_square(*pieces))]
    )
    (both_send,) = flow.sync(["enc_feed"], both_send)
    (both_send,) = flow.sync(
        [], both_send, begin=[("enc_feed", reduce_lines(flow.ended["enc_feed"]))]
    )
    (both_send,) = flow.sync(["pair"], both_send, hold=["enc", "enc_feed"])
    (both_send,) = flow.sync(["enc"], both_send)
    (both_send,) = flow.sync(
        [], both_send, begin=[("enc", reduce_lines(flow.ended["enc"]))]
    )
    flow.sync([], begin=[("rows_grad", one_stage((both_send, "c", 1)))])
    flow.sync(["rows_grad"])
    (got,) = flow.ended["rows_grad"]
    swapped = rows + BLOCK
    enc_rows = add(enc_keep, got[:swapped])
    dec_rows = add(dec_keep, got[swapped:])
    halos = jnp.concatenate([enc_rows[rows:], dec_rows[rows:]]).astype(BF16)
    flow.sync([], begin=[("halo_grad", one_stage((halos, "y", 1)))])
    flow.sync(["enc_feed"])
    others = [
        finish_group(flow.ended["pair"], 0),
        finish_group(flow.ended["pair"], 1),
        finish_group(flow.ended["enc_feed"]),
        finish_group(flow.ended["dec_feed"]),
    ]
    others = flow.sync(["halo_grad"], *others)
    flow.sync(["enc"])
    (halos,) = flow.ended["halo_grad"]
    at_start = jnp.logical_and(chip_y == 1, core == 0)
    at_end = jnp.logical_and(chip_y == 0, core == 1)

    def input_grad(dtotal, summed, halo):
        halo = halo.astype(F32)
        first = jnp.where(at_start, halo, 0.0)
        last = jnp.where(at_end, halo, 0.0)
        spread = jnp.concatenate([first, jnp.zeros((rows - 2 * BLOCK, width), F32), last])
        return dtotal + summed[:rows] + spread

    encoder_input_grad = input_grad(dtotal0, enc_rows, halos[:BLOCK])
    decoder_input_grad = input_grad(dtotal2, dec_rows, halos[BLOCK:])

    own_enc, far_enc = flow.ended["enc"]
    g_enc, payload = close(own_enc, far_enc, others, (dnorm0, dnorm1, dnorm2, dnorm3, dnorm4))
    sums = sum_stages(payload)
    grads = (g_enc, others[0], others[1], others[2], others[3])
    if norm_params.shape[2] == BLOCK // 2 and is_cube():
        split, total, grad_norm = update(me, sums, grads, masters, firsts, seconds)
        results = list(zip(*split))
    else:
        split, total, grad_norm = update(me, sums, grads, masters[:4], firsts[:4], seconds[:4])
        results = list(zip(*split))
        columns = norm_params.shape[2]
        g_norms = lax.dynamic_slice(total, (0, lax.axis_index(DP) * columns), (10, columns))
        factor = clip_bound / jnp.maximum(grad_norm, clip_bound)
        g_norms = g_norms.reshape(norm_params.shape) * factor
        results.append(
            adam_step(norm_params, norm_params_first, norm_params_second, g_norms, rate_norm, 0.0)
        )
    results = [
        tuple(turned(value) for value in result) if number in (1, 3) else result
        for number, result in enumerate(results)
    ]
    return (
        encoder_output,
        decoder_output,
        encoder_input_grad,
        decoder_input_grad,
        grad_norm,
        *(result[0] for result in results),
        *(result[1] for result in results),
        *(result[2] for result in results),
    )


def solution(mesh):
    dp, mp = mesh.shape["dp"], mesh.shape["mp"]
    fine = Mesh(mesh.devices.reshape(dp // 2, 2, mp // 2, 2), ALL)
    tokens = P(ALL, None)
    columns = P(None, DP, MP)
    turned = P(None, MP, DP)
    states = (columns, turned, columns, turned, P(None, None, DP))
    return jax.shard_map(
        on_device,
        mesh=fine,
        in_specs=(
            *((tokens,) * 4),
            P(DP, None),
            P(DP, None),
            P(DP, MP),
            *states,
            *states,
            *states,
        ),
        out_specs=(*((tokens,) * 4), P(), *states, *states, *states),
        check_vma=False,
    )
```
